32 devices in a mesh: section: 2 (over core), rows: 8 (over z, y), cols: 2 (over x).
Axes of the slice: x: 2, y: 2, z: 4, core: 2. Of those that a mesh axis runs over, the one named last changes fastest.
Arguments:
- latent: bfloat16 [4, 16, 64, 384], P('section', ('rows', 'cols')), may hold values from -6 to 6
- cache_one: bfloat16 [2, 16, 64, 384], P(None, ('rows', 'cols')), may hold values from -6 to 6
- cache_two: bfloat16 [2, 16, 64, 384], P(None, ('rows', 'cols')), may hold values from -6 to 6
- cache_time: bfloat16 [2, 16, 64, 384], P(None, 'rows', 'cols'), may hold values from -6 to 6
- cache_three: bfloat16 [2, 32, 128, 192], P(None, 'rows', 'cols'), may hold values from -6 to 6
- cache_four: bfloat16 [2, 32, 128, 192], P(None, 'rows', 'cols'), may hold values from -6 to 6
- gain_one: float32 [384], replicated, may hold values from 0.25 to 1.75
- gain_two: float32 [384], replicated, may hold values from 0.25 to 1.75
- gain_three: float32 [192], replicated, may hold values from 0.25 to 1.75
- gain_four: float32 [192], replicated, may hold values from 0.25 to 1.75
- weight_one: bfloat16 [10368, 384], replicated, may hold values from -0.0625 to 0.0625
- weight_two: bfloat16 [10368, 384], replicated, may hold values from -0.0625 to 0.0625
- weight_time: bfloat16 [1152, 768], replicated, may hold values from -0.1875 to 0.1875
- weight_upsample: bfloat16 [3456, 192], replicated, may hold values from -0.109375 to 0.109375
- weight_three: bfloat16 [5184, 192], replicated, may hold values from -0.078125 to 0.078125
- weight_four: bfloat16 [5184, 192], replicated, may hold values from -0.078125 to 0.078125
Outputs:
- decoded: bfloat16 [8, 32, 128, 192], P('section', 'rows', 'cols')
The draws below stay inside these ranges and needn't reach their ends.
All inputs are finite; a program needn't handle non-finite values.
Results may differ from the reference program's by a relative error of at most 0.0085.
Values may be sent and summed in bfloat16 or wider, within the bound.
No kernel may reach another device: no remote copies, remote signals or barrier semaphores. Data moves between devices by JAX's collectives and lax.ppermute only.
A program may use at most 128 MiB of HBM per device.

```python
import jax
import jax.numpy as jnp
from jax import lax

C1 = 384
C2 = 192
W = 64
FRAMES = 4
H = 16
H2 = 32
W2 = 128


def block_scale(stream_key, dims, cuts, least, largest):
    def one(axis_at, parts):
        heights = jax.random.uniform(jax.random.fold_in(jax.random.fold_in(stream_key, 6), axis_at), (parts,), jnp.float32, least / len(cuts), largest / len(cuts))
        return jnp.repeat(jnp.exp(heights), dims[axis_at] // parts).reshape((-1,) + (1,) * (len(dims) - axis_at - 1))

    level = one(*cuts[0])
    for cut in cuts[1:]:
        level = level * one(*cut)
    return level


def scatter_about(stream_key, dims, width, reach, split=(), held_as=jnp.bfloat16):
    drawn = jax.random.normal(stream_key, dims, jnp.float32) * width
    if len(split) > 0:
        drawn = block_scale(stream_key, dims, split, -0.22, 0.18) * drawn
    return jnp.clip(drawn, min=-reach, max=reach).astype(held_as)


def setup_inputs(seed: int = 0) -> dict:
    seeds = jax.random.split(jax.random.key(seed), 17)
    return {
        "latent": scatter_about(seeds[0], (FRAMES, H, W, C1), 1.0, 6.0, ((0, 2), (1, 16))),
        "cache_one": scatter_about(seeds[1], (2, H, W, C1), 1.0, 6.0, ((1, 16),)),
        "cache_two": scatter_about(seeds[2], (2, H, W, C1), 1.0, 6.0, ((1, 16),)),
        "cache_time": scatter_about(seeds[3], (2, H, W, C1), 1.0, 6.0, ((1, 8), (2, 2))),
        "cache_three": scatter_about(seeds[4], (2, H2, W2, C2), 1.0, 6.0, ((1, 8), (2, 2))),
        "cache_four": scatter_about(seeds[5], (2, H2, W2, C2), 1.0, 6.0, ((1, 8), (2, 2))),
        "gain_one": jnp.clip(1.0 + 0.15 * jax.random.normal(seeds[6], (C1,), jnp.float32), 0.25, 1.75),
        "gain_two": jnp.clip(1.0 + 0.15 * jax.random.normal(seeds[7], (C1,), jnp.float32), 0.25, 1.75),
        "gain_three": jnp.clip(1.0 + 0.15 * jax.random.normal(seeds[8], (C2,), jnp.float32), 0.25, 1.75),
        "gain_four": jnp.clip(1.0 + 0.15 * jax.random.normal(seeds[9], (C2,), jnp.float32), 0.25, 1.75),
        "weight_one": scatter_about(seeds[10], (27 * C1, C1), (27 * C1) ** -0.5, 0.0625),
        "weight_two": scatter_about(seeds[11], (27 * C1, C1), (27 * C1) ** -0.5, 0.0625),
        "weight_time": scatter_about(seeds[12], (3 * C1, 2 * C1), (3 * C1) ** -0.5, 0.1875),
        "weight_upsample": scatter_about(seeds[13], (9 * C1, C2), (9 * C1) ** -0.5, 0.109375),
        "weight_three": scatter_about(seeds[14], (27 * C2, C2), (27 * C2) ** -0.5, 0.078125),
        "weight_four": scatter_about(seeds[15], (27 * C2, C2), (27 * C2) ** -0.5, 0.078125),
    }


EPSILON = 1e-06

def activate(inputs, scales):
    widened = inputs.astype(jnp.float32)
    scaled = widened * lax.rsqrt(lax.optimization_barrier(jnp.mean(widened * widened, axis=-1, keepdims=True)) + EPSILON) * scales
    return jax.nn.silu(scaled).astype(jnp.bfloat16)

def conv_ext(extended, weight, time_taps):
    outputs = extended.shape[0] - time_taps + 1
    height = extended.shape[1] - 2
    breadth = extended.shape[2] - 2
    pieces = [extended[offset_t:offset_t + outputs, offset_y:offset_y + height, offset_x:offset_x + breadth, :] for offset_t in range(time_taps) for offset_y in range(3) for offset_x in range(3)]
    columns = jnp.concatenate(pieces, axis=-1)
    matrix = columns.reshape(outputs * height * breadth, columns.shape[-1])
    product = jnp.dot(matrix, weight, preferred_element_type=jnp.float32)
    return product.reshape(outputs, height, breadth, weight.shape[1])

def conv_full(sequence, weight, time_taps):
    padded = jnp.pad(sequence, ((0, 0), (1, 1), (1, 1), (0, 0)))
    outputs = sequence.shape[0] - time_taps + 1

    def single(position):
        window = lax.dynamic_slice_in_dim(padded, position, time_taps, 0)
        return conv_ext(window, weight, time_taps)[0]
    return lax.map(single, jnp.arange(outputs, dtype=jnp.int32))

def time_mix(sequence, weight):
    outputs = sequence.shape[0] - 2
    columns = jnp.concatenate([sequence[offset:offset + outputs] for offset in range(3)], axis=-1)
    matrix = columns.reshape(-1, columns.shape[-1])
    product = jnp.dot(matrix, weight, preferred_element_type=jnp.float32)
    return product.reshape(columns.shape[:3] + (weight.shape[1],))

def alternate(mixture):
    channels = mixture.shape[-1] // 2
    paired = jnp.stack([mixture[..., :channels], mixture[..., channels:]], axis=1)
    return paired.reshape((2 * mixture.shape[0],) + mixture.shape[1:3] + (channels,))

def enlarge(frames):
    return jnp.repeat(jnp.repeat(frames, 2, axis=1), 2, axis=2)

def reference(latent, cache_one, cache_two, cache_time, cache_three, cache_four, gain_one, gain_two, gain_three, gain_four, weight_one, weight_two, weight_time, weight_upsample, weight_three, weight_four):
    normed_one = activate(latent, gain_one)
    middle_one = conv_full(jnp.concatenate([cache_one, normed_one], axis=0), weight_one, 3)
    normed_two = activate(middle_one, gain_two)
    closing_one = conv_full(jnp.concatenate([cache_two, normed_two], axis=0), weight_two, 3)
    blocked = (latent.astype(jnp.float32) + closing_one).astype(jnp.bfloat16)
    mixture = time_mix(jnp.concatenate([cache_time, blocked], axis=0), weight_time).astype(jnp.bfloat16)
    doubled = alternate(mixture)
    lifted = conv_full(enlarge(doubled), weight_upsample, 1).astype(jnp.bfloat16)
    normed_three = activate(lifted, gain_three)
    middle_two = conv_full(jnp.concatenate([cache_three, normed_three], axis=0), weight_three, 3)
    normed_four = activate(middle_two, gain_four)
    closing_two = conv_full(jnp.concatenate([cache_four, normed_four], axis=0), weight_four, 3)
    return (lifted.astype(jnp.float32) + closing_two).astype(jnp.bfloat16)
```

```python
import functools

import jax
import jax.numpy as jnp
from jax import lax
from jax.experimental import pallas as pl
from jax.experimental.pallas import tpu as pltpu
from jax.sharding import PartitionSpec as P

EPSILON = 1e-06
HALO = 4
LANES = 256


def swapped(value, axis):
    return lax.ppermute(value, axis, [(0, 1), (1, 0)])


def shifted(value, axis, steps):
    count = lax.axis_size(axis)
    initial, last = (max(0, -steps), min(count, count - steps))
    return lax.ppermute(value, axis, [(source, source + steps) for source in range(initial, last)])


def silu(scaled):
    half = scaled * 0.5
    return half * (1.0 + jnp.tanh(half))


def activate(values, gain, mask):
    mean = jnp.mean(values * values, axis=-1, keepdims=True)
    return silu(values * (lax.rsqrt(mean + EPSILON) * mask) * gain)


def activate_pairs(values, gain, mask):
    channels = values.shape[-1] // 2
    squares = values * values
    first = lax.broadcasted_iota(jnp.int32, (1, 2 * channels), 1) < channels
    total = jnp.sum(squares, axis=-1, keepdims=True)
    low = jnp.sum(jnp.where(first, squares, 0.0), axis=-1, keepdims=True)
    scale_low = lax.rsqrt(low / channels + EPSILON) * mask
    scale_high = lax.rsqrt((total - low) / channels + EPSILON) * mask
    return silu(values * jnp.where(first, scale_low, scale_high) * gain)


def decode_kernel(
    wide,
    low2,
    low1,
    own,
    high1,
    high2,
    time_ref,
    three_ref,
    four_ref,
    masks,
    gains,
    weight_one,
    weight_two,
    weight_time,
    weight_up,
    weight_three,
    weight_four,
    out_ref,
    w1,
    w2,
    wt,
    wu,
    w3,
    w4,
    acc,
    x1e,
    x1o,
    x2e,
    x2o,
    mixed,
    de,
    do,
    x3e,
    x3o,
    x4e,
    x4o,
    lifted_ref,
    sems,
):
    f32, bf16 = jnp.float32, jnp.bfloat16
    channels = own.shape[-1]
    frames = own.shape[0] - 4
    pieces = (low2, low1, own, high1, high2)
    copies_one = [
        pltpu.make_async_copy(
            weight_one.at[:, dx], w1.at[:, :, pl.ds(dx * channels, channels)], sems.at[dx]
        )
        for dx in range(3)
    ]
    copies_two = [
        pltpu.make_async_copy(
            weight_two.at[:, dx], w2.at[:, :, pl.ds(dx * channels, channels)], sems.at[3 + dx]
        )
        for dx in range(3)
    ]
    copy_time = pltpu.make_async_copy(weight_time, wt, sems.at[6])
    copy_up = pltpu.make_async_copy(weight_up, wu, sems.at[7])
    copy_three = pltpu.make_async_copy(weight_three, w3, sems.at[8])
    copy_four = pltpu.make_async_copy(weight_four, w4, sems.at[9])
    for copy in copies_one + copies_two + [copy_time, copy_up, copy_three, copy_four]:
        copy.start()

    def rows_of(refs, index):
        return jnp.concatenate([ref[index].astype(f32) for ref in refs], axis=0)

    def store(even, odd, slot, values, height):
        even[pl.ds(slot * (height * wide), height * wide), :] = values.astype(bf16)
        odd[pl.ds(slot * ((height - 2) * wide), (height - 2) * wide), :] = values[
            wide : (height - 1) * wide
        ].astype(bf16)

    def taps(even, odd, count, height, dt, dy):
        inner = (height - 2) * wide
        if dy == 1:
            parts = [odd[pl.ds((f + dt) * inner, inner), :] for f in range(count)]
        else:
            parts = [
                even[pl.ds((f + dt) * height * wide + dy * wide, inner), :] for f in range(count)
            ]
        return jnp.concatenate(parts, axis=0)

    def product(even, odd, count, height, weights):
        rows = count * (height - 2) * wide

        def column(n, carry):
            lanes = pl.ds(pl.multiple_of(n * LANES, LANES), LANES)
            total = None
            for first, last in ((0, 4), (4, 8), (8, 9)):
                left = jnp.concatenate(
                    [taps(even, odd, count, height, t // 3, t % 3) for t in range(first, last)],
                    axis=1,
                )
                right = weights[first:last, :, lanes].reshape((last - first) * channels, LANES)
                part = jnp.dot(left, right, preferred_element_type=f32)
                total = part if total is None else total + part
            acc[0:rows, lanes] = total
            return carry

        lax.fori_loop(0, weights.shape[-1] // LANES, column, 0)

    def gather_low(start, size):
        center = acc[pl.ds(start, size), channels : 2 * channels]
        before = acc[pl.ds(start, size), 0:channels]
        after = acc[pl.ds(start, size), 2 * channels : 3 * channels]
        return center + pltpu.roll(before, 1, 0) + pltpu.roll(after, size - 1, 0)

    def gather_pairs(start, size):
        center = acc[pl.ds(start, size), 0:channels]
        side = acc[pl.ds(start, size), channels : 2 * channels]
        first = lax.broadcasted_iota(jnp.int32, (1, channels), 1) < channels // 2
        return center + jnp.where(first, pltpu.roll(side, 1, 0), pltpu.roll(side, size - 1, 0))

    def aligned(index, size):
        return pl.multiple_of(index * size, 16)

    gain = [gains[i : i + 1, :] for i in range(4)]

    for f in range(2):
        store(x1e, x1o, f, rows_of(pieces, frames + f), 10)

    def norm_one(f, carry):
        values = activate(rows_of(pieces, f), gain[0], 1.0)
        store(x1e, x1o, f + 2, values, 10)
        return carry

    lax.fori_loop(0, frames, norm_one, 0)
    for copy in copies_one:
        copy.wait()
    product(x1e, x1o, frames, 10, w1)

    for f in range(2):
        store(x2e, x2o, f, rows_of(pieces, frames + 2 + f)[wide : 9 * wide], 8)

    def norm_two(f, carry):
        size = 8 * wide
        values = activate(gather_low(aligned(f, size), size), gain[1], masks[0:size, 0:1])
        store(x2e, x2o, f + 2, values, 8)
        return carry

    lax.fori_loop(0, frames, norm_two, 0)
    for copy in copies_two:
        copy.wait()
    product(x2e, x2o, frames, 8, w2)

    size = 6 * wide
    mixed[0 : 2 * size, :] = time_ref[...]

    def residual_one(f, carry):
        values = gather_low(aligned(f, size), size) + rows_of(pieces[1:4], f)
        mixed[pl.ds(aligned(f + 2, size), size), :] = values.astype(bf16)
        return carry

    lax.fori_loop(0, frames, residual_one, 0)
    copy_time.wait()

    def mix(n, carry):
        lanes = pl.ds(pl.multiple_of(n * LANES, LANES), LANES)
        left = jnp.concatenate(
            [mixed[pl.ds(t * size, frames * size), :] for t in range(3)], axis=1
        )
        acc[0 : frames * size, lanes] = jnp.dot(left, wt[:, lanes], preferred_element_type=f32)
        return carry

    lax.fori_loop(0, 2 * channels // LANES, mix, 0)

    def double(t, carry):
        mask = masks[wide : wide + size, 0:1]
        for half in range(2):
            values = acc[pl.ds(aligned(t, size), size), half * channels : (half + 1) * channels]
            store(de, do, 2 * t + half, values * mask, 6)
        return carry

    lax.fori_loop(0, frames, double, 0)
    copy_up.wait()

    count = 2 * frames
    for py in range(2):

        def enlarge(n, carry):
            lanes = pl.ds(pl.multiple_of(n * LANES, LANES), LANES)
            left = jnp.concatenate(
                [taps(de, do, count, 6, 0, py), taps(de, do, count, 6, 0, py + 1)], axis=1
            )
            right = wu[2 * py : 2 * py + 2, :, lanes].reshape(2 * channels, LANES)
            acc[py * count * 4 * wide : (py + 1) * count * 4 * wide, lanes] = jnp.dot(
                left, right, preferred_element_type=f32
            )
            return carry

        lax.fori_loop(0, 2 * channels // LANES, enlarge, 0)

    store(x3e, x3o, 0, three_ref[0].astype(f32), 8)
    store(x3e, x3o, 1, three_ref[1].astype(f32), 8)

    def norm_three(f, carry):
        part = 4 * wide
        values = [
            gather_pairs(pl.multiple_of(py * count * part + f * part, 16), part).astype(bf16)
            for py in range(2)
        ]
        values = [v.astype(f32) for v in values]
        rows = jnp.concatenate(
            [values[h % 2][(h // 2) * wide : (h // 2 + 1) * wide] for h in range(8)], axis=0
        )
        lifted_ref[pl.ds(aligned(f, part), part), :] = rows[2 * wide : 6 * wide]
        begin = 8 * wide
        store(x3e, x3o, f + 2, activate_pairs(rows, gain[2], masks[begin : 2 * begin, 0:1]), 8)
        return carry

    lax.fori_loop(0, count, norm_three, 0)
    copy_three.wait()
    product(x3e, x3o, count, 8, w3)

    store(x4e, x4o, 0, four_ref[0].astype(f32), 6)
    store(x4e, x4o, 1, four_ref[1].astype(f32), 6)

    def norm_four(f, carry):
        begin = 9 * wide
        values = gather_pairs(aligned(f, size), size)
        store(x4e, x4o, f + 2, activate_pairs(values, gain[3], masks[begin : begin + size, 0:1]), 6)
        return carry

    lax.fori_loop(0, count, norm_four, 0)
    copy_four.wait()
    product(x4e, x4o, count, 6, w4)

    def finish(f, carry):
        part = 4 * wide
        start = aligned(f, part)
        values = gather_pairs(start, part) + lifted_ref[pl.ds(start, part), :]
        values = pltpu.roll(values, part - HALO, 0)
        for y in range(4):
            inner = wide - 2 * HALO
            out_ref[f, y] = values[y * wide : y * wide + inner].astype(bf16)
        return carry

    lax.fori_loop(0, count, finish, 0)


def decode(pieces, time, three, four, masks, gains, weights):
    bf16, f32 = jnp.bfloat16, jnp.float32
    units, _, channels = pieces[0].shape
    frames = units - 4
    count = 2 * frames
    wide = pieces[0].shape[1] // 2
    weight_one, weight_two, weight_time, weight_up, weight_three, weight_four = weights
    padded_lanes = -(-3 * channels // LANES) * LANES
    vmem = pl.BlockSpec(memory_space=pltpu.VMEM)
    anywhere = pl.BlockSpec(memory_space=pl.ANY)

    def planes(slots, height):
        return [
            pltpu.VMEM((slots * height * wide, channels), bf16),
            pltpu.VMEM((slots * (height - 2) * wide, channels), bf16),
        ]

    return pl.pallas_call(
        functools.partial(decode_kernel, wide),
        out_shape=jax.ShapeDtypeStruct((count, 4, wide - 2 * HALO, channels), bf16),
        in_specs=[vmem] * 10 + [anywhere] * 6,
        out_specs=vmem,
        scratch_shapes=[
            pltpu.VMEM((9, channels, padded_lanes), bf16),
            pltpu.VMEM((9, channels, padded_lanes), bf16),
            pltpu.VMEM(weight_time.shape, bf16),
            pltpu.VMEM(weight_up.shape, bf16),
            pltpu.VMEM(weight_three.shape, bf16),
            pltpu.VMEM(weight_four.shape, bf16),
            pltpu.VMEM((2 * count * 4 * wide, padded_lanes), f32),
            *planes(frames + 2, 10),
            *planes(frames + 2, 8),
            pltpu.VMEM(((frames + 2) * 6 * wide, channels), bf16),
            *planes(count, 6),
            *planes(count + 2, 8),
            *planes(count + 2, 6),
            pltpu.VMEM((count * 4 * wide, channels), f32),
            pltpu.SemaphoreType.DMA((10,)),
        ],
        compiler_params=pltpu.CompilerParams(vmem_limit_bytes=60 * 1024 * 1024),
        name="decode",
    )(*pieces, time, three, four, masks, gains, *weights)


def pair_weights(weight, channels):
    taps = weight.reshape(9, 3, channels, channels)
    none = jnp.zeros_like(taps[:, 0])
    even = jnp.concatenate([taps[:, 1], taps[:, 0], none, taps[:, 2]], axis=-1)
    odd = jnp.concatenate([taps[:, 2], taps[:, 1], taps[:, 0], none], axis=-1)
    return jnp.concatenate([even, odd], axis=1)


def enlarge_weights(weight, channels):
    taps = weight.reshape(3, 3, -1, channels).astype(jnp.float32)
    rows = [taps[0], taps[1] + taps[2], taps[0] + taps[1], taps[2]]
    parts = [jnp.concatenate([r[1] + r[2], r[0] + r[1], r[0], r[2]], axis=-1) for r in rows]
    return jnp.stack(parts).astype(jnp.bfloat16)


def body(
    latent,
    cache_one,
    cache_two,
    cache_time,
    cache_three,
    cache_four,
    gain_one,
    gain_two,
    gain_three,
    gain_four,
    weight_one,
    weight_two,
    weight_time,
    weight_upsample,
    weight_three,
    weight_four,
):
    section, row, col = (lax.axis_index(name) for name in ("section", "rows", "cols"))
    sections, row_count, col_count = (lax.axis_size(name) for name in ("section", "rows", "cols"))
    width, channels = latent.shape[2:]
    tile = width // col_count
    part = tile // sections
    wide = part + 2 * HALO
    half = weight_three.shape[1]

    def windows(array, which):
        padded = jnp.pad(array[:, 0], ((0, 0), (HALO, HALO), (0, 0)))
        return jnp.stack(
            [
                lax.dynamic_slice_in_dim(padded, c * tile + which * part, wide, 1)
                for c in range(col_count)
            ]
        )

    kept = windows(latent, section)
    arrived = swapped(windows(latent, 1 - section), "section")
    low = section == 0
    units = jnp.concatenate(
        [
            jnp.where(low, kept, arrived),
            jnp.where(low, arrived, kept),
            windows(cache_one, section),
            windows(cache_two, section),
        ],
        axis=1,
    )
    mine = lax.dynamic_index_in_dim(units, col, 0, keepdims=False)
    theirs = swapped(lax.dynamic_index_in_dim(units, 1 - col, 0, keepdims=False), "cols")
    left = col == 0
    own = jnp.concatenate([jnp.where(left, mine, theirs), jnp.where(left, theirs, mine)], axis=1)
    pieces = [
        shifted(own, "rows", 2),
        shifted(own, "rows", 1),
        own,
        shifted(own, "rows", -1),
        shifted(own, "rows", -2),
    ]

    def paired(array):
        return array.reshape(array.shape[0], array.shape[1], tile, channels)

    tiles = jnp.concatenate([cache_time, paired(cache_three), paired(cache_four)], axis=1)
    edge = jnp.where(left, tiles[:, :, tile - HALO :], tiles[:, :, :HALO])
    edge = swapped(edge, "cols")
    nothing = jnp.zeros_like(edge)
    tiles = jnp.concatenate(
        [jnp.where(left, nothing, edge), tiles, jnp.where(left, edge, nothing)], axis=2
    )
    tiles = lax.dynamic_slice_in_dim(tiles, section * part, wide, 2)
    time, three, four = tiles[:, 0:2], tiles[:, 2:6], tiles[:, 6:10]
    above = shifted(jnp.concatenate([time, three[:, 2:], four[:, 3:]], axis=1), "rows", 1)
    below = shifted(jnp.concatenate([time, three[:, :2], four[:, :1]], axis=1), "rows", -1)
    time = jnp.concatenate([above[:, 0:2], time, below[:, 0:2]], axis=1)
    three = jnp.concatenate([above[:, 2:4], three, below[:, 2:4]], axis=1)
    four = jnp.concatenate([above[:, 4:], four, below[:, 4:]], axis=1)

    height = 2 * row_count
    columns = col * tile + section * part - HALO + jnp.arange(wide, dtype=jnp.int32)
    inside = (columns >= 0) & (columns < width)

    def mask(first, count, limit):
        lines = first + jnp.arange(count, dtype=jnp.int32)
        good = (lines >= 0) & (lines < limit)
        return (good[:, None] & inside[None, :]).reshape(-1)

    masks = jnp.concatenate(
        [mask(2 * row - 3, 8, height), mask(4 * row - 2, 8, 2 * height)]
    ).astype(jnp.float32)
    masks = jnp.broadcast_to(masks[:, None], (masks.shape[0], 128))
    gains = jnp.stack(
        [gain_one, gain_two, jnp.tile(gain_three, 2), jnp.tile(gain_four, 2)]
    ).astype(jnp.float32)

    frames = decode(
        pieces,
        time.reshape(-1, channels),
        three.reshape(2, -1, channels),
        four.reshape(2, -1, channels),
        masks,
        gains,
        (
            weight_one.reshape(9, 3, channels, channels),
            weight_two.reshape(9, 3, channels, channels),
            weight_time,
            enlarge_weights(weight_upsample, half),
            pair_weights(weight_three, half),
            pair_weights(weight_four, half),
        ),
    )
    count = frames.shape[0] // sections
    given = lax.dynamic_slice_in_dim(frames, (1 - section) * count, count, 0)
    kept = lax.dynamic_slice_in_dim(frames, section * count, count, 0)
    arrived = swapped(given, "section")
    joined = jnp.concatenate(
        [jnp.where(low, kept, arrived), jnp.where(low, arrived, kept)], axis=2
    )
    return joined.reshape(count, 4, 2 * tile, half)


def solution(mesh):
    placed = (
        P("section", ("rows", "cols"), None, None),
        P(None, ("rows", "cols"), None, None),
        P(None, ("rows", "cols"), None, None),
        P(None, "rows", "cols", None),
        P(None, "rows", "cols", None),
        P(None, "rows", "cols", None),
    ) + (P(),) * 10
    return jax.shard_map(
        body,
        mesh=mesh,
        in_specs=placed,
        out_specs=P("section", "rows", "cols", None),
        check_vma=False,
    )
```

```python
import functools

import jax
import jax.numpy as jnp
from jax import lax
from jax.experimental import pallas as pl
from jax.experimental.pallas import tpu as pltpu
from jax.sharding import PartitionSpec as P

EPSILON = 1e-06
HALO = 4
LANES = 256
BF16 = jnp.bfloat16
F32 = jnp.float32


def swapped(value, axis):
    return lax.ppermute(value, axis, [(0, 1), (1, 0)])


def shifted(value, axis, steps):
    count = lax.axis_size(axis)
    initial, last = (max(0, -steps), min(count, count - steps))
    return lax.ppermute(value, axis, [(source, source + steps) for source in range(initial, last)])


def silu(scaled):
    half = scaled * 0.5
    return half * (1.0 + jnp.tanh(half))


def activate(values, gain, mask):
    mean = jnp.mean(values * values, axis=-1, keepdims=True)
    return silu(values * (lax.rsqrt(mean + EPSILON) * mask) * gain)


def activate_pairs(values, gain, mask):
    channels = values.shape[-1] // 2
    squares = values * values
    first = lax.broadcasted_iota(jnp.int32, (1, 2 * channels), 1) < channels
    total = jnp.sum(squares, axis=-1, keepdims=True)
    low = jnp.sum(jnp.where(first, squares, 0.0), axis=-1, keepdims=True)
    scale_low = lax.rsqrt(low / channels + EPSILON) * mask
    scale_high = lax.rsqrt((total - low) / channels + EPSILON) * mask
    return silu(values * jnp.where(first, scale_low, scale_high) * gain)


def merge(even, odd, channels):
    turned = pltpu.roll(odd, channels - 128, 1)
    first = lax.broadcasted_iota(jnp.int32, (1, 128), 1) < channels - 128
    middle = jnp.where(first, even[:, 128:], turned[:, :128])
    return jnp.concatenate([even[:, :128], middle, turned[:, 128:]], axis=1)


def aligned(index, size):
    return pl.multiple_of(index * size, 16)


def line_mask(place, wide, first, count, limit, width):
    columns = place[2] + lax.broadcasted_iota(jnp.int32, (wide, 1), 0)
    inside = jnp.where((columns >= 0) & (columns < width), 1.0, 0.0)
    lines = []
    for i in range(count):
        line = first + i
        lines.append(inside * jnp.where((line >= 0) & (line < limit), 1.0, 0.0))
    return jnp.concatenate(lines, axis=0)


def store(even, odd, slot, values, height, wide):
    even[pl.ds(slot * (height * wide), height * wide), :] = values.astype(BF16)
    odd[pl.ds(slot * ((height - 2) * wide), (height - 2) * wide), :] = values[
        wide : (height - 1) * wide
    ].astype(BF16)


def taps(even, odd, begin, count, height, wide, dt, dy, lanes=slice(None)):
    inner = (height - 2) * wide
    if dy == 1:
        parts = [odd[pl.ds((begin + f + dt) * inner, inner), lanes] for f in range(count)]
    else:
        parts = [
            even[pl.ds((begin + f + dt) * height * wide + dy * wide, inner), lanes]
            for f in range(count)
        ]
    return jnp.concatenate(parts, axis=0)


def low_product(acc, even, odd, count, height, wide, weights):
    rows = count * (height - 2) * wide
    channels = weights.shape[1]

    def column(n, carry):
        lanes = pl.ds(pl.multiple_of(n * LANES, LANES), LANES)
        total = None
        for first, last in ((0, 4), (4, 8), (8, 9)):
            left = jnp.concatenate(
                [
                    taps(even, odd, 0, count, height, wide, t // 3, t % 3)
                    for t in range(first, last)
                ],
                axis=1,
            )
            right = weights[first:last, :, lanes].reshape((last - first) * channels, LANES)
            part = jnp.dot(left, right, preferred_element_type=F32)
            total = part if total is None else total + part
        acc[n, 0:rows, :] = total
        return carry

    lax.fori_loop(0, weights.shape[-1] // LANES, column, 0)


def low_sum(acc, start, size):
    rows = pl.ds(start, size)
    before = jnp.concatenate([acc[0, rows, :], acc[1, rows, 0:128]], axis=1)
    center = jnp.concatenate([acc[1, rows, 128:256], acc[2, rows, :]], axis=1)
    after = jnp.concatenate([acc[3, rows, :], acc[4, rows, 0:128]], axis=1)
    return center + pltpu.roll(before, 1, 0) + pltpu.roll(after, size - 1, 0)


def high_product(acc, even, odd, count, height, wide, weights, sides):
    rows = count * (height - 2) * wide
    channels = weights.shape[-1]

    def center(o, carry):
        total = None
        for first, last in ((0, 4), (4, 8), (8, 9)):
            left = jnp.concatenate(
                [
                    taps(even, odd, 0, count, height, wide, t // 3, t % 3)
                    for t in range(first, last)
                ],
                axis=1,
            )
            begin = pl.multiple_of((1 - o) * channels, 16)
            right = weights[first:last, pl.ds(begin, 2 * channels), :]
            right = right.reshape((last - first) * 2 * channels, channels)
            part = jnp.dot(left, right, preferred_element_type=F32)
            total = part if total is None else total + part
        acc[o, 0:rows, 0:channels] = total
        return carry

    lax.fori_loop(0, 2, center, 0)

    def side(o, carry):
        lanes = pl.ds(pl.multiple_of((1 - o) * 128, 128), LANES)
        left = jnp.concatenate(
            [taps(even, odd, 0, count, height, wide, t // 3, t % 3, lanes) for t in range(9)],
            axis=1,
        )
        right = sides[o].reshape(9 * LANES, channels)
        acc[2 + o, 0:rows, 0:channels] = jnp.dot(left, right, preferred_element_type=F32)
        return carry

    lax.fori_loop(0, 2, side, 0)


def high_sum(acc, start, size, channels):
    rows = pl.ds(start, size)
    even = acc[0, rows, :] + pltpu.roll(acc[2, rows, :], 1, 0)
    odd = acc[1, rows, :] + pltpu.roll(acc[3, rows, :], size - 1, 0)
    return merge(even, odd, channels)


def pack_kernel(wide, tile, part, place, latent, arrived, one, two, mine, theirs, spread):
    section, col = place[0], place[1]
    width, channels = latent.shape[1:]
    empty = jnp.zeros((spread.shape[1] - width, channels), F32)

    def put(slot, values):
        spread[slot] = pltpu.roll(
            jnp.concatenate([values.astype(F32), empty], axis=0), HALO, 0
        )

    for i in range(2):
        put(2 * section + i, latent[i])
        put(2 * (1 - section) + i, arrived[i])
        put(4 + i, one[i])
        put(6 + i, two[i])
    for slot in range(8):
        for ref, which in ((mine, col), (theirs, 1 - col)):
            begin = pl.multiple_of(which * tile + section * part, 8)
            ref[slot] = spread[slot, pl.ds(begin, wide), :].astype(BF16)


def pack(place, latent, arrived, one, two, wide, tile, part):
    width, channels = latent.shape[1:]
    vmem = pl.BlockSpec(memory_space=pltpu.VMEM)
    return pl.pallas_call(
        functools.partial(pack_kernel, wide, tile, part),
        out_shape=[jax.ShapeDtypeStruct((8, wide, channels), BF16)] * 2,
        in_specs=[pl.BlockSpec(memory_space=pltpu.SMEM)] + [vmem] * 4,
        out_specs=[vmem] * 2,
        scratch_shapes=[pltpu.VMEM((8, width + 16, channels), F32)],
        name="pack",
    )(place, latent, arrived, one, two)


def first_kernel(
    wide,
    sizes,
    place,
    low2,
    low1,
    own,
    high1,
    high2,
    gain_one,
    gain_two,
    weight_one,
    weight_two,
    out_ref,
    w1,
    w2,
    acc,
    x1e,
    x1o,
    x2e,
    x2o,
    sems,
):
    channels = own.shape[-1]
    frames = own.shape[1] - 4
    height, width = sizes
    col, row = place[1], place[3]
    pieces = (low2, low1, own, high1, high2)

    def load(source, target, base):
        return [
            pltpu.make_async_copy(
                source.at[:, dx], target.at[:, :, pl.ds(dx * channels, channels)], sems.at[base + dx]
            )
            for dx in range(3)
        ]

    copies_one = load(weight_one, w1, 0)
    copies_two = load(weight_two, w2, 3)
    for copy in copies_one:
        copy.start()

    def rows_of(refs, index):
        return jnp.concatenate(
            [ref[lax.rem(y + col, 2), index].astype(F32) for ref in refs for y in range(2)], axis=0
        )

    for f in range(2):
        store(x1e, x1o, f, rows_of(pieces, frames + f), 10, wide)
        store(x2e, x2o, f, rows_of(pieces, frames + 2 + f)[wide : 9 * wide], 8, wide)

    def norm_one(f, carry):
        values = activate(rows_of(pieces, f), gain_one[...], 1.0)
        store(x1e, x1o, f + 2, values, 10, wide)
        return carry

    lax.fori_loop(0, frames, norm_one, 0)
    for copy in copies_one:
        copy.wait()
    for copy in copies_two:
        copy.start()
    low_product(acc, x1e, x1o, frames, 10, wide, w1)

    mask = line_mask(place, wide, 2 * row - 3, 8, height, width)

    def norm_two(f, carry):
        size = 8 * wide
        values = activate(low_sum(acc, aligned(f, size), size), gain_two[...], mask)
        store(x2e, x2o, f + 2, values, 8, wide)
        return carry

    lax.fori_loop(0, frames, norm_two, 0)
    for copy in copies_two:
        copy.wait()
    low_product(acc, x2e, x2o, frames, 8, wide, w2)

    def residual(f, carry):
        size = 6 * wide
        values = low_sum(acc, aligned(f, size), size) + rows_of(pieces[1:4], f)
        out_ref[pl.ds(aligned(f, size), size), :] = values.astype(BF16)
        return carry

    lax.fori_loop(0, frames, residual, 0)


def planes(slots, height, wide, channels):
    return [
        pltpu.VMEM((slots * height * wide, channels), BF16),
        pltpu.VMEM((slots * (height - 2) * wide, channels), BF16),
    ]


def first_block(place, pieces, gain_one, gain_two, weight_one, weight_two, sizes):
    _, units, wide, channels = pieces[0].shape
    frames = units - 4
    slots = -(-3 * channels // LANES)
    vmem = pl.BlockSpec(memory_space=pltpu.VMEM)
    anywhere = pl.BlockSpec(memory_space=pl.ANY)
    return pl.pallas_call(
        functools.partial(first_kernel, wide, sizes),
        out_shape=jax.ShapeDtypeStruct((frames * 6 * wide, channels), BF16),
        in_specs=[pl.BlockSpec(memory_space=pltpu.SMEM)] + [vmem] * 7 + [anywhere] * 2,
        out_specs=vmem,
        scratch_shapes=[
            pltpu.VMEM((9, channels, slots * LANES), BF16),
            pltpu.VMEM((9, channels, slots * LANES), BF16),
            pltpu.VMEM((slots, frames * 8 * wide, LANES), F32),
            *planes(frames + 2, 10, wide, channels),
            *planes(frames + 2, 8, wide, channels),
            pltpu.SemaphoreType.DMA((6,)),
        ],
        compiler_params=pltpu.CompilerParams(vmem_limit_bytes=48 * 1024 * 1024),
        cost_estimate=pl.CostEstimate(
            flops=2 * 27 * channels * channels * frames * 14 * wide,
            bytes_accessed=2 * 54 * channels * channels,
            transcendentals=0,
        ),
        name="first_block",
    )(place, *pieces, gain_one, gain_two, weight_one, weight_two)


def second_kernel(
    wide,
    sizes,
    place,
    blocked,
    time_ref,
    three_ref,
    four_ref,
    gain_three,
    gain_four,
    weight_time,
    weight_up,
    weight_three,
    weight_four,
    out_ref,
    wt,
    wr,
    wu,
    w3,
    s3,
    w4,
    s4,
    acc,
    mixed,
    de,
    do,
    x3e,
    x3o,
    x4e,
    x4o,
    lifted_ref,
    sems,
):
    channels = blocked.shape[-1]
    half = channels // 2
    size = 6 * wide
    frames = blocked.shape[0] // size
    count = 2 * frames
    height, width = sizes
    row = place[3]

    def load_high(source, target, sides, base):
        blank = LANES - half
        return [
            pltpu.make_async_copy(source, target, sems.at[base]),
            pltpu.make_async_copy(
                source.at[:, pl.ds(0, half), :],
                sides.at[0, :, pl.ds(blank, half), :],
                sems.at[base + 1],
            ),
            pltpu.make_async_copy(
                source.at[:, pl.ds(2 * half, half), :],
                sides.at[1, :, pl.ds(0, half), :],
                sems.at[base + 2],
            ),
        ]

    copy_time = pltpu.make_async_copy(weight_time, wt, sems.at[0])
    copy_up = pltpu.make_async_copy(weight_up, wr, sems.at[1])
    copies_three = load_high(weight_three, w3, s3, 2)
    copies_four = load_high(weight_four, w4, s4, 5)
    copy_time.start()
    copy_up.start()
    for copy in copies_three + copies_four:
        copy.start()

    blank = jnp.zeros((9, LANES - half, half), BF16)
    for sides in (s3, s4):
        sides[0, :, 0 : LANES - half, :] = blank
        sides[1, :, half:LANES, :] = blank

    mixed[0 : 2 * size, :] = time_ref[...]
    mixed[2 * size : (frames + 2) * size, :] = blocked[...]
    copy_time.wait()

    def mix(n, carry):
        lanes = pl.ds(pl.multiple_of(n * LANES, LANES), LANES)
        left = jnp.concatenate(
            [mixed[pl.ds(t * size, frames * size), :] for t in range(3)], axis=1
        )
        acc[n, 0 : frames * size, :] = jnp.dot(left, wt[:, lanes], preferred_element_type=F32)
        return carry

    lax.fori_loop(0, 2 * channels // LANES, mix, 0)
    mask_low = line_mask(place, wide, 2 * row - 2, 6, height, width)

    def double(t, carry):
        rows = pl.ds(aligned(t, size), size)
        first = jnp.concatenate([acc[0, rows, :], acc[1, rows, 0:128]], axis=1)
        second = jnp.concatenate([acc[1, rows, 128:256], acc[2, rows, :]], axis=1)
        store(de, do, 2 * t, first * mask_low, 6, wide)
        store(de, do, 2 * t + 1, second * mask_low, 6, wide)
        return carry

    lax.fori_loop(0, frames, double, 0)
    copy_up.wait()

    chunk = 16

    def combine(k, carry):
        rows = pl.ds(aligned(k, chunk), chunk)
        taken = [[wr[3 * dy + dx, rows, :].astype(F32) for dx in range(3)] for dy in range(3)]
        gap = jnp.zeros((chunk, LANES - half), F32)
        for slot, dys in enumerate(((0,), (1, 2), (0, 1), (2,))):
            line = [sum(taken[dy][dx] for dy in dys) for dx in range(3)]
            line = [jnp.concatenate([part, gap], axis=1) for part in line]
            into = pl.ds(aligned(k, chunk) + (slot % 2) * channels, chunk)
            wu[slot // 2, into, 0:channels] = merge(
                line[1] + line[2], line[0] + line[1], half
            ).astype(BF16)
            wu[slot // 2, into, channels : 2 * channels] = merge(line[0], line[2], half).astype(
                BF16
            )
        return carry

    lax.fori_loop(0, channels // chunk, combine, 0)

    for py in range(2):

        def enlarge(n, carry):
            lanes = pl.ds(pl.multiple_of(n * LANES, LANES), LANES)
            left = jnp.concatenate(
                [taps(de, do, 0, count, 6, wide, 0, py), taps(de, do, 0, count, 6, wide, 0, py + 1)],
                axis=1,
            )
            acc[n, py * count * 4 * wide : (py + 1) * count * 4 * wide, :] = jnp.dot(
                left, wu[py, :, lanes], preferred_element_type=F32
            )
            return carry

        lax.fori_loop(0, 2 * channels // LANES, enlarge, 0)

    for f in range(2):
        store(x3e, x3o, f, three_ref[f].astype(F32), 8, wide)
        store(x4e, x4o, f, four_ref[f].astype(F32), 6, wide)
    gain3 = jnp.concatenate([gain_three[...], gain_three[...]], axis=1)
    gain4 = jnp.concatenate([gain_four[...], gain_four[...]], axis=1)
    mask_three = line_mask(place, wide, 4 * row - 2, 8, 2 * height, width)
    first_half = lax.broadcasted_iota(jnp.int32, (1, channels), 1) < half
    part = 4 * wide

    def norm_three(f, carry):
        values = []
        for py in range(2):
            rows = pl.ds(pl.multiple_of(py * count * part + f * part, 16), part)
            center = jnp.concatenate([acc[0, rows, :], acc[1, rows, 0:128]], axis=1)
            side = jnp.concatenate([acc[1, rows, 128:256], acc[2, rows, :]], axis=1)
            side = jnp.where(first_half, pltpu.roll(side, 1, 0), pltpu.roll(side, part - 1, 0))
            values.append((center + side).astype(BF16).astype(F32))
        lifted = jnp.concatenate(
            [values[h % 2][(h // 2) * wide : (h // 2 + 1) * wide] for h in range(8)], axis=0
        )
        lifted_ref[pl.ds(aligned(f, part), part), :] = lifted[2 * wide : 6 * wide]
        store(x3e, x3o, f + 2, activate_pairs(lifted, gain3, mask_three), 8, wide)
        return carry

    lax.fori_loop(0, count, norm_three, 0)
    for copy in copies_three:
        copy.wait()
    high_product(acc, x3e, x3o, count, 8, wide, w3, s3)

    mask_four = mask_three[wide : 7 * wide]

    def norm_four(f, carry):
        values = high_sum(acc, aligned(f, size), size, half)
        store(x4e, x4o, f + 2, activate_pairs(values, gain4, mask_four), 6, wide)
        return carry

    lax.fori_loop(0, count, norm_four, 0)
    for copy in copies_four:
        copy.wait()
    high_product(acc, x4e, x4o, count, 6, wide, w4, s4)

    def finish(f, carry):
        start = aligned(f, part)
        values = high_sum(acc, start, part, half) + lifted_ref[pl.ds(start, part), :]
        values = pltpu.roll(values, part - HALO, 0)
        for y in range(4):
            inner = wide - 2 * HALO
            out_ref[f, y] = values[y * wide : y * wide + inner].astype(BF16)
        return carry

    lax.fori_loop(0, count, finish, 0)


def second_block(place, blocked, time, three, four, gains, weights, sizes, wide):
    channels = blocked.shape[-1]
    half = channels // 2
    frames = blocked.shape[0] // (6 * wide)
    count = 2 * frames
    weight_time, weight_up, weight_three, weight_four = weights
    vmem = pl.BlockSpec(memory_space=pltpu.VMEM)
    anywhere = pl.BlockSpec(memory_space=pl.ANY)
    return pl.pallas_call(
        functools.partial(second_kernel, wide, sizes),
        out_shape=jax.ShapeDtypeStruct((count, 4, wide - 2 * HALO, channels), BF16),
        in_specs=[pl.BlockSpec(memory_space=pltpu.SMEM)] + [vmem] * 6 + [anywhere] * 4,
        out_specs=vmem,
        scratch_shapes=[
            pltpu.VMEM(weight_time.shape, BF16),
            pltpu.VMEM(weight_up.shape, BF16),
            pltpu.VMEM((2, 2 * channels, 2 * channels), BF16),
            pltpu.VMEM(weight_three.shape, BF16),
            pltpu.VMEM((2, 9, LANES, half), BF16),
            pltpu.VMEM(weight_four.shape, BF16),
            pltpu.VMEM((2, 9, LANES, half), BF16),
            pltpu.VMEM((4, 2 * count * 4 * wide, LANES), F32),
            pltpu.VMEM(((frames + 2) * 6 * wide, channels), BF16),
            *planes(count, 6, wide, channels),
            *planes(count + 2, 8, wide, channels),
            *planes(count + 2, 6, wide, channels),
            pltpu.VMEM((count * 4 * wide, channels), F32),
            pltpu.SemaphoreType.DMA((8,)),
        ],
        compiler_params=pltpu.CompilerParams(vmem_limit_bytes=48 * 1024 * 1024),
        name="second_block",
    )(place, blocked, time, three, four, *gains, *weights)


def body(
    latent,
    cache_one,
    cache_two,
    cache_time,
    cache_three,
    cache_four,
    gain_one,
    gain_two,
    gain_three,
    gain_four,
    weight_one,
    weight_two,
    weight_time,
    weight_upsample,
    weight_three,
    weight_four,
):
    section, row, col = (lax.axis_index(name) for name in ("section", "rows", "cols"))
    sections, row_count, col_count = (lax.axis_size(name) for name in ("section", "rows", "cols"))
    width, channels = latent.shape[2:]
    tile = width // col_count
    part = tile // sections
    wide = part + 2 * HALO
    half = weight_three.shape[1]
    sizes = (2 * row_count, width)
    place = jnp.stack([section, col, col * tile + section * part - HALO, row]).astype(jnp.int32)

    latent = latent.reshape(latent.shape[0], width, channels)
    arrived = swapped(latent, "section")
    mine, theirs = pack(
        place, latent, arrived, cache_one[:, 0], cache_two[:, 0], wide, tile, part
    )
    theirs = swapped(theirs, "cols")
    own = jnp.stack([mine, theirs])
    pieces = [
        shifted(own, "rows", 2),
        shifted(own, "rows", 1),
        own,
        shifted(own, "rows", -1),
        shifted(own, "rows", -2),
    ]
    blocked = first_block(
        place,
        pieces,
        gain_one.reshape(1, -1),
        gain_two.reshape(1, -1),
        weight_one.reshape(9, 3, channels, channels),
        weight_two.reshape(9, 3, channels, channels),
        sizes,
    )

    def paired(array):
        return array.reshape(array.shape[0], array.shape[1], tile, channels)

    left = col == 0
    tiles = jnp.concatenate([cache_time, paired(cache_three), paired(cache_four)], axis=1)
    edge = jnp.where(left, tiles[:, :, tile - HALO :], tiles[:, :, :HALO])
    edge = swapped(edge, "cols")
    nothing = jnp.zeros_like(edge)
    tiles = jnp.concatenate(
        [jnp.where(left, nothing, edge), tiles, jnp.where(left, edge, nothing)], axis=2
    )
    tiles = lax.dynamic_slice_in_dim(tiles, section * part, wide, 2)
    time, three, four = tiles[:, 0:2], tiles[:, 2:6], tiles[:, 6:10]
    above = shifted(jnp.concatenate([time, three[:, 2:], four[:, 3:]], axis=1), "rows", 1)
    below = shifted(jnp.concatenate([time, three[:, :2], four[:, :1]], axis=1), "rows", -1)
    time = jnp.concatenate([above[:, 0:2], time, below[:, 0:2]], axis=1)
    three = jnp.concatenate([above[:, 2:4], three, below[:, 2:4]], axis=1)
    four = jnp.concatenate([above[:, 4:], four, below[:, 4:]], axis=1)

    frames = second_block(
        place,
        blocked,
        time.reshape(-1, channels),
        three.reshape(2, -1, channels),
        four.reshape(2, -1, channels),
        (gain_three.reshape(1, -1), gain_four.reshape(1, -1)),
        (
            weight_time,
            weight_upsample.reshape(9, channels, half),
            weight_three.reshape(9, 3 * half, half),
            weight_four.reshape(9, 3 * half, half),
        ),
        sizes,
        wide,
    )
    count = frames.shape[0] // sections
    given = lax.dynamic_slice_in_dim(frames, (1 - section) * count, count, 0)
    kept = lax.dynamic_slice_in_dim(frames, section * count, count, 0)
    arrived = swapped(given, "section")
    low = section == 0
    joined = jnp.concatenate(
        [jnp.where(low, kept, arrived), jnp.where(low, arrived, kept)], axis=2
    )
    return joined.reshape(count, 4, 2 * tile, half)


def solution(mesh):
    placed = (
        P("section", ("rows", "cols"), None, None),
        P(None, ("rows", "cols"), None, None),
        P(None, ("rows", "cols"), None, None),
        P(None, "rows", "cols", None),
        P(None, "rows", "cols", None),
        P(None, "rows", "cols", None),
    ) + (P(),) * 10
    return jax.shard_map(
        body,
        mesh=mesh,
        in_specs=placed,
        out_specs=P("section", "rows", "cols", None),
        check_vma=False,
    )
```

```python
import functools

import jax
import jax.numpy as jnp
from jax import lax
from jax.experimental import pallas as pl
from jax.experimental.pallas import tpu as pltpu
from jax.sharding import PartitionSpec as P

EPSILON = 1e-06
HALO = 4
LANES = 256
BF16 = jnp.bfloat16
F32 = jnp.float32


def swapped(value, axis):
    return lax.ppermute(value, axis, [(0, 1), (1, 0)])


def shifted(value, axis, steps):
    count = lax.axis_size(axis)
    initial, last = (max(0, -steps), min(count, count - steps))
    return lax.ppermute(value, axis, [(source, source + steps) for source in range(initial, last)])


def silu(scaled):
    half = scaled * 0.5
    return half * (1.0 + jnp.tanh(half))


def activate(values, gain, mask):
    mean = jnp.mean(values * values, axis=-1, keepdims=True)
    return silu(values * (lax.rsqrt(mean + EPSILON) * mask) * gain)


def activate_pairs(values, gain, mask):
    channels = values.shape[-1] // 2
    squares = values * values
    first = lax.broadcasted_iota(jnp.int32, (1, 2 * channels), 1) < channels
    total = jnp.sum(squares, axis=-1, keepdims=True)
    low = jnp.sum(jnp.where(first, squares, 0.0), axis=-1, keepdims=True)
    scale_low = lax.rsqrt(low / channels + EPSILON) * mask
    scale_high = lax.rsqrt((total - low) / channels + EPSILON) * mask
    return silu(values * jnp.where(first, scale_low, scale_high) * gain)


def merge(even, odd, channels):
    turned = pltpu.roll(odd, channels - 128, 1)
    first = lax.broadcasted_iota(jnp.int32, (1, 128), 1) < channels - 128
    middle = jnp.where(first, even[:, 128:], turned[:, :128])
    return jnp.concatenate([even[:, :128], middle, turned[:, 128:]], axis=1)


def aligned(index, size):
    return pl.multiple_of(index * size, 16)


def line_mask(place, wide, first, count, limit, width):
    columns = place[2] + lax.broadcasted_iota(jnp.int32, (wide, 1), 0)
    inside = jnp.where((columns >= 0) & (columns < width), 1.0, 0.0)
    lines = []
    for i in range(count):
        line = first + i
        lines.append(inside * jnp.where((line >= 0) & (line < limit), 1.0, 0.0))
    return jnp.concatenate(lines, axis=0)


def store(even, odd, slot, values, height, wide):
    even[pl.ds(slot * (height * wide), height * wide), :] = values.astype(BF16)
    odd[pl.ds(slot * ((height - 2) * wide), (height - 2) * wide), :] = values[
        wide : (height - 1) * wide
    ].astype(BF16)


def taps(even, odd, begin, count, height, wide, dt, dy, lanes=slice(None)):
    inner = (height - 2) * wide
    if dy == 1:
        parts = [odd[pl.ds((begin + f + dt) * inner, inner), lanes] for f in range(count)]
    else:
        parts = [
            even[pl.ds((begin + f + dt) * height * wide + dy * wide, inner), lanes]
            for f in range(count)
        ]
    return jnp.concatenate(parts, axis=0)


def low_product(acc, even, odd, count, height, wide, weights):
    rows = count * (height - 2) * wide
    channels = weights.shape[1]
    lanes = 3 * channels
    for n in range(-(-lanes // LANES)):
        size = min(LANES, lanes - n * LANES)
        total = None
        for first, last in ((0, 4), (4, 8), (8, 9)):
            left = jnp.concatenate(
                [
                    taps(even, odd, 0, count, height, wide, t // 3, t % 3)
                    for t in range(first, last)
                ],
                axis=1,
            )
            right = []
            for t in range(first, last):
                parts = []
                for dx in range(3):
                    begin = max(n * LANES - dx * channels, 0)
                    end = min(n * LANES + size - dx * channels, channels)
                    if begin < end:
                        base = (3 * t + dx) * channels
                        parts.append(weights[base : base + channels, begin:end])
                right.append(jnp.concatenate(parts, axis=1))
            right = jnp.concatenate(right, axis=0)
            part = jnp.dot(left, right, preferred_element_type=F32)
            total = part if total is None else total + part
        acc[n, 0:rows, 0:size] = total


def low_sum(acc, start, size):
    rows = pl.ds(start, size)
    before = jnp.concatenate([acc[0, rows, :], acc[1, rows, 0:128]], axis=1)
    center = jnp.concatenate([acc[1, rows, 128:256], acc[2, rows, :]], axis=1)
    after = jnp.concatenate([acc[3, rows, :], acc[4, rows, 0:128]], axis=1)
    return center + pltpu.roll(before, 1, 0) + pltpu.roll(after, size - 1, 0)


def high_product(acc, even, odd, count, height, wide, weights, sides):
    rows = count * (height - 2) * wide
    channels = weights.shape[-1]

    def center(o, carry):
        total = None
        for first, last in ((0, 4), (4, 8), (8, 9)):
            left = jnp.concatenate(
                [
                    taps(even, odd, 0, count, height, wide, t // 3, t % 3)
                    for t in range(first, last)
                ],
                axis=1,
            )
            begin = pl.multiple_of((1 - o) * channels, 16)
            right = weights[first:last, pl.ds(begin, 2 * channels), :]
            right = right.reshape((last - first) * 2 * channels, channels)
            part = jnp.dot(left, right, preferred_element_type=F32)
            total = part if total is None else total + part
        acc[o, 0:rows, 0:channels] = total
        return carry

    lax.fori_loop(0, 2, center, 0)

    def side(o, carry):
        lanes = pl.ds(pl.multiple_of((1 - o) * 128, 128), LANES)
        left = jnp.concatenate(
            [taps(even, odd, 0, count, height, wide, t // 3, t % 3, lanes) for t in range(9)],
            axis=1,
        )
        right = sides[o].reshape(9 * LANES, channels)
        acc[2 + o, 0:rows, 0:channels] = jnp.dot(left, right, preferred_element_type=F32)
        return carry

    lax.fori_loop(0, 2, side, 0)


def high_sum(acc, start, size, channels):
    rows = pl.ds(start, size)
    even = acc[0, rows, :] + pltpu.roll(acc[2, rows, :], 1, 0)
    odd = acc[1, rows, :] + pltpu.roll(acc[3, rows, :], size - 1, 0)
    return merge(even, odd, channels)


def pack_kernel(wide, tile, part, place, latent, arrived, one, two, mine, theirs, spread):
    section, col = place[0], place[1]
    width, channels = latent.shape[1:]
    empty = jnp.zeros((spread.shape[1] - width, channels), F32)

    def put(slot, values):
        spread[slot] = pltpu.roll(
            jnp.concatenate([values.astype(F32), empty], axis=0), HALO, 0
        )

    for i in range(2):
        put(2 * section + i, latent[i])
        put(2 * (1 - section) + i, arrived[i])
        put(4 + i, one[i])
        put(6 + i, two[i])
    for slot in range(8):
        for ref, which in ((mine, col), (theirs, 1 - col)):
            begin = pl.multiple_of(which * tile + section * part, 8)
            ref[slot] = spread[slot, pl.ds(begin, wide), :].astype(BF16)


def pack(place, latent, arrived, one, two, wide, tile, part):
    width, channels = latent.shape[1:]
    vmem = pl.BlockSpec(memory_space=pltpu.VMEM)
    return pl.pallas_call(
        functools.partial(pack_kernel, wide, tile, part),
        out_shape=[jax.ShapeDtypeStruct((8, wide, channels), BF16)] * 2,
        in_specs=[pl.BlockSpec(memory_space=pltpu.SMEM)] + [vmem] * 4,
        out_specs=[vmem] * 2,
        scratch_shapes=[pltpu.VMEM((8, width + 16, channels), F32)],
        name="pack",
    )(place, latent, arrived, one, two)


def first_kernel(
    wide,
    sizes,
    place,
    low2,
    low1,
    own,
    high1,
    high2,
    gain_one,
    gain_two,
    w1,
    w2,
    out_ref,
    acc,
    x1e,
    x1o,
    x2e,
    x2o,
):
    channels = own.shape[-1]
    frames = own.shape[1] - 4
    height, width = sizes
    col, row = place[1], place[3]
    pieces = (low2, low1, own, high1, high2)

    def rows_of(refs, index):
        return jnp.concatenate(
            [ref[lax.rem(y + col, 2), index].astype(F32) for ref in refs for y in range(2)], axis=0
        )

    for f in range(2):
        store(x1e, x1o, f, rows_of(pieces, frames + f), 10, wide)
        store(x2e, x2o, f, rows_of(pieces, frames + 2 + f)[wide : 9 * wide], 8, wide)

    def norm_one(f, carry):
        values = activate(rows_of(pieces, f), gain_one[...], 1.0)
        store(x1e, x1o, f + 2, values, 10, wide)
        return carry

    lax.fori_loop(0, frames, norm_one, 0)
    low_product(acc, x1e, x1o, frames, 10, wide, w1)

    mask = line_mask(place, wide, 2 * row - 3, 8, height, width)

    def norm_two(f, carry):
        size = 8 * wide
        values = activate(low_sum(acc, aligned(f, size), size), gain_two[...], mask)
        store(x2e, x2o, f + 2, values, 8, wide)
        return carry

    lax.fori_loop(0, frames, norm_two, 0)
    low_product(acc, x2e, x2o, frames, 8, wide, w2)

    def residual(f, carry):
        size = 6 * wide
        values = low_sum(acc, aligned(f, size), size) + rows_of(pieces[1:4], f)
        out_ref[pl.ds(aligned(f, size), size), :] = values.astype(BF16)
        return carry

    lax.fori_loop(0, frames, residual, 0)


def planes(slots, height, wide, channels):
    return [
        pltpu.VMEM((slots * height * wide, channels), BF16),
        pltpu.VMEM((slots * (height - 2) * wide, channels), BF16),
    ]


def first_block(place, pieces, gain_one, gain_two, weight_one, weight_two, sizes):
    _, units, wide, channels = pieces[0].shape
    frames = units - 4
    slots = -(-3 * channels // LANES)
    vmem = pl.BlockSpec(memory_space=pltpu.VMEM)
    return pl.pallas_call(
        functools.partial(first_kernel, wide, sizes),
        out_shape=jax.ShapeDtypeStruct((frames * 6 * wide, channels), BF16),
        in_specs=[pl.BlockSpec(memory_space=pltpu.SMEM)] + [vmem] * 9,
        out_specs=vmem,
        scratch_shapes=[
            pltpu.VMEM((slots, frames * 8 * wide, LANES), F32),
            *planes(frames + 2, 10, wide, channels),
            *planes(frames + 2, 8, wide, channels),
        ],
        compiler_params=pltpu.CompilerParams(vmem_limit_bytes=16 * 1024 * 1024),
        cost_estimate=pl.CostEstimate(
            flops=2 * 27 * channels * channels * frames * 14 * wide,
            bytes_accessed=2 * 54 * channels * channels,
            transcendentals=0,
        ),
        name="first_block",
    )(place, *pieces, gain_one, gain_two, weight_one, weight_two)


def second_kernel(
    wide,
    sizes,
    place,
    blocked,
    time_ref,
    three_ref,
    four_ref,
    gain_three,
    gain_four,
    weight_time,
    weight_up,
    weight_three,
    weight_four,
    out_ref,
    wt,
    wr,
    wu,
    w3,
    s3,
    w4,
    s4,
    acc,
    mixed,
    de,
    do,
    x3e,
    x3o,
    x4e,
    x4o,
    lifted_ref,
    sems,
):
    channels = blocked.shape[-1]
    half = channels // 2
    size = 6 * wide
    frames = blocked.shape[0] // size
    count = 2 * frames
    height, width = sizes
    row = place[3]

    def load_high(source, target, sides, base):
        blank = LANES - half
        return [
            pltpu.make_async_copy(source, target, sems.at[base]),
            pltpu.make_async_copy(
                source.at[:, pl.ds(0, half), :],
                sides.at[0, :, pl.ds(blank, half), :],
                sems.at[base + 1],
            ),
            pltpu.make_async_copy(
                source.at[:, pl.ds(2 * half, half), :],
                sides.at[1, :, pl.ds(0, half), :],
                sems.at[base + 2],
            ),
        ]

    copy_time = pltpu.make_async_copy(weight_time, wt, sems.at[0])
    copy_up = pltpu.make_async_copy(weight_up, wr, sems.at[1])
    copies_three = load_high(weight_three, w3, s3, 2)
    copies_four = load_high(weight_four, w4, s4, 5)
    copy_time.start()
    copy_up.start()
    for copy in copies_three + copies_four:
        copy.start()

    blank = jnp.zeros((9, LANES - half, half), BF16)
    for sides in (s3, s4):
        sides[0, :, 0 : LANES - half, :] = blank
        sides[1, :, half:LANES, :] = blank

    mixed[0 : 2 * size, :] = time_ref[...]
    mixed[2 * size : (frames + 2) * size, :] = blocked[...]
    copy_time.wait()

    def mix(n, carry):
        lanes = pl.ds(pl.multiple_of(n * LANES, LANES), LANES)
        left = jnp.concatenate(
            [mixed[pl.ds(t * size, frames * size), :] for t in range(3)], axis=1
        )
        acc[n, 0 : frames * size, :] = jnp.dot(left, wt[:, lanes], preferred_element_type=F32)
        return carry

    lax.fori_loop(0, 2 * channels // LANES, mix, 0)
    mask_low = line_mask(place, wide, 2 * row - 2, 6, height, width)

    def double(t, carry):
        rows = pl.ds(aligned(t, size), size)
        first = jnp.concatenate([acc[0, rows, :], acc[1, rows, 0:128]], axis=1)
        second = jnp.concatenate([acc[1, rows, 128:256], acc[2, rows, :]], axis=1)
        store(de, do, 2 * t, first * mask_low, 6, wide)
        store(de, do, 2 * t + 1, second * mask_low, 6, wide)
        return carry

    lax.fori_loop(0, frames, double, 0)
    copy_up.wait()

    chunk = 16

    def combine(k, carry):
        rows = pl.ds(aligned(k, chunk), chunk)
        taken = [[wr[3 * dy + dx, rows, :].astype(F32) for dx in range(3)] for dy in range(3)]
        gap = jnp.zeros((chunk, LANES - half), F32)
        for slot, dys in enumerate(((0,), (1, 2), (0, 1), (2,))):
            line = [sum(taken[dy][dx] for dy in dys) for dx in range(3)]
            line = [jnp.concatenate([part, gap], axis=1) for part in line]
            into = pl.ds(aligned(k, chunk) + (slot % 2) * channels, chunk)
            wu[slot // 2, into, 0:channels] = merge(
                line[1] + line[2], line[0] + line[1], half
            ).astype(BF16)
            wu[slot // 2, into, channels : 2 * channels] = merge(line[0], line[2], half).astype(
                BF16
            )
        return carry

    lax.fori_loop(0, channels // chunk, combine, 0)

    for py in range(2):

        def enlarge(n, carry):
            lanes = pl.ds(pl.multiple_of(n * LANES, LANES), LANES)
            left = jnp.concatenate(
                [taps(de, do, 0, count, 6, wide, 0, py), taps(de, do, 0, count, 6, wide, 0, py + 1)],
                axis=1,
            )
            acc[n, py * count * 4 * wide : (py + 1) * count * 4 * wide, :] = jnp.dot(
                left, wu[py, :, lanes], preferred_element_type=F32
            )
            return carry

        lax.fori_loop(0, 2 * channels // LANES, enlarge, 0)

    for f in range(2):
        store(x3e, x3o, f, three_ref[f].astype(F32), 8, wide)
        store(x4e, x4o, f, four_ref[f].astype(F32), 6, wide)
    gain3 = jnp.concatenate([gain_three[...], gain_three[...]], axis=1)
    gain4 = jnp.concatenate([gain_four[...], gain_four[...]], axis=1)
    mask_three = line_mask(place, wide, 4 * row - 2, 8, 2 * height, width)
    first_half = lax.broadcasted_iota(jnp.int32, (1, channels), 1) < half
    part = 4 * wide

    def norm_three(f, carry):
        values = []
        for py in range(2):
            rows = pl.ds(pl.multiple_of(py * count * part + f * part, 16), part)
            center = jnp.concatenate([acc[0, rows, :], acc[1, rows, 0:128]], axis=1)
            side = jnp.concatenate([acc[1, rows, 128:256], acc[2, rows, :]], axis=1)
            side = jnp.where(first_half, pltpu.roll(side, 1, 0), pltpu.roll(side, part - 1, 0))
            values.append((center + side).astype(BF16).astype(F32))
        lifted = jnp.concatenate(
            [values[h % 2][(h // 2) * wide : (h // 2 + 1) * wide] for h in range(8)], axis=0
        )
        lifted_ref[pl.ds(aligned(f, part), part), :] = lifted[2 * wide : 6 * wide]
        store(x3e, x3o, f + 2, activate_pairs(lifted, gain3, mask_three), 8, wide)
        return carry

    lax.fori_loop(0, count, norm_three, 0)
    for copy in copies_three:
        copy.wait()
    high_product(acc, x3e, x3o, count, 8, wide, w3, s3)

    mask_four = mask_three[wide : 7 * wide]

    def norm_four(f, carry):
        values = high_sum(acc, aligned(f, size), size, half)
        store(x4e, x4o, f + 2, activate_pairs(values, gain4, mask_four), 6, wide)
        return carry

    lax.fori_loop(0, count, norm_four, 0)
    for copy in copies_four:
        copy.wait()
    high_product(acc, x4e, x4o, count, 6, wide, w4, s4)

    def finish(f, carry):
        start = aligned(f, part)
        values = high_sum(acc, start, part, half) + lifted_ref[pl.ds(start, part), :]
        values = pltpu.roll(values, part - HALO, 0)
        for y in range(4):
            inner = wide - 2 * HALO
            out_ref[f, y] = values[y * wide : y * wide + inner].astype(BF16)
        return carry

    lax.fori_loop(0, count, finish, 0)


def second_block(place, blocked, time, three, four, gains, weights, sizes, wide):
    channels = blocked.shape[-1]
    half = channels // 2
    frames = blocked.shape[0] // (6 * wide)
    count = 2 * frames
    weight_time, weight_up, weight_three, weight_four = weights
    vmem = pl.BlockSpec(memory_space=pltpu.VMEM)
    anywhere = pl.BlockSpec(memory_space=pl.ANY)
    return pl.pallas_call(
        functools.partial(second_kernel, wide, sizes),
        out_shape=jax.ShapeDtypeStruct((count, 4, wide - 2 * HALO, channels), BF16),
        in_specs=[pl.BlockSpec(memory_space=pltpu.SMEM)] + [vmem] * 6 + [anywhere] * 4,
        out_specs=vmem,
        scratch_shapes=[
            pltpu.VMEM(weight_time.shape, BF16),
            pltpu.VMEM(weight_up.shape, BF16),
            pltpu.VMEM((2, 2 * channels, 2 * channels), BF16),
            pltpu.VMEM(weight_three.shape, BF16),
            pltpu.VMEM((2, 9, LANES, half), BF16),
            pltpu.VMEM(weight_four.shape, BF16),
            pltpu.VMEM((2, 9, LANES, half), BF16),
            pltpu.VMEM((4, 2 * count * 4 * wide, LANES), F32),
            pltpu.VMEM(((frames + 2) * 6 * wide, channels), BF16),
            *planes(count, 6, wide, channels),
            *planes(count + 2, 8, wide, channels),
            *planes(count + 2, 6, wide, channels),
            pltpu.VMEM((count * 4 * wide, channels), F32),
            pltpu.SemaphoreType.DMA((8,)),
        ],
        compiler_params=pltpu.CompilerParams(vmem_limit_bytes=48 * 1024 * 1024),
        name="second_block",
    )(place, blocked, time, three, four, *gains, *weights)


def body(
    latent,
    cache_one,
    cache_two,
    cache_time,
    cache_three,
    cache_four,
    gain_one,
    gain_two,
    gain_three,
    gain_four,
    weight_one,
    weight_two,
    weight_time,
    weight_upsample,
    weight_three,
    weight_four,
):
    section, row, col = (lax.axis_index(name) for name in ("section", "rows", "cols"))
    sections, row_count, col_count = (lax.axis_size(name) for name in ("section", "rows", "cols"))
    width, channels = latent.shape[2:]
    tile = width // col_count
    part = tile // sections
    wide = part + 2 * HALO
    half = weight_three.shape[1]
    sizes = (2 * row_count, width)
    place = jnp.stack([section, col, col * tile + section * part - HALO, row]).astype(jnp.int32)

    latent = latent.reshape(latent.shape[0], width, channels)
    arrived = swapped(latent, "section")
    mine, theirs = pack(
        place, latent, arrived, cache_one[:, 0], cache_two[:, 0], wide, tile, part
    )
    theirs = swapped(theirs, "cols")
    own = jnp.stack([mine, theirs])
    pieces = [
        shifted(own, "rows", 2),
        shifted(own, "rows", 1),
        own,
        shifted(own, "rows", -1),
        shifted(own, "rows", -2),
    ]
    blocked = first_block(
        place,
        pieces,
        gain_one.reshape(1, -1),
        gain_two.reshape(1, -1),
        weight_one,
        weight_two,
        sizes,
    )

    def paired(array):
        return array.reshape(array.shape[0], array.shape[1], tile, channels)

    left = col == 0
    cache_time, cache_three, cache_four, _ = lax.optimization_barrier(
        (cache_time, cache_three, cache_four, mine)
    )
    tiles = jnp.concatenate([cache_time, paired(cache_three), paired(cache_four)], axis=1)
    edge = jnp.where(left, tiles[:, :, tile - HALO :], tiles[:, :, :HALO])
    edge = swapped(edge, "cols")
    tiles, edge, weight_upsample, weight_three, weight_four, _ = lax.optimization_barrier(
        (tiles, edge, weight_upsample, weight_three, weight_four, own)
    )
    nothing = jnp.zeros_like(edge)
    tiles = jnp.concatenate(
        [jnp.where(left, nothing, edge), tiles, jnp.where(left, edge, nothing)], axis=2
    )
    tiles = lax.dynamic_slice_in_dim(tiles, section * part, wide, 2)
    time, three, four = tiles[:, 0:2], tiles[:, 2:6], tiles[:, 6:10]
    above = shifted(jnp.concatenate([time, three[:, 2:], four[:, 3:]], axis=1), "rows", 1)
    below = shifted(jnp.concatenate([time, three[:, :2], four[:, :1]], axis=1), "rows", -1)
    time = jnp.concatenate([above[:, 0:2], time, below[:, 0:2]], axis=1)
    three = jnp.concatenate([above[:, 2:4], three, below[:, 2:4]], axis=1)
    four = jnp.concatenate([above[:, 4:], four, below[:, 4:]], axis=1)

    frames = second_block(
        place,
        blocked,
        time.reshape(-1, channels),
        three.reshape(2, -1, channels),
        four.reshape(2, -1, channels),
        (gain_three.reshape(1, -1), gain_four.reshape(1, -1)),
        (
            weight_time,
            weight_upsample.reshape(9, channels, half),
            weight_three.reshape(9, 3 * half, half),
            weight_four.reshape(9, 3 * half, half),
        ),
        sizes,
        wide,
    )
    count = frames.shape[0] // sections
    given = lax.dynamic_slice_in_dim(frames, (1 - section) * count, count, 0)
    kept = lax.dynamic_slice_in_dim(frames, section * count, count, 0)
    arrived = swapped(given, "section")
    low = section == 0
    joined = jnp.concatenate(
        [jnp.where(low, kept, arrived), jnp.where(low, arrived, kept)], axis=2
    )
    return joined.reshape(count, 4, 2 * tile, half)


def solution(mesh):
    placed = (
        P("section", ("rows", "cols"), None, None),
        P(None, ("rows", "cols"), None, None),
        P(None, ("rows", "cols"), None, None),
        P(None, "rows", "cols", None),
        P(None, "rows", "cols", None),
        P(None, "rows", "cols", None),
    ) + (P(),) * 10
    return jax.shard_map(
        body,
        mesh=mesh,
        in_specs=placed,
        out_specs=P("section", "rows", "cols", None),
        check_vma=False,
    )
```

```python
import functools

import jax
import jax.numpy as jnp
from jax import lax
from jax.experimental import pallas as pl
from jax.experimental.pallas import tpu as pltpu
from jax.sharding import PartitionSpec as P

EPSILON = 1e-06
HALO = 4
LANES = 256
BF16 = jnp.bfloat16
F32 = jnp.float32


def swapped(value, axis):
    return lax.ppermute(value, axis, [(0, 1), (1, 0)])


def shifted(value, axis, steps):
    count = lax.axis_size(axis)
    initial, last = (max(0, -steps), min(count, count - steps))
    return lax.ppermute(value, axis, [(source, source + steps) for source in range(initial, last)])


def silu(scaled):
    half = scaled * 0.5
    return half * (1.0 + jnp.tanh(half))


def activate(values, gain, mask):
    mean = jnp.mean(values * values, axis=-1, keepdims=True)
    return silu(values * (lax.rsqrt(mean + EPSILON) * mask) * gain)


def activate_pairs(values, gain, mask):
    channels = values.shape[-1] // 2
    squares = values * values
    first = lax.broadcasted_iota(jnp.int32, (1, 2 * channels), 1) < channels
    total = jnp.sum(squares, axis=-1, keepdims=True)
    low = jnp.sum(jnp.where(first, squares, 0.0), axis=-1, keepdims=True)
    scale_low = lax.rsqrt(low / channels + EPSILON) * mask
    scale_high = lax.rsqrt((total - low) / channels + EPSILON) * mask
    return silu(values * jnp.where(first, scale_low, scale_high) * gain)


def merge(even, odd, channels):
    turned = pltpu.roll(odd, channels - 128, 1)
    first = lax.broadcasted_iota(jnp.int32, (1, 128), 1) < channels - 128
    middle = jnp.where(first, even[:, 128:], turned[:, :128])
    return jnp.concatenate([even[:, :128], middle, turned[:, 128:]], axis=1)


def aligned(index, size):
    return pl.multiple_of(index * size, 16)


def line_mask(place, wide, first, count, limit, width):
    columns = place[2] + lax.broadcasted_iota(jnp.int32, (wide, 1), 0)
    inside = jnp.where((columns >= 0) & (columns < width), 1.0, 0.0)
    lines = []
    for i in range(count):
        line = first + i
        lines.append(inside * jnp.where((line >= 0) & (line < limit), 1.0, 0.0))
    return jnp.concatenate(lines, axis=0)


def store(even, odd, slot, values, height, wide):
    even[pl.ds(slot * (height * wide), height * wide), :] = values.astype(BF16)
    odd[pl.ds(slot * ((height - 2) * wide), (height - 2) * wide), :] = values[
        wide : (height - 1) * wide
    ].astype(BF16)


def taps(even, odd, begin, count, height, wide, dt, dy, lanes=slice(None)):
    inner = (height - 2) * wide
    if dy == 1:
        parts = [odd[pl.ds((begin + f + dt) * inner, inner), lanes] for f in range(count)]
    else:
        parts = [
            even[pl.ds((begin + f + dt) * height * wide + dy * wide, inner), lanes]
            for f in range(count)
        ]
    return jnp.concatenate(parts, axis=0)


def low_product(acc, even, odd, count, height, wide, weights, copies):
    rows = count * (height - 2) * wide
    channels = weights.shape[1]
    lanes = 3 * channels
    waited = 0
    for n in range(-(-lanes // LANES)):
        begin, end = n * LANES, min((n + 1) * LANES, lanes)
        while waited * channels < end:
            copies[waited].wait()
            waited += 1
        total = None
        for first, last in ((0, 4), (4, 8), (8, 9)):
            left = jnp.concatenate(
                [
                    taps(even, odd, 0, count, height, wide, t // 3, t % 3)
                    for t in range(first, last)
                ],
                axis=1,
            )
            right = weights[first:last, :, begin:end].reshape((last - first) * channels, -1)
            part = jnp.dot(left, right, preferred_element_type=F32)
            total = part if total is None else total + part
        acc[n, 0:rows, 0 : end - begin] = total


def low_sum(acc, start, size):
    rows = pl.ds(start, size)
    before = jnp.concatenate([acc[0, rows, :], acc[1, rows, 0:128]], axis=1)
    center = jnp.concatenate([acc[1, rows, 128:256], acc[2, rows, :]], axis=1)
    after = jnp.concatenate([acc[3, rows, :], acc[4, rows, 0:128]], axis=1)
    return center + pltpu.roll(before, 1, 0) + pltpu.roll(after, size - 1, 0)


def high_product(acc, even, odd, count, height, wide, weights, sides):
    rows = count * (height - 2) * wide
    channels = weights.shape[-1]

    def center(o, carry):
        total = None
        for first, last in ((0, 4), (4, 8), (8, 9)):
            left = jnp.concatenate(
                [
                    taps(even, odd, 0, count, height, wide, t // 3, t % 3)
                    for t in range(first, last)
                ],
                axis=1,
            )
            begin = pl.multiple_of((1 - o) * channels, 16)
            right = weights[first:last, pl.ds(begin, 2 * channels), :]
            right = right.reshape((last - first) * 2 * channels, channels)
            part = jnp.dot(left, right, preferred_element_type=F32)
            total = part if total is None else total + part
        acc[o, 0:rows, 0:channels] = total
        return carry

    lax.fori_loop(0, 2, center, 0)

    def side(o, carry):
        lanes = pl.ds(pl.multiple_of((1 - o) * 128, 128), LANES)
        left = jnp.concatenate(
            [taps(even, odd, 0, count, height, wide, t // 3, t % 3, lanes) for t in range(9)],
            axis=1,
        )
        right = sides[o].reshape(9 * LANES, channels)
        acc[2 + o, 0:rows, 0:channels] = jnp.dot(left, right, preferred_element_type=F32)
        return carry

    lax.fori_loop(0, 2, side, 0)


def high_sum(acc, start, size, channels):
    rows = pl.ds(start, size)
    even = acc[0, rows, :] + pltpu.roll(acc[2, rows, :], 1, 0)
    odd = acc[1, rows, :] + pltpu.roll(acc[3, rows, :], size - 1, 0)
    return merge(even, odd, channels)


def pack_kernel(wide, tile, part, place, latent, arrived, one, two, mine, theirs, spread):
    section, col = place[0], place[1]
    width, channels = latent.shape[1:]
    empty = jnp.zeros((spread.shape[1] - width, channels), F32)

    def put(slot, values):
        spread[slot] = pltpu.roll(
            jnp.concatenate([values.astype(F32), empty], axis=0), HALO, 0
        )

    for i in range(2):
        put(2 * section + i, latent[i])
        put(2 * (1 - section) + i, arrived[i])
        put(4 + i, one[i])
        put(6 + i, two[i])
    for slot in range(8):
        for ref, which in ((mine, col), (theirs, 1 - col)):
            begin = pl.multiple_of(which * tile + section * part, 8)
            ref[slot] = spread[slot, pl.ds(begin, wide), :].astype(BF16)


def pack(place, latent, arrived, one, two, wide, tile, part):
    width, channels = latent.shape[1:]
    vmem = pl.BlockSpec(memory_space=pltpu.VMEM)
    return pl.pallas_call(
        functools.partial(pack_kernel, wide, tile, part),
        out_shape=[jax.ShapeDtypeStruct((8, wide, channels), BF16)] * 2,
        in_specs=[pl.BlockSpec(memory_space=pltpu.SMEM)] + [vmem] * 4,
        out_specs=[vmem] * 2,
        scratch_shapes=[pltpu.VMEM((8, width + 16, channels), F32)],
        name="pack",
    )(place, latent, arrived, one, two)


def first_kernel(
    wide,
    sizes,
    place,
    above,
    own,
    below,
    gain_one,
    gain_two,
    weight_one,
    weight_two,
    out_ref,
    w1,
    w2,
    acc,
    x1e,
    x1o,
    x2e,
    x2o,
    sems,
):
    channels = own.shape[-1]
    frames = own.shape[1] - 4
    height, width = sizes
    col, row = place[1], place[3]
    pieces = (above, own, below)

    def load(source, target, base):
        return [
            pltpu.make_async_copy(
                source.at[:, dx], target.at[:, :, pl.ds(dx * channels, channels)], sems.at[base + dx]
            )
            for dx in range(3)
        ]

    copies_one = load(weight_one, w1, 0)
    copies_two = load(weight_two, w2, 3)
    for copy in copies_one + copies_two:
        copy.start()

    def rows_of(refs, index):
        return jnp.concatenate(
            [ref[lax.rem(y + col, 2), index].astype(F32) for ref in refs for y in range(2)], axis=0
        )

    for f in range(2):
        store(x1e, x1o, f, rows_of(pieces, frames + f), 6, wide)
        store(x2e, x2o, f, rows_of(pieces, frames + 2 + f)[wide : 5 * wide], 4, wide)

    def norm_one(f, carry):
        values = activate(rows_of(pieces, f), gain_one[...], 1.0)
        store(x1e, x1o, f + 2, values, 6, wide)
        return carry

    lax.fori_loop(0, frames, norm_one, 0)
    low_product(acc, x1e, x1o, frames, 6, wide, w1, copies_one)

    mask = line_mask(place, wide, 2 * row - 1, 4, height, width)

    def norm_two(f, carry):
        size = 4 * wide
        values = activate(low_sum(acc, aligned(f, size), size), gain_two[...], mask)
        store(x2e, x2o, f + 2, values, 4, wide)
        return carry

    lax.fori_loop(0, frames, norm_two, 0)
    low_product(acc, x2e, x2o, frames, 4, wide, w2, copies_two)

    def residual(f, carry):
        size = 2 * wide
        values = low_sum(acc, aligned(f, size), size) + rows_of((own,), f)
        out_ref[f] = values.astype(BF16)
        return carry

    lax.fori_loop(0, frames, residual, 0)


def planes(slots, height, wide, channels):
    return [
        pltpu.VMEM((slots * height * wide, channels), BF16),
        pltpu.VMEM((slots * (height - 2) * wide, channels), BF16),
    ]


def first_block(place, pieces, gain_one, gain_two, weight_one, weight_two, sizes):
    _, units, wide, channels = pieces[0].shape
    frames = units - 4
    slots = -(-3 * channels // LANES)
    vmem = pl.BlockSpec(memory_space=pltpu.VMEM)
    anywhere = pl.BlockSpec(memory_space=pl.ANY)
    return pl.pallas_call(
        functools.partial(first_kernel, wide, sizes),
        out_shape=jax.ShapeDtypeStruct((frames, 2 * wide, channels), BF16),
        in_specs=[pl.BlockSpec(memory_space=pltpu.SMEM)] + [vmem] * 5 + [anywhere] * 2,
        out_specs=vmem,
        scratch_shapes=[
            pltpu.VMEM((9, channels, slots * LANES), BF16),
            pltpu.VMEM((9, channels, slots * LANES), BF16),
            pltpu.VMEM((slots, frames * 4 * wide, LANES), F32),
            *planes(frames + 2, 6, wide, channels),
            *planes(frames + 2, 4, wide, channels),
            pltpu.SemaphoreType.DMA((6,)),
        ],
        compiler_params=pltpu.CompilerParams(vmem_limit_bytes=40 * 1024 * 1024),
        cost_estimate=pl.CostEstimate(
            flops=2 * 27 * channels * channels * frames * 6 * wide,
            bytes_accessed=2 * 54 * channels * channels,
            transcendentals=0,
        ),
        name="first_block",
    )(place, *pieces, gain_one, gain_two, weight_one, weight_two)


def second_kernel(
    wide,
    sizes,
    place,
    above,
    blocked,
    below,
    time_ref,
    three_ref,
    four_ref,
    gain_three,
    gain_four,
    weight_time,
    weight_up,
    weight_three,
    weight_four,
    out_ref,
    wt,
    wr,
    wu,
    w3,
    s3,
    w4,
    s4,
    acc,
    mixed,
    de,
    do,
    x3e,
    x3o,
    x4e,
    x4o,
    lifted_ref,
    sems,
):
    channels = blocked.shape[-1]
    half = channels // 2
    size = 6 * wide
    frames = blocked.shape[0]
    count = 2 * frames
    height, width = sizes
    row = place[3]

    def load_high(source, target, sides, base):
        blank = LANES - half
        return [
            pltpu.make_async_copy(source, target, sems.at[base]),
            pltpu.make_async_copy(
                source.at[:, pl.ds(0, half), :],
                sides.at[0, :, pl.ds(blank, half), :],
                sems.at[base + 1],
            ),
            pltpu.make_async_copy(
                source.at[:, pl.ds(2 * half, half), :],
                sides.at[1, :, pl.ds(0, half), :],
                sems.at[base + 2],
            ),
        ]

    copy_time = pltpu.make_async_copy(weight_time, wt, sems.at[0])
    copy_up = pltpu.make_async_copy(weight_up, wr, sems.at[1])
    copies_three = load_high(weight_three, w3, s3, 2)
    copies_four = load_high(weight_four, w4, s4, 5)
    copy_time.start()
    copy_up.start()
    for copy in copies_three + copies_four:
        copy.start()

    blank = jnp.zeros((9, LANES - half, half), BF16)
    for sides in (s3, s4):
        sides[0, :, 0 : LANES - half, :] = blank
        sides[1, :, half:LANES, :] = blank

    mixed[0 : 2 * size, :] = time_ref[...]
    for f in range(frames):
        for i, ref in enumerate((above, blocked, below)):
            begin = (f + 2) * size + i * 2 * wide
            mixed[begin : begin + 2 * wide, :] = ref[f]
    copy_time.wait()

    def mix(n, carry):
        lanes = pl.ds(pl.multiple_of(n * LANES, LANES), LANES)
        left = jnp.concatenate(
            [mixed[pl.ds(t * size, frames * size), :] for t in range(3)], axis=1
        )
        acc[n, 0 : frames * size, :] = jnp.dot(left, wt[:, lanes], preferred_element_type=F32)
        return carry

    lax.fori_loop(0, 2 * channels // LANES, mix, 0)
    mask_low = line_mask(place, wide, 2 * row - 2, 6, height, width)

    def double(t, carry):
        rows = pl.ds(aligned(t, size), size)
        first = jnp.concatenate([acc[0, rows, :], acc[1, rows, 0:128]], axis=1)
        second = jnp.concatenate([acc[1, rows, 128:256], acc[2, rows, :]], axis=1)
        store(de, do, 2 * t, first * mask_low, 6, wide)
        store(de, do, 2 * t + 1, second * mask_low, 6, wide)
        return carry

    lax.fori_loop(0, frames, double, 0)
    copy_up.wait()

    chunk = 16

    def combine(k, carry):
        rows = pl.ds(aligned(k, chunk), chunk)
        taken = [[wr[3 * dy + dx, rows, :].astype(F32) for dx in range(3)] for dy in range(3)]
        gap = jnp.zeros((chunk, LANES - half), F32)
        for slot, dys in enumerate(((0,), (1, 2), (0, 1), (2,))):
            line = [sum(taken[dy][dx] for dy in dys) for dx in range(3)]
            line = [jnp.concatenate([part, gap], axis=1) for part in line]
            into = pl.ds(aligned(k, chunk) + (slot % 2) * channels, chunk)
            wu[slot // 2, into, 0:channels] = merge(
                line[1] + line[2], line[0] + line[1], half
            ).astype(BF16)
            wu[slot // 2, into, channels : 2 * channels] = merge(line[0], line[2], half).astype(
                BF16
            )
        return carry

    lax.fori_loop(0, channels // chunk, combine, 0)

    for py in range(2):

        def enlarge(n, carry):
            lanes = pl.ds(pl.multiple_of(n * LANES, LANES), LANES)
            left = jnp.concatenate(
                [taps(de, do, 0, count, 6, wide, 0, py), taps(de, do, 0, count, 6, wide, 0, py + 1)],
                axis=1,
            )
            acc[n, py * count * 4 * wide : (py + 1) * count * 4 * wide, :] = jnp.dot(
                left, wu[py, :, lanes], preferred_element_type=F32
            )
            return carry

        lax.fori_loop(0, 2 * channels // LANES, enlarge, 0)

    for f in range(2):
        store(x3e, x3o, f, three_ref[f].astype(F32), 8, wide)
        store(x4e, x4o, f, four_ref[f].astype(F32), 6, wide)
    gain3 = jnp.concatenate([gain_three[...], gain_three[...]], axis=1)
    gain4 = jnp.concatenate([gain_four[...], gain_four[...]], axis=1)
    mask_three = line_mask(place, wide, 4 * row - 2, 8, 2 * height, width)
    first_half = lax.broadcasted_iota(jnp.int32, (1, channels), 1) < half
    part = 4 * wide

    def norm_three(f, carry):
        values = []
        for py in range(2):
            rows = pl.ds(pl.multiple_of(py * count * part + f * part, 16), part)
            center = jnp.concatenate([acc[0, rows, :], acc[1, rows, 0:128]], axis=1)
            side = jnp.concatenate([acc[1, rows, 128:256], acc[2, rows, :]], axis=1)
            side = jnp.where(first_half, pltpu.roll(side, 1, 0), pltpu.roll(side, part - 1, 0))
            values.append((center + side).astype(BF16).astype(F32))
        lifted = jnp.concatenate(
            [values[h % 2][(h // 2) * wide : (h // 2 + 1) * wide] for h in range(8)], axis=0
        )
        lifted_ref[pl.ds(aligned(f, part), part), :] = lifted[2 * wide : 6 * wide]
        store(x3e, x3o, f + 2, activate_pairs(lifted, gain3, mask_three), 8, wide)
        return carry

    lax.fori_loop(0, count, norm_three, 0)
    for copy in copies_three:
        copy.wait()
    high_product(acc, x3e, x3o, count, 8, wide, w3, s3)

    mask_four = mask_three[wide : 7 * wide]

    def norm_four(f, carry):
        values = high_sum(acc, aligned(f, size), size, half)
        store(x4e, x4o, f + 2, activate_pairs(values, gain4, mask_four), 6, wide)
        return carry

    lax.fori_loop(0, count, norm_four, 0)
    for copy in copies_four:
        copy.wait()
    high_product(acc, x4e, x4o, count, 6, wide, w4, s4)

    def finish(f, carry):
        start = aligned(f, part)
        values = high_sum(acc, start, part, half) + lifted_ref[pl.ds(start, part), :]
        values = pltpu.roll(values, part - HALO, 0)
        for y in range(4):
            inner = wide - 2 * HALO
            out_ref[f, y] = values[y * wide : y * wide + inner].astype(BF16)
        return carry

    lax.fori_loop(0, count, finish, 0)


def second_block(place, pieces, time, three, four, gains, weights, sizes, wide):
    frames, _, channels = pieces[0].shape
    half = channels // 2
    count = 2 * frames
    weight_time, weight_up, weight_three, weight_four = weights
    vmem = pl.BlockSpec(memory_space=pltpu.VMEM)
    anywhere = pl.BlockSpec(memory_space=pl.ANY)
    return pl.pallas_call(
        functools.partial(second_kernel, wide, sizes),
        out_shape=jax.ShapeDtypeStruct((count, 4, wide - 2 * HALO, channels), BF16),
        in_specs=[pl.BlockSpec(memory_space=pltpu.SMEM)] + [vmem] * 8 + [anywhere] * 4,
        out_specs=vmem,
        scratch_shapes=[
            pltpu.VMEM(weight_time.shape, BF16),
            pltpu.VMEM(weight_up.shape, BF16),
            pltpu.VMEM((2, 2 * channels, 2 * channels), BF16),
            pltpu.VMEM(weight_three.shape, BF16),
            pltpu.VMEM((2, 9, LANES, half), BF16),
            pltpu.VMEM(weight_four.shape, BF16),
            pltpu.VMEM((2, 9, LANES, half), BF16),
            pltpu.VMEM((4, 2 * count * 4 * wide, LANES), F32),
            pltpu.VMEM(((frames + 2) * 6 * wide, channels), BF16),
            *planes(count, 6, wide, channels),
            *planes(count + 2, 8, wide, channels),
            *planes(count + 2, 6, wide, channels),
            pltpu.VMEM((count * 4 * wide, channels), F32),
            pltpu.SemaphoreType.DMA((8,)),
        ],
        compiler_params=pltpu.CompilerParams(vmem_limit_bytes=48 * 1024 * 1024),
        name="second_block",
    )(place, *pieces, time, three, four, *gains, *weights)


def body(
    latent,
    cache_one,
    cache_two,
    cache_time,
    cache_three,
    cache_four,
    gain_one,
    gain_two,
    gain_three,
    gain_four,
    weight_one,
    weight_two,
    weight_time,
    weight_upsample,
    weight_three,
    weight_four,
):
    section, row, col = (lax.axis_index(name) for name in ("section", "rows", "cols"))
    sections, row_count, col_count = (lax.axis_size(name) for name in ("section", "rows", "cols"))
    width, channels = latent.shape[2:]
    tile = width // col_count
    part = tile // sections
    wide = part + 2 * HALO
    half = weight_three.shape[1]
    sizes = (2 * row_count, width)
    place = jnp.stack([section, col, col * tile + section * part - HALO, row]).astype(jnp.int32)

    latent = latent.reshape(latent.shape[0], width, channels)
    arrived = swapped(latent, "section")
    mine, theirs = pack(
        place, latent, arrived, cache_one[:, 0], cache_two[:, 0], wide, tile, part
    )
    theirs = swapped(theirs, "cols")
    own = jnp.stack([mine, theirs])
    pieces = [shifted(own, "rows", 1), own, shifted(own, "rows", -1)]
    blocked = first_block(
        place,
        pieces,
        gain_one.reshape(1, -1),
        gain_two.reshape(1, -1),
        weight_one.reshape(9, 3, channels, channels),
        weight_two.reshape(9, 3, channels, channels),
        sizes,
    )
    blocks = [shifted(blocked, "rows", 1), blocked, shifted(blocked, "rows", -1)]

    def paired(array):
        return array.reshape(array.shape[0], array.shape[1], tile, channels)

    left = col == 0
    cache_time, cache_three, cache_four, _ = lax.optimization_barrier(
        (cache_time, cache_three, cache_four, mine)
    )
    tiles = jnp.concatenate([cache_time, paired(cache_three), paired(cache_four)], axis=1)
    edge = jnp.where(left, tiles[:, :, tile - HALO :], tiles[:, :, :HALO])
    edge = swapped(edge, "cols")
    weight_upsample, weight_three, _ = lax.optimization_barrier(
        (weight_upsample, weight_three, own)
    )
    weight_four, _ = lax.optimization_barrier((weight_four, blocked))
    nothing = jnp.zeros_like(edge)
    tiles = jnp.concatenate(
        [jnp.where(left, nothing, edge), tiles, jnp.where(left, edge, nothing)], axis=2
    )
    tiles = lax.dynamic_slice_in_dim(tiles, section * part, wide, 2)
    time, three, four = tiles[:, 0:2], tiles[:, 2:6], tiles[:, 6:10]
    above = jnp.concatenate([time, three[:, 2:], four[:, 3:]], axis=1)
    below = jnp.concatenate([time, three[:, :2], four[:, :1]], axis=1)
    above, below, *_ = lax.optimization_barrier((above, below, *pieces))
    above, below = shifted(above, "rows", 1), shifted(below, "rows", -1)
    time = jnp.concatenate([above[:, 0:2], time, below[:, 0:2]], axis=1)
    three = jnp.concatenate([above[:, 2:4], three, below[:, 2:4]], axis=1)
    four = jnp.concatenate([above[:, 4:], four, below[:, 4:]], axis=1)

    frames = second_block(
        place,
        blocks,
        time.reshape(-1, channels),
        three.reshape(2, -1, channels),
        four.reshape(2, -1, channels),
        (gain_three.reshape(1, -1), gain_four.reshape(1, -1)),
        (
            weight_time,
            weight_upsample.reshape(9, channels, half),
            weight_three.reshape(9, 3 * half, half),
            weight_four.reshape(9, 3 * half, half),
        ),
        sizes,
        wide,
    )
    count = frames.shape[0] // sections
    given = lax.dynamic_slice_in_dim(frames, (1 - section) * count, count, 0)
    kept = lax.dynamic_slice_in_dim(frames, section * count, count, 0)
    arrived = swapped(given, "section")
    low = section == 0
    joined = jnp.concatenate(
        [jnp.where(low, kept, arrived), jnp.where(low, arrived, kept)], axis=2
    )
    return joined.reshape(count, 4, 2 * tile, half)


def solution(mesh):
    placed = (
        P("section", ("rows", "cols"), None, None),
        P(None, ("rows", "cols"), None, None),
        P(None, ("rows", "cols"), None, None),
        P(None, "rows", "cols", None),
        P(None, "rows", "cols", None),
        P(None, "rows", "cols", None),
    ) + (P(),) * 10
    return jax.shard_map(
        body,
        mesh=mesh,
        in_specs=placed,
        out_specs=P("section", "rows", "cols", None),
        check_vma=False,
    )
```

```python
import functools

import jax
import jax.numpy as jnp
from jax import lax
from jax.experimental import pallas as pl
from jax.experimental.pallas import tpu as pltpu
from jax.sharding import PartitionSpec as P

EPSILON = 1e-06
HALO = 4
LANES = 256
BF16 = jnp.bfloat16
F32 = jnp.float32


def swapped(value, axis):
    return lax.ppermute(value, axis, [(0, 1), (1, 0)])


def shifted(value, axis, steps):
    count = lax.axis_size(axis)
    initial, last = (max(0, -steps), min(count, count - steps))
    return lax.ppermute(value, axis, [(source, source + steps) for source in range(initial, last)])


def silu(scaled):
    half = scaled * 0.5
    return half * (1.0 + jnp.tanh(half))


def activate(values, gain, mask):
    mean = jnp.mean(values * values, axis=-1, keepdims=True)
    return silu(values * (lax.rsqrt(mean + EPSILON) * mask) * gain)


def activate_pairs(values, gain, mask):
    channels = values.shape[-1] // 2
    squares = values * values
    first = lax.broadcasted_iota(jnp.int32, (1, 2 * channels), 1) < channels
    total = jnp.sum(squares, axis=-1, keepdims=True)
    low = jnp.sum(jnp.where(first, squares, 0.0), axis=-1, keepdims=True)
    scale_low = lax.rsqrt(low / channels + EPSILON) * mask
    scale_high = lax.rsqrt((total - low) / channels + EPSILON) * mask
    return silu(values * jnp.where(first, scale_low, scale_high) * gain)


def merge(even, odd, channels):
    turned = pltpu.roll(odd, channels - 128, 1)
    first = lax.broadcasted_iota(jnp.int32, (1, 128), 1) < channels - 128
    middle = jnp.where(first, even[:, 128:], turned[:, :128])
    return jnp.concatenate([even[:, :128], middle, turned[:, 128:]], axis=1)


def aligned(index, size):
    return pl.multiple_of(index * size, 16)


def line_mask(place, wide, first, count, limit, width):
    columns = place[2] + lax.broadcasted_iota(jnp.int32, (wide, 1), 0)
    inside = jnp.where((columns >= 0) & (columns < width), 1.0, 0.0)
    lines = []
    for i in range(count):
        line = first + i
        lines.append(inside * jnp.where((line >= 0) & (line < limit), 1.0, 0.0))
    return jnp.concatenate(lines, axis=0)


def store(even, odd, slot, values, height, wide):
    even[pl.ds(slot * (height * wide), height * wide), :] = values.astype(BF16)
    odd[pl.ds(slot * ((height - 2) * wide), (height - 2) * wide), :] = values[
        wide : (height - 1) * wide
    ].astype(BF16)


def taps(even, odd, begin, count, height, wide, dt, dy, lanes=slice(None)):
    inner = (height - 2) * wide
    if dy == 1:
        parts = [odd[pl.ds((begin + f + dt) * inner, inner), lanes] for f in range(count)]
    else:
        parts = [
            even[pl.ds((begin + f + dt) * height * wide + dy * wide, inner), lanes]
            for f in range(count)
        ]
    return jnp.concatenate(parts, axis=0)


def low_product(acc, even, odd, count, height, wide, weights, copies):
    rows = count * (height - 2) * wide
    channels = weights.shape[1]
    lanes = 3 * channels
    waited = 0
    for n in range(-(-lanes // LANES)):
        begin, end = n * LANES, min((n + 1) * LANES, lanes)
        while waited * channels < end:
            copies[waited].wait()
            waited += 1
        total = None
        for first, last in ((0, 4), (4, 8), (8, 9)):
            left = jnp.concatenate(
                [
                    taps(even, odd, 0, count, height, wide, t // 3, t % 3)
                    for t in range(first, last)
                ],
                axis=1,
            )
            right = weights[first:last, :, begin:end].reshape((last - first) * channels, -1)
            part = jnp.dot(left, right, preferred_element_type=F32)
            total = part if total is None else total + part
        acc[n, 0:rows, 0 : end - begin] = total


def low_sum(acc, start, size):
    rows = pl.ds(start, size)
    before = jnp.concatenate([acc[0, rows, :], acc[1, rows, 0:128]], axis=1)
    center = jnp.concatenate([acc[1, rows, 128:256], acc[2, rows, :]], axis=1)
    after = jnp.concatenate([acc[3, rows, :], acc[4, rows, 0:128]], axis=1)
    return center + pltpu.roll(before, 1, 0) + pltpu.roll(after, size - 1, 0)


def high_product(acc, even, odd, count, height, wide, weights, sides):
    rows = count * (height - 2) * wide
    channels = weights.shape[-1]

    def center(o, carry):
        total = None
        for first, last in ((0, 4), (4, 8), (8, 9)):
            left = jnp.concatenate(
                [
                    taps(even, odd, 0, count, height, wide, t // 3, t % 3)
                    for t in range(first, last)
                ],
                axis=1,
            )
            begin = pl.multiple_of((1 - o) * channels, 16)
            right = weights[first:last, pl.ds(begin, 2 * channels), :]
            right = right.reshape((last - first) * 2 * channels, channels)
            part = jnp.dot(left, right, preferred_element_type=F32)
            total = part if total is None else total + part
        acc[o, 0:rows, 0:channels] = total
        return carry

    lax.fori_loop(0, 2, center, 0)

    def side(o, carry):
        lanes = pl.ds(pl.multiple_of((1 - o) * 128, 128), LANES)
        left = jnp.concatenate(
            [taps(even, odd, 0, count, height, wide, t // 3, t % 3, lanes) for t in range(9)],
            axis=1,
        )
        right = sides[o].reshape(9 * LANES, channels)
        acc[2 + o, 0:rows, 0:channels] = jnp.dot(left, right, preferred_element_type=F32)
        return carry

    lax.fori_loop(0, 2, side, 0)


def high_sum(acc, start, size, channels):
    rows = pl.ds(start, size)
    even = acc[0, rows, :] + pltpu.roll(acc[2, rows, :], 1, 0)
    odd = acc[1, rows, :] + pltpu.roll(acc[3, rows, :], size - 1, 0)
    return merge(even, odd, channels)


def pack_kernel(wide, tile, part, place, latent, arrived, one, two, mine, theirs, spread):
    section, col = place[0], place[1]
    width, channels = latent.shape[1:]
    empty = jnp.zeros((spread.shape[1] - width, channels), F32)

    def put(slot, values):
        spread[slot] = pltpu.roll(
            jnp.concatenate([values.astype(F32), empty], axis=0), HALO, 0
        )

    for i in range(2):
        put(2 * section + i, latent[i])
        put(2 * (1 - section) + i, arrived[i])
        put(4 + i, one[i])
        put(6 + i, two[i])
    for slot in range(8):
        for ref, which in ((mine, col), (theirs, 1 - col)):
            begin = pl.multiple_of(which * tile + section * part, 8)
            ref[slot] = spread[slot, pl.ds(begin, wide), :].astype(BF16)


def pack(place, latent, arrived, one, two, wide, tile, part):
    width, channels = latent.shape[1:]
    vmem = pl.BlockSpec(memory_space=pltpu.VMEM)
    return pl.pallas_call(
        functools.partial(pack_kernel, wide, tile, part),
        out_shape=[jax.ShapeDtypeStruct((8, wide, channels), BF16)] * 2,
        in_specs=[pl.BlockSpec(memory_space=pltpu.SMEM)] + [vmem] * 4,
        out_specs=[vmem] * 2,
        scratch_shapes=[pltpu.VMEM((8, width + 16, channels), F32)],
        name="pack",
    )(place, latent, arrived, one, two)


def stack_kernel(place, mine, theirs, later, own, up, down):
    del later
    count = mine.shape[0] - 2
    own[0], own[1] = mine[...], theirs[...]
    for ref, y in ((up, 1), (down, 0)):
        ref[0:count], ref[count : 2 * count] = mine[0:count], theirs[0:count]
        here = lax.rem(y + place[1], 2) == 0
        ref[2 * count :] = jnp.where(here, mine[count:], theirs[count:])


def stack(place, mine, theirs, later):
    units, wide, channels = mine.shape
    vmem = pl.BlockSpec(memory_space=pltpu.VMEM)
    lines = 2 * units - 2
    return pl.pallas_call(
        stack_kernel,
        out_shape=[jax.ShapeDtypeStruct((2, units, wide, channels), BF16)]
        + [jax.ShapeDtypeStruct((lines, wide, channels), BF16)] * 2,
        in_specs=[pl.BlockSpec(memory_space=pltpu.SMEM)]
        + [vmem] * 2
        + [pl.BlockSpec(memory_space=pl.ANY)],
        out_specs=[vmem] * 3,
        name="stack",
    )(place, mine, theirs, later)


def tiles_kernel(time, three, four, own, up, down, low, high):
    half = three.shape[-1]
    slot = 0
    for f in range(2):
        for y in range(2):
            line = time[f, y]
            own[slot] = line
            up[2 * f + y] = line
            down[2 * f + y] = line
            slot += 1
    for ref, base, depth in ((three, 4, 2), (four, 8, 1)):
        for f in range(2):
            for y in range(4):
                values = ref[f, y].astype(F32)
                low[...] = values[:, :128]
                high[:, 0 : half - 128] = values[:, 128:]
                count = values.shape[0] // 2
                even, odd = (
                    jnp.concatenate(
                        [part[pl.ds(o, count, stride=2), :] for part in (low, high)], axis=1
                    )
                    for o in range(2)
                )
                line = merge(even, odd, half).astype(BF16)
                own[slot] = line
                if y >= 4 - depth:
                    up[base + depth * f + y - (4 - depth)] = line
                if y < depth:
                    down[base + depth * f + y] = line
                slot += 1


def pair_tiles(time, three, four):
    tile, channels = time.shape[2:]
    vmem = pl.BlockSpec(memory_space=pltpu.VMEM)
    return pl.pallas_call(
        tiles_kernel,
        out_shape=[jax.ShapeDtypeStruct((n, tile, channels), BF16) for n in (20, 10, 10)],
        in_specs=[vmem] * 3,
        out_specs=[vmem] * 3,
        scratch_shapes=[pltpu.VMEM((three.shape[2], 128), F32)] * 2,
        name="pair_tiles",
    )(time, three, four)


def edges_kernel(place, own, above, below, edge):
    left = place[1] == 0
    slot = 0
    for ref in (own, above, below):
        for i in range(ref.shape[0]):
            line = ref[i].astype(F32)
            edge[slot] = jnp.where(left, line[-8:], line[:8]).astype(BF16)
            slot += 1


def tile_edges(place, own, above, below):
    channels = own.shape[-1]
    vmem = pl.BlockSpec(memory_space=pltpu.VMEM)
    lines = own.shape[0] + above.shape[0] + below.shape[0]
    return pl.pallas_call(
        edges_kernel,
        out_shape=jax.ShapeDtypeStruct((lines, 8, channels), BF16),
        in_specs=[pl.BlockSpec(memory_space=pltpu.SMEM)] + [vmem] * 3,
        out_specs=vmem,
        name="tile_edges",
    )(place, own, above, below)


def windows_kernel(wide, place, own, above, below, edge, time, three, four):
    first, left = place[0] == 0, place[1] == 0
    part = wide - 2 * HALO
    width = own.shape[1] + 16
    empty = jnp.zeros((8, own.shape[-1]), F32)

    def line(ref, index, slot):
        side = edge[slot].astype(F32)
        whole = jnp.concatenate(
            [
                jnp.where(left, empty, side),
                ref[index].astype(F32),
                jnp.where(left, side, empty),
            ],
            axis=0,
        )
        begin = 8 - HALO
        low = pltpu.roll(whole, width - begin, 0)[:wide]
        high = pltpu.roll(whole, width - begin - part, 0)[:wide]
        return jnp.where(first, low, high)

    def lines(ref, offset, begin, count):
        return [line(ref, i, offset + i) for i in range(begin, begin + count)]

    n = own.shape[0]
    m = n + above.shape[0]
    for f in range(2):
        for ref, base, start, count, depth in (
            (time, 0, 0, 2, 2),
            (three, 4, 4, 4, 2),
            (four, 12, 8, 4, 1),
        ):
            parts = lines(above, n, start + depth * f, depth)
            parts += lines(own, 0, base + count * f, count)
            parts += lines(below, m, start + depth * f, depth)
            ref[f] = jnp.concatenate(parts, axis=0).astype(BF16)


def tile_windows(place, own, above, below, edge, wide):
    channels = own.shape[-1]
    vmem = pl.BlockSpec(memory_space=pltpu.VMEM)
    return pl.pallas_call(
        functools.partial(windows_kernel, wide),
        out_shape=[jax.ShapeDtypeStruct((2, n * wide, channels), BF16) for n in (6, 8, 6)],
        in_specs=[pl.BlockSpec(memory_space=pltpu.SMEM)] + [vmem] * 4,
        out_specs=[vmem] * 3,
        name="tile_windows",
    )(place, own, above, below, edge)


def combine_kernel(wr, wu):
    channels, half = wr.shape[1:]
    chunk = 32

    def combine(k, carry):
        rows = pl.ds(aligned(k, chunk), chunk)
        taken = [[wr[3 * dy + dx, rows, :].astype(F32) for dx in range(3)] for dy in range(3)]
        gap = jnp.zeros((chunk, LANES - half), F32)
        for slot, dys in enumerate(((0,), (1, 2), (0, 1), (2,))):
            line = [sum(taken[dy][dx] for dy in dys) for dx in range(3)]
            line = [jnp.concatenate([part, gap], axis=1) for part in line]
            into = pl.ds(aligned(k, chunk) + (slot % 2) * channels, chunk)
            wu[slot // 2, into, 0:channels] = merge(
                line[1] + line[2], line[0] + line[1], half
            ).astype(BF16)
            wu[slot // 2, into, channels : 2 * channels] = merge(line[0], line[2], half).astype(
                BF16
            )
        return carry

    lax.fori_loop(0, channels // chunk, combine, 0)


def combine_weights(weight):
    channels = weight.shape[1]
    vmem = pl.BlockSpec(memory_space=pltpu.VMEM)
    return pl.pallas_call(
        combine_kernel,
        out_shape=jax.ShapeDtypeStruct((2, 2 * channels, 2 * channels), BF16),
        in_specs=[vmem],
        out_specs=vmem,
        name="combine_weights",
    )(weight)


def first_kernel(
    wide,
    sizes,
    place,
    above,
    own,
    below,
    gain_one,
    gain_two,
    weight_one,
    weight_two,
    later_one,
    later_two,
    out_ref,
    w1,
    w2,
    acc,
    x1e,
    x1o,
    x2e,
    x2o,
    sems,
):
    channels = own.shape[-1]
    frames = own.shape[1] - 4
    height, width = sizes
    col, row = place[1], place[3]
    units = frames + 2
    del later_one, later_two

    def load(source, target, base):
        return [
            pltpu.make_async_copy(
                source.at[:, dx], target.at[:, :, pl.ds(dx * channels, channels)], sems.at[base + dx]
            )
            for dx in range(3)
        ]

    copies_one = load(weight_one, w1, 0)
    copies_two = load(weight_two, w2, 3)
    for copy in copies_one + copies_two:
        copy.start()

    slots = [lax.rem(y + col, 2) for y in range(2)]

    def own_rows(index):
        return [own[slot, index].astype(F32) for slot in slots]

    def rows_of(index):
        first = [above[slot * units + index].astype(F32) for slot in slots]
        last = [below[slot * units + index].astype(F32) for slot in slots]
        return jnp.concatenate(first + own_rows(index) + last, axis=0)

    for f in range(2):
        store(x1e, x1o, f, rows_of(frames + f), 6, wide)
        first, last = above[2 * units + f].astype(F32), below[2 * units + f].astype(F32)
        values = jnp.concatenate([first] + own_rows(units + f) + [last], axis=0)
        store(x2e, x2o, f, values, 4, wide)

    def norm_one(f, carry):
        values = activate(rows_of(f), gain_one[...], 1.0)
        store(x1e, x1o, f + 2, values, 6, wide)
        return carry

    lax.fori_loop(0, frames, norm_one, 0)
    low_product(acc, x1e, x1o, frames, 6, wide, w1, copies_one)

    mask = line_mask(place, wide, 2 * row - 1, 4, height, width)

    def norm_two(f, carry):
        size = 4 * wide
        values = activate(low_sum(acc, aligned(f, size), size), gain_two[...], mask)
        store(x2e, x2o, f + 2, values, 4, wide)
        return carry

    lax.fori_loop(0, frames, norm_two, 0)
    low_product(acc, x2e, x2o, frames, 4, wide, w2, copies_two)

    def residual(f, carry):
        size = 2 * wide
        values = low_sum(acc, aligned(f, size), size) + jnp.concatenate(own_rows(f), axis=0)
        out_ref[f] = values.astype(BF16)
        return carry

    lax.fori_loop(0, frames, residual, 0)


def planes(slots, height, wide, channels):
    return [
        pltpu.VMEM((slots * height * wide, channels), BF16),
        pltpu.VMEM((slots * (height - 2) * wide, channels), BF16),
    ]


def first_block(place, pieces, gain_one, gain_two, weight_one, weight_two, later, sizes):
    _, units, wide, channels = pieces[1].shape
    frames = units - 4
    slots = -(-3 * channels // LANES)
    vmem = pl.BlockSpec(memory_space=pltpu.VMEM)
    anywhere = pl.BlockSpec(memory_space=pl.ANY)
    return pl.pallas_call(
        functools.partial(first_kernel, wide, sizes),
        out_shape=jax.ShapeDtypeStruct((frames, 2 * wide, channels), BF16),
        in_specs=[pl.BlockSpec(memory_space=pltpu.SMEM)] + [vmem] * 5 + [anywhere] * 4,
        out_specs=vmem,
        scratch_shapes=[
            pltpu.VMEM((9, channels, slots * LANES), BF16),
            pltpu.VMEM((9, channels, slots * LANES), BF16),
            pltpu.VMEM((slots, frames * 4 * wide, LANES), F32),
            *planes(frames + 2, 6, wide, channels),
            *planes(frames + 2, 4, wide, channels),
            pltpu.SemaphoreType.DMA((6,)),
        ],
        compiler_params=pltpu.CompilerParams(vmem_limit_bytes=52 * 1024 * 1024),
        cost_estimate=pl.CostEstimate(
            flops=2 * 27 * channels * channels * frames * 6 * wide,
            bytes_accessed=2 * 54 * channels * channels,
            transcendentals=0,
        ),
        name="first_block",
    )(place, *pieces, gain_one, gain_two, weight_one, weight_two, *later)


def second_kernel(
    wide,
    sizes,
    place,
    above,
    blocked,
    below,
    time_ref,
    three_ref,
    four_ref,
    gain_three,
    gain_four,
    wt,
    wu,
    weight_three,
    weight_four,
    out_ref,
    w3,
    s3,
    w4,
    s4,
    acc,
    mixed,
    de,
    do,
    x3e,
    x3o,
    x4e,
    x4o,
    lifted_ref,
    sems,
):
    channels = blocked.shape[-1]
    half = channels // 2
    size = 6 * wide
    frames = blocked.shape[0]
    count = 2 * frames
    height, width = sizes
    row = place[3]

    def load_high(source, target, sides, base):
        blank = LANES - half
        return [
            pltpu.make_async_copy(source, target, sems.at[base]),
            pltpu.make_async_copy(
                source.at[:, pl.ds(0, half), :],
                sides.at[0, :, pl.ds(blank, half), :],
                sems.at[base + 1],
            ),
            pltpu.make_async_copy(
                source.at[:, pl.ds(2 * half, half), :],
                sides.at[1, :, pl.ds(0, half), :],
                sems.at[base + 2],
            ),
        ]

    copies_three = load_high(weight_three, w3, s3, 0)
    copies_four = load_high(weight_four, w4, s4, 3)
    for copy in copies_three + copies_four:
        copy.start()

    blank = jnp.zeros((9, LANES - half, half), BF16)
    for sides in (s3, s4):
        sides[0, :, 0 : LANES - half, :] = blank
        sides[1, :, half:LANES, :] = blank

    for f in range(2):
        mixed[f * size : (f + 1) * size, :] = time_ref[f]
    for f in range(frames):
        for i, ref in enumerate((above, blocked, below)):
            begin = (f + 2) * size + i * 2 * wide
            mixed[begin : begin + 2 * wide, :] = ref[f]

    def mix(n, carry):
        lanes = pl.ds(pl.multiple_of(n * LANES, LANES), LANES)
        left = jnp.concatenate(
            [mixed[pl.ds(t * size, frames * size), :] for t in range(3)], axis=1
        )
        acc[n, 0 : frames * size, :] = jnp.dot(left, wt[:, lanes], preferred_element_type=F32)
        return carry

    lax.fori_loop(0, 2 * channels // LANES, mix, 0)
    mask_low = line_mask(place, wide, 2 * row - 2, 6, height, width)

    def double(t, carry):
        rows = pl.ds(aligned(t, size), size)
        first = jnp.concatenate([acc[0, rows, :], acc[1, rows, 0:128]], axis=1)
        second = jnp.concatenate([acc[1, rows, 128:256], acc[2, rows, :]], axis=1)
        store(de, do, 2 * t, first * mask_low, 6, wide)
        store(de, do, 2 * t + 1, second * mask_low, 6, wide)
        return carry

    lax.fori_loop(0, frames, double, 0)

    for py in range(2):

        def enlarge(n, carry):
            lanes = pl.ds(pl.multiple_of(n * LANES, LANES), LANES)
            left = jnp.concatenate(
                [taps(de, do, 0, count, 6, wide, 0, py), taps(de, do, 0, count, 6, wide, 0, py + 1)],
                axis=1,
            )
            acc[n, py * count * 4 * wide : (py + 1) * count * 4 * wide, :] = jnp.dot(
                left, wu[py, :, lanes], preferred_element_type=F32
            )
            return carry

        lax.fori_loop(0, 2 * channels // LANES, enlarge, 0)

    for f in range(2):
        store(x3e, x3o, f, three_ref[f].astype(F32), 8, wide)
        store(x4e, x4o, f, four_ref[f].astype(F32), 6, wide)
    gain3 = jnp.concatenate([gain_three[...], gain_three[...]], axis=1)
    gain4 = jnp.concatenate([gain_four[...], gain_four[...]], axis=1)
    mask_three = line_mask(place, wide, 4 * row - 2, 8, 2 * height, width)
    first_half = lax.broadcasted_iota(jnp.int32, (1, channels), 1) < half
    part = 4 * wide

    def norm_three(f, carry):
        values = []
        for py in range(2):
            rows = pl.ds(pl.multiple_of(py * count * part + f * part, 16), part)
            center = jnp.concatenate([acc[0, rows, :], acc[1, rows, 0:128]], axis=1)
            side = jnp.concatenate([acc[1, rows, 128:256], acc[2, rows, :]], axis=1)
            side = jnp.where(first_half, pltpu.roll(side, 1, 0), pltpu.roll(side, part - 1, 0))
            values.append((center + side).astype(BF16).astype(F32))
        lifted = jnp.concatenate(
            [values[h % 2][(h // 2) * wide : (h // 2 + 1) * wide] for h in range(8)], axis=0
        )
        lifted_ref[pl.ds(aligned(f, part), part), :] = lifted[2 * wide : 6 * wide]
        store(x3e, x3o, f + 2, activate_pairs(lifted, gain3, mask_three), 8, wide)
        return carry

    lax.fori_loop(0, count, norm_three, 0)
    for copy in copies_three:
        copy.wait()
    high_product(acc, x3e, x3o, count, 8, wide, w3, s3)

    mask_four = mask_three[wide : 7 * wide]

    def norm_four(f, carry):
        values = high_sum(acc, aligned(f, size), size, half)
        store(x4e, x4o, f + 2, activate_pairs(values, gain4, mask_four), 6, wide)
        return carry

    lax.fori_loop(0, count, norm_four, 0)
    for copy in copies_four:
        copy.wait()
    high_product(acc, x4e, x4o, count, 6, wide, w4, s4)

    def finish(f, carry):
        start = aligned(f, part)
        values = high_sum(acc, start, part, half) + lifted_ref[pl.ds(start, part), :]
        values = pltpu.roll(values, part - HALO, 0)
        for y in range(4):
            inner = wide - 2 * HALO
            out_ref[f, y] = values[y * wide : y * wide + inner].astype(BF16)
        return carry

    lax.fori_loop(0, count, finish, 0)


def second_block(place, pieces, time, three, four, gains, weights, sizes, wide):
    frames, _, channels = pieces[0].shape
    half = channels // 2
    count = 2 * frames
    weight_time, weight_up, weight_three, weight_four = weights
    vmem = pl.BlockSpec(memory_space=pltpu.VMEM)
    anywhere = pl.BlockSpec(memory_space=pl.ANY)
    return pl.pallas_call(
        functools.partial(second_kernel, wide, sizes),
        out_shape=jax.ShapeDtypeStruct((count, 4, wide - 2 * HALO, channels), BF16),
        in_specs=[pl.BlockSpec(memory_space=pltpu.SMEM)] + [vmem] * 10 + [anywhere] * 2,
        out_specs=vmem,
        scratch_shapes=[
            pltpu.VMEM(weight_three.shape, BF16),
            pltpu.VMEM((2, 9, LANES, half), BF16),
            pltpu.VMEM(weight_four.shape, BF16),
            pltpu.VMEM((2, 9, LANES, half), BF16),
            pltpu.VMEM((4, 2 * count * 4 * wide, LANES), F32),
            pltpu.VMEM(((frames + 2) * 6 * wide, channels), BF16),
            *planes(count, 6, wide, channels),
            *planes(count + 2, 8, wide, channels),
            *planes(count + 2, 6, wide, channels),
            pltpu.VMEM((count * 4 * wide, channels), F32),
            pltpu.SemaphoreType.DMA((6,)),
        ],
        compiler_params=pltpu.CompilerParams(vmem_limit_bytes=48 * 1024 * 1024),
        name="second_block",
    )(place, *pieces, time, three, four, *gains, *weights)


def body(
    latent,
    cache_one,
    cache_two,
    cache_time,
    cache_three,
    cache_four,
    gain_one,
    gain_two,
    gain_three,
    gain_four,
    weight_one,
    weight_two,
    weight_time,
    weight_upsample,
    weight_three,
    weight_four,
):
    section, row, col = (lax.axis_index(name) for name in ("section", "rows", "cols"))
    sections, row_count, col_count = (lax.axis_size(name) for name in ("section", "rows", "cols"))
    width, channels = latent.shape[2:]
    tile = width // col_count
    part = tile // sections
    wide = part + 2 * HALO
    half = weight_three.shape[1]
    sizes = (2 * row_count, width)
    place = jnp.stack([section, col, col * tile + section * part - HALO, row]).astype(jnp.int32)

    latent = latent.reshape(latent.shape[0], width, channels)
    arrived = swapped(latent, "section")
    mine, theirs = pack(
        place, latent, arrived, cache_one[:, 0], cache_two[:, 0], wide, tile, part
    )
    weight_four, mine = lax.optimization_barrier((weight_four, mine))
    weight_four = weight_four.reshape(9, 3 * half, half)
    own, up, down = stack(place, mine, swapped(theirs, "cols"), weight_four)
    pieces = [shifted(up, "rows", 1), own, shifted(down, "rows", -1)]

    cache_time, cache_three, cache_four, weight_upsample, weight_three, _ = (
        lax.optimization_barrier(
            (cache_time, cache_three, cache_four, weight_upsample, weight_three, own)
        )
    )
    weight_three = weight_three.reshape(9, 3 * half, half)
    weight_upsample = weight_upsample.reshape(9, channels, half)
    tiles, up, down = pair_tiles(cache_time, cache_three, cache_four)
    above, below = shifted(up, "rows", 1), shifted(down, "rows", -1)

    blocked = first_block(
        place,
        pieces,
        gain_one.reshape(1, -1),
        gain_two.reshape(1, -1),
        weight_one.reshape(9, 3, channels, channels),
        weight_two.reshape(9, 3, channels, channels),
        (weight_three, weight_upsample),
        sizes,
    )
    blocks = [shifted(blocked, "rows", 1), blocked, shifted(blocked, "rows", -1)]

    above, below, weight_upsample, _ = lax.optimization_barrier(
        (above, below, weight_upsample, blocked)
    )
    edge = swapped(tile_edges(place, tiles, above, below), "cols")
    time, three, four = tile_windows(place, tiles, above, below, edge, wide)

    frames = second_block(
        place,
        blocks,
        time,
        three,
        four,
        (gain_three.reshape(1, -1), gain_four.reshape(1, -1)),
        (
            weight_time,
            combine_weights(weight_upsample),
            weight_three,
            weight_four,
        ),
        sizes,
        wide,
    )
    count = frames.shape[0] // sections
    given = lax.dynamic_slice_in_dim(frames, (1 - section) * count, count, 0)
    kept = lax.dynamic_slice_in_dim(frames, section * count, count, 0)
    arrived = swapped(given, "section")
    low = section == 0
    joined = jnp.concatenate(
        [jnp.where(low, kept, arrived), jnp.where(low, arrived, kept)], axis=2
    )
    return joined.reshape(count, 4, 2 * tile, half)


def solution(mesh):
    placed = (
        P("section", ("rows", "cols"), None, None),
        P(None, ("rows", "cols"), None, None),
        P(None, ("rows", "cols"), None, None),
        P(None, "rows", "cols", None),
        P(None, "rows", "cols", None),
        P(None, "rows", "cols", None),
    ) + (P(),) * 10
    return jax.shard_map(
        body,
        mesh=mesh,
        in_specs=placed,
        out_specs=P("section", "rows", "cols", None),
        check_vma=False,
    )
```

```python
import functools

import jax
import jax.numpy as jnp
from jax import lax
from jax.experimental import pallas as pl
from jax.experimental.pallas import tpu as pltpu
from jax.sharding import PartitionSpec as P

EPSILON = 1e-06
HALO = 4
LANES = 256
BF16 = jnp.bfloat16
F32 = jnp.float32


def swapped(value, axis):
    return lax.ppermute(value, axis, [(0, 1), (1, 0)])


def shifted(value, axis, steps):
    count = lax.axis_size(axis)
    initial, last = (max(0, -steps), min(count, count - steps))
    return lax.ppermute(value, axis, [(source, source + steps) for source in range(initial, last)])


def silu(scaled):
    half = scaled * 0.5
    return half * (1.0 + jnp.tanh(half))


def activate(values, gain, mask):
    mean = jnp.mean(values * values, axis=-1, keepdims=True)
    return silu(values * (lax.rsqrt(mean + EPSILON) * mask) * gain)


def activate_pairs(values, gain, mask):
    channels = values.shape[-1] // 2
    squares = values * values
    first = lax.broadcasted_iota(jnp.int32, (1, 2 * channels), 1) < channels
    total = jnp.sum(squares, axis=-1, keepdims=True)
    low = jnp.sum(jnp.where(first, squares, 0.0), axis=-1, keepdims=True)
    scale_low = lax.rsqrt(low / channels + EPSILON) * mask
    scale_high = lax.rsqrt((total - low) / channels + EPSILON) * mask
    return silu(values * jnp.where(first, scale_low, scale_high) * gain)


def merge(even, odd, channels):
    turned = pltpu.roll(odd, channels - 128, 1)
    first = lax.broadcasted_iota(jnp.int32, (1, 128), 1) < channels - 128
    middle = jnp.where(first, even[:, 128:], turned[:, :128])
    return jnp.concatenate([even[:, :128], middle, turned[:, 128:]], axis=1)


def aligned(index, size):
    return pl.multiple_of(index * size, 16)


def line_mask(place, wide, first, count, limit, width):
    columns = place[2] + lax.broadcasted_iota(jnp.int32, (wide, 1), 0)
    inside = jnp.where((columns >= 0) & (columns < width), 1.0, 0.0)
    lines = []
    for i in range(count):
        line = first + i
        lines.append(inside * jnp.where((line >= 0) & (line < limit), 1.0, 0.0))
    return jnp.concatenate(lines, axis=0)


def store(even, odd, slot, values, height, wide):
    even[pl.ds(slot * (height * wide), height * wide), :] = values.astype(BF16)
    odd[pl.ds(slot * ((height - 2) * wide), (height - 2) * wide), :] = values[
        wide : (height - 1) * wide
    ].astype(BF16)


def taps(even, odd, begin, count, height, wide, dt, dy, lanes=slice(None)):
    inner = (height - 2) * wide
    if dy == 1:
        parts = [odd[pl.ds((begin + f + dt) * inner, inner), lanes] for f in range(count)]
    else:
        parts = [
            even[pl.ds((begin + f + dt) * height * wide + dy * wide, inner), lanes]
            for f in range(count)
        ]
    return jnp.concatenate(parts, axis=0)


def low_product(acc, even, odd, count, height, wide, weights, copies):
    rows = count * (height - 2) * wide
    channels = weights.shape[1]
    lanes = 3 * channels
    waited = 0
    for n in range(-(-lanes // LANES)):
        begin, end = n * LANES, min((n + 1) * LANES, lanes)
        while waited * channels < end:
            copies[waited].wait()
            waited += 1
        total = None
        for first, last in ((0, 4), (4, 8), (8, 9)):
            left = jnp.concatenate(
                [
                    taps(even, odd, 0, count, height, wide, t // 3, t % 3)
                    for t in range(first, last)
                ],
                axis=1,
            )
            right = weights[first:last, :, begin:end].reshape((last - first) * channels, -1)
            part = jnp.dot(left, right, preferred_element_type=F32)
            total = part if total is None else total + part
        acc[n, 0:rows, 0 : end - begin] = total


def low_sum(acc, start, size):
    rows = pl.ds(start, size)
    before = jnp.concatenate([acc[0, rows, :], acc[1, rows, 0:128]], axis=1)
    center = jnp.concatenate([acc[1, rows, 128:256], acc[2, rows, :]], axis=1)
    after = jnp.concatenate([acc[3, rows, :], acc[4, rows, 0:128]], axis=1)
    return center + pltpu.roll(before, 1, 0) + pltpu.roll(after, size - 1, 0)


def transposed_dot(left, right):
    return lax.dot_general(left, right, (((1,), (1,)), ((), ())), preferred_element_type=F32)


def high_product(acc, even, odd, count, height, wide, weights):
    rows = count * (height - 2) * wide
    channels = weights.shape[1] // 9

    def column(n, carry):
        outputs = pl.ds(pl.multiple_of(n * LANES, LANES), LANES)
        total = None
        for first, last in ((0, 4), (4, 8), (8, 9)):
            left = jnp.concatenate(
                [
                    taps(even, odd, 0, count, height, wide, t // 3, t % 3)
                    for t in range(first, last)
                ],
                axis=1,
            )
            part = transposed_dot(left, weights[outputs, first * channels : last * channels])
            total = part if total is None else total + part
        acc[n, 0:rows, :] = total
        return carry

    lax.fori_loop(0, weights.shape[0] // LANES, column, 0)


def high_sum(acc, start, size):
    rows = pl.ds(start, size)
    center = jnp.concatenate([acc[0, rows, :], acc[1, rows, 0:128]], axis=1)
    side = jnp.concatenate([acc[1, rows, 128:256], acc[2, rows, :]], axis=1)
    channels = center.shape[1]
    first = lax.broadcasted_iota(jnp.int32, (1, channels), 1) < channels // 2
    return center + jnp.where(first, pltpu.roll(side, 1, 0), pltpu.roll(side, size - 1, 0))


def pack_kernel(
    wide,
    tile,
    part,
    place,
    latent,
    arrived,
    one,
    two,
    time,
    three,
    four,
    gain_one,
    gain_two,
    gain_three,
    gain_four,
    mine,
    theirs,
    tiles,
    gains,
    spread,
    low,
    high,
):
    section, col = place[0], place[1]
    width, channels = latent.shape[1:]
    half = three.shape[-1]
    empty = jnp.zeros((spread.shape[1] - width, channels), F32)

    def put(slot, values):
        spread[slot] = pltpu.roll(
            jnp.concatenate([values.astype(F32), empty], axis=0), HALO, 0
        )

    for i in range(2):
        put(2 * section + i, latent[i])
        put(2 * (1 - section) + i, arrived[i])
        put(4 + i, one[i])
        put(6 + i, two[i])
    for slot in range(8):
        for ref, which in ((mine, col), (theirs, 1 - col)):
            begin = pl.multiple_of(which * tile + section * part, 8)
            ref[slot] = spread[slot, pl.ds(begin, wide), :].astype(BF16)

    lines = [time[f, y].astype(F32) for f in range(2) for y in range(2)]
    for ref in (three, four):
        for f in range(2):
            for y in range(4):
                values = ref[f, y].astype(F32)
                low[...] = values[:, :128]
                high[:, 0 : half - 128] = values[:, 128:]
                count = values.shape[0] // 2
                even, odd = (
                    jnp.concatenate(
                        [lanes[pl.ds(o, count, stride=2), :] for lanes in (low, high)], axis=1
                    )
                    for o in range(2)
                )
                lines.append(merge(even, odd, half))
    for i, line in enumerate(lines):
        tiles[i] = line.astype(BF16)

    left = col == 0
    upper = lax.broadcasted_iota(jnp.int32, (8, 1), 0) < HALO
    blocks = []
    for i in range(0, len(lines), 2):
        one_line, two_line = lines[i], lines[i + 1]
        last = jnp.where(upper, pltpu.roll(one_line[-8:], HALO, 0), two_line[-8:])
        first = jnp.where(upper, one_line[:8], pltpu.roll(two_line[:8], HALO, 0))
        blocks.append(jnp.where(left, last, first))
    gap = jnp.zeros_like(blocks[0])
    count = wide // 8
    for i in range(theirs.shape[0] - 8):
        group = (blocks + [gap] * count)[i * count : (i + 1) * count]
        theirs[8 + i] = jnp.concatenate(group, axis=0).astype(BF16)

    pairs = [jnp.concatenate([g[...], g[...]], axis=1) for g in (gain_three, gain_four)]
    for i, values in enumerate([gain_one[...], gain_two[...]] + pairs):
        gains[i : i + 1, :] = values


def pack(place, latent, arrived, one, two, time, three, four, gains, wide, tile, part):
    width, channels = latent.shape[1:]
    vmem = pl.BlockSpec(memory_space=pltpu.VMEM)
    lines = 20
    extra = -(-lines * HALO // wide)
    return pl.pallas_call(
        functools.partial(pack_kernel, wide, tile, part),
        out_shape=[
            jax.ShapeDtypeStruct((8, wide, channels), BF16),
            jax.ShapeDtypeStruct((8 + extra, wide, channels), BF16),
            jax.ShapeDtypeStruct((lines, tile, channels), BF16),
            jax.ShapeDtypeStruct((8, channels), F32),
        ],
        in_specs=[pl.BlockSpec(memory_space=pltpu.SMEM)] + [vmem] * 11,
        out_specs=[vmem] * 4,
        scratch_shapes=[
            pltpu.VMEM((8, width + 16, channels), F32),
            pltpu.VMEM((three.shape[2], 128), F32),
            pltpu.VMEM((three.shape[2], 128), F32),
        ],
        name="pack",
    )(place, latent, arrived, one, two, time, three, four, *gains)


def stack_kernel(
    wide, place, mine, theirs, tiles, later, own, up, down, windows, tile_up, tile_down
):
    del later
    section, col = place[0], place[1]
    count = mine.shape[0] - 2
    own[0], own[1] = mine[...], theirs[0 : count + 2]
    for ref, y in ((up, 1), (down, 0)):
        ref[0:count], ref[count : 2 * count] = mine[0:count], theirs[0:count]
        here = lax.rem(y + col, 2) == 0
        ref[2 * count :] = jnp.where(here, mine[count:], theirs[count : count + 2])

    part = wide - 2 * HALO
    upper = lax.broadcasted_iota(jnp.int32, (8, 1), 0) < HALO
    groups = wide // 8
    for i in range(tiles.shape[0]):
        line = tiles[i].astype(F32)
        block = i // 2
        begin = block % groups * 8
        edge = theirs[count + 2 + block // groups].astype(F32)[begin : begin + 8]
        turned = pltpu.roll(edge, HALO, 0)
        before, after = (edge, turned) if i % 2 == 0 else (turned, edge)
        first = pltpu.roll(line, HALO, 0)[:wide]
        head = jnp.where(upper, jnp.where(col == 1, before, 0.0), first[:8])
        first = jnp.concatenate([head, first[8:]], axis=0)
        last = pltpu.roll(line, line.shape[0] - (part - HALO), 0)[:wide]
        tail = jnp.where(upper, last[-8:], jnp.where(col == 0, after, 0.0))
        last = jnp.concatenate([last[:-8], tail], axis=0)
        line = jnp.where(section == 0, first, last).astype(BF16)
        windows[i] = line
        if i < 4:
            tile_up[i] = line
            tile_down[i] = line
            continue
        f, y = (i - 4) % 8 // 4, (i - 4) % 4
        base, depth = (4, 2) if i < 12 else (8, 1)
        if y >= 4 - depth:
            tile_up[base + depth * f + y - (4 - depth)] = line
        if y < depth:
            tile_down[base + depth * f + y] = line


def stack(place, mine, theirs, tiles, later):
    units, wide, channels = mine.shape
    vmem = pl.BlockSpec(memory_space=pltpu.VMEM)
    lines = 2 * units - 2
    shapes = [(2, units), (lines,), (lines,), (tiles.shape[0],), (10,), (10,)]
    return pl.pallas_call(
        functools.partial(stack_kernel, wide),
        out_shape=[jax.ShapeDtypeStruct(shape + (wide, channels), BF16) for shape in shapes],
        in_specs=[pl.BlockSpec(memory_space=pltpu.SMEM)]
        + [vmem] * 3
        + [pl.BlockSpec(memory_space=pl.ANY)],
        out_specs=[vmem] * 6,
        name="stack",
    )(place, mine, theirs, tiles, later)


def align_kernel(weight, out):
    half = weight.shape[0]
    chunk = 16

    def move(k, carry):
        for t in range(9):
            base = 3 * t * half
            first = base // 128 * 128
            width = min(-(-(base + 3 * half - first) // 128) * 128, weight.shape[1] - first)
            values = weight[pl.ds(aligned(k, chunk), chunk), first : first + width].astype(F32)
            values = values[:, base - first : base - first + 3 * half]
            none = jnp.zeros((chunk, half), F32)
            blocks = (
                values[:, half:],
                values[:, : 2 * half],
                jnp.concatenate([none, values[:, :half]], axis=1),
                jnp.concatenate([values[:, 2 * half :], none], axis=1),
            )
            for n, block in enumerate(blocks):
                rows = pl.ds(aligned(k, chunk) + n * half, chunk)
                out[rows, 2 * half * t : 2 * half * (t + 1)] = block.astype(BF16)
        return carry

    lax.fori_loop(0, half // chunk, move, 0)


def align_weights(weight):
    half = weight.shape[1]
    vmem = pl.BlockSpec(memory_space=pltpu.VMEM)
    return pl.pallas_call(
        align_kernel,
        out_shape=jax.ShapeDtypeStruct((4 * half, 18 * half), BF16),
        in_specs=[vmem],
        out_specs=vmem,
        name="align_weights",
    )(weight.T)


def combine_kernel(weight, out):
    half = weight.shape[0]
    channels = weight.shape[1] // 9
    chunk = 16

    def combine(k, carry):
        rows = pl.ds(aligned(k, chunk), chunk)
        taken = [
            [
                weight[rows, (3 * dy + dx) * channels : (3 * dy + dx + 1) * channels].astype(F32)
                for dx in range(3)
            ]
            for dy in range(3)
        ]
        for slot, dys in enumerate(((0,), (1, 2), (0, 1), (2,))):
            line = [sum(taken[dy][dx] for dy in dys) for dx in range(3)]
            lanes = slice(slot % 2 * channels, (slot % 2 + 1) * channels)
            for n, block in enumerate((line[1] + line[2], line[0] + line[1], line[0], line[2])):
                into = pl.ds(aligned(k, chunk) + n * half, chunk)
                out[slot // 2, into, lanes] = block.astype(BF16)
        return carry

    lax.fori_loop(0, half // chunk, combine, 0)


def combine_weights(weight):
    channels = 2 * weight.shape[1]
    vmem = pl.BlockSpec(memory_space=pltpu.VMEM)
    return pl.pallas_call(
        combine_kernel,
        out_shape=jax.ShapeDtypeStruct((2, 2 * channels, 2 * channels), BF16),
        in_specs=[vmem],
        out_specs=vmem,
        name="combine_weights",
    )(weight.T)


def first_kernel(
    wide,
    sizes,
    place,
    above,
    own,
    below,
    gains,
    weight_one,
    weight_two,
    later_one,
    later_two,
    out_ref,
    w1,
    w2,
    acc,
    x1e,
    x1o,
    x2e,
    x2o,
    sems,
):
    channels = own.shape[-1]
    frames = own.shape[1] - 4
    height, width = sizes
    col, row = place[1], place[3]
    units = frames + 2
    del later_one, later_two

    def load(source, target, base):
        return [
            pltpu.make_async_copy(
                source.at[:, dx], target.at[:, :, pl.ds(dx * channels, channels)], sems.at[base + dx]
            )
            for dx in range(3)
        ]

    copies_one = load(weight_one, w1, 0)
    copies_two = load(weight_two, w2, 3)
    for copy in copies_one + copies_two:
        copy.start()

    slots = [lax.rem(y + col, 2) for y in range(2)]

    def own_rows(index):
        return [own[slot, index].astype(F32) for slot in slots]

    def rows_of(index):
        first = [above[slot * units + index].astype(F32) for slot in slots]
        last = [below[slot * units + index].astype(F32) for slot in slots]
        return jnp.concatenate(first + own_rows(index) + last, axis=0)

    for f in range(2):
        store(x1e, x1o, f, rows_of(frames + f), 6, wide)
        first, last = above[2 * units + f].astype(F32), below[2 * units + f].astype(F32)
        values = jnp.concatenate([first] + own_rows(units + f) + [last], axis=0)
        store(x2e, x2o, f, values, 4, wide)

    def norm_one(f, carry):
        values = activate(rows_of(f), gains[0:1, :], 1.0)
        store(x1e, x1o, f + 2, values, 6, wide)
        return carry

    lax.fori_loop(0, frames, norm_one, 0)
    low_product(acc, x1e, x1o, frames, 6, wide, w1, copies_one)

    mask = line_mask(place, wide, 2 * row - 1, 4, height, width)

    def norm_two(f, carry):
        size = 4 * wide
        values = activate(low_sum(acc, aligned(f, size), size), gains[1:2, :], mask)
        store(x2e, x2o, f + 2, values, 4, wide)
        return carry

    lax.fori_loop(0, frames, norm_two, 0)
    low_product(acc, x2e, x2o, frames, 4, wide, w2, copies_two)

    def residual(f, carry):
        size = 2 * wide
        values = low_sum(acc, aligned(f, size), size) + jnp.concatenate(own_rows(f), axis=0)
        out_ref[f] = values.astype(BF16)
        return carry

    lax.fori_loop(0, frames, residual, 0)


def planes(slots, height, wide, channels):
    return [
        pltpu.VMEM((slots * height * wide, channels), BF16),
        pltpu.VMEM((slots * (height - 2) * wide, channels), BF16),
    ]


def first_block(place, pieces, gains, weight_one, weight_two, later, sizes):
    _, units, wide, channels = pieces[1].shape
    frames = units - 4
    slots = -(-3 * channels // LANES)
    vmem = pl.BlockSpec(memory_space=pltpu.VMEM)
    anywhere = pl.BlockSpec(memory_space=pl.ANY)
    return pl.pallas_call(
        functools.partial(first_kernel, wide, sizes),
        out_shape=jax.ShapeDtypeStruct((frames, 2 * wide, channels), BF16),
        in_specs=[pl.BlockSpec(memory_space=pltpu.SMEM)] + [vmem] * 4 + [anywhere] * 4,
        out_specs=vmem,
        scratch_shapes=[
            pltpu.VMEM((9, channels, slots * LANES), BF16),
            pltpu.VMEM((9, channels, slots * LANES), BF16),
            pltpu.VMEM((slots, frames * 4 * wide, LANES), F32),
            *planes(frames + 2, 6, wide, channels),
            *planes(frames + 2, 4, wide, channels),
            pltpu.SemaphoreType.DMA((6,)),
        ],
        compiler_params=pltpu.CompilerParams(vmem_limit_bytes=46 * 1024 * 1024),
        cost_estimate=pl.CostEstimate(
            flops=2 * 27 * channels * channels * frames * 6 * wide,
            bytes_accessed=2 * 54 * channels * channels,
            transcendentals=0,
        ),
        name="first_block",
    )(place, *pieces, gains, weight_one, weight_two, *later)


def second_kernel(
    wide,
    sizes,
    place,
    above,
    blocked,
    below,
    tile_above,
    windows,
    tile_below,
    gains,
    weight_time,
    weight_up,
    weight_three,
    weight_four,
    out_ref,
    wt,
    wu,
    w3,
    w4,
    acc,
    mixed,
    de,
    do,
    x3e,
    x3o,
    x4e,
    x4o,
    lifted_ref,
    sems,
):
    channels = blocked.shape[-1]
    half = channels // 2
    size = 6 * wide
    frames = blocked.shape[0]
    count = 2 * frames
    height, width = sizes
    row = place[3]
    copies = [
        pltpu.make_async_copy(source, target, sems.at[i])
        for i, (source, target) in enumerate(
            ((weight_time, wt), (weight_up, wu), (weight_three, w3), (weight_four, w4))
        )
    ]
    for copy in copies:
        copy.start()

    def cached(start, base, lines, depth, f):
        parts = [tile_above[start + depth * f + i] for i in range(depth)]
        parts += [windows[base + lines * f + i] for i in range(lines)]
        parts += [tile_below[start + depth * f + i] for i in range(depth)]
        return jnp.concatenate([line.astype(F32) for line in parts], axis=0)

    for f in range(2):
        mixed[f * size : (f + 1) * size, :] = cached(0, 0, 2, 2, f).astype(BF16)
    for f in range(frames):
        for i, ref in enumerate((above, blocked, below)):
            begin = (f + 2) * size + i * 2 * wide
            mixed[begin : begin + 2 * wide, :] = ref[f]

    copies[0].wait()

    def mix(n, carry):
        lanes = pl.ds(pl.multiple_of(n * LANES, LANES), LANES)
        left = jnp.concatenate(
            [mixed[pl.ds(t * size, frames * size), :] for t in range(3)], axis=1
        )
        acc[n, 0 : frames * size, :] = jnp.dot(left, wt[:, lanes], preferred_element_type=F32)
        return carry

    lax.fori_loop(0, 2 * channels // LANES, mix, 0)
    mask_low = line_mask(place, wide, 2 * row - 2, 6, height, width)

    def double(t, carry):
        rows = pl.ds(aligned(t, size), size)
        first = jnp.concatenate([acc[0, rows, :], acc[1, rows, 0:128]], axis=1)
        second = jnp.concatenate([acc[1, rows, 128:256], acc[2, rows, :]], axis=1)
        store(de, do, 2 * t, first * mask_low, 6, wide)
        store(de, do, 2 * t + 1, second * mask_low, 6, wide)
        return carry

    lax.fori_loop(0, frames, double, 0)

    copies[1].wait()

    for py in range(2):

        def enlarge(n, carry):
            lanes = pl.ds(pl.multiple_of(n * LANES, LANES), LANES)
            left = jnp.concatenate(
                [taps(de, do, 0, count, 6, wide, 0, py), taps(de, do, 0, count, 6, wide, 0, py + 1)],
                axis=1,
            )
            acc[n, py * count * 4 * wide : (py + 1) * count * 4 * wide, :] = transposed_dot(
                left, wu[py, lanes, :]
            )
            return carry

        lax.fori_loop(0, 2 * channels // LANES, enlarge, 0)

    for f in range(2):
        store(x3e, x3o, f, cached(4, 4, 4, 2, f), 8, wide)
        store(x4e, x4o, f, cached(8, 12, 4, 1, f), 6, wide)
    gain3, gain4 = gains[2:3, :], gains[3:4, :]
    mask_three = line_mask(place, wide, 4 * row - 2, 8, 2 * height, width)
    part = 4 * wide

    def norm_three(f, carry):
        values = []
        for py in range(2):
            start = pl.multiple_of(py * count * part + f * part, 16)
            values.append(high_sum(acc, start, part).astype(BF16).astype(F32))
        lifted = jnp.concatenate(
            [values[h % 2][(h // 2) * wide : (h // 2 + 1) * wide] for h in range(8)], axis=0
        )
        lifted_ref[pl.ds(aligned(f, part), part), :] = lifted[2 * wide : 6 * wide]
        store(x3e, x3o, f + 2, activate_pairs(lifted, gain3, mask_three), 8, wide)
        return carry

    lax.fori_loop(0, count, norm_three, 0)
    copies[2].wait()
    high_product(acc, x3e, x3o, count, 8, wide, w3)

    mask_four = mask_three[wide : 7 * wide]

    def norm_four(f, carry):
        values = high_sum(acc, aligned(f, size), size)
        store(x4e, x4o, f + 2, activate_pairs(values, gain4, mask_four), 6, wide)
        return carry

    lax.fori_loop(0, count, norm_four, 0)
    copies[3].wait()
    high_product(acc, x4e, x4o, count, 6, wide, w4)

    def finish(f, carry):
        start = aligned(f, part)
        values = high_sum(acc, start, part) + lifted_ref[pl.ds(start, part), :]
        values = pltpu.roll(values, part - HALO, 0)
        for y in range(4):
            inner = wide - 2 * HALO
            out_ref[f, y] = values[y * wide : y * wide + inner].astype(BF16)
        return carry

    lax.fori_loop(0, count, finish, 0)


def second_block(place, pieces, tiles, gains, weights, sizes, wide):
    frames, _, channels = pieces[0].shape
    count = 2 * frames
    vmem = pl.BlockSpec(memory_space=pltpu.VMEM)
    anywhere = pl.BlockSpec(memory_space=pl.ANY)
    return pl.pallas_call(
        functools.partial(second_kernel, wide, sizes),
        out_shape=jax.ShapeDtypeStruct((count, 4, wide - 2 * HALO, channels), BF16),
        in_specs=[pl.BlockSpec(memory_space=pltpu.SMEM)] + [vmem] * 7 + [anywhere] * 4,
        out_specs=vmem,
        scratch_shapes=[
            *(pltpu.VMEM(weight.shape, BF16) for weight in weights),
            pltpu.VMEM((3, 2 * count * 4 * wide, LANES), F32),
            pltpu.VMEM(((frames + 2) * 6 * wide, channels), BF16),
            *planes(count, 6, wide, channels),
            *planes(count + 2, 8, wide, channels),
            *planes(count + 2, 6, wide, channels),
            pltpu.VMEM((count * 4 * wide, channels), F32),
            pltpu.SemaphoreType.DMA((4,)),
        ],
        compiler_params=pltpu.CompilerParams(vmem_limit_bytes=44 * 1024 * 1024),
        name="second_block",
    )(place, *pieces, *tiles, gains, *weights)


def body(
    latent,
    cache_one,
    cache_two,
    cache_time,
    cache_three,
    cache_four,
    gain_one,
    gain_two,
    gain_three,
    gain_four,
    weight_one,
    weight_two,
    weight_time,
    weight_upsample,
    weight_three,
    weight_four,
):
    section, row, col = (lax.axis_index(name) for name in ("section", "rows", "cols"))
    sections, row_count, col_count = (lax.axis_size(name) for name in ("section", "rows", "cols"))
    width, channels = latent.shape[2:]
    tile = width // col_count
    part = tile // sections
    wide = part + 2 * HALO
    half = weight_three.shape[1]
    sizes = (2 * row_count, width)
    place = jnp.stack([section, col, col * tile + section * part - HALO, row]).astype(jnp.int32)

    latent = latent.reshape(latent.shape[0], width, channels)
    arrived = swapped(latent, "section")
    mine, theirs, tiles, gains = pack(
        place,
        latent,
        arrived,
        cache_one[:, 0],
        cache_two[:, 0],
        cache_time,
        cache_three,
        cache_four,
        [gain.reshape(1, -1) for gain in (gain_one, gain_two, gain_three, gain_four)],
        wide,
        tile,
        part,
    )
    weight_three, mine = lax.optimization_barrier((weight_three, mine))
    weight_three = align_weights(weight_three)
    own, up, down, windows, tile_up, tile_down = stack(
        place, mine, swapped(theirs, "cols"), tiles, weight_three
    )
    pieces = [shifted(up, "rows", 1), own, shifted(down, "rows", -1)]
    tiles = [shifted(tile_up, "rows", 1), windows, shifted(tile_down, "rows", -1)]
    weight_upsample, weight_four, own = lax.optimization_barrier(
        (weight_upsample, weight_four, own)
    )
    weight_upsample = combine_weights(weight_upsample)
    weight_four = align_weights(weight_four)
    blocked = first_block(
        place,
        pieces,
        gains,
        weight_one.reshape(9, 3, channels, channels),
        weight_two.reshape(9, 3, channels, channels),
        (weight_upsample, weight_four),
        sizes,
    )
    blocks = [shifted(blocked, "rows", 1), blocked, shifted(blocked, "rows", -1)]
    frames = second_block(
        place,
        blocks,
        tiles,
        gains,
        (weight_time, weight_upsample, weight_three, weight_four),
        sizes,
        wide,
    )
    count = frames.shape[0] // sections
    given = lax.dynamic_slice_in_dim(frames, (1 - section) * count, count, 0)
    kept = lax.dynamic_slice_in_dim(frames, section * count, count, 0)
    arrived = swapped(given, "section")
    low = section == 0
    joined = jnp.concatenate(
        [jnp.where(low, kept, arrived), jnp.where(low, arrived, kept)], axis=2
    )
    return joined.reshape(count, 4, 2 * tile, half)


def solution(mesh):
    placed = (
        P("section", ("rows", "cols"), None, None),
        P(None, ("rows", "cols"), None, None),
        P(None, ("rows", "cols"), None, None),
        P(None, "rows", "cols", None),
        P(None, "rows", "cols", None),
        P(None, "rows", "cols", None),
    ) + (P(),) * 10
    return jax.shard_map(
        body,
        mesh=mesh,
        in_specs=placed,
        out_specs=P("section", "rows", "cols", None),
        check_vma=False,
    )
```

```python
import functools

import jax
import jax.numpy as jnp
from jax import lax
from jax.experimental import pallas as pl
from jax.experimental.pallas import tpu as pltpu
from jax.sharding import PartitionSpec as P

EPSILON = 1e-06
HALO = 4
LANES = 256
BF16 = jnp.bfloat16
F32 = jnp.float32


def swapped(value, axis):
    return lax.ppermute(value, axis, [(0, 1), (1, 0)])


def shifted(value, axis, steps):
    count = lax.axis_size(axis)
    initial, last = (max(0, -steps), min(count, count - steps))
    return lax.ppermute(value, axis, [(source, source + steps) for source in range(initial, last)])


def silu(scaled):
    half = scaled * 0.5
    return half * (1.0 + jnp.tanh(half))


def activate(values, gain, mask):
    mean = jnp.mean(values * values, axis=-1, keepdims=True)
    return silu(values * (lax.rsqrt(mean + EPSILON) * mask) * gain)


def activate_pairs(values, gain, mask):
    channels = values.shape[-1] // 2
    squares = values * values
    first = lax.broadcasted_iota(jnp.int32, (1, 2 * channels), 1) < channels
    total = jnp.sum(squares, axis=-1, keepdims=True)
    low = jnp.sum(jnp.where(first, squares, 0.0), axis=-1, keepdims=True)
    scale_low = lax.rsqrt(low / channels + EPSILON) * mask
    scale_high = lax.rsqrt((total - low) / channels + EPSILON) * mask
    return silu(values * jnp.where(first, scale_low, scale_high) * gain)


def merge(even, odd, channels):
    turned = pltpu.roll(odd, channels - 128, 1)
    first = lax.broadcasted_iota(jnp.int32, (1, 128), 1) < channels - 128
    middle = jnp.where(first, even[:, 128:], turned[:, :128])
    return jnp.concatenate([even[:, :128], middle, turned[:, 128:]], axis=1)


def aligned(index, size):
    return pl.multiple_of(index * size, 16)


def line_mask(place, wide, first, count, limit, width):
    columns = place[2] + lax.broadcasted_iota(jnp.int32, (wide, 1), 0)
    inside = jnp.where((columns >= 0) & (columns < width), 1.0, 0.0)
    lines = []
    for i in range(count):
        line = first + i
        lines.append(inside * jnp.where((line >= 0) & (line < limit), 1.0, 0.0))
    return jnp.concatenate(lines, axis=0)


def store(even, odd, slot, values, height, wide):
    even[pl.ds(slot * (height * wide), height * wide), :] = values.astype(BF16)
    odd[pl.ds(slot * ((height - 2) * wide), (height - 2) * wide), :] = values[
        wide : (height - 1) * wide
    ].astype(BF16)


def taps(even, odd, begin, count, height, wide, dt, dy, lanes=slice(None)):
    inner = (height - 2) * wide
    if dy == 1:
        parts = [odd[pl.ds((begin + f + dt) * inner, inner), lanes] for f in range(count)]
    else:
        parts = [
            even[pl.ds((begin + f + dt) * height * wide + dy * wide, inner), lanes]
            for f in range(count)
        ]
    return jnp.concatenate(parts, axis=0)


def low_product(acc, even, odd, count, height, wide, weights, copies):
    rows = count * (height - 2) * wide
    channels = weights.shape[1]
    lanes = 3 * channels
    waited = 0
    for n in range(-(-lanes // LANES)):
        begin, end = n * LANES, min((n + 1) * LANES, lanes)
        while waited * channels < end:
            copies[waited].wait()
            waited += 1
        total = None
        for first, last in ((0, 4), (4, 8), (8, 9)):
            left = jnp.concatenate(
                [
                    taps(even, odd, 0, count, height, wide, t // 3, t % 3)
                    for t in range(first, last)
                ],
                axis=1,
            )
            right = weights[first:last, :, begin:end].reshape((last - first) * channels, -1)
            part = jnp.dot(left, right, preferred_element_type=F32)
            total = part if total is None else total + part
        acc[n, 0:rows, 0 : end - begin] = total


def low_sum(acc, start, size):
    rows = pl.ds(start, size)
    before = jnp.concatenate([acc[0, rows, :], acc[1, rows, 0:128]], axis=1)
    center = jnp.concatenate([acc[1, rows, 128:256], acc[2, rows, :]], axis=1)
    after = jnp.concatenate([acc[3, rows, :], acc[4, rows, 0:128]], axis=1)
    return center + pltpu.roll(before, 1, 0) + pltpu.roll(after, size - 1, 0)


def transposed_dot(left, right):
    return lax.dot_general(left, right, (((1,), (1,)), ((), ())), preferred_element_type=F32)


def high_product(acc, even, odd, count, height, wide, weights):
    rows = count * (height - 2) * wide
    channels = weights.shape[1] // 9

    def column(n, carry):
        outputs = pl.ds(pl.multiple_of(n * LANES, LANES), LANES)
        total = None
        for first, last in ((0, 4), (4, 8), (8, 9)):
            left = jnp.concatenate(
                [
                    taps(even, odd, 0, count, height, wide, t // 3, t % 3)
                    for t in range(first, last)
                ],
                axis=1,
            )
            part = transposed_dot(left, weights[outputs, first * channels : last * channels])
            total = part if total is None else total + part
        acc[n, 0:rows, :] = total
        return carry

    lax.fori_loop(0, weights.shape[0] // LANES, column, 0)


def high_sum(acc, start, size):
    rows = pl.ds(start, size)
    center = jnp.concatenate([acc[0, rows, :], acc[1, rows, 0:128]], axis=1)
    side = jnp.concatenate([acc[1, rows, 128:256], acc[2, rows, :]], axis=1)
    channels = center.shape[1]
    first = lax.broadcasted_iota(jnp.int32, (1, channels), 1) < channels // 2
    return center + jnp.where(first, pltpu.roll(side, 1, 0), pltpu.roll(side, size - 1, 0))


def pack_kernel(
    wide,
    tile,
    part,
    place,
    latent,
    arrived,
    one,
    two,
    time,
    three,
    four,
    mine,
    theirs,
    tiles,
    spread,
    low,
    high,
):
    section, col = place[0], place[1]
    width, channels = latent.shape[1:]
    half = three.shape[-1]
    empty = jnp.zeros((spread.shape[1] - width, channels), F32)

    def put(slot, values):
        spread[slot] = pltpu.roll(
            jnp.concatenate([values.astype(F32), empty], axis=0), HALO, 0
        )

    for i in range(2):
        put(2 * section + i, latent[i])
        put(2 * (1 - section) + i, arrived[i])
        put(4 + i, one[i])
        put(6 + i, two[i])
    for slot in range(8):
        for ref, which in ((mine, col), (theirs, 1 - col)):
            begin = pl.multiple_of(which * tile + section * part, 8)
            ref[slot] = spread[slot, pl.ds(begin, wide), :].astype(BF16)

    lines = [time[f, y].astype(F32) for f in range(2) for y in range(2)]
    for ref in (three, four):
        for f in range(2):
            for y in range(4):
                values = ref[f, y].astype(F32)
                low[...] = values[:, :128]
                high[:, 0 : half - 128] = values[:, 128:]
                count = values.shape[0] // 2
                even, odd = (
                    jnp.concatenate(
                        [lanes[pl.ds(o, count, stride=2), :] for lanes in (low, high)], axis=1
                    )
                    for o in range(2)
                )
                lines.append(merge(even, odd, half))
    for i, line in enumerate(lines):
        tiles[i] = line.astype(BF16)

    left = col == 0
    upper = lax.broadcasted_iota(jnp.int32, (8, 1), 0) < HALO
    blocks = []
    for i in range(0, len(lines), 2):
        one_line, two_line = lines[i], lines[i + 1]
        last = jnp.where(upper, pltpu.roll(one_line[-8:], HALO, 0), two_line[-8:])
        first = jnp.where(upper, one_line[:8], pltpu.roll(two_line[:8], HALO, 0))
        blocks.append(jnp.where(left, last, first))
    gap = jnp.zeros_like(blocks[0])
    count = wide // 8
    for i in range(theirs.shape[0] - 8):
        group = (blocks + [gap] * count)[i * count : (i + 1) * count]
        theirs[8 + i] = jnp.concatenate(group, axis=0).astype(BF16)


def pack(place, latent, arrived, one, two, time, three, four, wide, tile, part):
    width, channels = latent.shape[1:]
    vmem = pl.BlockSpec(memory_space=pltpu.VMEM)
    lines = 20
    extra = -(-lines * HALO // wide)
    return pl.pallas_call(
        functools.partial(pack_kernel, wide, tile, part),
        out_shape=[
            jax.ShapeDtypeStruct((8, wide, channels), BF16),
            jax.ShapeDtypeStruct((8 + extra, wide, channels), BF16),
            jax.ShapeDtypeStruct((lines, tile, channels), BF16),
        ],
        in_specs=[pl.BlockSpec(memory_space=pltpu.SMEM)] + [vmem] * 7,
        out_specs=[vmem] * 3,
        scratch_shapes=[
            pltpu.VMEM((8, width + 16, channels), F32),
            pltpu.VMEM((three.shape[2], 128), F32),
            pltpu.VMEM((three.shape[2], 128), F32),
        ],
        compiler_params=pltpu.CompilerParams(vmem_limit_bytes=8 * 1024 * 1024),
        name="pack",
    )(place, latent, arrived, one, two, time, three, four)


def stack_kernel(
    wide, place, mine, theirs, tiles, later, own, up, down, windows, tile_up, tile_down
):
    del later
    section, col = place[0], place[1]
    count = mine.shape[0] - 2
    own[0], own[1] = mine[...], theirs[0 : count + 2]
    for ref, y in ((up, 1), (down, 0)):
        ref[0:count], ref[count : 2 * count] = mine[0:count], theirs[0:count]
        here = lax.rem(y + col, 2) == 0
        ref[2 * count :] = jnp.where(here, mine[count:], theirs[count : count + 2])

    part = wide - 2 * HALO
    upper = lax.broadcasted_iota(jnp.int32, (8, 1), 0) < HALO
    groups = wide // 8
    for i in range(tiles.shape[0]):
        line = tiles[i].astype(F32)
        block = i // 2
        begin = block % groups * 8
        edge = theirs[count + 2 + block // groups].astype(F32)[begin : begin + 8]
        turned = pltpu.roll(edge, HALO, 0)
        before, after = (edge, turned) if i % 2 == 0 else (turned, edge)
        first = pltpu.roll(line, HALO, 0)[:wide]
        head = jnp.where(upper, jnp.where(col == 1, before, 0.0), first[:8])
        first = jnp.concatenate([head, first[8:]], axis=0)
        last = pltpu.roll(line, line.shape[0] - (part - HALO), 0)[:wide]
        tail = jnp.where(upper, last[-8:], jnp.where(col == 0, after, 0.0))
        last = jnp.concatenate([last[:-8], tail], axis=0)
        line = jnp.where(section == 0, first, last).astype(BF16)
        windows[i] = line
        if i < 4:
            tile_up[i] = line
            tile_down[i] = line
            continue
        f, y = (i - 4) % 8 // 4, (i - 4) % 4
        base, depth = (4, 2) if i < 12 else (8, 1)
        if y >= 4 - depth:
            tile_up[base + depth * f + y - (4 - depth)] = line
        if y < depth:
            tile_down[base + depth * f + y] = line


def stack(place, mine, theirs, tiles, later):
    units, wide, channels = mine.shape
    vmem = pl.BlockSpec(memory_space=pltpu.VMEM)
    lines = 2 * units - 2
    shapes = [(2, units), (lines,), (lines,), (tiles.shape[0],), (10,), (10,)]
    return pl.pallas_call(
        functools.partial(stack_kernel, wide),
        out_shape=[jax.ShapeDtypeStruct(shape + (wide, channels), BF16) for shape in shapes],
        in_specs=[pl.BlockSpec(memory_space=pltpu.SMEM)]
        + [vmem] * 3
        + [pl.BlockSpec(memory_space=pl.ANY)],
        out_specs=[vmem] * 6,
        compiler_params=pltpu.CompilerParams(vmem_limit_bytes=8 * 1024 * 1024),
        name="stack",
    )(place, mine, theirs, tiles, later)


def align_kernel(weight, out):
    half = weight.shape[0]
    chunk = 16
    tail = half - 128
    low = lax.broadcasted_iota(jnp.int32, (1, 128), 1) < tail

    def move(k, carry):
        here = aligned(k, chunk)
        none = jnp.zeros((chunk, 128), F32)
        for t in range(9):
            base = 3 * t * half
            first = base // 128 * 128
            last = min(first + 640, weight.shape[1])
            values = weight[pl.ds(here, chunk), first:last].astype(F32)
            if last < first + 640:
                values = jnp.concatenate(
                    [values[:, :512], jnp.concatenate([values[:, 512:], none[:, tail:]], axis=1)],
                    axis=1,
                )
            turned = pltpu.roll(values, 640 - tail, 1)
            tiles = [values[:, 128 * i : 128 * (i + 1)] for i in range(5)]
            moved = [turned[:, 128 * i : 128 * (i + 1)] for i in range(5)]
            if base == first:
                blocks = (
                    moved[1:4],
                    tiles[0:3],
                    [none, jnp.where(low, 0.0, moved[4]), moved[0]],
                    [tiles[3], jnp.where(low, tiles[4], 0.0), none],
                )
            else:
                blocks = (
                    tiles[2:5],
                    moved[0:3],
                    [none, jnp.where(low, 0.0, tiles[0]), tiles[1]],
                    [moved[3], jnp.where(low, moved[4], 0.0), none],
                )
            for n, block in enumerate(blocks):
                into = pl.ds(here + n * half, chunk)
                out[into, 2 * half * t : 2 * half * (t + 1)] = jnp.concatenate(
                    block, axis=1
                ).astype(BF16)
        return carry

    lax.fori_loop(0, half // chunk, move, 0)


def align_weights(weight):
    half = weight.shape[1]
    vmem = pl.BlockSpec(memory_space=pltpu.VMEM)
    return pl.pallas_call(
        align_kernel,
        out_shape=jax.ShapeDtypeStruct((4 * half, 18 * half), BF16),
        in_specs=[vmem],
        out_specs=vmem,
        compiler_params=pltpu.CompilerParams(vmem_limit_bytes=8 * 1024 * 1024),
        name="align_weights",
    )(weight.T)


def combine_kernel(weight, out):
    half = weight.shape[0]
    channels = weight.shape[1] // 9
    chunk = 16

    def combine(k, carry):
        rows = pl.ds(aligned(k, chunk), chunk)
        taken = [
            [
                weight[rows, (3 * dy + dx) * channels : (3 * dy + dx + 1) * channels].astype(F32)
                for dx in range(3)
            ]
            for dy in range(3)
        ]
        for slot, dys in enumerate(((0,), (1, 2), (0, 1), (2,))):
            line = [sum(taken[dy][dx] for dy in dys) for dx in range(3)]
            lanes = slice(slot % 2 * channels, (slot % 2 + 1) * channels)
            for n, block in enumerate((line[1] + line[2], line[0] + line[1], line[0], line[2])):
                into = pl.ds(aligned(k, chunk) + n * half, chunk)
                out[slot // 2, into, lanes] = block.astype(BF16)
        return carry

    lax.fori_loop(0, half // chunk, combine, 0)


def combine_weights(weight):
    channels = 2 * weight.shape[1]
    vmem = pl.BlockSpec(memory_space=pltpu.VMEM)
    return pl.pallas_call(
        combine_kernel,
        out_shape=jax.ShapeDtypeStruct((2, 2 * channels, 2 * channels), BF16),
        in_specs=[vmem],
        out_specs=vmem,
        compiler_params=pltpu.CompilerParams(vmem_limit_bytes=8 * 1024 * 1024),
        name="combine_weights",
    )(weight.T)


def first_kernel(
    wide,
    sizes,
    place,
    above,
    own,
    below,
    gains,
    weight_one,
    weight_two,
    later,
    out_ref,
    w1,
    w2,
    acc,
    x1e,
    x1o,
    x2e,
    x2o,
    sems,
):
    channels = own.shape[-1]
    frames = own.shape[1] - 4
    height, width = sizes
    col, row = place[1], place[3]
    units = frames + 2
    del later

    def load(source, target, base):
        return [
            pltpu.make_async_copy(
                source.at[:, dx], target.at[:, :, pl.ds(dx * channels, channels)], sems.at[base + dx]
            )
            for dx in range(3)
        ]

    copies_one = load(weight_one, w1, 0)
    copies_two = load(weight_two, w2, 3)
    for copy in copies_one + copies_two:
        copy.start()

    slots = [lax.rem(y + col, 2) for y in range(2)]

    def own_rows(index):
        return [own[slot, index].astype(F32) for slot in slots]

    def rows_of(index):
        first = [above[slot * units + index].astype(F32) for slot in slots]
        last = [below[slot * units + index].astype(F32) for slot in slots]
        return jnp.concatenate(first + own_rows(index) + last, axis=0)

    for f in range(2):
        store(x1e, x1o, f, rows_of(frames + f), 6, wide)
        first, last = above[2 * units + f].astype(F32), below[2 * units + f].astype(F32)
        values = jnp.concatenate([first] + own_rows(units + f) + [last], axis=0)
        store(x2e, x2o, f, values, 4, wide)

    def norm_one(f, carry):
        values = activate(rows_of(f), gains[0:1, :], 1.0)
        store(x1e, x1o, f + 2, values, 6, wide)
        return carry

    lax.fori_loop(0, frames, norm_one, 0)
    low_product(acc, x1e, x1o, frames, 6, wide, w1, copies_one)

    mask = line_mask(place, wide, 2 * row - 1, 4, height, width)

    def norm_two(f, carry):
        size = 4 * wide
        values = activate(low_sum(acc, aligned(f, size), size), gains[1:2, :], mask)
        store(x2e, x2o, f + 2, values, 4, wide)
        return carry

    lax.fori_loop(0, frames, norm_two, 0)
    low_product(acc, x2e, x2o, frames, 4, wide, w2, copies_two)

    def residual(f, carry):
        size = 2 * wide
        values = low_sum(acc, aligned(f, size), size) + jnp.concatenate(own_rows(f), axis=0)
        out_ref[f] = values.astype(BF16)
        return carry

    lax.fori_loop(0, frames, residual, 0)


def planes(slots, height, wide, channels):
    return [
        pltpu.VMEM((slots * height * wide, channels), BF16),
        pltpu.VMEM((slots * (height - 2) * wide, channels), BF16),
    ]


def first_block(place, pieces, gains, weight_one, weight_two, later, sizes):
    _, units, wide, channels = pieces[1].shape
    frames = units - 4
    slots = -(-3 * channels // LANES)
    vmem = pl.BlockSpec(memory_space=pltpu.VMEM)
    anywhere = pl.BlockSpec(memory_space=pl.ANY)
    return pl.pallas_call(
        functools.partial(first_kernel, wide, sizes),
        out_shape=jax.ShapeDtypeStruct((frames, 2 * wide, channels), BF16),
        in_specs=[pl.BlockSpec(memory_space=pltpu.SMEM)]
        + [vmem] * 4
        + [pl.BlockSpec(memory_space=pltpu.HBM)] * 2
        + [anywhere],
        out_specs=vmem,
        scratch_shapes=[
            pltpu.VMEM((9, channels, slots * LANES), BF16),
            pltpu.VMEM((9, channels, slots * LANES), BF16),
            pltpu.VMEM((slots, frames * 4 * wide, LANES), F32),
            *planes(frames + 2, 6, wide, channels),
            *planes(frames + 2, 4, wide, channels),
            pltpu.SemaphoreType.DMA((6,)),
        ],
        compiler_params=pltpu.CompilerParams(vmem_limit_bytes=50 * 1024 * 1024),
        cost_estimate=pl.CostEstimate(
            flops=2 * 27 * channels * channels * frames * 6 * wide,
            bytes_accessed=2 * 54 * channels * channels,
            transcendentals=0,
        ),
        name="first_block",
    )(place, *pieces, gains, weight_one, weight_two, later)


def second_kernel(
    wide,
    sizes,
    place,
    above,
    blocked,
    below,
    tile_above,
    windows,
    tile_below,
    gains,
    weight_time,
    weight_up,
    weight_three,
    weight_four,
    out_ref,
    wt,
    wu,
    w3,
    w4,
    acc,
    mixed,
    de,
    do,
    x3e,
    x3o,
    x4e,
    x4o,
    lifted_ref,
    sems,
):
    channels = blocked.shape[-1]
    half = channels // 2
    size = 6 * wide
    frames = blocked.shape[0]
    count = 2 * frames
    height, width = sizes
    row = place[3]
    copies = [
        pltpu.make_async_copy(source, target, sems.at[i])
        for i, (source, target) in enumerate(
            ((weight_time, wt), (weight_up, wu), (weight_three, w3), (weight_four, w4))
        )
    ]
    for copy in copies:
        copy.start()

    def cached(start, base, lines, depth, f):
        parts = [tile_above[start + depth * f + i] for i in range(depth)]
        parts += [windows[base + lines * f + i] for i in range(lines)]
        parts += [tile_below[start + depth * f + i] for i in range(depth)]
        return jnp.concatenate([line.astype(F32) for line in parts], axis=0)

    for f in range(2):
        mixed[f * size : (f + 1) * size, :] = cached(0, 0, 2, 2, f).astype(BF16)
    for f in range(frames):
        for i, ref in enumerate((above, blocked, below)):
            begin = (f + 2) * size + i * 2 * wide
            mixed[begin : begin + 2 * wide, :] = ref[f]

    copies[0].wait()

    def mix(n, carry):
        lanes = pl.ds(pl.multiple_of(n * LANES, LANES), LANES)
        left = jnp.concatenate(
            [mixed[pl.ds(t * size, frames * size), :] for t in range(3)], axis=1
        )
        acc[n, 0 : frames * size, :] = jnp.dot(left, wt[:, lanes], preferred_element_type=F32)
        return carry

    lax.fori_loop(0, 2 * channels // LANES, mix, 0)
    mask_low = line_mask(place, wide, 2 * row - 2, 6, height, width)

    def double(t, carry):
        rows = pl.ds(aligned(t, size), size)
        first = jnp.concatenate([acc[0, rows, :], acc[1, rows, 0:128]], axis=1)
        second = jnp.concatenate([acc[1, rows, 128:256], acc[2, rows, :]], axis=1)
        store(de, do, 2 * t, first * mask_low, 6, wide)
        store(de, do, 2 * t + 1, second * mask_low, 6, wide)
        return carry

    lax.fori_loop(0, frames, double, 0)

    copies[1].wait()

    for py in range(2):

        def enlarge(n, carry):
            lanes = pl.ds(pl.multiple_of(n * LANES, LANES), LANES)
            left = jnp.concatenate(
                [taps(de, do, 0, count, 6, wide, 0, py), taps(de, do, 0, count, 6, wide, 0, py + 1)],
                axis=1,
            )
            acc[n, py * count * 4 * wide : (py + 1) * count * 4 * wide, :] = transposed_dot(
                left, wu[py, lanes, :]
            )
            return carry

        lax.fori_loop(0, 2 * channels // LANES, enlarge, 0)

    for f in range(2):
        store(x3e, x3o, f, cached(4, 4, 4, 2, f), 8, wide)
        store(x4e, x4o, f, cached(8, 12, 4, 1, f), 6, wide)
    gain3, gain4 = gains[2:3, :], gains[3:4, :]
    mask_three = line_mask(place, wide, 4 * row - 2, 8, 2 * height, width)
    part = 4 * wide

    def norm_three(f, carry):
        values = []
        for py in range(2):
            start = pl.multiple_of(py * count * part + f * part, 16)
            values.append(high_sum(acc, start, part).astype(BF16).astype(F32))
        lifted = jnp.concatenate(
            [values[h % 2][(h // 2) * wide : (h // 2 + 1) * wide] for h in range(8)], axis=0
        )
        lifted_ref[pl.ds(aligned(f, part), part), :] = lifted[2 * wide : 6 * wide]
        store(x3e, x3o, f + 2, activate_pairs(lifted, gain3, mask_three), 8, wide)
        return carry

    lax.fori_loop(0, count, norm_three, 0)
    copies[2].wait()
    high_product(acc, x3e, x3o, count, 8, wide, w3)

    mask_four = mask_three[wide : 7 * wide]

    def norm_four(f, carry):
        values = high_sum(acc, aligned(f, size), size)
        store(x4e, x4o, f + 2, activate_pairs(values, gain4, mask_four), 6, wide)
        return carry

    lax.fori_loop(0, count, norm_four, 0)
    copies[3].wait()
    high_product(acc, x4e, x4o, count, 6, wide, w4)

    def finish(f, carry):
        start = aligned(f, part)
        values = high_sum(acc, start, part) + lifted_ref[pl.ds(start, part), :]
        values = pltpu.roll(values, part - HALO, 0)
        for y in range(4):
            inner = wide - 2 * HALO
            out_ref[f, y] = values[y * wide : y * wide + inner].astype(BF16)
        return carry

    lax.fori_loop(0, count, finish, 0)


def second_block(place, pieces, tiles, gains, weights, sizes, wide):
    frames, _, channels = pieces[0].shape
    count = 2 * frames
    vmem = pl.BlockSpec(memory_space=pltpu.VMEM)
    anywhere = pl.BlockSpec(memory_space=pl.ANY)
    return pl.pallas_call(
        functools.partial(second_kernel, wide, sizes),
        out_shape=jax.ShapeDtypeStruct((count, 4, wide - 2 * HALO, channels), BF16),
        in_specs=[pl.BlockSpec(memory_space=pltpu.SMEM)]
        + [vmem] * 7
        + [pl.BlockSpec(memory_space=pltpu.HBM)]
        + [anywhere] * 3,
        out_specs=vmem,
        scratch_shapes=[
            *(pltpu.VMEM(weight.shape, BF16) for weight in weights),
            pltpu.VMEM((3, 2 * count * 4 * wide, LANES), F32),
            pltpu.VMEM(((frames + 2) * 6 * wide, channels), BF16),
            *planes(count, 6, wide, channels),
            *planes(count + 2, 8, wide, channels),
            *planes(count + 2, 6, wide, channels),
            pltpu.VMEM((count * 4 * wide, channels), F32),
            pltpu.SemaphoreType.DMA((4,)),
        ],
        compiler_params=pltpu.CompilerParams(vmem_limit_bytes=40 * 1024 * 1024),
        name="second_block",
    )(place, *pieces, *tiles, gains, *weights)


def body(
    latent,
    cache_one,
    cache_two,
    cache_time,
    cache_three,
    cache_four,
    gain_one,
    gain_two,
    gain_three,
    gain_four,
    weight_one,
    weight_two,
    weight_time,
    weight_upsample,
    weight_three,
    weight_four,
):
    section, row, col = (lax.axis_index(name) for name in ("section", "rows", "cols"))
    sections, row_count, col_count = (lax.axis_size(name) for name in ("section", "rows", "cols"))
    width, channels = latent.shape[2:]
    tile = width // col_count
    part = tile // sections
    wide = part + 2 * HALO
    half = weight_three.shape[1]
    sizes = (2 * row_count, width)
    place = jnp.stack([section, col, col * tile + section * part - HALO, row]).astype(jnp.int32)

    gains = jnp.stack([gain_one, gain_two, jnp.tile(gain_three, 2), jnp.tile(gain_four, 2)])

    latent = latent.reshape(latent.shape[0], width, channels)
    arrived = swapped(latent, "section")
    mine, theirs, tiles = pack(
        place,
        latent,
        arrived,
        cache_one[:, 0],
        cache_two[:, 0],
        cache_time,
        cache_three,
        cache_four,
        wide,
        tile,
        part,
    )
    weight_three, mine = lax.optimization_barrier((weight_three, mine))
    weight_three = align_weights(weight_three)
    own, up, down, windows, tile_up, tile_down = stack(
        place, mine, swapped(theirs, "cols"), tiles, weight_three
    )
    pieces = [shifted(up, "rows", 1), own, shifted(down, "rows", -1)]
    tiles = [shifted(tile_up, "rows", 1), windows, shifted(tile_down, "rows", -1)]
    weight_upsample, own = lax.optimization_barrier((weight_upsample, own))
    weight_upsample = combine_weights(weight_upsample)
    blocked = first_block(
        place,
        pieces,
        gains,
        weight_one.reshape(9, 3, channels, channels),
        weight_two.reshape(9, 3, channels, channels),
        weight_upsample,
        sizes,
    )
    blocks = [shifted(blocked, "rows", 1), blocked, shifted(blocked, "rows", -1)]
    weight_four, _ = lax.optimization_barrier((weight_four, blocked))
    weight_four = align_weights(weight_four)
    frames = second_block(
        place,
        blocks,
        tiles,
        gains,
        (weight_time, weight_upsample, weight_three, weight_four),
        sizes,
        wide,
    )
    count = frames.shape[0] // sections
    given = lax.dynamic_slice_in_dim(frames, (1 - section) * count, count, 0)
    kept = lax.dynamic_slice_in_dim(frames, section * count, count, 0)
    arrived = swapped(given, "section")
    low = section == 0
    joined = jnp.concatenate(
        [jnp.where(low, kept, arrived), jnp.where(low, arrived, kept)], axis=2
    )
    return joined.reshape(count, 4, 2 * tile, half)


def solution(mesh):
    placed = (
        P("section", ("rows", "cols"), None, None),
        P(None, ("rows", "cols"), None, None),
        P(None, ("rows", "cols"), None, None),
        P(None, "rows", "cols", None),
        P(None, "rows", "cols", None),
        P(None, "rows", "cols", None),
    ) + (P(),) * 10
    return jax.shard_map(
        body,
        mesh=mesh,
        in_specs=placed,
        out_specs=P("section", "rows", "cols", None),
        check_vma=False,
    )
```

```python
import functools

import jax
import jax.numpy as jnp
from jax import lax
from jax.experimental import pallas as pl
from jax.experimental.pallas import tpu as pltpu
from jax.sharding import PartitionSpec as P

EPSILON = 1e-06
HALO = 4
LANES = 256
BF16 = jnp.bfloat16
F32 = jnp.float32


def swapped(value, axis):
    return lax.ppermute(value, axis, [(0, 1), (1, 0)])


def shifted(value, axis, steps):
    count = lax.axis_size(axis)
    initial, last = (max(0, -steps), min(count, count - steps))
    return lax.ppermute(value, axis, [(source, source + steps) for source in range(initial, last)])


def silu(scaled):
    half = scaled * 0.5
    return half * (1.0 + jnp.tanh(half))


def activate(values, gain, mask):
    mean = jnp.mean(values * values, axis=-1, keepdims=True)
    return silu(values * (lax.rsqrt(mean + EPSILON) * mask) * gain)


def activate_pairs(values, gain, mask):
    channels = values.shape[-1] // 2
    squares = values * values
    first = lax.broadcasted_iota(jnp.int32, (1, 2 * channels), 1) < channels
    total = jnp.sum(squares, axis=-1, keepdims=True)
    low = jnp.sum(jnp.where(first, squares, 0.0), axis=-1, keepdims=True)
    scale_low = lax.rsqrt(low / channels + EPSILON) * mask
    scale_high = lax.rsqrt((total - low) / channels + EPSILON) * mask
    return silu(values * jnp.where(first, scale_low, scale_high) * gain)


def merge(even, odd, channels):
    turned = pltpu.roll(odd, channels - 128, 1)
    first = lax.broadcasted_iota(jnp.int32, (1, 128), 1) < channels - 128
    middle = jnp.where(first, even[:, 128:], turned[:, :128])
    return jnp.concatenate([even[:, :128], middle, turned[:, 128:]], axis=1)


def aligned(index, size):
    return pl.multiple_of(index * size, 16)


def line_mask(place, wide, first, count, limit, width):
    columns = place[2] + lax.broadcasted_iota(jnp.int32, (wide, 1), 0)
    inside = jnp.where((columns >= 0) & (columns < width), 1.0, 0.0)
    lines = []
    for i in range(count):
        line = first + i
        lines.append(inside * jnp.where((line >= 0) & (line < limit), 1.0, 0.0))
    return jnp.concatenate(lines, axis=0)


def store(even, odd, slot, values, height, wide):
    even[pl.ds(slot * (height * wide), height * wide), :] = values.astype(BF16)
    odd[pl.ds(slot * ((height - 2) * wide), (height - 2) * wide), :] = values[
        wide : (height - 1) * wide
    ].astype(BF16)


def taps(even, odd, begin, count, height, wide, dt, dy, lanes=slice(None)):
    inner = (height - 2) * wide
    if dy == 1:
        parts = [odd[pl.ds((begin + f + dt) * inner, inner), lanes] for f in range(count)]
    else:
        parts = [
            even[pl.ds((begin + f + dt) * height * wide + dy * wide, inner), lanes]
            for f in range(count)
        ]
    return jnp.concatenate(parts, axis=0)


def low_product(acc, even, odd, count, height, wide, weights, copies):
    rows = count * (height - 2) * wide
    channels = weights.shape[1]
    lanes = 3 * channels
    waited = 0
    for n in range(-(-lanes // LANES)):
        begin, end = n * LANES, min((n + 1) * LANES, lanes)
        while waited * channels < end:
            copies[waited].wait()
            waited += 1
        total = None
        for first, last in ((0, 4), (4, 8), (8, 9)):
            left = jnp.concatenate(
                [
                    taps(even, odd, 0, count, height, wide, t // 3, t % 3)
                    for t in range(first, last)
                ],
                axis=1,
            )
            right = weights[first:last, :, begin:end].reshape((last - first) * channels, -1)
            part = jnp.dot(left, right, preferred_element_type=F32)
            total = part if total is None else total + part
        acc[n, 0:rows, 0 : end - begin] = total


def low_sum(acc, start, size):
    rows = pl.ds(start, size)
    before = jnp.concatenate([acc[0, rows, :], acc[1, rows, 0:128]], axis=1)
    center = jnp.concatenate([acc[1, rows, 128:256], acc[2, rows, :]], axis=1)
    after = jnp.concatenate([acc[3, rows, :], acc[4, rows, 0:128]], axis=1)
    return center + pltpu.roll(before, 1, 0) + pltpu.roll(after, size - 1, 0)


def transposed_dot(left, right):
    return lax.dot_general(left, right, (((1,), (1,)), ((), ())), preferred_element_type=F32)


def high_product(acc, even, odd, count, height, wide, weights):
    rows = count * (height - 2) * wide
    channels = weights.shape[1] // 9

    def column(n, carry):
        outputs = pl.ds(pl.multiple_of(n * LANES, LANES), LANES)
        total = None
        for first, last in ((0, 4), (4, 8), (8, 9)):
            left = jnp.concatenate(
                [
                    taps(even, odd, 0, count, height, wide, t // 3, t % 3)
                    for t in range(first, last)
                ],
                axis=1,
            )
            part = transposed_dot(left, weights[outputs, first * channels : last * channels])
            total = part if total is None else total + part
        acc[n, 0:rows, :] = total
        return carry

    lax.fori_loop(0, weights.shape[0] // LANES, column, 0)


def high_sum(acc, start, size):
    rows = pl.ds(start, size)
    center = jnp.concatenate([acc[0, rows, :], acc[1, rows, 0:128]], axis=1)
    side = jnp.concatenate([acc[1, rows, 128:256], acc[2, rows, :]], axis=1)
    channels = center.shape[1]
    first = lax.broadcasted_iota(jnp.int32, (1, channels), 1) < channels // 2
    return center + jnp.where(first, pltpu.roll(side, 1, 0), pltpu.roll(side, size - 1, 0))


def pack_kernel(
    wide,
    tile,
    part,
    place,
    latent,
    arrived,
    one,
    two,
    time,
    three,
    four,
    mine,
    theirs,
    tiles,
    spread,
    low,
    high,
):
    section, col = place[0], place[1]
    width, channels = latent.shape[1:]
    half = three.shape[-1]
    empty = jnp.zeros((spread.shape[1] - width, channels), F32)

    def put(slot, values):
        spread[slot] = pltpu.roll(
            jnp.concatenate([values.astype(F32), empty], axis=0), HALO, 0
        )

    for i in range(2):
        put(2 * section + i, latent[i])
        put(2 * (1 - section) + i, arrived[i])
        put(4 + i, one[i])
        put(6 + i, two[i])
    for slot in range(8):
        for ref, which in ((mine, col), (theirs, 1 - col)):
            begin = pl.multiple_of(which * tile + section * part, 8)
            ref[slot] = spread[slot, pl.ds(begin, wide), :].astype(BF16)

    lines = [time[f, y].astype(F32) for f in range(2) for y in range(2)]
    for ref in (three, four):
        for f in range(2):
            for y in range(4):
                values = ref[f, y].astype(F32)
                low[...] = values[:, :128]
                high[:, 0 : half - 128] = values[:, 128:]
                count = values.shape[0] // 2
                even, odd = (
                    jnp.concatenate(
                        [lanes[pl.ds(o, count, stride=2), :] for lanes in (low, high)], axis=1
                    )
                    for o in range(2)
                )
                lines.append(merge(even, odd, half))
    for i, line in enumerate(lines):
        tiles[i] = line.astype(BF16)

    left = col == 0
    upper = lax.broadcasted_iota(jnp.int32, (8, 1), 0) < HALO
    blocks = []
    for i in range(0, len(lines), 2):
        one_line, two_line = lines[i], lines[i + 1]
        last = jnp.where(upper, pltpu.roll(one_line[-8:], HALO, 0), two_line[-8:])
        first = jnp.where(upper, one_line[:8], pltpu.roll(two_line[:8], HALO, 0))
        blocks.append(jnp.where(left, last, first))
    gap = jnp.zeros_like(blocks[0])
    count = wide // 8
    for i in range(theirs.shape[0] - 8):
        group = (blocks + [gap] * count)[i * count : (i + 1) * count]
        theirs[8 + i] = jnp.concatenate(group, axis=0).astype(BF16)


def pack(place, latent, arrived, one, two, time, three, four, wide, tile, part):
    width, channels = latent.shape[1:]
    vmem = pl.BlockSpec(memory_space=pltpu.VMEM)
    lines = 20
    extra = -(-lines * HALO // wide)
    return pl.pallas_call(
        functools.partial(pack_kernel, wide, tile, part),
        out_shape=[
            jax.ShapeDtypeStruct((8, wide, channels), BF16),
            jax.ShapeDtypeStruct((8 + extra, wide, channels), BF16),
            jax.ShapeDtypeStruct((lines, tile, channels), BF16),
        ],
        in_specs=[pl.BlockSpec(memory_space=pltpu.SMEM)] + [vmem] * 7,
        out_specs=[vmem] * 3,
        scratch_shapes=[
            pltpu.VMEM((8, width + 16, channels), F32),
            pltpu.VMEM((three.shape[2], 128), F32),
            pltpu.VMEM((three.shape[2], 128), F32),
        ],
        compiler_params=pltpu.CompilerParams(vmem_limit_bytes=60 * 1024 * 1024),
        name="pack",
    )(place, latent, arrived, one, two, time, three, four)


def stack_kernel(
    wide, place, mine, theirs, tiles, later, own, up, down, windows, tile_up, tile_down
):
    del later
    section, col = place[0], place[1]
    count = mine.shape[0] - 2
    own[0], own[1] = mine[...], theirs[0 : count + 2]
    for ref, y in ((up, 1), (down, 0)):
        ref[0:count], ref[count : 2 * count] = mine[0:count], theirs[0:count]
        here = lax.rem(y + col, 2) == 0
        ref[2 * count :] = jnp.where(here, mine[count:], theirs[count : count + 2])

    part = wide - 2 * HALO
    upper = lax.broadcasted_iota(jnp.int32, (8, 1), 0) < HALO
    groups = wide // 8
    for i in range(tiles.shape[0]):
        line = tiles[i].astype(F32)
        block = i // 2
        begin = block % groups * 8
        edge = theirs[count + 2 + block // groups].astype(F32)[begin : begin + 8]
        turned = pltpu.roll(edge, HALO, 0)
        before, after = (edge, turned) if i % 2 == 0 else (turned, edge)
        first = pltpu.roll(line, HALO, 0)[:wide]
        head = jnp.where(upper, jnp.where(col == 1, before, 0.0), first[:8])
        first = jnp.concatenate([head, first[8:]], axis=0)
        last = pltpu.roll(line, line.shape[0] - (part - HALO), 0)[:wide]
        tail = jnp.where(upper, last[-8:], jnp.where(col == 0, after, 0.0))
        last = jnp.concatenate([last[:-8], tail], axis=0)
        line = jnp.where(section == 0, first, last).astype(BF16)
        windows[i] = line
        if i < 4:
            tile_up[i] = line
            tile_down[i] = line
            continue
        f, y = (i - 4) % 8 // 4, (i - 4) % 4
        base, depth = (4, 2) if i < 12 else (8, 1)
        if y >= 4 - depth:
            tile_up[base + depth * f + y - (4 - depth)] = line
        if y < depth:
            tile_down[base + depth * f + y] = line


def stack(place, mine, theirs, tiles, later):
    units, wide, channels = mine.shape
    vmem = pl.BlockSpec(memory_space=pltpu.VMEM)
    lines = 2 * units - 2
    shapes = [(2, units), (lines,), (lines,), (tiles.shape[0],), (10,), (10,)]
    return pl.pallas_call(
        functools.partial(stack_kernel, wide),
        out_shape=[jax.ShapeDtypeStruct(shape + (wide, channels), BF16) for shape in shapes],
        in_specs=[pl.BlockSpec(memory_space=pltpu.SMEM)]
        + [vmem] * 3
        + [pl.BlockSpec(memory_space=pl.ANY)],
        out_specs=[vmem] * 6,
        compiler_params=pltpu.CompilerParams(vmem_limit_bytes=8 * 1024 * 1024),
        name="stack",
    )(place, mine, theirs, tiles, later)


def align_kernel(weight, out):
    half = weight.shape[0]
    chunk = 16
    tail = half - 128
    low = lax.broadcasted_iota(jnp.int32, (1, 128), 1) < tail

    def move(k, carry):
        here = aligned(k, chunk)
        none = jnp.zeros((chunk, 128), F32)
        for t in range(9):
            base = 3 * t * half
            first = base // 128 * 128
            last = min(first + 640, weight.shape[1])
            values = weight[pl.ds(here, chunk), first:last].astype(F32)
            if last < first + 640:
                values = jnp.concatenate(
                    [values[:, :512], jnp.concatenate([values[:, 512:], none[:, tail:]], axis=1)],
                    axis=1,
                )
            turned = pltpu.roll(values, 640 - tail, 1)
            tiles = [values[:, 128 * i : 128 * (i + 1)] for i in range(5)]
            moved = [turned[:, 128 * i : 128 * (i + 1)] for i in range(5)]
            if base == first:
                blocks = (
                    moved[1:4],
                    tiles[0:3],
                    [none, jnp.where(low, 0.0, moved[4]), moved[0]],
                    [tiles[3], jnp.where(low, tiles[4], 0.0), none],
                )
            else:
                blocks = (
                    tiles[2:5],
                    moved[0:3],
                    [none, jnp.where(low, 0.0, tiles[0]), tiles[1]],
                    [moved[3], jnp.where(low, moved[4], 0.0), none],
                )
            for n, block in enumerate(blocks):
                into = pl.ds(here + n * half, chunk)
                out[into, 2 * half * t : 2 * half * (t + 1)] = jnp.concatenate(
                    block, axis=1
                ).astype(BF16)
        return carry

    lax.fori_loop(0, half // chunk, move, 0)


def align_weights(weight):
    half = weight.shape[1]
    vmem = pl.BlockSpec(memory_space=pltpu.VMEM)
    return pl.pallas_call(
        align_kernel,
        out_shape=jax.ShapeDtypeStruct((4 * half, 18 * half), BF16),
        in_specs=[vmem],
        out_specs=vmem,
        compiler_params=pltpu.CompilerParams(vmem_limit_bytes=8 * 1024 * 1024),
        name="align_weights",
    )(weight.T)


def combine_kernel(weight, out):
    half = weight.shape[0]
    channels = weight.shape[1] // 9
    chunk = 16

    def combine(k, carry):
        rows = pl.ds(aligned(k, chunk), chunk)
        taken = [
            [
                weight[rows, (3 * dy + dx) * channels : (3 * dy + dx + 1) * channels].astype(F32)
                for dx in range(3)
            ]
            for dy in range(3)
        ]
        for slot, dys in enumerate(((0,), (1, 2), (0, 1), (2,))):
            line = [sum(taken[dy][dx] for dy in dys) for dx in range(3)]
            lanes = slice(slot % 2 * channels, (slot % 2 + 1) * channels)
            for n, block in enumerate((line[1] + line[2], line[0] + line[1], line[0], line[2])):
                into = pl.ds(aligned(k, chunk) + n * half, chunk)
                out[slot // 2, into, lanes] = block.astype(BF16)
        return carry

    lax.fori_loop(0, half // chunk, combine, 0)


def combine_weights(weight):
    channels = 2 * weight.shape[1]
    vmem = pl.BlockSpec(memory_space=pltpu.VMEM)
    return pl.pallas_call(
        combine_kernel,
        out_shape=jax.ShapeDtypeStruct((2, 2 * channels, 2 * channels), BF16),
        in_specs=[vmem],
        out_specs=vmem,
        compiler_params=pltpu.CompilerParams(vmem_limit_bytes=8 * 1024 * 1024),
        name="combine_weights",
    )(weight.T)


def first_kernel(
    wide,
    sizes,
    place,
    above,
    own,
    below,
    gains,
    weight_one,
    weight_two,
    later,
    out_ref,
    w1,
    w2,
    acc,
    x1e,
    x1o,
    x2e,
    x2o,
    sems,
):
    channels = own.shape[-1]
    frames = own.shape[1] - 4
    height, width = sizes
    col, row = place[1], place[3]
    units = frames + 2
    del later

    def load(source, target, base):
        return [
            pltpu.make_async_copy(
                source.at[:, dx], target.at[:, :, pl.ds(dx * channels, channels)], sems.at[base + dx]
            )
            for dx in range(3)
        ]

    copies_one = load(weight_one, w1, 0)
    copies_two = load(weight_two, w2, 3)
    for copy in copies_one + copies_two:
        copy.start()

    slots = [lax.rem(y + col, 2) for y in range(2)]

    def own_rows(index):
        return [own[slot, index].astype(F32) for slot in slots]

    def rows_of(index):
        first = [above[slot * units + index].astype(F32) for slot in slots]
        last = [below[slot * units + index].astype(F32) for slot in slots]
        return jnp.concatenate(first + own_rows(index) + last, axis=0)

    for f in range(2):
        store(x1e, x1o, f, rows_of(frames + f), 6, wide)
        first, last = above[2 * units + f].astype(F32), below[2 * units + f].astype(F32)
        values = jnp.concatenate([first] + own_rows(units + f) + [last], axis=0)
        store(x2e, x2o, f, values, 4, wide)

    def norm_one(f, carry):
        values = activate(rows_of(f), gains[0:1, :], 1.0)
        store(x1e, x1o, f + 2, values, 6, wide)
        return carry

    lax.fori_loop(0, frames, norm_one, 0)
    low_product(acc, x1e, x1o, frames, 6, wide, w1, copies_one)

    mask = line_mask(place, wide, 2 * row - 1, 4, height, width)

    def norm_two(f, carry):
        size = 4 * wide
        values = activate(low_sum(acc, aligned(f, size), size), gains[1:2, :], mask)
        store(x2e, x2o, f + 2, values, 4, wide)
        return carry

    lax.fori_loop(0, frames, norm_two, 0)
    low_product(acc, x2e, x2o, frames, 4, wide, w2, copies_two)

    def residual(f, carry):
        size = 2 * wide
        values = low_sum(acc, aligned(f, size), size) + jnp.concatenate(own_rows(f), axis=0)
        out_ref[f] = values.astype(BF16)
        return carry

    lax.fori_loop(0, frames, residual, 0)


def planes(slots, height, wide, channels):
    return [
        pltpu.VMEM((slots * height * wide, channels), BF16),
        pltpu.VMEM((slots * (height - 2) * wide, channels), BF16),
    ]


def first_block(place, pieces, gains, weight_one, weight_two, later, sizes):
    _, units, wide, channels = pieces[1].shape
    frames = units - 4
    slots = -(-3 * channels // LANES)
    vmem = pl.BlockSpec(memory_space=pltpu.VMEM)
    anywhere = pl.BlockSpec(memory_space=pl.ANY)
    return pl.pallas_call(
        functools.partial(first_kernel, wide, sizes),
        out_shape=jax.ShapeDtypeStruct((frames, 2 * wide, channels), BF16),
        in_specs=[pl.BlockSpec(memory_space=pltpu.SMEM)]
        + [vmem] * 4
        + [pl.BlockSpec(memory_space=pltpu.HBM)] * 2
        + [anywhere],
        out_specs=vmem,
        scratch_shapes=[
            pltpu.VMEM((9, channels, slots * LANES), BF16),
            pltpu.VMEM((9, channels, slots * LANES), BF16),
            pltpu.VMEM((slots, frames * 4 * wide, LANES), F32),
            *planes(frames + 2, 6, wide, channels),
            *planes(frames + 2, 4, wide, channels),
            pltpu.SemaphoreType.DMA((6,)),
        ],
        compiler_params=pltpu.CompilerParams(vmem_limit_bytes=50 * 1024 * 1024),
        cost_estimate=pl.CostEstimate(
            flops=2 * 27 * channels * channels * frames * 6 * wide,
            bytes_accessed=2 * 54 * channels * channels,
            transcendentals=0,
        ),
        name="first_block",
    )(place, *pieces, gains, weight_one, weight_two, later)


def second_kernel(
    wide,
    sizes,
    place,
    above,
    blocked,
    below,
    tile_above,
    windows,
    tile_below,
    gains,
    wt,
    wu,
    w3,
    w4,
    out_ref,
    acc,
    mixed,
    de,
    do,
    x3e,
    x3o,
    x4e,
    x4o,
    lifted_ref,
):
    channels = blocked.shape[-1]
    half = channels // 2
    size = 6 * wide
    frames = blocked.shape[0]
    count = 2 * frames
    height, width = sizes
    row = place[3]

    def cached(start, base, lines, depth, f):
        parts = [tile_above[start + depth * f + i] for i in range(depth)]
        parts += [windows[base + lines * f + i] for i in range(lines)]
        parts += [tile_below[start + depth * f + i] for i in range(depth)]
        return jnp.concatenate([line.astype(F32) for line in parts], axis=0)

    for f in range(2):
        mixed[f * size : (f + 1) * size, :] = cached(0, 0, 2, 2, f).astype(BF16)
    for f in range(frames):
        for i, ref in enumerate((above, blocked, below)):
            begin = (f + 2) * size + i * 2 * wide
            mixed[begin : begin + 2 * wide, :] = ref[f]


    def mix(n, carry):
        lanes = pl.ds(pl.multiple_of(n * LANES, LANES), LANES)
        left = jnp.concatenate(
            [mixed[pl.ds(t * size, frames * size), :] for t in range(3)], axis=1
        )
        acc[n, 0 : frames * size, :] = jnp.dot(left, wt[:, lanes], preferred_element_type=F32)
        return carry

    lax.fori_loop(0, 2 * channels // LANES, mix, 0)
    mask_low = line_mask(place, wide, 2 * row - 2, 6, height, width)

    def double(t, carry):
        rows = pl.ds(aligned(t, size), size)
        first = jnp.concatenate([acc[0, rows, :], acc[1, rows, 0:128]], axis=1)
        second = jnp.concatenate([acc[1, rows, 128:256], acc[2, rows, :]], axis=1)
        store(de, do, 2 * t, first * mask_low, 6, wide)
        store(de, do, 2 * t + 1, second * mask_low, 6, wide)
        return carry

    lax.fori_loop(0, frames, double, 0)


    for py in range(2):

        def enlarge(n, carry):
            lanes = pl.ds(pl.multiple_of(n * LANES, LANES), LANES)
            left = jnp.concatenate(
                [taps(de, do, 0, count, 6, wide, 0, py), taps(de, do, 0, count, 6, wide, 0, py + 1)],
                axis=1,
            )
            acc[n, py * count * 4 * wide : (py + 1) * count * 4 * wide, :] = transposed_dot(
                left, wu[py, lanes, :]
            )
            return carry

        lax.fori_loop(0, 2 * channels // LANES, enlarge, 0)

    for f in range(2):
        store(x3e, x3o, f, cached(4, 4, 4, 2, f), 8, wide)
        store(x4e, x4o, f, cached(8, 12, 4, 1, f), 6, wide)
    gain3, gain4 = gains[2:3, :], gains[3:4, :]
    mask_three = line_mask(place, wide, 4 * row - 2, 8, 2 * height, width)
    part = 4 * wide

    def norm_three(f, carry):
        values = []
        for py in range(2):
            start = pl.multiple_of(py * count * part + f * part, 16)
            values.append(high_sum(acc, start, part).astype(BF16).astype(F32))
        lifted = jnp.concatenate(
            [values[h % 2][(h // 2) * wide : (h // 2 + 1) * wide] for h in range(8)], axis=0
        )
        lifted_ref[pl.ds(aligned(f, part), part), :] = lifted[2 * wide : 6 * wide]
        store(x3e, x3o, f + 2, activate_pairs(lifted, gain3, mask_three), 8, wide)
        return carry

    lax.fori_loop(0, count, norm_three, 0)
    high_product(acc, x3e, x3o, count, 8, wide, w3)

    mask_four = mask_three[wide : 7 * wide]

    def norm_four(f, carry):
        values = high_sum(acc, aligned(f, size), size)
        store(x4e, x4o, f + 2, activate_pairs(values, gain4, mask_four), 6, wide)
        return carry

    lax.fori_loop(0, count, norm_four, 0)
    high_product(acc, x4e, x4o, count, 6, wide, w4)

    def finish(f, carry):
        start = aligned(f, part)
        values = high_sum(acc, start, part) + lifted_ref[pl.ds(start, part), :]
        values = pltpu.roll(values, part - HALO, 0)
        for y in range(4):
            inner = wide - 2 * HALO
            out_ref[f, y] = values[y * wide : y * wide + inner].astype(BF16)
        return carry

    lax.fori_loop(0, count, finish, 0)


def second_block(place, pieces, tiles, gains, weights, sizes, wide):
    frames, _, channels = pieces[0].shape
    count = 2 * frames
    vmem = pl.BlockSpec(memory_space=pltpu.VMEM)
    return pl.pallas_call(
        functools.partial(second_kernel, wide, sizes),
        out_shape=jax.ShapeDtypeStruct((count, 4, wide - 2 * HALO, channels), BF16),
        in_specs=[pl.BlockSpec(memory_space=pltpu.SMEM)]
        + [vmem] * 11,
        out_specs=vmem,
        scratch_shapes=[
            pltpu.VMEM((3, 2 * count * 4 * wide, LANES), F32),
            pltpu.VMEM(((frames + 2) * 6 * wide, channels), BF16),
            *planes(count, 6, wide, channels),
            *planes(count + 2, 8, wide, channels),
            *planes(count + 2, 6, wide, channels),
            pltpu.VMEM((count * 4 * wide, channels), F32),
        ],
        compiler_params=pltpu.CompilerParams(vmem_limit_bytes=34 * 1024 * 1024),
        name="second_block",
    )(place, *pieces, *tiles, gains, *weights)


def body(
    latent,
    cache_one,
    cache_two,
    cache_time,
    cache_three,
    cache_four,
    gain_one,
    gain_two,
    gain_three,
    gain_four,
    weight_one,
    weight_two,
    weight_time,
    weight_upsample,
    weight_three,
    weight_four,
):
    section, row, col = (lax.axis_index(name) for name in ("section", "rows", "cols"))
    sections, row_count, col_count = (lax.axis_size(name) for name in ("section", "rows", "cols"))
    width, channels = latent.shape[2:]
    tile = width // col_count
    part = tile // sections
    wide = part + 2 * HALO
    half = weight_three.shape[1]
    sizes = (2 * row_count, width)
    place = jnp.stack([section, col, col * tile + section * part - HALO, row]).astype(jnp.int32)

    gains = jnp.stack([gain_one, gain_two, jnp.tile(gain_three, 2), jnp.tile(gain_four, 2)])

    latent = latent.reshape(latent.shape[0], width, channels)
    arrived = swapped(latent, "section")
    mine, theirs, tiles = pack(
        place,
        latent,
        arrived,
        cache_one[:, 0],
        cache_two[:, 0],
        cache_time,
        cache_three,
        cache_four,
        wide,
        tile,
        part,
    )
    weight_three, mine = lax.optimization_barrier((weight_three, mine))
    weight_three = align_weights(weight_three)
    own, up, down, windows, tile_up, tile_down = stack(
        place, mine, swapped(theirs, "cols"), tiles, weight_three
    )
    pieces = [shifted(up, "rows", 1), own, shifted(down, "rows", -1)]
    tiles = [shifted(tile_up, "rows", 1), windows, shifted(tile_down, "rows", -1)]
    weight_upsample, own = lax.optimization_barrier((weight_upsample, own))
    weight_upsample = combine_weights(weight_upsample)
    blocked = first_block(
        place,
        pieces,
        gains,
        weight_one.reshape(9, 3, channels, channels),
        weight_two.reshape(9, 3, channels, channels),
        weight_upsample,
        sizes,
    )
    blocks = [shifted(blocked, "rows", 1), blocked, shifted(blocked, "rows", -1)]
    weight_four, _ = lax.optimization_barrier((weight_four, blocked))
    weight_four = align_weights(weight_four)
    frames = second_block(
        place,
        blocks,
        tiles,
        gains,
        (weight_time, weight_upsample, weight_three, weight_four),
        sizes,
        wide,
    )
    count = frames.shape[0] // sections
    given = lax.dynamic_slice_in_dim(frames, (1 - section) * count, count, 0)
    kept = lax.dynamic_slice_in_dim(frames, section * count, count, 0)
    arrived = swapped(given, "section")
    low = section == 0
    joined = jnp.concatenate(
        [jnp.where(low, kept, arrived), jnp.where(low, arrived, kept)], axis=2
    )
    return joined.reshape(count, 4, 2 * tile, half)


def solution(mesh):
    placed = (
        P("section", ("rows", "cols"), None, None),
        P(None, ("rows", "cols"), None, None),
        P(None, ("rows", "cols"), None, None),
        P(None, "rows", "cols", None),
        P(None, "rows", "cols", None),
        P(None, "rows", "cols", None),
    ) + (P(),) * 10
    return jax.shard_map(
        body,
        mesh=mesh,
        in_specs=placed,
        out_specs=P("section", "rows", "cols", None),
        check_vma=False,
    )
```

```python
import functools

import jax
import jax.numpy as jnp
from jax import lax
from jax.experimental import pallas as pl
from jax.experimental.pallas import tpu as pltpu
from jax.sharding import PartitionSpec as P

EPSILON = 1e-06
HALO = 4
LANES = 256
BF16 = jnp.bfloat16
F32 = jnp.float32


def swapped(value, axis):
    return lax.ppermute(value, axis, [(0, 1), (1, 0)])


def paired(value, axis, first):
    pairs = [(i, i + 1) for i in range(first, lax.axis_size(axis) - 1, 2)]
    return lax.ppermute(value, axis, pairs + [(high, low) for low, high in pairs])


def silu(scaled):
    half = scaled * 0.5
    return half * (1.0 + jnp.tanh(half))


def activate(values, gain, mask):
    mean = jnp.mean(values * values, axis=-1, keepdims=True)
    return silu(values * (lax.rsqrt(mean + EPSILON) * mask) * gain)


def activate_pairs(values, gain, mask):
    channels = values.shape[-1] // 2
    squares = values * values
    first = lax.broadcasted_iota(jnp.int32, (1, 2 * channels), 1) < channels
    total = jnp.sum(squares, axis=-1, keepdims=True)
    low = jnp.sum(jnp.where(first, squares, 0.0), axis=-1, keepdims=True)
    scale_low = lax.rsqrt(low / channels + EPSILON) * mask
    scale_high = lax.rsqrt((total - low) / channels + EPSILON) * mask
    return silu(values * jnp.where(first, scale_low, scale_high) * gain)


def merge(even, odd, channels):
    turned = pltpu.roll(odd, channels - 128, 1)
    first = lax.broadcasted_iota(jnp.int32, (1, 128), 1) < channels - 128
    middle = jnp.where(first, even[:, 128:], turned[:, :128])
    return jnp.concatenate([even[:, :128], middle, turned[:, 128:]], axis=1)


def aligned(index, size):
    return pl.multiple_of(index * size, 16)


def line_mask(place, wide, first, count, limit, width):
    columns = place[2] + lax.broadcasted_iota(jnp.int32, (wide, 1), 0)
    inside = jnp.where((columns >= 0) & (columns < width), 1.0, 0.0)
    lines = []
    for i in range(count):
        line = first + i
        lines.append(inside * jnp.where((line >= 0) & (line < limit), 1.0, 0.0))
    return jnp.concatenate(lines, axis=0)


def store(even, odd, slot, values, height, wide):
    even[pl.ds(slot * (height * wide), height * wide), :] = values.astype(BF16)
    odd[pl.ds(slot * ((height - 2) * wide), (height - 2) * wide), :] = values[
        wide : (height - 1) * wide
    ].astype(BF16)


def taps(even, odd, begin, count, height, wide, dt, dy, lanes=slice(None)):
    inner = (height - 2) * wide
    if dy == 1:
        parts = [odd[pl.ds((begin + f + dt) * inner, inner), lanes] for f in range(count)]
    else:
        parts = [
            even[pl.ds((begin + f + dt) * height * wide + dy * wide, inner), lanes]
            for f in range(count)
        ]
    return jnp.concatenate(parts, axis=0)


def low_product(acc, even, odd, count, height, wide, weights, copies):
    rows = count * (height - 2) * wide
    channels = weights.shape[1]
    needed = [dx * channels // LANES for dx in range(3)]

    def column(n, carry):
        for copy, when in zip(copies, needed):
            pl.when(n == when)(copy.wait)
        lanes = pl.ds(pl.multiple_of(n * LANES, LANES), LANES)
        total = None
        for first, last in ((0, 4), (4, 8), (8, 9)):
            left = jnp.concatenate(
                [
                    taps(even, odd, 0, count, height, wide, t // 3, t % 3)
                    for t in range(first, last)
                ],
                axis=1,
            )
            right = weights[first:last, :, lanes].reshape((last - first) * channels, LANES)
            part = jnp.dot(left, right, preferred_element_type=F32)
            total = part if total is None else total + part
        acc[n, 0:rows, :] = total
        return carry

    lax.fori_loop(0, weights.shape[-1] // LANES, column, 0)


def low_sum(acc, start, size):
    rows = pl.ds(start, size)
    before = jnp.concatenate([acc[0, rows, :], acc[1, rows, 0:128]], axis=1)
    center = jnp.concatenate([acc[1, rows, 128:256], acc[2, rows, :]], axis=1)
    after = jnp.concatenate([acc[3, rows, :], acc[4, rows, 0:128]], axis=1)
    return center + pltpu.roll(before, 1, 0) + pltpu.roll(after, size - 1, 0)


def transposed_dot(left, right):
    return lax.dot_general(left, right, (((1,), (1,)), ((), ())), preferred_element_type=F32)


def high_product(acc, even, odd, count, height, wide, weights):
    rows = count * (height - 2) * wide
    channels = weights.shape[1] // 9

    def column(n, carry):
        outputs = pl.ds(pl.multiple_of(n * LANES, LANES), LANES)
        total = None
        for first, last in ((0, 4), (4, 8), (8, 9)):
            left = jnp.concatenate(
                [
                    taps(even, odd, 0, count, height, wide, t // 3, t % 3)
                    for t in range(first, last)
                ],
                axis=1,
            )
            part = transposed_dot(left, weights[outputs, first * channels : last * channels])
            total = part if total is None else total + part
        acc[n, 0:rows, :] = total
        return carry

    lax.fori_loop(0, weights.shape[0] // LANES, column, 0)


def high_sum(acc, start, size):
    rows = pl.ds(start, size)
    center = jnp.concatenate([acc[0, rows, :], acc[1, rows, 0:128]], axis=1)
    side = jnp.concatenate([acc[1, rows, 128:256], acc[2, rows, :]], axis=1)
    channels = center.shape[1]
    first = lax.broadcasted_iota(jnp.int32, (1, channels), 1) < channels // 2
    return center + jnp.where(first, pltpu.roll(side, 1, 0), pltpu.roll(side, size - 1, 0))


def pack_kernel(
    wide,
    tile,
    part,
    place,
    latent,
    arrived,
    one,
    two,
    time,
    three,
    four,
    mine,
    theirs,
    tiles,
    spread,
    low,
    high,
):
    section, col = place[0], place[1]
    width, channels = latent.shape[1:]
    half = three.shape[-1]
    empty = jnp.zeros((spread.shape[1] - width, channels), F32)

    def put(slot, values):
        spread[slot] = pltpu.roll(
            jnp.concatenate([values.astype(F32), empty], axis=0), HALO, 0
        )

    for i in range(2):
        put(2 * section + i, latent[i])
        put(2 * (1 - section) + i, arrived[i])
        put(4 + i, one[i])
        put(6 + i, two[i])
    for slot in range(8):
        for ref, which in ((mine, col), (theirs, 1 - col)):
            begin = pl.multiple_of(which * tile + section * part, 8)
            ref[slot] = spread[slot, pl.ds(begin, wide), :].astype(BF16)

    lines = [time[f, y].astype(F32) for f in range(2) for y in range(2)]
    for ref in (three, four):
        for f in range(2):
            for y in range(4):
                values = ref[f, y].astype(F32)
                low[...] = values[:, :128]
                high[:, 0 : half - 128] = values[:, 128:]
                count = values.shape[0] // 2
                even, odd = (
                    jnp.concatenate(
                        [lanes[pl.ds(o, count, stride=2), :] for lanes in (low, high)], axis=1
                    )
                    for o in range(2)
                )
                lines.append(merge(even, odd, half))
    for i, line in enumerate(lines):
        tiles[i] = line.astype(BF16)

    left = col == 0
    upper = lax.broadcasted_iota(jnp.int32, (8, 1), 0) < HALO
    blocks = []
    for i in range(0, len(lines), 2):
        one_line, two_line = lines[i], lines[i + 1]
        last = jnp.where(upper, pltpu.roll(one_line[-8:], HALO, 0), two_line[-8:])
        first = jnp.where(upper, one_line[:8], pltpu.roll(two_line[:8], HALO, 0))
        blocks.append(jnp.where(left, last, first))
    gap = jnp.zeros_like(blocks[0])
    count = wide // 8
    for i in range(theirs.shape[0] - 8):
        group = (blocks + [gap] * count)[i * count : (i + 1) * count]
        theirs[8 + i] = jnp.concatenate(group, axis=0).astype(BF16)


def pack(place, latent, arrived, one, two, time, three, four, wide, tile, part):
    width, channels = latent.shape[1:]
    vmem = pl.BlockSpec(memory_space=pltpu.VMEM)
    lines = 20
    extra = -(-lines * HALO // wide)
    return pl.pallas_call(
        functools.partial(pack_kernel, wide, tile, part),
        out_shape=[
            jax.ShapeDtypeStruct((8, wide, channels), BF16),
            jax.ShapeDtypeStruct((8 + extra, wide, channels), BF16),
            jax.ShapeDtypeStruct((lines, tile, channels), BF16),
        ],
        in_specs=[pl.BlockSpec(memory_space=pltpu.SMEM)] + [vmem] * 7,
        out_specs=[vmem] * 3,
        scratch_shapes=[
            pltpu.VMEM((8, width + 16, channels), F32),
            pltpu.VMEM((three.shape[2], 128), F32),
            pltpu.VMEM((three.shape[2], 128), F32),
        ],
        compiler_params=pltpu.CompilerParams(vmem_limit_bytes=60 * 1024 * 1024),
        name="pack",
    )(place, latent, arrived, one, two, time, three, four)


def stack_kernel(
    wide, place, mine, theirs, tiles, later, own, near, far, windows, tile_near, tile_far
):
    del later
    section, col = place[0], place[1]
    count = mine.shape[0] - 2
    own[0], own[1] = mine[...], theirs[0 : count + 2]
    parity = lax.rem(place[3], 2)
    for ref, y in ((near, 1 - parity), (far, parity)):
        ref[0:count], ref[count : 2 * count] = mine[0:count], theirs[0:count]
        here = lax.rem(y + col, 2) == 0
        ref[2 * count :] = jnp.where(here, mine[count:], theirs[count : count + 2])

    part = wide - 2 * HALO
    upper = lax.broadcasted_iota(jnp.int32, (8, 1), 0) < HALO
    groups = wide // 8
    for i in range(tiles.shape[0]):
        line = tiles[i].astype(F32)
        block = i // 2
        begin = block % groups * 8
        edge = theirs[count + 2 + block // groups].astype(F32)[begin : begin + 8]
        turned = pltpu.roll(edge, HALO, 0)
        before, after = (edge, turned) if i % 2 == 0 else (turned, edge)
        first = pltpu.roll(line, HALO, 0)[:wide]
        head = jnp.where(upper, jnp.where(col == 1, before, 0.0), first[:8])
        first = jnp.concatenate([head, first[8:]], axis=0)
        last = pltpu.roll(line, line.shape[0] - (part - HALO), 0)[:wide]
        tail = jnp.where(upper, last[-8:], jnp.where(col == 0, after, 0.0))
        last = jnp.concatenate([last[:-8], tail], axis=0)
        line = jnp.where(section == 0, first, last).astype(BF16)
        windows[i] = line
    is_even = parity == 0
    for base, start, count, depth in ((0, 0, 2, 2), (4, 4, 4, 2), (12, 8, 4, 1)):
        for f in range(2):
            for j in range(depth):
                slot = start + depth * f + j
                high = windows[base + count * f + j]
                low = windows[base + count * f + count - depth + j]
                tile_near[slot] = jnp.where(is_even, low, high)
                tile_far[slot] = jnp.where(is_even, high, low)


def stack(place, mine, theirs, tiles, later):
    units, wide, channels = mine.shape
    vmem = pl.BlockSpec(memory_space=pltpu.VMEM)
    lines = 2 * units - 2
    shapes = [(2, units), (lines,), (lines,), (tiles.shape[0],), (10,), (10,)]
    return pl.pallas_call(
        functools.partial(stack_kernel, wide),
        out_shape=[jax.ShapeDtypeStruct(shape + (wide, channels), BF16) for shape in shapes],
        in_specs=[pl.BlockSpec(memory_space=pltpu.SMEM)]
        + [vmem] * 3
        + [pl.BlockSpec(memory_space=pl.ANY)],
        out_specs=[vmem] * 6,
        compiler_params=pltpu.CompilerParams(vmem_limit_bytes=8 * 1024 * 1024),
        name="stack",
    )(place, mine, theirs, tiles, later)


def align_kernel(weight, out):
    half = weight.shape[0]
    chunk = 16
    tail = half - 128
    low = lax.broadcasted_iota(jnp.int32, (1, 128), 1) < tail

    def move(k, carry):
        here = aligned(k, chunk)
        none = jnp.zeros((chunk, 128), F32)
        for t in range(9):
            base = 3 * t * half
            first = base // 128 * 128
            last = min(first + 640, weight.shape[1])
            values = weight[pl.ds(here, chunk), first:last].astype(F32)
            if last < first + 640:
                values = jnp.concatenate(
                    [values[:, :512], jnp.concatenate([values[:, 512:], none[:, tail:]], axis=1)],
                    axis=1,
                )
            turned = pltpu.roll(values, 640 - tail, 1)
            tiles = [values[:, 128 * i : 128 * (i + 1)] for i in range(5)]
            moved = [turned[:, 128 * i : 128 * (i + 1)] for i in range(5)]
            if base == first:
                blocks = (
                    moved[1:4],
                    tiles[0:3],
                    [none, jnp.where(low, 0.0, moved[4]), moved[0]],
                    [tiles[3], jnp.where(low, tiles[4], 0.0), none],
                )
            else:
                blocks = (
                    tiles[2:5],
                    moved[0:3],
                    [none, jnp.where(low, 0.0, tiles[0]), tiles[1]],
                    [moved[3], jnp.where(low, moved[4], 0.0), none],
                )
            for n, block in enumerate(blocks):
                into = pl.ds(here + n * half, chunk)
                out[into, 2 * half * t : 2 * half * (t + 1)] = jnp.concatenate(
                    block, axis=1
                ).astype(BF16)
        return carry

    lax.fori_loop(0, half // chunk, move, 0)


def align_weights(weight):
    half = weight.shape[1]
    vmem = pl.BlockSpec(memory_space=pltpu.VMEM)
    return pl.pallas_call(
        align_kernel,
        out_shape=jax.ShapeDtypeStruct((4 * half, 18 * half), BF16),
        in_specs=[vmem],
        out_specs=vmem,
        compiler_params=pltpu.CompilerParams(vmem_limit_bytes=8 * 1024 * 1024),
        name="align_weights",
    )(weight.T)


def combine_kernel(weight, out):
    half = weight.shape[0]
    channels = weight.shape[1] // 9
    chunk = 16

    def combine(k, carry):
        rows = pl.ds(aligned(k, chunk), chunk)
        taken = [
            [
                weight[rows, (3 * dy + dx) * channels : (3 * dy + dx + 1) * channels].astype(F32)
                for dx in range(3)
            ]
            for dy in range(3)
        ]
        for slot, dys in enumerate(((0,), (1, 2), (0, 1), (2,))):
            line = [sum(taken[dy][dx] for dy in dys) for dx in range(3)]
            lanes = slice(slot % 2 * channels, (slot % 2 + 1) * channels)
            for n, block in enumerate((line[1] + line[2], line[0] + line[1], line[0], line[2])):
                into = pl.ds(aligned(k, chunk) + n * half, chunk)
                out[slot // 2, into, lanes] = block.astype(BF16)
        return carry

    lax.fori_loop(0, half // chunk, combine, 0)


def combine_weights(weight):
    channels = 2 * weight.shape[1]
    vmem = pl.BlockSpec(memory_space=pltpu.VMEM)
    return pl.pallas_call(
        combine_kernel,
        out_shape=jax.ShapeDtypeStruct((2, 2 * channels, 2 * channels), BF16),
        in_specs=[vmem],
        out_specs=vmem,
        compiler_params=pltpu.CompilerParams(vmem_limit_bytes=8 * 1024 * 1024),
        name="combine_weights",
    )(weight.T)


def first_kernel(
    wide,
    sizes,
    place,
    near,
    own,
    far,
    gains,
    weight_one,
    weight_two,
    later,
    out_ref,
    w1,
    w2,
    acc,
    x1e,
    x1o,
    x2e,
    x2o,
    sems,
):
    channels = own.shape[-1]
    frames = own.shape[1] - 4
    height, width = sizes
    col, row = place[1], place[3]
    units = frames + 2
    del later

    def load(source, target, base):
        return [
            pltpu.make_async_copy(
                source.at[:, dx], target.at[:, :, pl.ds(dx * channels, channels)], sems.at[base + dx]
            )
            for dx in range(3)
        ]

    copies_one = load(weight_one, w1, 0)
    copies_two = load(weight_two, w2, 3)
    for copy in copies_one + copies_two:
        copy.start()

    slots = [lax.rem(y + col, 2) for y in range(2)]

    is_even = lax.rem(row, 2) == 0

    def own_rows(index):
        return [own[slot, index].astype(F32) for slot in slots]

    def above(line):
        return jnp.where(is_even, far[line].astype(F32), near[line].astype(F32))

    def below(line):
        return jnp.where(is_even, near[line].astype(F32), far[line].astype(F32))

    def rows_of(index):
        first = [above(slot * units + index) for slot in slots]
        last = [below(slot * units + index) for slot in slots]
        return jnp.concatenate(first + own_rows(index) + last, axis=0)

    for f in range(2):
        store(x1e, x1o, f, rows_of(frames + f), 6, wide)
        first, last = above(2 * units + f), below(2 * units + f)
        values = jnp.concatenate([first] + own_rows(units + f) + [last], axis=0)
        store(x2e, x2o, f, values, 4, wide)

    def norm_one(f, carry):
        values = activate(rows_of(f), gains[0:1, :], 1.0)
        store(x1e, x1o, f + 2, values, 6, wide)
        return carry

    lax.fori_loop(0, frames, norm_one, 0)
    low_product(acc, x1e, x1o, frames, 6, wide, w1, copies_one)

    mask = line_mask(place, wide, 2 * row - 1, 4, height, width)

    def norm_two(f, carry):
        size = 4 * wide
        values = activate(low_sum(acc, aligned(f, size), size), gains[1:2, :], mask)
        store(x2e, x2o, f + 2, values, 4, wide)
        return carry

    lax.fori_loop(0, frames, norm_two, 0)
    low_product(acc, x2e, x2o, frames, 4, wide, w2, copies_two)

    def residual(f, carry):
        size = 2 * wide
        values = low_sum(acc, aligned(f, size), size) + jnp.concatenate(own_rows(f), axis=0)
        out_ref[f] = values.astype(BF16)
        return carry

    lax.fori_loop(0, frames, residual, 0)


def planes(slots, height, wide, channels):
    return [
        pltpu.VMEM((slots * height * wide, channels), BF16),
        pltpu.VMEM((slots * (height - 2) * wide, channels), BF16),
    ]


def first_block(place, pieces, gains, weight_one, weight_two, later, sizes):
    _, units, wide, channels = pieces[1].shape
    frames = units - 4
    slots = -(-3 * channels // LANES)
    vmem = pl.BlockSpec(memory_space=pltpu.VMEM)
    anywhere = pl.BlockSpec(memory_space=pl.ANY)
    return pl.pallas_call(
        functools.partial(first_kernel, wide, sizes),
        out_shape=jax.ShapeDtypeStruct((frames, 2 * wide, channels), BF16),
        in_specs=[pl.BlockSpec(memory_space=pltpu.SMEM)]
        + [vmem] * 4
        + [pl.BlockSpec(memory_space=pltpu.HBM)] * 2
        + [anywhere],
        out_specs=vmem,
        scratch_shapes=[
            pltpu.VMEM((9, channels, slots * LANES), BF16),
            pltpu.VMEM((9, channels, slots * LANES), BF16),
            pltpu.VMEM((slots, frames * 4 * wide, LANES), F32),
            *planes(frames + 2, 6, wide, channels),
            *planes(frames + 2, 4, wide, channels),
            pltpu.SemaphoreType.DMA((6,)),
        ],
        compiler_params=pltpu.CompilerParams(vmem_limit_bytes=50 * 1024 * 1024),
        cost_estimate=pl.CostEstimate(
            flops=2 * 27 * channels * channels * frames * 6 * wide,
            bytes_accessed=2 * 54 * channels * channels,
            transcendentals=0,
        ),
        name="first_block",
    )(place, *pieces, gains, weight_one, weight_two, later)


def second_kernel(
    wide,
    sizes,
    place,
    near,
    blocked,
    far,
    tile_near,
    windows,
    tile_far,
    gains,
    wt,
    wu,
    w3,
    w4,
    out_ref,
    acc,
    mixed,
    de,
    do,
    x3e,
    x3o,
    x4e,
    x4o,
    lifted_ref,
):
    channels = blocked.shape[-1]
    half = channels // 2
    size = 6 * wide
    frames = blocked.shape[0]
    count = 2 * frames
    height, width = sizes
    row = place[3]

    is_even = lax.rem(row, 2) == 0

    def chosen(when, one, other, index):
        return jnp.where(when, one[index].astype(F32), other[index].astype(F32))

    def cached(start, base, lines, depth, f):
        slots = [start + depth * f + i for i in range(depth)]
        parts = [chosen(is_even, tile_far, tile_near, slot) for slot in slots]
        parts += [windows[base + lines * f + i].astype(F32) for i in range(lines)]
        parts += [chosen(is_even, tile_near, tile_far, slot) for slot in slots]
        return jnp.concatenate(parts, axis=0)

    for f in range(2):
        mixed[f * size : (f + 1) * size, :] = cached(0, 0, 2, 2, f).astype(BF16)
    for f in range(frames):
        first, last = chosen(is_even, far, near, f), chosen(is_even, near, far, f)
        for i, values in enumerate((first.astype(BF16), blocked[f], last.astype(BF16))):
            begin = (f + 2) * size + i * 2 * wide
            mixed[begin : begin + 2 * wide, :] = values


    def mix(n, carry):
        lanes = pl.ds(pl.multiple_of(n * LANES, LANES), LANES)
        left = jnp.concatenate(
            [mixed[pl.ds(t * size, frames * size), :] for t in range(3)], axis=1
        )
        acc[n, 0 : frames * size, :] = jnp.dot(left, wt[:, lanes], preferred_element_type=F32)
        return carry

    lax.fori_loop(0, 2 * channels // LANES, mix, 0)
    mask_low = line_mask(place, wide, 2 * row - 2, 6, height, width)

    def double(t, carry):
        rows = pl.ds(aligned(t, size), size)
        first = jnp.concatenate([acc[0, rows, :], acc[1, rows, 0:128]], axis=1)
        second = jnp.concatenate([acc[1, rows, 128:256], acc[2, rows, :]], axis=1)
        store(de, do, 2 * t, first * mask_low, 6, wide)
        store(de, do, 2 * t + 1, second * mask_low, 6, wide)
        return carry

    lax.fori_loop(0, frames, double, 0)


    for py in range(2):

        def enlarge(n, carry):
            lanes = pl.ds(pl.multiple_of(n * LANES, LANES), LANES)
            left = jnp.concatenate(
                [taps(de, do, 0, count, 6, wide, 0, py), taps(de, do, 0, count, 6, wide, 0, py + 1)],
                axis=1,
            )
            acc[n, py * count * 4 * wide : (py + 1) * count * 4 * wide, :] = transposed_dot(
                left, wu[py, lanes, :]
            )
            return carry

        lax.fori_loop(0, 2 * channels // LANES, enlarge, 0)

    for f in range(2):
        store(x3e, x3o, f, cached(4, 4, 4, 2, f), 8, wide)
        store(x4e, x4o, f, cached(8, 12, 4, 1, f), 6, wide)
    gain3, gain4 = gains[2:3, :], gains[3:4, :]
    mask_three = line_mask(place, wide, 4 * row - 2, 8, 2 * height, width)
    part = 4 * wide

    def norm_three(f, carry):
        values = []
        for py in range(2):
            start = pl.multiple_of(py * count * part + f * part, 16)
            values.append(high_sum(acc, start, part).astype(BF16).astype(F32))
        lifted = jnp.concatenate(
            [values[h % 2][(h // 2) * wide : (h // 2 + 1) * wide] for h in range(8)], axis=0
        )
        lifted_ref[pl.ds(aligned(f, part), part), :] = lifted[2 * wide : 6 * wide]
        store(x3e, x3o, f + 2, activate_pairs(lifted, gain3, mask_three), 8, wide)
        return carry

    lax.fori_loop(0, count, norm_three, 0)
    high_product(acc, x3e, x3o, count, 8, wide, w3)

    mask_four = mask_three[wide : 7 * wide]

    def norm_four(f, carry):
        values = high_sum(acc, aligned(f, size), size)
        store(x4e, x4o, f + 2, activate_pairs(values, gain4, mask_four), 6, wide)
        return carry

    lax.fori_loop(0, count, norm_four, 0)
    high_product(acc, x4e, x4o, count, 6, wide, w4)

    def finish(f, carry):
        start = aligned(f, part)
        values = high_sum(acc, start, part) + lifted_ref[pl.ds(start, part), :]
        values = pltpu.roll(values, part - HALO, 0)
        for y in range(4):
            inner = wide - 2 * HALO
            out_ref[f, y] = values[y * wide : y * wide + inner].astype(BF16)
        return carry

    lax.fori_loop(0, count, finish, 0)


def second_block(place, pieces, tiles, gains, weights, sizes, wide):
    frames, _, channels = pieces[0].shape
    count = 2 * frames
    vmem = pl.BlockSpec(memory_space=pltpu.VMEM)
    return pl.pallas_call(
        functools.partial(second_kernel, wide, sizes),
        out_shape=jax.ShapeDtypeStruct((count, 4, wide - 2 * HALO, channels), BF16),
        in_specs=[pl.BlockSpec(memory_space=pltpu.SMEM)]
        + [vmem] * 11,
        out_specs=vmem,
        scratch_shapes=[
            pltpu.VMEM((3, 2 * count * 4 * wide, LANES), F32),
            pltpu.VMEM(((frames + 2) * 6 * wide, channels), BF16),
            *planes(count, 6, wide, channels),
            *planes(count + 2, 8, wide, channels),
            *planes(count + 2, 6, wide, channels),
            pltpu.VMEM((count * 4 * wide, channels), F32),
        ],
        compiler_params=pltpu.CompilerParams(vmem_limit_bytes=34 * 1024 * 1024),
        name="second_block",
    )(place, *pieces, *tiles, gains, *weights)


def body(
    latent,
    cache_one,
    cache_two,
    cache_time,
    cache_three,
    cache_four,
    gain_one,
    gain_two,
    gain_three,
    gain_four,
    weight_one,
    weight_two,
    weight_time,
    weight_upsample,
    weight_three,
    weight_four,
):
    section, row, col = (lax.axis_index(name) for name in ("section", "rows", "cols"))
    sections, row_count, col_count = (lax.axis_size(name) for name in ("section", "rows", "cols"))
    width, channels = latent.shape[2:]
    tile = width // col_count
    part = tile // sections
    wide = part + 2 * HALO
    half = weight_three.shape[1]
    sizes = (2 * row_count, width)
    place = jnp.stack([section, col, col * tile + section * part - HALO, row]).astype(jnp.int32)

    gains = jnp.stack([gain_one, gain_two, jnp.tile(gain_three, 2), jnp.tile(gain_four, 2)])

    latent = latent.reshape(latent.shape[0], width, channels)
    arrived = swapped(latent, "section")
    mine, theirs, tiles = pack(
        place,
        latent,
        arrived,
        cache_one[:, 0],
        cache_two[:, 0],
        cache_time,
        cache_three,
        cache_four,
        wide,
        tile,
        part,
    )
    weight_three, mine = lax.optimization_barrier((weight_three, mine))
    weight_three = align_weights(weight_three)
    own, near, far, windows, tile_near, tile_far = stack(
        place, mine, swapped(theirs, "cols"), tiles, weight_three
    )
    pieces = [paired(near, "rows", 0), own, paired(far, "rows", 1)]
    tiles = [paired(tile_near, "rows", 0), windows, paired(tile_far, "rows", 1)]
    weight_upsample, own = lax.optimization_barrier((weight_upsample, own))
    weight_upsample = combine_weights(weight_upsample)
    blocked = first_block(
        place,
        pieces,
        gains,
        weight_one.reshape(9, 3, channels, channels),
        weight_two.reshape(9, 3, channels, channels),
        weight_upsample,
        sizes,
    )
    blocks = [paired(blocked, "rows", 0), blocked, paired(blocked, "rows", 1)]
    weight_four, _ = lax.optimization_barrier((weight_four, blocked))
    weight_four = align_weights(weight_four)
    frames = second_block(
        place,
        blocks,
        tiles,
        gains,
        (weight_time, weight_upsample, weight_three, weight_four),
        sizes,
        wide,
    )
    count = frames.shape[0] // sections
    given = lax.dynamic_slice_in_dim(frames, (1 - section) * count, count, 0)
    kept = lax.dynamic_slice_in_dim(frames, section * count, count, 0)
    arrived = swapped(given, "section")
    low = section == 0
    joined = jnp.concatenate(
        [jnp.where(low, kept, arrived), jnp.where(low, arrived, kept)], axis=2
    )
    return joined.reshape(count, 4, 2 * tile, half)


def solution(mesh):
    placed = (
        P("section", ("rows", "cols"), None, None),
        P(None, ("rows", "cols"), None, None),
        P(None, ("rows", "cols"), None, None),
        P(None, "rows", "cols", None),
        P(None, "rows", "cols", None),
        P(None, "rows", "cols", None),
    ) + (P(),) * 10
    return jax.shard_map(
        body,
        mesh=mesh,
        in_specs=placed,
        out_specs=P("section", "rows", "cols", None),
        check_vma=False,
    )
```

```python
import functools

import jax
import jax.numpy as jnp
from jax import lax
from jax.experimental import pallas as pl
from jax.experimental.pallas import tpu as pltpu
from jax.sharding import PartitionSpec as P

EPSILON = 1e-06
HALO = 4
LANES = 256
BF16 = jnp.bfloat16
F32 = jnp.float32


def swapped(value, axis):
    return lax.ppermute(value, axis, [(0, 1), (1, 0)])


def paired(value, axis, first):
    pairs = [(i, i + 1) for i in range(first, lax.axis_size(axis) - 1, 2)]
    return lax.ppermute(value, axis, pairs + [(high, low) for low, high in pairs])


def silu(scaled):
    half = scaled * 0.5
    return half * (1.0 + jnp.tanh(half))


def activate(values, gain, mask):
    mean = jnp.mean(values * values, axis=-1, keepdims=True)
    return silu(values * (lax.rsqrt(mean + EPSILON) * mask) * gain)


def activate_pairs(values, gain, mask):
    channels = values.shape[-1] // 2
    squares = values * values
    first = lax.broadcasted_iota(jnp.int32, (1, 2 * channels), 1) < channels
    total = jnp.sum(squares, axis=-1, keepdims=True)
    low = jnp.sum(jnp.where(first, squares, 0.0), axis=-1, keepdims=True)
    scale_low = lax.rsqrt(low / channels + EPSILON) * mask
    scale_high = lax.rsqrt((total - low) / channels + EPSILON) * mask
    return silu(values * jnp.where(first, scale_low, scale_high) * gain)


def merge(even, odd, channels):
    turned = pltpu.roll(odd, channels - 128, 1)
    first = lax.broadcasted_iota(jnp.int32, (1, 128), 1) < channels - 128
    middle = jnp.where(first, even[:, 128:], turned[:, :128])
    return jnp.concatenate([even[:, :128], middle, turned[:, 128:]], axis=1)


def aligned(index, size):
    return pl.multiple_of(index * size, 16)


def line_mask(place, wide, first, count, limit, width):
    columns = place[2] + lax.broadcasted_iota(jnp.int32, (wide, 1), 0)
    inside = jnp.where((columns >= 0) & (columns < width), 1.0, 0.0)
    lines = []
    for i in range(count):
        line = first + i
        lines.append(inside * jnp.where((line >= 0) & (line < limit), 1.0, 0.0))
    return jnp.concatenate(lines, axis=0)


def store(even, odd, slot, values, height, wide):
    even[pl.ds(slot * (height * wide), height * wide), :] = values.astype(BF16)
    odd[pl.ds(slot * ((height - 2) * wide), (height - 2) * wide), :] = values[
        wide : (height - 1) * wide
    ].astype(BF16)


def taps(even, odd, begin, count, height, wide, dt, dy, lanes=slice(None)):
    inner = (height - 2) * wide
    if dy == 1:
        parts = [odd[pl.ds((begin + f + dt) * inner, inner), lanes] for f in range(count)]
    else:
        parts = [
            even[pl.ds((begin + f + dt) * height * wide + dy * wide, inner), lanes]
            for f in range(count)
        ]
    return jnp.concatenate(parts, axis=0)


def low_product(acc, even, odd, count, height, wide, weights, copies):
    rows = count * (height - 2) * wide
    channels = weights.shape[1]
    needed = [dx * channels // LANES for dx in range(3)]

    def column(n, carry):
        for copy, when in zip(copies, needed):
            pl.when(n == when)(copy.wait)
        lanes = pl.ds(pl.multiple_of(n * LANES, LANES), LANES)
        total = None
        for first, last in ((0, 4), (4, 8), (8, 9)):
            left = jnp.concatenate(
                [
                    taps(even, odd, 0, count, height, wide, t // 3, t % 3)
                    for t in range(first, last)
                ],
                axis=1,
            )
            right = weights[first:last, :, lanes].reshape((last - first) * channels, LANES)
            part = jnp.dot(left, right, preferred_element_type=F32)
            total = part if total is None else total + part
        acc[n, 0:rows, :] = total
        return carry

    lax.fori_loop(0, weights.shape[-1] // LANES, column, 0)


def low_sum(acc, start, size):
    rows = pl.ds(start, size)
    before = jnp.concatenate([acc[0, rows, :], acc[1, rows, 0:128]], axis=1)
    center = jnp.concatenate([acc[1, rows, 128:256], acc[2, rows, :]], axis=1)
    after = jnp.concatenate([acc[3, rows, :], acc[4, rows, 0:128]], axis=1)
    return center + pltpu.roll(before, 1, 0) + pltpu.roll(after, size - 1, 0)


def transposed_dot(left, right):
    return lax.dot_general(left, right, (((1,), (1,)), ((), ())), preferred_element_type=F32)


def high_product(acc, even, odd, count, height, wide, weights):
    rows = count * (height - 2) * wide
    channels = weights.shape[1] // 9

    def column(n, carry):
        outputs = pl.ds(pl.multiple_of(n * LANES, LANES), LANES)
        total = None
        for first, last in ((0, 4), (4, 8), (8, 9)):
            left = jnp.concatenate(
                [
                    taps(even, odd, 0, count, height, wide, t // 3, t % 3)
                    for t in range(first, last)
                ],
                axis=1,
            )
            part = transposed_dot(left, weights[outputs, first * channels : last * channels])
            total = part if total is None else total + part
        acc[n, 0:rows, :] = total
        return carry

    lax.fori_loop(0, weights.shape[0] // LANES, column, 0)


def high_sum(acc, start, size):
    rows = pl.ds(start, size)
    center = jnp.concatenate([acc[0, rows, :], acc[1, rows, 0:128]], axis=1)
    side = jnp.concatenate([acc[1, rows, 128:256], acc[2, rows, :]], axis=1)
    channels = center.shape[1]
    first = lax.broadcasted_iota(jnp.int32, (1, channels), 1) < channels // 2
    return center + jnp.where(first, pltpu.roll(side, 1, 0), pltpu.roll(side, size - 1, 0))


def pack_kernel(
    wide,
    tile,
    part,
    place,
    latent,
    arrived,
    one,
    two,
    time,
    three,
    four,
    mine,
    theirs,
    tiles,
    spread,
    low,
    high,
):
    section, col = place[0], place[1]
    width, channels = latent.shape[1:]
    half = three.shape[-1]
    empty = jnp.zeros((spread.shape[1] - width, channels), F32)

    def put(slot, values):
        spread[slot] = pltpu.roll(
            jnp.concatenate([values.astype(F32), empty], axis=0), HALO, 0
        )

    for i in range(2):
        put(2 * section + i, latent[i])
        put(2 * (1 - section) + i, arrived[i])
        put(4 + i, one[i])
        put(6 + i, two[i])
    for slot in range(8):
        for ref, which in ((mine, col), (theirs, 1 - col)):
            begin = pl.multiple_of(which * tile + section * part, 8)
            ref[slot] = spread[slot, pl.ds(begin, wide), :].astype(BF16)

    lines = [time[f, y].astype(F32) for f in range(2) for y in range(2)]
    for ref in (three, four):
        for f in range(2):
            for y in range(4):
                values = ref[f, y].astype(F32)
                low[...] = values[:, :128]
                high[:, 0 : half - 128] = values[:, 128:]
                count = values.shape[0] // 2
                even, odd = (
                    jnp.concatenate(
                        [lanes[pl.ds(o, count, stride=2), :] for lanes in (low, high)], axis=1
                    )
                    for o in range(2)
                )
                lines.append(merge(even, odd, half))
    for i, line in enumerate(lines):
        tiles[i] = line.astype(BF16)

    left = col == 0
    upper = lax.broadcasted_iota(jnp.int32, (8, 1), 0) < HALO
    blocks = []
    for i in range(0, len(lines), 2):
        one_line, two_line = lines[i], lines[i + 1]
        last = jnp.where(upper, pltpu.roll(one_line[-8:], HALO, 0), two_line[-8:])
        first = jnp.where(upper, one_line[:8], pltpu.roll(two_line[:8], HALO, 0))
        blocks.append(jnp.where(left, last, first))
    gap = jnp.zeros_like(blocks[0])
    count = wide // 8
    for i in range(theirs.shape[0] - 8):
        group = (blocks + [gap] * count)[i * count : (i + 1) * count]
        theirs[8 + i] = jnp.concatenate(group, axis=0).astype(BF16)


def pack(place, latent, arrived, one, two, time, three, four, wide, tile, part):
    width, channels = latent.shape[1:]
    vmem = pl.BlockSpec(memory_space=pltpu.VMEM)
    lines = 20
    extra = -(-lines * HALO // wide)
    return pl.pallas_call(
        functools.partial(pack_kernel, wide, tile, part),
        out_shape=[
            jax.ShapeDtypeStruct((8, wide, channels), BF16),
            jax.ShapeDtypeStruct((8 + extra, wide, channels), BF16),
            jax.ShapeDtypeStruct((lines, tile, channels), BF16),
        ],
        in_specs=[pl.BlockSpec(memory_space=pltpu.SMEM)] + [vmem] * 7,
        out_specs=[vmem] * 3,
        scratch_shapes=[
            pltpu.VMEM((8, width + 16, channels), F32),
            pltpu.VMEM((three.shape[2], 128), F32),
            pltpu.VMEM((three.shape[2], 128), F32),
        ],
        compiler_params=pltpu.CompilerParams(vmem_limit_bytes=60 * 1024 * 1024),
        name="pack",
    )(place, latent, arrived, one, two, time, three, four)


def stack_kernel(
    wide, place, mine, theirs, tiles, later, own, near, far, windows, tile_near, tile_far
):
    del later
    section, col = place[0], place[1]
    count = mine.shape[0] - 2
    own[0], own[1] = mine[...], theirs[0 : count + 2]
    parity = lax.rem(place[3], 2)
    for ref, y in ((near, 1 - parity), (far, parity)):
        ref[0:count], ref[count : 2 * count] = mine[0:count], theirs[0:count]
        here = lax.rem(y + col, 2) == 0
        ref[2 * count :] = jnp.where(here, mine[count:], theirs[count : count + 2])

    part = wide - 2 * HALO
    upper = lax.broadcasted_iota(jnp.int32, (8, 1), 0) < HALO
    groups = wide // 8
    for i in range(tiles.shape[0]):
        line = tiles[i].astype(F32)
        block = i // 2
        begin = block % groups * 8
        edge = theirs[count + 2 + block // groups].astype(F32)[begin : begin + 8]
        turned = pltpu.roll(edge, HALO, 0)
        before, after = (edge, turned) if i % 2 == 0 else (turned, edge)
        first = pltpu.roll(line, HALO, 0)[:wide]
        head = jnp.where(upper, jnp.where(col == 1, before, 0.0), first[:8])
        first = jnp.concatenate([head, first[8:]], axis=0)
        last = pltpu.roll(line, line.shape[0] - (part - HALO), 0)[:wide]
        tail = jnp.where(upper, last[-8:], jnp.where(col == 0, after, 0.0))
        last = jnp.concatenate([last[:-8], tail], axis=0)
        line = jnp.where(section == 0, first, last).astype(BF16)
        windows[i] = line
    is_even = parity == 0
    for base, start, count, depth in ((0, 0, 2, 2), (4, 4, 4, 2), (12, 8, 4, 1)):
        for f in range(2):
            for j in range(depth):
                slot = start + depth * f + j
                high = windows[base + count * f + j]
                low = windows[base + count * f + count - depth + j]
                tile_near[slot] = jnp.where(is_even, low, high)
                tile_far[slot] = jnp.where(is_even, high, low)


def stack(place, mine, theirs, tiles, later):
    units, wide, channels = mine.shape
    vmem = pl.BlockSpec(memory_space=pltpu.VMEM)
    lines = 2 * units - 2
    shapes = [(2, units), (lines,), (lines,), (tiles.shape[0],), (10,), (10,)]
    return pl.pallas_call(
        functools.partial(stack_kernel, wide),
        out_shape=[jax.ShapeDtypeStruct(shape + (wide, channels), BF16) for shape in shapes],
        in_specs=[pl.BlockSpec(memory_space=pltpu.SMEM)]
        + [vmem] * 3
        + [pl.BlockSpec(memory_space=pl.ANY)],
        out_specs=[vmem] * 6,
        compiler_params=pltpu.CompilerParams(vmem_limit_bytes=8 * 1024 * 1024),
        name="stack",
    )(place, mine, theirs, tiles, later)


def align_kernel(weight, out):
    half = weight.shape[0]
    chunk = 16
    tail = half - 128
    low = lax.broadcasted_iota(jnp.int32, (1, 128), 1) < tail

    def move(k, carry):
        here = aligned(k, chunk)
        none = jnp.zeros((chunk, 128), F32)
        for t in range(9):
            base = 3 * t * half
            first = base // 128 * 128
            last = min(first + 640, weight.shape[1])
            values = weight[pl.ds(here, chunk), first:last].astype(F32)
            if last < first + 640:
                values = jnp.concatenate(
                    [values[:, :512], jnp.concatenate([values[:, 512:], none[:, tail:]], axis=1)],
                    axis=1,
                )
            turned = pltpu.roll(values, 640 - tail, 1)
            tiles = [values[:, 128 * i : 128 * (i + 1)] for i in range(5)]
            moved = [turned[:, 128 * i : 128 * (i + 1)] for i in range(5)]
            if base == first:
                blocks = (
                    moved[1:4],
                    tiles[0:3],
                    [none, jnp.where(low, 0.0, moved[4]), moved[0]],
                    [tiles[3], jnp.where(low, tiles[4], 0.0), none],
                )
            else:
                blocks = (
                    tiles[2:5],
                    moved[0:3],
                    [none, jnp.where(low, 0.0, tiles[0]), tiles[1]],
                    [moved[3], jnp.where(low, moved[4], 0.0), none],
                )
            for n, block in enumerate(blocks):
                into = pl.ds(here + n * half, chunk)
                out[into, 2 * half * t : 2 * half * (t + 1)] = jnp.concatenate(
                    block, axis=1
                ).astype(BF16)
        return carry

    lax.fori_loop(0, half // chunk, move, 0)


def align_weights(weight):
    half = weight.shape[1]
    vmem = pl.BlockSpec(memory_space=pltpu.VMEM)
    return pl.pallas_call(
        align_kernel,
        out_shape=jax.ShapeDtypeStruct((4 * half, 18 * half), BF16),
        in_specs=[vmem],
        out_specs=vmem,
        compiler_params=pltpu.CompilerParams(vmem_limit_bytes=8 * 1024 * 1024),
        name="align_weights",
    )(weight.T)


def combine_kernel(weight, out):
    half = weight.shape[0]
    channels = weight.shape[1] // 9
    chunk = 16

    def combine(k, carry):
        rows = pl.ds(aligned(k, chunk), chunk)
        taken = [
            [
                weight[rows, (3 * dy + dx) * channels : (3 * dy + dx + 1) * channels].astype(F32)
                for dx in range(3)
            ]
            for dy in range(3)
        ]
        for slot, dys in enumerate(((0,), (1, 2), (0, 1), (2,))):
            line = [sum(taken[dy][dx] for dy in dys) for dx in range(3)]
            lanes = slice(slot % 2 * channels, (slot % 2 + 1) * channels)
            for n, block in enumerate((line[1] + line[2], line[0] + line[1], line[0], line[2])):
                into = pl.ds(aligned(k, chunk) + n * half, chunk)
                out[slot // 2, into, lanes] = block.astype(BF16)
        return carry

    lax.fori_loop(0, half // chunk, combine, 0)


def combine_weights(weight):
    channels = 2 * weight.shape[1]
    vmem = pl.BlockSpec(memory_space=pltpu.VMEM)
    return pl.pallas_call(
        combine_kernel,
        out_shape=jax.ShapeDtypeStruct((2, 2 * channels, 2 * channels), BF16),
        in_specs=[vmem],
        out_specs=vmem,
        compiler_params=pltpu.CompilerParams(vmem_limit_bytes=8 * 1024 * 1024),
        name="combine_weights",
    )(weight.T)


def first_kernel(
    wide,
    sizes,
    place,
    near,
    own,
    far,
    gains,
    weight_one,
    weight_two,
    later_one,
    later_two,
    out_ref,
    w1,
    w2,
    acc,
    x1e,
    x1o,
    x2e,
    x2o,
    sems,
):
    channels = own.shape[-1]
    frames = own.shape[1] - 4
    height, width = sizes
    col, row = place[1], place[3]
    units = frames + 2
    del later_one, later_two

    def load(source, target, base):
        return [
            pltpu.make_async_copy(
                source.at[:, dx], target.at[:, :, pl.ds(dx * channels, channels)], sems.at[base + dx]
            )
            for dx in range(3)
        ]

    copies_one = load(weight_one, w1, 0)
    copies_two = load(weight_two, w2, 3)
    for copy in copies_one + copies_two:
        copy.start()

    slots = [lax.rem(y + col, 2) for y in range(2)]

    is_even = lax.rem(row, 2) == 0

    def own_rows(index):
        return [own[slot, index].astype(F32) for slot in slots]

    def above(line):
        return jnp.where(is_even, far[line].astype(F32), near[line].astype(F32))

    def below(line):
        return jnp.where(is_even, near[line].astype(F32), far[line].astype(F32))

    def rows_of(index):
        first = [above(slot * units + index) for slot in slots]
        last = [below(slot * units + index) for slot in slots]
        return jnp.concatenate(first + own_rows(index) + last, axis=0)

    for f in range(2):
        store(x1e, x1o, f, rows_of(frames + f), 6, wide)
        first, last = above(2 * units + f), below(2 * units + f)
        values = jnp.concatenate([first] + own_rows(units + f) + [last], axis=0)
        store(x2e, x2o, f, values, 4, wide)

    def norm_one(f, carry):
        values = activate(rows_of(f), gains[0:1, :], 1.0)
        store(x1e, x1o, f + 2, values, 6, wide)
        return carry

    lax.fori_loop(0, frames, norm_one, 0)
    low_product(acc, x1e, x1o, frames, 6, wide, w1, copies_one)

    mask = line_mask(place, wide, 2 * row - 1, 4, height, width)

    def norm_two(f, carry):
        size = 4 * wide
        values = activate(low_sum(acc, aligned(f, size), size), gains[1:2, :], mask)
        store(x2e, x2o, f + 2, values, 4, wide)
        return carry

    lax.fori_loop(0, frames, norm_two, 0)
    low_product(acc, x2e, x2o, frames, 4, wide, w2, copies_two)

    def residual(f, carry):
        size = 2 * wide
        values = low_sum(acc, aligned(f, size), size) + jnp.concatenate(own_rows(f), axis=0)
        out_ref[f] = values.astype(BF16)
        return carry

    lax.fori_loop(0, frames, residual, 0)


def planes(slots, height, wide, channels):
    return [
        pltpu.VMEM((slots * height * wide, channels), BF16),
        pltpu.VMEM((slots * (height - 2) * wide, channels), BF16),
    ]


def first_block(place, pieces, gains, weight_one, weight_two, later, sizes):
    _, units, wide, channels = pieces[1].shape
    frames = units - 4
    slots = -(-3 * channels // LANES)
    vmem = pl.BlockSpec(memory_space=pltpu.VMEM)
    anywhere = pl.BlockSpec(memory_space=pl.ANY)
    return pl.pallas_call(
        functools.partial(first_kernel, wide, sizes),
        out_shape=jax.ShapeDtypeStruct((frames, 2 * wide, channels), BF16),
        in_specs=[pl.BlockSpec(memory_space=pltpu.SMEM)]
        + [vmem] * 4
        + [pl.BlockSpec(memory_space=pltpu.HBM)] * 2
        + [anywhere] * 2,
        out_specs=vmem,
        scratch_shapes=[
            pltpu.VMEM((9, channels, slots * LANES), BF16),
            pltpu.VMEM((9, channels, slots * LANES), BF16),
            pltpu.VMEM((slots, frames * 4 * wide, LANES), F32),
            *planes(frames + 2, 6, wide, channels),
            *planes(frames + 2, 4, wide, channels),
            pltpu.SemaphoreType.DMA((6,)),
        ],
        compiler_params=pltpu.CompilerParams(vmem_limit_bytes=44 * 1024 * 1024),
        cost_estimate=pl.CostEstimate(
            flops=2 * 27 * channels * channels * frames * 6 * wide,
            bytes_accessed=2 * 54 * channels * channels,
            transcendentals=0,
        ),
        name="first_block",
    )(place, *pieces, gains, weight_one, weight_two, *later)


def second_kernel(
    wide,
    sizes,
    place,
    near,
    blocked,
    far,
    tile_near,
    windows,
    tile_far,
    gains,
    wt,
    wu,
    w3,
    w4,
    out_ref,
    acc,
    mixed,
    de,
    do,
    x3e,
    x3o,
    x4e,
    x4o,
    lifted_ref,
):
    channels = blocked.shape[-1]
    half = channels // 2
    size = 6 * wide
    frames = blocked.shape[0]
    count = 2 * frames
    height, width = sizes
    row = place[3]

    is_even = lax.rem(row, 2) == 0

    def chosen(when, one, other, index):
        return jnp.where(when, one[index].astype(F32), other[index].astype(F32))

    def cached(start, base, lines, depth, f):
        slots = [start + depth * f + i for i in range(depth)]
        parts = [chosen(is_even, tile_far, tile_near, slot) for slot in slots]
        parts += [windows[base + lines * f + i].astype(F32) for i in range(lines)]
        parts += [chosen(is_even, tile_near, tile_far, slot) for slot in slots]
        return jnp.concatenate(parts, axis=0)

    for f in range(2):
        mixed[f * size : (f + 1) * size, :] = cached(0, 0, 2, 2, f).astype(BF16)
    for f in range(frames):
        first, last = chosen(is_even, far, near, f), chosen(is_even, near, far, f)
        for i, values in enumerate((first.astype(BF16), blocked[f], last.astype(BF16))):
            begin = (f + 2) * size + i * 2 * wide
            mixed[begin : begin + 2 * wide, :] = values


    def mix(n, carry):
        lanes = pl.ds(pl.multiple_of(n * LANES, LANES), LANES)
        left = jnp.concatenate(
            [mixed[pl.ds(t * size, frames * size), :] for t in range(3)], axis=1
        )
        acc[n, 0 : frames * size, :] = jnp.dot(left, wt[:, lanes], preferred_element_type=F32)
        return carry

    lax.fori_loop(0, 2 * channels // LANES, mix, 0)
    mask_low = line_mask(place, wide, 2 * row - 2, 6, height, width)

    def double(t, carry):
        rows = pl.ds(aligned(t, size), size)
        first = jnp.concatenate([acc[0, rows, :], acc[1, rows, 0:128]], axis=1)
        second = jnp.concatenate([acc[1, rows, 128:256], acc[2, rows, :]], axis=1)
        store(de, do, 2 * t, first * mask_low, 6, wide)
        store(de, do, 2 * t + 1, second * mask_low, 6, wide)
        return carry

    lax.fori_loop(0, frames, double, 0)


    for py in range(2):

        def enlarge(n, carry):
            lanes = pl.ds(pl.multiple_of(n * LANES, LANES), LANES)
            left = jnp.concatenate(
                [taps(de, do, 0, count, 6, wide, 0, py), taps(de, do, 0, count, 6, wide, 0, py + 1)],
                axis=1,
            )
            acc[n, py * count * 4 * wide : (py + 1) * count * 4 * wide, :] = transposed_dot(
                left, wu[py, lanes, :]
            )
            return carry

        lax.fori_loop(0, 2 * channels // LANES, enlarge, 0)

    for f in range(2):
        store(x3e, x3o, f, cached(4, 4, 4, 2, f), 8, wide)
        store(x4e, x4o, f, cached(8, 12, 4, 1, f), 6, wide)
    gain3, gain4 = gains[2:3, :], gains[3:4, :]
    mask_three = line_mask(place, wide, 4 * row - 2, 8, 2 * height, width)
    part = 4 * wide

    def norm_three(f, carry):
        values = []
        for py in range(2):
            start = pl.multiple_of(py * count * part + f * part, 16)
            values.append(high_sum(acc, start, part).astype(BF16).astype(F32))
        lifted = jnp.concatenate(
            [values[h % 2][(h // 2) * wide : (h // 2 + 1) * wide] for h in range(8)], axis=0
        )
        lifted_ref[pl.ds(aligned(f, part), part), :] = lifted[2 * wide : 6 * wide]
        store(x3e, x3o, f + 2, activate_pairs(lifted, gain3, mask_three), 8, wide)
        return carry

    lax.fori_loop(0, count, norm_three, 0)
    high_product(acc, x3e, x3o, count, 8, wide, w3)

    mask_four = mask_three[wide : 7 * wide]

    def norm_four(f, carry):
        values = high_sum(acc, aligned(f, size), size)
        store(x4e, x4o, f + 2, activate_pairs(values, gain4, mask_four), 6, wide)
        return carry

    lax.fori_loop(0, count, norm_four, 0)
    high_product(acc, x4e, x4o, count, 6, wide, w4)

    def finish(f, carry):
        start = aligned(f, part)
        values = high_sum(acc, start, part) + lifted_ref[pl.ds(start, part), :]
        values = pltpu.roll(values, part - HALO, 0)
        for y in range(4):
            inner = wide - 2 * HALO
            out_ref[f, y] = values[y * wide : y * wide + inner].astype(BF16)
        return carry

    lax.fori_loop(0, count, finish, 0)


def second_block(place, pieces, tiles, gains, weights, sizes, wide):
    frames, _, channels = pieces[0].shape
    count = 2 * frames
    vmem = pl.BlockSpec(memory_space=pltpu.VMEM)
    return pl.pallas_call(
        functools.partial(second_kernel, wide, sizes),
        out_shape=jax.ShapeDtypeStruct((count, 4, wide - 2 * HALO, channels), BF16),
        in_specs=[pl.BlockSpec(memory_space=pltpu.SMEM)]
        + [vmem] * 11,
        out_specs=vmem,
        scratch_shapes=[
            pltpu.VMEM((3, 2 * count * 4 * wide, LANES), F32),
            pltpu.VMEM(((frames + 2) * 6 * wide, channels), BF16),
            *planes(count, 6, wide, channels),
            *planes(count + 2, 8, wide, channels),
            *planes(count + 2, 6, wide, channels),
            pltpu.VMEM((count * 4 * wide, channels), F32),
        ],
        compiler_params=pltpu.CompilerParams(vmem_limit_bytes=34 * 1024 * 1024),
        name="second_block",
    )(place, *pieces, *tiles, gains, *weights)


def body(
    latent,
    cache_one,
    cache_two,
    cache_time,
    cache_three,
    cache_four,
    gain_one,
    gain_two,
    gain_three,
    gain_four,
    weight_one,
    weight_two,
    weight_time,
    weight_upsample,
    weight_three,
    weight_four,
):
    section, row, col = (lax.axis_index(name) for name in ("section", "rows", "cols"))
    sections, row_count, col_count = (lax.axis_size(name) for name in ("section", "rows", "cols"))
    width, channels = latent.shape[2:]
    tile = width // col_count
    part = tile // sections
    wide = part + 2 * HALO
    half = weight_three.shape[1]
    sizes = (2 * row_count, width)
    place = jnp.stack([section, col, col * tile + section * part - HALO, row]).astype(jnp.int32)

    gains = jnp.stack([gain_one, gain_two, jnp.tile(gain_three, 2), jnp.tile(gain_four, 2)])

    latent = latent.reshape(latent.shape[0], width, channels)
    arrived = swapped(latent, "section")
    mine, theirs, tiles = pack(
        place,
        latent,
        arrived,
        cache_one[:, 0],
        cache_two[:, 0],
        cache_time,
        cache_three,
        cache_four,
        wide,
        tile,
        part,
    )
    weight_three, mine = lax.optimization_barrier((weight_three, mine))
    weight_three = align_weights(weight_three)
    own, near, far, windows, tile_near, tile_far = stack(
        place, mine, swapped(theirs, "cols"), tiles, weight_three
    )
    pieces = [paired(near, "rows", 0), own, paired(far, "rows", 1)]
    weight_upsample, weight_four, _ = lax.optimization_barrier((weight_upsample, weight_four, own))
    weight_upsample = combine_weights(weight_upsample)
    weight_four = align_weights(weight_four)
    tile_near, tile_far, *_ = lax.optimization_barrier((tile_near, tile_far, *pieces))
    tiles = [paired(tile_near, "rows", 0), windows, paired(tile_far, "rows", 1)]
    blocked = first_block(
        place,
        pieces,
        gains,
        weight_one.reshape(9, 3, channels, channels),
        weight_two.reshape(9, 3, channels, channels),
        (weight_upsample, weight_four),
        sizes,
    )
    blocks = [paired(blocked, "rows", 0), blocked, paired(blocked, "rows", 1)]
    frames = second_block(
        place,
        blocks,
        tiles,
        gains,
        (weight_time, weight_upsample, weight_three, weight_four),
        sizes,
        wide,
    )
    count = frames.shape[0] // sections
    given = lax.dynamic_slice_in_dim(frames, (1 - section) * count, count, 0)
    kept = lax.dynamic_slice_in_dim(frames, section * count, count, 0)
    arrived = swapped(given, "section")
    low = section == 0
    joined = jnp.concatenate(
        [jnp.where(low, kept, arrived), jnp.where(low, arrived, kept)], axis=2
    )
    return joined.reshape(count, 4, 2 * tile, half)


def solution(mesh):
    placed = (
        P("section", ("rows", "cols"), None, None),
        P(None, ("rows", "cols"), None, None),
        P(None, ("rows", "cols"), None, None),
        P(None, "rows", "cols", None),
        P(None, "rows", "cols", None),
        P(None, "rows", "cols", None),
    ) + (P(),) * 10
    return jax.shard_map(
        body,
        mesh=mesh,
        in_specs=placed,
        out_specs=P("section", "rows", "cols", None),
        check_vma=False,
    )
```

```python
import functools

import jax
import jax.numpy as jnp
from jax import lax
from jax.experimental import pallas as pl
from jax.experimental.pallas import tpu as pltpu
from jax.sharding import PartitionSpec as P

EPSILON = 1e-06
HALO = 4
LANES = 256
BF16 = jnp.bfloat16
F32 = jnp.float32


def swapped(value, axis):
    return lax.ppermute(value, axis, [(0, 1), (1, 0)])


def paired(value, axis, first):
    pairs = [(i, i + 1) for i in range(first, lax.axis_size(axis) - 1, 2)]
    return lax.ppermute(value, axis, pairs + [(high, low) for low, high in pairs])


def silu(scaled):
    half = scaled * 0.5
    return half * (1.0 + jnp.tanh(half))


def activate(values, gain, mask):
    mean = jnp.mean(values * values, axis=-1, keepdims=True)
    return silu(values * (lax.rsqrt(mean + EPSILON) * mask) * gain)


def activate_pairs(values, gain, mask):
    channels = values.shape[-1] // 2
    squares = values * values
    first = lax.broadcasted_iota(jnp.int32, (1, 2 * channels), 1) < channels
    total = jnp.sum(squares, axis=-1, keepdims=True)
    low = jnp.sum(jnp.where(first, squares, 0.0), axis=-1, keepdims=True)
    scale_low = lax.rsqrt(low / channels + EPSILON) * mask
    scale_high = lax.rsqrt((total - low) / channels + EPSILON) * mask
    return silu(values * jnp.where(first, scale_low, scale_high) * gain)


def merge(even, odd, channels):
    turned = pltpu.roll(odd, channels - 128, 1)
    first = lax.broadcasted_iota(jnp.int32, (1, 128), 1) < channels - 128
    middle = jnp.where(first, even[:, 128:], turned[:, :128])
    return jnp.concatenate([even[:, :128], middle, turned[:, 128:]], axis=1)


def aligned(index, size):
    return pl.multiple_of(index * size, 16)


def line_mask(place, wide, first, count, limit, width):
    columns = place[2] + lax.broadcasted_iota(jnp.int32, (wide, 1), 0)
    inside = jnp.where((columns >= 0) & (columns < width), 1.0, 0.0)
    lines = []
    for i in range(count):
        line = first + i
        lines.append(inside * jnp.where((line >= 0) & (line < limit), 1.0, 0.0))
    return jnp.concatenate(lines, axis=0)


def store(even, odd, slot, values, height, wide):
    even[pl.ds(slot * (height * wide), height * wide), :] = values.astype(BF16)
    odd[pl.ds(slot * ((height - 2) * wide), (height - 2) * wide), :] = values[
        wide : (height - 1) * wide
    ].astype(BF16)


def taps(even, odd, begin, count, height, wide, dt, dy, lanes=slice(None)):
    inner = (height - 2) * wide
    if dy == 1:
        parts = [odd[pl.ds((begin + f + dt) * inner, inner), lanes] for f in range(count)]
    else:
        parts = [
            even[pl.ds((begin + f + dt) * height * wide + dy * wide, inner), lanes]
            for f in range(count)
        ]
    return jnp.concatenate(parts, axis=0)


def low_product(acc, even, odd, count, height, wide, weights, copies):
    rows = count * (height - 2) * wide
    channels = weights.shape[1]
    needed = [dx * channels // LANES for dx in range(3)]

    def column(n, carry):
        for copy, when in zip(copies, needed):
            pl.when(n == when)(copy.wait)
        lanes = pl.ds(pl.multiple_of(n * LANES, LANES), LANES)
        total = None
        for first, last in ((0, 4), (4, 8), (8, 9)):
            left = jnp.concatenate(
                [
                    taps(even, odd, 0, count, height, wide, t // 3, t % 3)
                    for t in range(first, last)
                ],
                axis=1,
            )
            right = weights[first:last, :, lanes].reshape((last - first) * channels, LANES)
            part = jnp.dot(left, right, preferred_element_type=F32)
            total = part if total is None else total + part
        acc[n, 0:rows, :] = total
        return carry

    lax.fori_loop(0, weights.shape[-1] // LANES, column, 0)


def low_sum(acc, start, size):
    rows = pl.ds(start, size)
    before = jnp.concatenate([acc[0, rows, :], acc[1, rows, 0:128]], axis=1)
    center = jnp.concatenate([acc[1, rows, 128:256], acc[2, rows, :]], axis=1)
    after = jnp.concatenate([acc[3, rows, :], acc[4, rows, 0:128]], axis=1)
    return center + pltpu.roll(before, 1, 0) + pltpu.roll(after, size - 1, 0)


def transposed_dot(left, right):
    return lax.dot_general(left, right, (((1,), (1,)), ((), ())), preferred_element_type=F32)


def split_frames(count):
    first = count // 4
    second = first + (count - first) // 2
    return (0, first), (first, second), (second, count)


def group_slots(group, groups):
    first, last = groups[group]
    return (0 if group == 0 else first + 2), last + 2


def grouped_taps(planes, groups, frames, height, wide, dt, dy):
    inner = (height - 2) * wide
    parts = []
    for f in frames:
        for group, (even, odd) in enumerate(planes):
            first, last = group_slots(group, groups)
            if first <= f + dt < last:
                slot = f + dt - first
                if dy == 1:
                    parts.append(odd[slot * inner : (slot + 1) * inner, :])
                else:
                    begin = slot * height * wide + dy * wide
                    parts.append(even[begin : begin + inner, :])
    return jnp.concatenate(parts, axis=0)


def high_column(n, acc, planes, groups, group, height, wide, weights):
    channels = weights.shape[1] // 9
    outputs = pl.ds(pl.multiple_of(n * LANES, LANES), LANES)
    total = None
    for first, last in ((0, 4), (4, 8), (8, 9)):
        left = jnp.concatenate(
            [
                grouped_taps(planes, groups, range(*groups[group]), height, wide, t // 3, t % 3)
                for t in range(first, last)
            ],
            axis=1,
        )
        part = transposed_dot(left, weights[outputs, first * channels : last * channels])
        total = part if total is None else total + part
    acc[n] = total


def high_sum(acc, start, size):
    rows = pl.ds(start, size)
    center = jnp.concatenate([acc[0, rows, :], acc[1, rows, 0:128]], axis=1)
    side = jnp.concatenate([acc[1, rows, 128:256], acc[2, rows, :]], axis=1)
    channels = center.shape[1]
    first = lax.broadcasted_iota(jnp.int32, (1, channels), 1) < channels // 2
    return center + jnp.where(first, pltpu.roll(side, 1, 0), pltpu.roll(side, size - 1, 0))


def pack_kernel(
    wide,
    tile,
    part,
    place,
    latent,
    arrived,
    one,
    two,
    time,
    three,
    four,
    mine,
    theirs,
    tiles,
    spread,
    low,
    high,
):
    section, col = place[0], place[1]
    width, channels = latent.shape[1:]
    half = three.shape[-1]
    empty = jnp.zeros((spread.shape[1] - width, channels), F32)

    def put(slot, values):
        spread[slot] = pltpu.roll(
            jnp.concatenate([values.astype(F32), empty], axis=0), HALO, 0
        )

    for i in range(2):
        put(2 * section + i, latent[i])
        put(2 * (1 - section) + i, arrived[i])
        put(4 + i, one[i])
        put(6 + i, two[i])
    for slot in range(8):
        for ref, which in ((mine, col), (theirs, 1 - col)):
            begin = pl.multiple_of(which * tile + section * part, 8)
            ref[slot] = spread[slot, pl.ds(begin, wide), :].astype(BF16)

    lines = [time[f, y].astype(F32) for f in range(2) for y in range(2)]
    for ref in (three, four):
        for f in range(2):
            for y in range(4):
                values = ref[f, y].astype(F32)
                low[...] = values[:, :128]
                high[:, 0 : half - 128] = values[:, 128:]
                count = values.shape[0] // 2
                even, odd = (
                    jnp.concatenate(
                        [lanes[pl.ds(o, count, stride=2), :] for lanes in (low, high)], axis=1
                    )
                    for o in range(2)
                )
                lines.append(merge(even, odd, half))
    for i, line in enumerate(lines):
        tiles[i] = line.astype(BF16)

    left = col == 0
    upper = lax.broadcasted_iota(jnp.int32, (8, 1), 0) < HALO
    blocks = []
    for i in range(0, len(lines), 2):
        one_line, two_line = lines[i], lines[i + 1]
        last = jnp.where(upper, pltpu.roll(one_line[-8:], HALO, 0), two_line[-8:])
        first = jnp.where(upper, one_line[:8], pltpu.roll(two_line[:8], HALO, 0))
        blocks.append(jnp.where(left, last, first))
    gap = jnp.zeros_like(blocks[0])
    count = wide // 8
    for i in range(theirs.shape[0] - 8):
        group = (blocks + [gap] * count)[i * count : (i + 1) * count]
        theirs[8 + i] = jnp.concatenate(group, axis=0).astype(BF16)


def pack(place, latent, arrived, one, two, time, three, four, wide, tile, part):
    width, channels = latent.shape[1:]
    vmem = pl.BlockSpec(memory_space=pltpu.VMEM)
    lines = 20
    extra = -(-lines * HALO // wide)
    return pl.pallas_call(
        functools.partial(pack_kernel, wide, tile, part),
        out_shape=[
            jax.ShapeDtypeStruct((8, wide, channels), BF16),
            jax.ShapeDtypeStruct((8 + extra, wide, channels), BF16),
            jax.ShapeDtypeStruct((lines, tile, channels), BF16),
        ],
        in_specs=[pl.BlockSpec(memory_space=pltpu.SMEM)] + [vmem] * 7,
        out_specs=[vmem] * 3,
        scratch_shapes=[
            pltpu.VMEM((8, width + 16, channels), F32),
            pltpu.VMEM((three.shape[2], 128), F32),
            pltpu.VMEM((three.shape[2], 128), F32),
        ],
        compiler_params=pltpu.CompilerParams(vmem_limit_bytes=60 * 1024 * 1024),
        name="pack",
    )(place, latent, arrived, one, two, time, three, four)


def stack_kernel(
    wide, place, mine, theirs, tiles, later, own, near, far, windows, tile_near, tile_far
):
    del later
    section, col = place[0], place[1]
    count = mine.shape[0] - 2
    own[0], own[1] = mine[...], theirs[0 : count + 2]
    parity = lax.rem(place[3], 2)
    for ref, y in ((near, 1 - parity), (far, parity)):
        ref[0:count], ref[count : 2 * count] = mine[0:count], theirs[0:count]
        here = lax.rem(y + col, 2) == 0
        ref[2 * count :] = jnp.where(here, mine[count:], theirs[count : count + 2])

    part = wide - 2 * HALO
    upper = lax.broadcasted_iota(jnp.int32, (8, 1), 0) < HALO
    groups = wide // 8
    for i in range(tiles.shape[0]):
        line = tiles[i].astype(F32)
        block = i // 2
        begin = block % groups * 8
        edge = theirs[count + 2 + block // groups].astype(F32)[begin : begin + 8]
        turned = pltpu.roll(edge, HALO, 0)
        before, after = (edge, turned) if i % 2 == 0 else (turned, edge)
        first = pltpu.roll(line, HALO, 0)[:wide]
        head = jnp.where(upper, jnp.where(col == 1, before, 0.0), first[:8])
        first = jnp.concatenate([head, first[8:]], axis=0)
        last = pltpu.roll(line, line.shape[0] - (part - HALO), 0)[:wide]
        tail = jnp.where(upper, last[-8:], jnp.where(col == 0, after, 0.0))
        last = jnp.concatenate([last[:-8], tail], axis=0)
        line = jnp.where(section == 0, first, last).astype(BF16)
        windows[i] = line
    is_even = parity == 0
    for base, start, count, depth in ((0, 0, 2, 2), (4, 4, 4, 2), (12, 8, 4, 1)):
        for f in range(2):
            for j in range(depth):
                slot = start + depth * f + j
                high = windows[base + count * f + j]
                low = windows[base + count * f + count - depth + j]
                tile_near[slot] = jnp.where(is_even, low, high)
                tile_far[slot] = jnp.where(is_even, high, low)


def stack(place, mine, theirs, tiles, later):
    units, wide, channels = mine.shape
    vmem = pl.BlockSpec(memory_space=pltpu.VMEM)
    lines = 2 * units - 2
    shapes = [(2, units), (lines,), (lines,), (tiles.shape[0],), (10,), (10,)]
    return pl.pallas_call(
        functools.partial(stack_kernel, wide),
        out_shape=[jax.ShapeDtypeStruct(shape + (wide, channels), BF16) for shape in shapes],
        in_specs=[pl.BlockSpec(memory_space=pltpu.SMEM)]
        + [vmem] * 3
        + [pl.BlockSpec(memory_space=pl.ANY)],
        out_specs=[vmem] * 6,
        compiler_params=pltpu.CompilerParams(vmem_limit_bytes=8 * 1024 * 1024),
        name="stack",
    )(place, mine, theirs, tiles, later)


def align_kernel(weight, out):
    half = weight.shape[0]
    chunk = 16
    tail = half - 128
    low = lax.broadcasted_iota(jnp.int32, (1, 128), 1) < tail

    def move(k, carry):
        here = aligned(k, chunk)
        none = jnp.zeros((chunk, 128), F32)
        for t in range(9):
            base = 3 * t * half
            first = base // 128 * 128
            last = min(first + 640, weight.shape[1])
            values = weight[pl.ds(here, chunk), first:last].astype(F32)
            if last < first + 640:
                values = jnp.concatenate(
                    [values[:, :512], jnp.concatenate([values[:, 512:], none[:, tail:]], axis=1)],
                    axis=1,
                )
            turned = pltpu.roll(values, 640 - tail, 1)
            tiles = [values[:, 128 * i : 128 * (i + 1)] for i in range(5)]
            moved = [turned[:, 128 * i : 128 * (i + 1)] for i in range(5)]
            if base == first:
                blocks = (
                    moved[1:4],
                    tiles[0:3],
                    [none, jnp.where(low, 0.0, moved[4]), moved[0]],
                    [tiles[3], jnp.where(low, tiles[4], 0.0), none],
                )
            else:
                blocks = (
                    tiles[2:5],
                    moved[0:3],
                    [none, jnp.where(low, 0.0, tiles[0]), tiles[1]],
                    [moved[3], jnp.where(low, moved[4], 0.0), none],
                )
            for n, block in enumerate(blocks):
                into = pl.ds(here + n * half, chunk)
                out[into, 2 * half * t : 2 * half * (t + 1)] = jnp.concatenate(
                    block, axis=1
                ).astype(BF16)
        return carry

    lax.fori_loop(0, half // chunk, move, 0)


def align_weights(weight):
    half = weight.shape[1]
    vmem = pl.BlockSpec(memory_space=pltpu.VMEM)
    return pl.pallas_call(
        align_kernel,
        out_shape=jax.ShapeDtypeStruct((4 * half, 18 * half), BF16),
        in_specs=[vmem],
        out_specs=vmem,
        compiler_params=pltpu.CompilerParams(vmem_limit_bytes=8 * 1024 * 1024),
        name="align_weights",
    )(weight.T)


def combine_kernel(weight, out):
    half = weight.shape[0]
    channels = weight.shape[1] // 9
    chunk = 16

    def combine(k, carry):
        rows = pl.ds(aligned(k, chunk), chunk)
        taken = [
            [
                weight[rows, (3 * dy + dx) * channels : (3 * dy + dx + 1) * channels].astype(F32)
                for dx in range(3)
            ]
            for dy in range(3)
        ]
        for slot, dys in enumerate(((0,), (1, 2), (0, 1), (2,))):
            line = [sum(taken[dy][dx] for dy in dys) for dx in range(3)]
            lanes = slice(slot % 2 * channels, (slot % 2 + 1) * channels)
            for n, block in enumerate((line[1] + line[2], line[0] + line[1], line[0], line[2])):
                into = pl.ds(aligned(k, chunk) + n * half, chunk)
                out[slot // 2, into, lanes] = block.astype(BF16)
        return carry

    lax.fori_loop(0, half // chunk, combine, 0)


def combine_weights(weight):
    channels = 2 * weight.shape[1]
    vmem = pl.BlockSpec(memory_space=pltpu.VMEM)
    return pl.pallas_call(
        combine_kernel,
        out_shape=jax.ShapeDtypeStruct((2, 2 * channels, 2 * channels), BF16),
        in_specs=[vmem],
        out_specs=vmem,
        compiler_params=pltpu.CompilerParams(vmem_limit_bytes=8 * 1024 * 1024),
        name="combine_weights",
    )(weight.T)


def first_kernel(
    wide,
    sizes,
    place,
    near,
    own,
    far,
    gains,
    weight_one,
    weight_two,
    later,
    out_ref,
    w1,
    w2,
    acc,
    x1e,
    x1o,
    x2e,
    x2o,
    sems,
):
    channels = own.shape[-1]
    frames = own.shape[1] - 4
    height, width = sizes
    col, row = place[1], place[3]
    units = frames + 2
    del later

    def load(source, target, base):
        return [
            pltpu.make_async_copy(
                source.at[:, dx], target.at[:, :, pl.ds(dx * channels, channels)], sems.at[base + dx]
            )
            for dx in range(3)
        ]

    copies_one = load(weight_one, w1, 0)
    copies_two = load(weight_two, w2, 3)
    for copy in copies_one + copies_two:
        copy.start()

    slots = [lax.rem(y + col, 2) for y in range(2)]

    is_even = lax.rem(row, 2) == 0

    def own_rows(index):
        return [own[slot, index].astype(F32) for slot in slots]

    def above(line):
        return jnp.where(is_even, far[line].astype(F32), near[line].astype(F32))

    def below(line):
        return jnp.where(is_even, near[line].astype(F32), far[line].astype(F32))

    def rows_of(index):
        first = [above(slot * units + index) for slot in slots]
        last = [below(slot * units + index) for slot in slots]
        return jnp.concatenate(first + own_rows(index) + last, axis=0)

    for f in range(2):
        store(x1e, x1o, f, rows_of(frames + f), 6, wide)
        first, last = above(2 * units + f), below(2 * units + f)
        values = jnp.concatenate([first] + own_rows(units + f) + [last], axis=0)
        store(x2e, x2o, f, values, 4, wide)

    def norm_one(f, carry):
        values = activate(rows_of(f), gains[0:1, :], 1.0)
        store(x1e, x1o, f + 2, values, 6, wide)
        return carry

    lax.fori_loop(0, frames, norm_one, 0)
    low_product(acc, x1e, x1o, frames, 6, wide, w1, copies_one)

    mask = line_mask(place, wide, 2 * row - 1, 4, height, width)

    def norm_two(f, carry):
        size = 4 * wide
        values = activate(low_sum(acc, aligned(f, size), size), gains[1:2, :], mask)
        store(x2e, x2o, f + 2, values, 4, wide)
        return carry

    lax.fori_loop(0, frames, norm_two, 0)
    low_product(acc, x2e, x2o, frames, 4, wide, w2, copies_two)

    def residual(f, carry):
        size = 2 * wide
        values = low_sum(acc, aligned(f, size), size) + jnp.concatenate(own_rows(f), axis=0)
        out_ref[f] = values.astype(BF16)
        return carry

    lax.fori_loop(0, frames, residual, 0)


def planes(slots, height, wide, channels):
    return [
        pltpu.VMEM((slots * height * wide, channels), BF16),
        pltpu.VMEM((slots * (height - 2) * wide, channels), BF16),
    ]


def first_block(place, pieces, gains, weight_one, weight_two, later, sizes):
    _, units, wide, channels = pieces[1].shape
    frames = units - 4
    slots = -(-3 * channels // LANES)
    vmem = pl.BlockSpec(memory_space=pltpu.VMEM)
    anywhere = pl.BlockSpec(memory_space=pl.ANY)
    return pl.pallas_call(
        functools.partial(first_kernel, wide, sizes),
        out_shape=jax.ShapeDtypeStruct((frames, 2 * wide, channels), BF16),
        in_specs=[pl.BlockSpec(memory_space=pltpu.SMEM)]
        + [vmem] * 4
        + [pl.BlockSpec(memory_space=pltpu.HBM)] * 2
        + [anywhere],
        out_specs=vmem,
        scratch_shapes=[
            pltpu.VMEM((9, channels, slots * LANES), BF16),
            pltpu.VMEM((9, channels, slots * LANES), BF16),
            pltpu.VMEM((slots, frames * 4 * wide, LANES), F32),
            *planes(frames + 2, 6, wide, channels),
            *planes(frames + 2, 4, wide, channels),
            pltpu.SemaphoreType.DMA((6,)),
        ],
        compiler_params=pltpu.CompilerParams(vmem_limit_bytes=50 * 1024 * 1024),
        cost_estimate=pl.CostEstimate(
            flops=2 * 27 * channels * channels * frames * 6 * wide,
            bytes_accessed=2 * 54 * channels * channels,
            transcendentals=0,
        ),
        name="first_block",
    )(place, *pieces, gains, weight_one, weight_two, later)


def second_kernel(
    wide,
    sizes,
    place,
    near,
    blocked,
    far,
    tile_near,
    windows,
    tile_far,
    gains,
    wt,
    wu,
    w3,
    w4,
    out_ref,
    acc,
    mixed,
    de,
    do,
    lifted_ref,
    *buffers,
):
    ups, threes, fours = buffers[0:3], buffers[3:6], buffers[6:9]
    planes_three = [buffers[9 + 2 * g : 11 + 2 * g] for g in range(3)]
    planes_four = [buffers[15 + 2 * g : 17 + 2 * g] for g in range(3)]
    channels = blocked.shape[-1]
    half = channels // 2
    size = 6 * wide
    frames = blocked.shape[0]
    count = 2 * frames
    groups = split_frames(count)
    height, width = sizes
    row = place[3]

    is_even = lax.rem(row, 2) == 0

    def chosen(when, one, other, index):
        return jnp.where(when, one[index].astype(F32), other[index].astype(F32))

    def cached(start, base, lines, depth, f):
        slots = [start + depth * f + i for i in range(depth)]
        parts = [chosen(is_even, tile_far, tile_near, slot) for slot in slots]
        parts += [windows[base + lines * f + i].astype(F32) for i in range(lines)]
        parts += [chosen(is_even, tile_near, tile_far, slot) for slot in slots]
        return jnp.concatenate(parts, axis=0)

    for f in range(2):
        mixed[f * size : (f + 1) * size, :] = cached(0, 0, 2, 2, f).astype(BF16)
    for f in range(frames):
        first, last = chosen(is_even, far, near, f), chosen(is_even, near, far, f)
        for i, values in enumerate((first.astype(BF16), blocked[f], last.astype(BF16))):
            begin = (f + 2) * size + i * 2 * wide
            mixed[begin : begin + 2 * wide, :] = values


    def mix(n, carry):
        lanes = pl.ds(pl.multiple_of(n * LANES, LANES), LANES)
        left = jnp.concatenate(
            [mixed[pl.ds(t * size, frames * size), :] for t in range(3)], axis=1
        )
        acc[n, 0 : frames * size, :] = jnp.dot(left, wt[:, lanes], preferred_element_type=F32)
        return carry

    lax.fori_loop(0, 2 * channels // LANES, mix, 0)
    mask_low = line_mask(place, wide, 2 * row - 2, 6, height, width)

    def double(t, carry):
        rows = pl.ds(aligned(t, size), size)
        first = jnp.concatenate([acc[0, rows, :], acc[1, rows, 0:128]], axis=1)
        second = jnp.concatenate([acc[1, rows, 128:256], acc[2, rows, :]], axis=1)
        store(de, do, 2 * t, first * mask_low, 6, wide)
        store(de, do, 2 * t + 1, second * mask_low, 6, wide)
        return carry

    lax.fori_loop(0, frames, double, 0)


    for f in range(2):
        store(*planes_three[0], f, cached(4, 4, 4, 2, f), 8, wide)
        store(*planes_four[0], f, cached(8, 12, 4, 1, f), 6, wide)
    gain3, gain4 = gains[2:3, :], gains[3:4, :]
    mask_three = line_mask(place, wide, 4 * row - 2, 8, 2 * height, width)
    mask_four = mask_three[wide : 7 * wide]
    part = 4 * wide

    def enlarge(group, n):
        first, last = groups[group]
        lanes = pl.ds(pl.multiple_of(n * LANES, LANES), LANES)
        rows = (last - first) * part
        for py in range(2):
            left = jnp.concatenate(
                [
                    taps(de, do, first, last - first, 6, wide, 0, py),
                    taps(de, do, first, last - first, 6, wide, 0, py + 1),
                ],
                axis=1,
            )
            ups[group][n, py * rows : (py + 1) * rows, :] = transposed_dot(left, wu[py, lanes, :])

    def local(group, f):
        return jnp.minimum(f, groups[group][1] - groups[group][0] - 1)

    def norm_three(group, f):
        first, last = groups[group]
        f = local(group, f)
        values = [
            high_sum(ups[group], aligned(f + py * (last - first), part), part)
            .astype(BF16)
            .astype(F32)
            for py in range(2)
        ]
        lifted = jnp.concatenate(
            [values[h % 2][(h // 2) * wide : (h // 2 + 1) * wide] for h in range(8)], axis=0
        )
        lifted_ref[pl.ds(aligned(f + first, part), part), :] = lifted[2 * wide : 6 * wide]
        slot = f + (2 if group == 0 else 0)
        store(*planes_three[group], slot, activate_pairs(lifted, gain3, mask_three), 8, wide)

    def norm_four(group, f):
        f = local(group, f)
        values = high_sum(threes[group], aligned(f, size), size)
        slot = f + (2 if group == 0 else 0)
        store(*planes_four[group], slot, activate_pairs(values, gain4, mask_four), 6, wide)

    def finish(group, f):
        first = groups[group][0]
        f = local(group, f)
        rows = pl.ds(aligned(f + first, part), part)
        values = high_sum(fours[group], aligned(f, part), part) + lifted_ref[rows, :]
        values = pltpu.roll(values, part - HALO, 0)
        for y in range(4):
            inner = wide - 2 * HALO
            out_ref[f + first, y] = values[y * wide : y * wide + inner].astype(BF16)

    def third(group, n):
        high_column(n, threes[group], planes_three, groups, group, 8, wide, w3)

    def fourth(group, n):
        high_column(n, fours[group], planes_four, groups, group, 6, wide, w4)

    for product, vector in (
        ((enlarge, 0), None),
        ((enlarge, 1), (norm_three, 0)),
        ((enlarge, 2), (norm_three, 1)),
        ((third, 0), (norm_three, 2)),
        ((third, 1), (norm_four, 0)),
        ((third, 2), (norm_four, 1)),
        ((fourth, 0), (norm_four, 2)),
        ((fourth, 1), (finish, 0)),
        ((fourth, 2), (finish, 1)),
        (None, (finish, 2)),
    ):

        def step(n, carry, product=product, vector=vector):
            for work in (product, vector):
                if work is not None:
                    work[0](work[1], n)
            return carry

        steps = max(2 * channels // LANES, *(last - first for first, last in groups))
        lax.fori_loop(0, steps, step, 0)


def second_block(place, pieces, tiles, gains, weights, sizes, wide):
    frames, _, channels = pieces[0].shape
    count = 2 * frames
    groups = split_frames(count)
    sizes_of = [last - first for first, last in groups]
    slots = [last - first for first, last in (group_slots(g, groups) for g in range(3))]
    vmem = pl.BlockSpec(memory_space=pltpu.VMEM)
    return pl.pallas_call(
        functools.partial(second_kernel, wide, sizes),
        out_shape=jax.ShapeDtypeStruct((count, 4, wide - 2 * HALO, channels), BF16),
        in_specs=[pl.BlockSpec(memory_space=pltpu.SMEM)]
        + [vmem] * 11,
        out_specs=vmem,
        scratch_shapes=[
            pltpu.VMEM((3, frames * 6 * wide, LANES), F32),
            pltpu.VMEM(((frames + 2) * 6 * wide, channels), BF16),
            *planes(count, 6, wide, channels),
            pltpu.VMEM((count * 4 * wide, channels), F32),
            *(pltpu.VMEM((3, n * 8 * wide, LANES), F32) for n in sizes_of),
            *(pltpu.VMEM((3, n * 6 * wide, LANES), F32) for n in sizes_of),
            *(pltpu.VMEM((3, n * 4 * wide, LANES), F32) for n in sizes_of),
            *(ref for n in slots for ref in planes(n, 8, wide, channels)),
            *(ref for n in slots for ref in planes(n, 6, wide, channels)),
        ],
        compiler_params=pltpu.CompilerParams(vmem_limit_bytes=34 * 1024 * 1024),
        name="second_block",
    )(place, *pieces, *tiles, gains, *weights)


def body(
    latent,
    cache_one,
    cache_two,
    cache_time,
    cache_three,
    cache_four,
    gain_one,
    gain_two,
    gain_three,
    gain_four,
    weight_one,
    weight_two,
    weight_time,
    weight_upsample,
    weight_three,
    weight_four,
):
    section, row, col = (lax.axis_index(name) for name in ("section", "rows", "cols"))
    sections, row_count, col_count = (lax.axis_size(name) for name in ("section", "rows", "cols"))
    width, channels = latent.shape[2:]
    tile = width // col_count
    part = tile // sections
    wide = part + 2 * HALO
    half = weight_three.shape[1]
    sizes = (2 * row_count, width)
    place = jnp.stack([section, col, col * tile + section * part - HALO, row]).astype(jnp.int32)

    gains = jnp.stack([gain_one, gain_two, jnp.tile(gain_three, 2), jnp.tile(gain_four, 2)])

    latent = latent.reshape(latent.shape[0], width, channels)
    arrived = swapped(latent, "section")
    mine, theirs, tiles = pack(
        place,
        latent,
        arrived,
        cache_one[:, 0],
        cache_two[:, 0],
        cache_time,
        cache_three,
        cache_four,
        wide,
        tile,
        part,
    )
    weight_three, mine = lax.optimization_barrier((weight_three, mine))
    weight_three = align_weights(weight_three)
    own, near, far, windows, tile_near, tile_far = stack(
        place, mine, swapped(theirs, "cols"), tiles, weight_three
    )
    pieces = [paired(near, "rows", 0), own, paired(far, "rows", 1)]
    tiles = [paired(tile_near, "rows", 0), windows, paired(tile_far, "rows", 1)]
    weight_upsample, own = lax.optimization_barrier((weight_upsample, own))
    weight_upsample = combine_weights(weight_upsample)
    blocked = first_block(
        place,
        pieces,
        gains,
        weight_one.reshape(9, 3, channels, channels),
        weight_two.reshape(9, 3, channels, channels),
        weight_upsample,
        sizes,
    )
    blocks = [paired(blocked, "rows", 0), blocked, paired(blocked, "rows", 1)]
    weight_four, _ = lax.optimization_barrier((weight_four, blocked))
    weight_four = align_weights(weight_four)
    frames = second_block(
        place,
        blocks,
        tiles,
        gains,
        (weight_time, weight_upsample, weight_three, weight_four),
        sizes,
        wide,
    )
    count = frames.shape[0] // sections
    given = lax.dynamic_slice_in_dim(frames, (1 - section) * count, count, 0)
    kept = lax.dynamic_slice_in_dim(frames, section * count, count, 0)
    arrived = swapped(given, "section")
    low = section == 0
    joined = jnp.concatenate(
        [jnp.where(low, kept, arrived), jnp.where(low, arrived, kept)], axis=2
    )
    return joined.reshape(count, 4, 2 * tile, half)


def solution(mesh):
    placed = (
        P("section", ("rows", "cols"), None, None),
        P(None, ("rows", "cols"), None, None),
        P(None, ("rows", "cols"), None, None),
        P(None, "rows", "cols", None),
        P(None, "rows", "cols", None),
        P(None, "rows", "cols", None),
    ) + (P(),) * 10
    return jax.shard_map(
        body,
        mesh=mesh,
        in_specs=placed,
        out_specs=P("section", "rows", "cols", None),
        check_vma=False,
    )
```

```python
import functools

import jax
import jax.numpy as jnp
from jax import lax
from jax.experimental import pallas as pl
from jax.experimental.pallas import tpu as pltpu
from jax.sharding import PartitionSpec as P

EPSILON = 1e-06
HALO = 4
LANES = 256
BF16 = jnp.bfloat16
F32 = jnp.float32


def swapped(value, axis):
    return lax.ppermute(value, axis, [(0, 1), (1, 0)])


def paired(value, axis, first):
    pairs = [(i, i + 1) for i in range(first, lax.axis_size(axis) - 1, 2)]
    return lax.ppermute(value, axis, pairs + [(high, low) for low, high in pairs])


def silu(scaled):
    half = scaled * 0.5
    return half * (1.0 + jnp.tanh(half))


def activate(values, gain, mask):
    mean = jnp.mean(values * values, axis=-1, keepdims=True)
    return silu(values * (lax.rsqrt(mean + EPSILON) * mask) * gain)


def activate_pairs(values, gain, mask):
    channels = values.shape[-1] // 2
    squares = values * values
    first = lax.broadcasted_iota(jnp.int32, (1, 2 * channels), 1) < channels
    total = jnp.sum(squares, axis=-1, keepdims=True)
    low = jnp.sum(jnp.where(first, squares, 0.0), axis=-1, keepdims=True)
    scale_low = lax.rsqrt(low / channels + EPSILON) * mask
    scale_high = lax.rsqrt((total - low) / channels + EPSILON) * mask
    return silu(values * jnp.where(first, scale_low, scale_high) * gain)


def merge(even, odd, channels):
    turned = pltpu.roll(odd, channels - 128, 1)
    first = lax.broadcasted_iota(jnp.int32, (1, 128), 1) < channels - 128
    middle = jnp.where(first, even[:, 128:], turned[:, :128])
    return jnp.concatenate([even[:, :128], middle, turned[:, 128:]], axis=1)


def aligned(index, size):
    return index * size if isinstance(index, int) else pl.multiple_of(index * size, 16)


def line_mask(place, wide, first, count, limit, width):
    columns = place[2] + lax.broadcasted_iota(jnp.int32, (wide, 1), 0)
    inside = jnp.where((columns >= 0) & (columns < width), 1.0, 0.0)
    lines = []
    for i in range(count):
        line = first + i
        lines.append(inside * jnp.where((line >= 0) & (line < limit), 1.0, 0.0))
    return jnp.concatenate(lines, axis=0)


def store(even, odd, slot, values, height, wide):
    even[pl.ds(slot * (height * wide), height * wide), :] = values.astype(BF16)
    odd[pl.ds(slot * ((height - 2) * wide), (height - 2) * wide), :] = values[
        wide : (height - 1) * wide
    ].astype(BF16)


def taps(even, odd, begin, count, height, wide, dt, dy, lanes=slice(None)):
    inner = (height - 2) * wide
    if dy == 1:
        parts = [odd[pl.ds((begin + f + dt) * inner, inner), lanes] for f in range(count)]
    else:
        parts = [
            even[pl.ds((begin + f + dt) * height * wide + dy * wide, inner), lanes]
            for f in range(count)
        ]
    return jnp.concatenate(parts, axis=0)


def low_product(acc, even, odd, count, height, wide, weights, copies):
    rows = count * (height - 2) * wide
    channels = weights.shape[1]
    needed = [dx * channels // LANES for dx in range(3)]

    def column(n, carry):
        for copy, when in zip(copies, needed):
            pl.when(n == when)(copy.wait)
        lanes = pl.ds(pl.multiple_of(n * LANES, LANES), LANES)
        left = jnp.concatenate(
            [taps(even, odd, 0, count, height, wide, t // 3, t % 3) for t in range(9)], axis=1
        )
        right = weights[:, :, lanes].reshape(9 * channels, LANES)
        acc[n, 0:rows, :] = jnp.dot(left, right, preferred_element_type=F32)
        return carry

    lax.fori_loop(0, weights.shape[-1] // LANES, column, 0)


def low_sum(acc, start, size):
    rows = pl.ds(start, size)
    before = jnp.concatenate([acc[0, rows, :], acc[1, rows, 0:128]], axis=1)
    center = jnp.concatenate([acc[1, rows, 128:256], acc[2, rows, :]], axis=1)
    after = jnp.concatenate([acc[3, rows, :], acc[4, rows, 0:128]], axis=1)
    return center + pltpu.roll(before, 1, 0) + pltpu.roll(after, size - 1, 0)


def transposed_dot(left, right):
    return lax.dot_general(left, right, (((1,), (1,)), ((), ())), preferred_element_type=F32)


def split_frames(count):
    first = count // 4
    second = first + (count - first) // 2
    return (0, first), (first, second), (second, count)


def group_slots(group, groups):
    first, last = groups[group]
    return (0 if group == 0 else first + 2), last + 2


def grouped_taps(planes, groups, frames, height, wide, dt, dy):
    inner = (height - 2) * wide
    parts = []
    for f in frames:
        for group, (even, odd) in enumerate(planes):
            first, last = group_slots(group, groups)
            if first <= f + dt < last:
                slot = f + dt - first
                if dy == 1:
                    parts.append(odd[slot * inner : (slot + 1) * inner, :])
                else:
                    begin = slot * height * wide + dy * wide
                    parts.append(even[begin : begin + inner, :])
    return jnp.concatenate(parts, axis=0)


def high_column(n, acc, planes, groups, group, height, wide, weights):
    left = jnp.concatenate(
        [
            grouped_taps(planes, groups, range(*groups[group]), height, wide, t // 3, t % 3)
            for t in range(9)
        ],
        axis=1,
    )
    acc[n] = transposed_dot(left, weights[n * LANES : (n + 1) * LANES, :])


def high_sum(acc, start, size):
    rows = pl.ds(start, size)
    center = jnp.concatenate([acc[0, rows, :], acc[1, rows, 0:128]], axis=1)
    side = jnp.concatenate([acc[1, rows, 128:256], acc[2, rows, :]], axis=1)
    channels = center.shape[1]
    first = lax.broadcasted_iota(jnp.int32, (1, channels), 1) < channels // 2
    return center + jnp.where(first, pltpu.roll(side, 1, 0), pltpu.roll(side, size - 1, 0))


def pack_kernel(
    wide,
    tile,
    part,
    place,
    latent,
    arrived,
    one,
    two,
    time,
    three,
    four,
    mine,
    theirs,
    tiles,
    spread,
    low,
    high,
):
    section, col = place[0], place[1]
    width, channels = latent.shape[1:]
    half = three.shape[-1]
    empty = jnp.zeros((spread.shape[1] - width, channels), F32)

    def put(slot, values):
        spread[slot] = pltpu.roll(
            jnp.concatenate([values.astype(F32), empty], axis=0), HALO, 0
        )

    for i in range(2):
        put(2 * section + i, latent[i])
        put(2 * (1 - section) + i, arrived[i])
        put(4 + i, one[i])
        put(6 + i, two[i])
    for slot in range(8):
        for ref, which in ((mine, col), (theirs, 1 - col)):
            begin = pl.multiple_of(which * tile + section * part, 8)
            ref[slot] = spread[slot, pl.ds(begin, wide), :].astype(BF16)

    lines = [time[f, y].astype(F32) for f in range(2) for y in range(2)]
    for ref in (three, four):
        for f in range(2):
            for y in range(4):
                values = ref[f, y].astype(F32)
                low[...] = values[:, :128]
                high[:, 0 : half - 128] = values[:, 128:]
                count = values.shape[0] // 2
                even, odd = (
                    jnp.concatenate(
                        [lanes[pl.ds(o, count, stride=2), :] for lanes in (low, high)], axis=1
                    )
                    for o in range(2)
                )
                lines.append(merge(even, odd, half))
    for i, line in enumerate(lines):
        tiles[i] = line.astype(BF16)

    left = col == 0
    upper = lax.broadcasted_iota(jnp.int32, (8, 1), 0) < HALO
    blocks = []
    for i in range(0, len(lines), 2):
        one_line, two_line = lines[i], lines[i + 1]
        last = jnp.where(upper, pltpu.roll(one_line[-8:], HALO, 0), two_line[-8:])
        first = jnp.where(upper, one_line[:8], pltpu.roll(two_line[:8], HALO, 0))
        blocks.append(jnp.where(left, last, first))
    gap = jnp.zeros_like(blocks[0])
    count = wide // 8
    for i in range(theirs.shape[0] - 8):
        group = (blocks + [gap] * count)[i * count : (i + 1) * count]
        theirs[8 + i] = jnp.concatenate(group, axis=0).astype(BF16)


def pack(place, latent, arrived, one, two, time, three, four, wide, tile, part):
    width, channels = latent.shape[1:]
    vmem = pl.BlockSpec(memory_space=pltpu.VMEM)
    lines = 20
    extra = -(-lines * HALO // wide)
    return pl.pallas_call(
        functools.partial(pack_kernel, wide, tile, part),
        out_shape=[
            jax.ShapeDtypeStruct((8, wide, channels), BF16),
            jax.ShapeDtypeStruct((8 + extra, wide, channels), BF16),
            jax.ShapeDtypeStruct((lines, tile, channels), BF16),
        ],
        in_specs=[pl.BlockSpec(memory_space=pltpu.SMEM)] + [vmem] * 7,
        out_specs=[vmem] * 3,
        scratch_shapes=[
            pltpu.VMEM((8, width + 16, channels), F32),
            pltpu.VMEM((three.shape[2], 128), F32),
            pltpu.VMEM((three.shape[2], 128), F32),
        ],
        compiler_params=pltpu.CompilerParams(vmem_limit_bytes=60 * 1024 * 1024),
        name="pack",
    )(place, latent, arrived, one, two, time, three, four)


def stack_kernel(
    wide, place, mine, theirs, tiles, later, own, near, far, windows, tile_near, tile_far
):
    del later
    section, col = place[0], place[1]
    count = mine.shape[0] - 2
    own[0], own[1] = mine[...], theirs[0 : count + 2]
    parity = lax.rem(place[3], 2)
    for ref, y in ((near, 1 - parity), (far, parity)):
        ref[0:count], ref[count : 2 * count] = mine[0:count], theirs[0:count]
        here = lax.rem(y + col, 2) == 0
        ref[2 * count :] = jnp.where(here, mine[count:], theirs[count : count + 2])

    part = wide - 2 * HALO
    upper = lax.broadcasted_iota(jnp.int32, (8, 1), 0) < HALO
    groups = wide // 8
    for i in range(tiles.shape[0]):
        line = tiles[i].astype(F32)
        block = i // 2
        begin = block % groups * 8
        edge = theirs[count + 2 + block // groups].astype(F32)[begin : begin + 8]
        turned = pltpu.roll(edge, HALO, 0)
        before, after = (edge, turned) if i % 2 == 0 else (turned, edge)
        first = pltpu.roll(line, HALO, 0)[:wide]
        head = jnp.where(upper, jnp.where(col == 1, before, 0.0), first[:8])
        first = jnp.concatenate([head, first[8:]], axis=0)
        last = pltpu.roll(line, line.shape[0] - (part - HALO), 0)[:wide]
        tail = jnp.where(upper, last[-8:], jnp.where(col == 0, after, 0.0))
        last = jnp.concatenate([last[:-8], tail], axis=0)
        line = jnp.where(section == 0, first, last).astype(BF16)
        windows[i] = line
    is_even = parity == 0
    for base, start, count, depth in ((0, 0, 2, 2), (4, 4, 4, 2), (12, 8, 4, 1)):
        for f in range(2):
            for j in range(depth):
                slot = start + depth * f + j
                high = windows[base + count * f + j]
                low = windows[base + count * f + count - depth + j]
                tile_near[slot] = jnp.where(is_even, low, high)
                tile_far[slot] = jnp.where(is_even, high, low)


def stack(place, mine, theirs, tiles, later):
    units, wide, channels = mine.shape
    vmem = pl.BlockSpec(memory_space=pltpu.VMEM)
    lines = 2 * units - 2
    shapes = [(2, units), (lines,), (lines,), (tiles.shape[0],), (10,), (10,)]
    return pl.pallas_call(
        functools.partial(stack_kernel, wide),
        out_shape=[jax.ShapeDtypeStruct(shape + (wide, channels), BF16) for shape in shapes],
        in_specs=[pl.BlockSpec(memory_space=pltpu.SMEM)]
        + [vmem] * 3
        + [pl.BlockSpec(memory_space=pl.ANY)],
        out_specs=[vmem] * 6,
        compiler_params=pltpu.CompilerParams(vmem_limit_bytes=8 * 1024 * 1024),
        name="stack",
    )(place, mine, theirs, tiles, later)


def align_kernel(weight, out):
    half = weight.shape[0]
    chunk = 16
    tail = half - 128
    low = lax.broadcasted_iota(jnp.int32, (1, 128), 1) < tail

    def move(k, carry):
        here = aligned(k, chunk)
        none = jnp.zeros((chunk, 128), F32)
        for t in range(9):
            base = 3 * t * half
            first = base // 128 * 128
            last = min(first + 640, weight.shape[1])
            values = weight[pl.ds(here, chunk), first:last].astype(F32)
            if last < first + 640:
                values = jnp.concatenate(
                    [values[:, :512], jnp.concatenate([values[:, 512:], none[:, tail:]], axis=1)],
                    axis=1,
                )
            turned = pltpu.roll(values, 640 - tail, 1)
            tiles = [values[:, 128 * i : 128 * (i + 1)] for i in range(5)]
            moved = [turned[:, 128 * i : 128 * (i + 1)] for i in range(5)]
            if base == first:
                blocks = (
                    moved[1:4],
                    tiles[0:3],
                    [none, jnp.where(low, 0.0, moved[4]), moved[0]],
                    [tiles[3], jnp.where(low, tiles[4], 0.0), none],
                )
            else:
                blocks = (
                    tiles[2:5],
                    moved[0:3],
                    [none, jnp.where(low, 0.0, tiles[0]), tiles[1]],
                    [moved[3], jnp.where(low, moved[4], 0.0), none],
                )
            for n, block in enumerate(blocks):
                into = pl.ds(here + n * half, chunk)
                out[into, 2 * half * t : 2 * half * (t + 1)] = jnp.concatenate(
                    block, axis=1
                ).astype(BF16)
        return carry

    lax.fori_loop(0, half // chunk, move, 0)


def align_weights(weight):
    half = weight.shape[1]
    vmem = pl.BlockSpec(memory_space=pltpu.VMEM)
    return pl.pallas_call(
        align_kernel,
        out_shape=jax.ShapeDtypeStruct((4 * half, 18 * half), BF16),
        in_specs=[vmem],
        out_specs=vmem,
        compiler_params=pltpu.CompilerParams(vmem_limit_bytes=8 * 1024 * 1024),
        name="align_weights",
    )(weight.T)


def combine_kernel(weight, out):
    half = weight.shape[0]
    channels = weight.shape[1] // 9
    chunk = 16

    def combine(k, carry):
        rows = pl.ds(aligned(k, chunk), chunk)
        taken = [
            [
                weight[rows, (3 * dy + dx) * channels : (3 * dy + dx + 1) * channels].astype(F32)
                for dx in range(3)
            ]
            for dy in range(3)
        ]
        for slot, dys in enumerate(((0,), (1, 2), (0, 1), (2,))):
            line = [sum(taken[dy][dx] for dy in dys) for dx in range(3)]
            lanes = slice(slot % 2 * channels, (slot % 2 + 1) * channels)
            for n, block in enumerate((line[1] + line[2], line[0] + line[1], line[0], line[2])):
                into = pl.ds(aligned(k, chunk) + n * half, chunk)
                out[slot // 2, into, lanes] = block.astype(BF16)
        return carry

    lax.fori_loop(0, half // chunk, combine, 0)


def combine_weights(weight):
    channels = 2 * weight.shape[1]
    vmem = pl.BlockSpec(memory_space=pltpu.VMEM)
    return pl.pallas_call(
        combine_kernel,
        out_shape=jax.ShapeDtypeStruct((2, 2 * channels, 2 * channels), BF16),
        in_specs=[vmem],
        out_specs=vmem,
        compiler_params=pltpu.CompilerParams(vmem_limit_bytes=8 * 1024 * 1024),
        name="combine_weights",
    )(weight.T)


def weight_copies(source, target, sems, base):
    channels = source.shape[-1]
    return [
        pltpu.make_async_copy(
            source.at[:, dx], target.at[:, :, pl.ds(dx * channels, channels)], sems.at[base + dx]
        )
        for dx in range(3)
    ]


def first_kernel(
    wide,
    sizes,
    place,
    near,
    own,
    far,
    gains,
    weight_one,
    weight_two,
    later,
    out_ref,
    w1,
    w2,
    acc,
    x1e,
    x1o,
    x2e,
    x2o,
    sems,
):
    channels = own.shape[-1]
    frames = own.shape[1] - 4
    height, width = sizes
    col, row = place[1], place[3]
    units = frames + 2
    del later

    copies_one = weight_copies(weight_one, w1, sems, 0)
    copies_two = weight_copies(weight_two, w2, sems, 3)
    copies_one[0].start()
    copies_one[1].start()

    slots = [lax.rem(y + col, 2) for y in range(2)]

    is_even = lax.rem(row, 2) == 0

    def own_rows(index):
        return [own[slot, index].astype(F32) for slot in slots]

    def above(line):
        return jnp.where(is_even, far[line].astype(F32), near[line].astype(F32))

    def below(line):
        return jnp.where(is_even, near[line].astype(F32), far[line].astype(F32))

    def rows_of(index):
        first = [above(slot * units + index) for slot in slots]
        last = [below(slot * units + index) for slot in slots]
        return jnp.concatenate(first + own_rows(index) + last, axis=0)

    for f in range(2):
        store(x1e, x1o, f, rows_of(frames + f), 6, wide)
        first, last = above(2 * units + f), below(2 * units + f)
        values = jnp.concatenate([first] + own_rows(units + f) + [last], axis=0)
        store(x2e, x2o, f, values, 4, wide)

    def norm_one(f, carry):
        values = activate(rows_of(f), gains[0:1, :], 1.0)
        store(x1e, x1o, f + 2, values, 6, wide)
        return carry

    lax.fori_loop(0, frames, norm_one, 0)
    for copy in [copies_one[2]] + copies_two:
        copy.start()
    low_product(acc, x1e, x1o, frames, 6, wide, w1, copies_one)

    mask = line_mask(place, wide, 2 * row - 1, 4, height, width)

    def norm_two(f, carry):
        size = 4 * wide
        values = activate(low_sum(acc, aligned(f, size), size), gains[1:2, :], mask)
        store(x2e, x2o, f + 2, values, 4, wide)
        return carry

    lax.fori_loop(0, frames, norm_two, 0)
    low_product(acc, x2e, x2o, frames, 4, wide, w2, copies_two)

    def residual(f, carry):
        size = 2 * wide
        values = low_sum(acc, aligned(f, size), size) + jnp.concatenate(own_rows(f), axis=0)
        out_ref[f] = values.astype(BF16)
        return carry

    lax.fori_loop(0, frames, residual, 0)


def planes(slots, height, wide, channels):
    return [
        pltpu.VMEM((slots * height * wide, channels), BF16),
        pltpu.VMEM((slots * (height - 2) * wide, channels), BF16),
    ]


def first_block(place, pieces, gains, weight_one, weight_two, later, sizes):
    _, units, wide, channels = pieces[1].shape
    frames = units - 4
    slots = -(-3 * channels // LANES)
    vmem = pl.BlockSpec(memory_space=pltpu.VMEM)
    anywhere = pl.BlockSpec(memory_space=pl.ANY)
    return pl.pallas_call(
        functools.partial(first_kernel, wide, sizes),
        out_shape=jax.ShapeDtypeStruct((frames, 2 * wide, channels), BF16),
        in_specs=[pl.BlockSpec(memory_space=pltpu.SMEM)]
        + [vmem] * 4
        + [pl.BlockSpec(memory_space=pltpu.HBM)] * 2
        + [anywhere],
        out_specs=vmem,
        scratch_shapes=[
            pltpu.VMEM((9, channels, slots * LANES), BF16),
            pltpu.VMEM((9, channels, slots * LANES), BF16),
            pltpu.VMEM((slots, frames * 4 * wide, LANES), F32),
            *planes(frames + 2, 6, wide, channels),
            *planes(frames + 2, 4, wide, channels),
            pltpu.SemaphoreType.DMA((6,)),
        ],
        compiler_params=pltpu.CompilerParams(vmem_limit_bytes=50 * 1024 * 1024),
        cost_estimate=pl.CostEstimate(
            flops=2 * 27 * channels * channels * frames * 6 * wide,
            bytes_accessed=2 * 54 * channels * channels,
            transcendentals=0,
        ),
        name="first_block",
    )(place, *pieces, gains, weight_one, weight_two, later)


def second_kernel(
    wide,
    sizes,
    place,
    near,
    blocked,
    far,
    tile_near,
    windows,
    tile_far,
    gains,
    wt,
    wu,
    w3,
    w4,
    out_ref,
    acc,
    mixed,
    de,
    do,
    lifted_ref,
    *buffers,
):
    ups, threes, fours = buffers[0:3], buffers[3:6], buffers[6:9]
    planes_three = [buffers[9 + 2 * g : 11 + 2 * g] for g in range(3)]
    planes_four = [buffers[15 + 2 * g : 17 + 2 * g] for g in range(3)]
    channels = blocked.shape[-1]
    half = channels // 2
    size = 6 * wide
    frames = blocked.shape[0]
    count = 2 * frames
    groups = split_frames(count)
    height, width = sizes
    row = place[3]

    is_even = lax.rem(row, 2) == 0

    def chosen(when, one, other, index):
        return jnp.where(when, one[index].astype(F32), other[index].astype(F32))

    def cached(start, base, lines, depth, f):
        slots = [start + depth * f + i for i in range(depth)]
        parts = [chosen(is_even, tile_far, tile_near, slot) for slot in slots]
        parts += [windows[base + lines * f + i].astype(F32) for i in range(lines)]
        parts += [chosen(is_even, tile_near, tile_far, slot) for slot in slots]
        return jnp.concatenate(parts, axis=0)

    for f in range(2):
        mixed[f * size : (f + 1) * size, :] = cached(0, 0, 2, 2, f).astype(BF16)
    for f in range(frames):
        first, last = chosen(is_even, far, near, f), chosen(is_even, near, far, f)
        for i, values in enumerate((first.astype(BF16), blocked[f], last.astype(BF16))):
            begin = (f + 2) * size + i * 2 * wide
            mixed[begin : begin + 2 * wide, :] = values


    def mix(n, carry):
        lanes = pl.ds(pl.multiple_of(n * LANES, LANES), LANES)
        left = jnp.concatenate(
            [mixed[pl.ds(t * size, frames * size), :] for t in range(3)], axis=1
        )
        acc[n, 0 : frames * size, :] = jnp.dot(left, wt[:, lanes], preferred_element_type=F32)
        return carry

    lax.fori_loop(0, 2 * channels // LANES, mix, 0)
    mask_low = line_mask(place, wide, 2 * row - 2, 6, height, width)

    def double(t, carry):
        rows = pl.ds(aligned(t, size), size)
        first = jnp.concatenate([acc[0, rows, :], acc[1, rows, 0:128]], axis=1)
        second = jnp.concatenate([acc[1, rows, 128:256], acc[2, rows, :]], axis=1)
        store(de, do, 2 * t, first * mask_low, 6, wide)
        store(de, do, 2 * t + 1, second * mask_low, 6, wide)
        return carry

    lax.fori_loop(0, frames, double, 0)


    for f in range(2):
        store(*planes_three[0], f, cached(4, 4, 4, 2, f), 8, wide)
        store(*planes_four[0], f, cached(8, 12, 4, 1, f), 6, wide)
    gain3, gain4 = gains[2:3, :], gains[3:4, :]
    mask_three = line_mask(place, wide, 4 * row - 2, 8, 2 * height, width)
    mask_four = mask_three[wide : 7 * wide]
    part = 4 * wide

    def enlarge(group, n):
        first, last = groups[group]
        lanes = slice(n * LANES, (n + 1) * LANES)
        rows = (last - first) * part
        for py in range(2):
            left = jnp.concatenate(
                [
                    taps(de, do, first, last - first, 6, wide, 0, py),
                    taps(de, do, first, last - first, 6, wide, 0, py + 1),
                ],
                axis=1,
            )
            ups[group][n, py * rows : (py + 1) * rows, :] = transposed_dot(left, wu[py, lanes, :])

    def norm_three(group, f):
        first, last = groups[group]
        values = [
            high_sum(ups[group], aligned(f + py * (last - first), part), part)
            .astype(BF16)
            .astype(F32)
            for py in range(2)
        ]
        lifted = jnp.concatenate(
            [values[h % 2][(h // 2) * wide : (h // 2 + 1) * wide] for h in range(8)], axis=0
        )
        lifted_ref[pl.ds(aligned(f + first, part), part), :] = lifted[2 * wide : 6 * wide]
        slot = f + (2 if group == 0 else 0)
        store(*planes_three[group], slot, activate_pairs(lifted, gain3, mask_three), 8, wide)

    def norm_four(group, f):
        values = high_sum(threes[group], aligned(f, size), size)
        slot = f + (2 if group == 0 else 0)
        store(*planes_four[group], slot, activate_pairs(values, gain4, mask_four), 6, wide)

    def finish(group, f):
        first = groups[group][0]
        rows = pl.ds(aligned(f + first, part), part)
        values = high_sum(fours[group], aligned(f, part), part) + lifted_ref[rows, :]
        values = pltpu.roll(values, part - HALO, 0)
        for y in range(4):
            inner = wide - 2 * HALO
            out_ref[f + first, y] = values[y * wide : y * wide + inner].astype(BF16)

    def third(group, n):
        high_column(n, threes[group], planes_three, groups, group, 8, wide, w3)

    def fourth(group, n):
        high_column(n, fours[group], planes_four, groups, group, 6, wide, w4)

    for product, vector in (
        ((enlarge, 0), None),
        ((enlarge, 1), (norm_three, 0)),
        ((enlarge, 2), (norm_three, 1)),
        ((third, 0), (norm_three, 2)),
        ((third, 1), (norm_four, 0)),
        ((third, 2), (norm_four, 1)),
        ((fourth, 0), (norm_four, 2)),
        ((fourth, 1), (finish, 0)),
        ((fourth, 2), (finish, 1)),
        (None, (finish, 2)),
    ):
        for n in range(max(2 * channels // LANES, *(last - first for first, last in groups))):
            if product is not None and n < 2 * channels // LANES:
                product[0](product[1], n)
            if vector is not None and n < groups[vector[1]][1] - groups[vector[1]][0]:
                vector[0](vector[1], n)


def second_block(place, pieces, tiles, gains, weights, sizes, wide):
    frames, _, channels = pieces[0].shape
    count = 2 * frames
    groups = split_frames(count)
    sizes_of = [last - first for first, last in groups]
    slots = [last - first for first, last in (group_slots(g, groups) for g in range(3))]
    vmem = pl.BlockSpec(memory_space=pltpu.VMEM)
    return pl.pallas_call(
        functools.partial(second_kernel, wide, sizes),
        out_shape=jax.ShapeDtypeStruct((count, 4, wide - 2 * HALO, channels), BF16),
        in_specs=[pl.BlockSpec(memory_space=pltpu.SMEM)]
        + [vmem] * 11,
        out_specs=vmem,
        scratch_shapes=[
            pltpu.VMEM((3, frames * 6 * wide, LANES), F32),
            pltpu.VMEM(((frames + 2) * 6 * wide, channels), BF16),
            *planes(count, 6, wide, channels),
            pltpu.VMEM((count * 4 * wide, channels), F32),
            *(pltpu.VMEM((3, n * 8 * wide, LANES), F32) for n in sizes_of),
            *(pltpu.VMEM((3, n * 6 * wide, LANES), F32) for n in sizes_of),
            *(pltpu.VMEM((3, n * 4 * wide, LANES), F32) for n in sizes_of),
            *(ref for n in slots for ref in planes(n, 8, wide, channels)),
            *(ref for n in slots for ref in planes(n, 6, wide, channels)),
        ],
        compiler_params=pltpu.CompilerParams(vmem_limit_bytes=34 * 1024 * 1024),
        name="second_block",
    )(place, *pieces, *tiles, gains, *weights)


def body(
    latent,
    cache_one,
    cache_two,
    cache_time,
    cache_three,
    cache_four,
    gain_one,
    gain_two,
    gain_three,
    gain_four,
    weight_one,
    weight_two,
    weight_time,
    weight_upsample,
    weight_three,
    weight_four,
):
    section, row, col = (lax.axis_index(name) for name in ("section", "rows", "cols"))
    sections, row_count, col_count = (lax.axis_size(name) for name in ("section", "rows", "cols"))
    width, channels = latent.shape[2:]
    tile = width // col_count
    part = tile // sections
    wide = part + 2 * HALO
    half = weight_three.shape[1]
    sizes = (2 * row_count, width)
    place = jnp.stack([section, col, col * tile + section * part - HALO, row]).astype(jnp.int32)

    gains = jnp.stack([gain_one, gain_two, jnp.tile(gain_three, 2), jnp.tile(gain_four, 2)])

    latent = latent.reshape(latent.shape[0], width, channels)
    arrived = swapped(latent, "section")
    mine, theirs, tiles = pack(
        place,
        latent,
        arrived,
        cache_one[:, 0],
        cache_two[:, 0],
        cache_time,
        cache_three,
        cache_four,
        wide,
        tile,
        part,
    )
    weight_three, mine = lax.optimization_barrier((weight_three, mine))
    weight_three = align_weights(weight_three)
    own, near, far, windows, tile_near, tile_far = stack(
        place, mine, swapped(theirs, "cols"), tiles, weight_three
    )
    pieces = [paired(near, "rows", 0), own, paired(far, "rows", 1)]
    tiles = [paired(tile_near, "rows", 0), windows, paired(tile_far, "rows", 1)]
    weight_upsample, own = lax.optimization_barrier((weight_upsample, own))
    weight_upsample = combine_weights(weight_upsample)
    blocked = first_block(
        place,
        pieces,
        gains,
        weight_one.reshape(9, 3, channels, channels),
        weight_two.reshape(9, 3, channels, channels),
        weight_upsample,
        sizes,
    )
    blocks = [paired(blocked, "rows", 0), blocked, paired(blocked, "rows", 1)]
    weight_four, _ = lax.optimization_barrier((weight_four, blocked))
    weight_four = align_weights(weight_four)
    frames = second_block(
        place,
        blocks,
        tiles,
        gains,
        (weight_time, weight_upsample, weight_three, weight_four),
        sizes,
        wide,
    )
    count = frames.shape[0] // sections
    given = lax.dynamic_slice_in_dim(frames, (1 - section) * count, count, 0)
    kept = lax.dynamic_slice_in_dim(frames, section * count, count, 0)
    arrived = swapped(given, "section")
    low = section == 0
    joined = jnp.concatenate(
        [jnp.where(low, kept, arrived), jnp.where(low, arrived, kept)], axis=2
    )
    return joined.reshape(count, 4, 2 * tile, half)


def solution(mesh):
    placed = (
        P("section", ("rows", "cols"), None, None),
        P(None, ("rows", "cols"), None, None),
        P(None, ("rows", "cols"), None, None),
        P(None, "rows", "cols", None),
        P(None, "rows", "cols", None),
        P(None, "rows", "cols", None),
    ) + (P(),) * 10
    return jax.shard_map(
        body,
        mesh=mesh,
        in_specs=placed,
        out_specs=P("section", "rows", "cols", None),
        check_vma=False,
    )
```

```python
import functools

import jax
import jax.numpy as jnp
from jax import lax
from jax.experimental import pallas as pl
from jax.experimental.pallas import tpu as pltpu
from jax.sharding import PartitionSpec as P

EPSILON = 1e-06
HALO = 4
LANES = 256
BF16 = jnp.bfloat16
F32 = jnp.float32


def swapped(value, axis):
    return lax.ppermute(value, axis, [(0, 1), (1, 0)])


def paired(value, axis, first):
    pairs = [(i, i + 1) for i in range(first, lax.axis_size(axis) - 1, 2)]
    return lax.ppermute(value, axis, pairs + [(high, low) for low, high in pairs])


def silu(scaled):
    half = scaled * 0.5
    return half * (1.0 + jnp.tanh(half))


def activate(values, gain, mask):
    mean = jnp.mean(values * values, axis=-1, keepdims=True)
    return silu(values * (lax.rsqrt(mean + EPSILON) * mask) * gain)


def activate_pairs(values, gain, mask):
    channels = values.shape[-1] // 2
    squares = values * values
    first = lax.broadcasted_iota(jnp.int32, (1, 2 * channels), 1) < channels
    total = jnp.sum(squares, axis=-1, keepdims=True)
    low = jnp.sum(jnp.where(first, squares, 0.0), axis=-1, keepdims=True)
    scale_low = lax.rsqrt(low / channels + EPSILON) * mask
    scale_high = lax.rsqrt((total - low) / channels + EPSILON) * mask
    return silu(values * jnp.where(first, scale_low, scale_high) * gain)


def merge(even, odd, channels):
    turned = pltpu.roll(odd, channels - 128, 1)
    first = lax.broadcasted_iota(jnp.int32, (1, 128), 1) < channels - 128
    middle = jnp.where(first, even[:, 128:], turned[:, :128])
    return jnp.concatenate([even[:, :128], middle, turned[:, 128:]], axis=1)


def aligned(index, size):
    return index * size if isinstance(index, int) else pl.multiple_of(index * size, 16)


def line_mask(place, wide, first, count, limit, width):
    columns = place[2] + lax.broadcasted_iota(jnp.int32, (wide, 1), 0)
    inside = jnp.where((columns >= 0) & (columns < width), 1.0, 0.0)
    lines = []
    for i in range(count):
        line = first + i
        lines.append(inside * jnp.where((line >= 0) & (line < limit), 1.0, 0.0))
    return jnp.concatenate(lines, axis=0)


def store(even, odd, slot, values, height, wide):
    even[pl.ds(slot * (height * wide), height * wide), :] = values.astype(BF16)
    odd[pl.ds(slot * ((height - 2) * wide), (height - 2) * wide), :] = values[
        wide : (height - 1) * wide
    ].astype(BF16)


def taps(even, odd, begin, count, height, wide, dt, dy, lanes=slice(None)):
    inner = (height - 2) * wide
    if dy == 1:
        parts = [odd[pl.ds((begin + f + dt) * inner, inner), lanes] for f in range(count)]
    else:
        parts = [
            even[pl.ds((begin + f + dt) * height * wide + dy * wide, inner), lanes]
            for f in range(count)
        ]
    return jnp.concatenate(parts, axis=0)


def low_product(acc, even, odd, count, height, wide, weights):
    rows = count * (height - 2) * wide
    channels = weights.shape[1]
    lanes = 3 * channels
    for n in range(-(-lanes // LANES)):
        begin, end = n * LANES, min((n + 1) * LANES, lanes)
        left = jnp.concatenate(
            [taps(even, odd, 0, count, height, wide, t // 3, t % 3) for t in range(9)], axis=1
        )
        right = []
        for t in range(9):
            parts = []
            for dx in range(3):
                low = max(begin - dx * channels, 0)
                high = min(end - dx * channels, channels)
                if low < high:
                    base = (3 * t + dx) * channels
                    parts.append(weights[base : base + channels, low:high])
            right.append(jnp.concatenate(parts, axis=1))
        right = jnp.concatenate(right, axis=0)
        acc[n, 0:rows, 0 : end - begin] = jnp.dot(left, right, preferred_element_type=F32)


def low_sum(acc, start, size):
    rows = pl.ds(start, size)
    before = jnp.concatenate([acc[0, rows, :], acc[1, rows, 0:128]], axis=1)
    center = jnp.concatenate([acc[1, rows, 128:256], acc[2, rows, :]], axis=1)
    after = jnp.concatenate([acc[3, rows, :], acc[4, rows, 0:128]], axis=1)
    return center + pltpu.roll(before, 1, 0) + pltpu.roll(after, size - 1, 0)


def transposed_dot(left, right):
    return lax.dot_general(left, right, (((1,), (1,)), ((), ())), preferred_element_type=F32)


def split_frames(count):
    first = count // 4
    second = first + (count - first) // 2
    return (0, first), (first, second), (second, count)


def group_slots(group, groups):
    first, last = groups[group]
    return (0 if group == 0 else first + 2), last + 2


def grouped_taps(planes, groups, frames, height, wide, dt, dy):
    inner = (height - 2) * wide
    parts = []
    for f in frames:
        for group, (even, odd) in enumerate(planes):
            first, last = group_slots(group, groups)
            if first <= f + dt < last:
                slot = f + dt - first
                if dy == 1:
                    parts.append(odd[slot * inner : (slot + 1) * inner, :])
                else:
                    begin = slot * height * wide + dy * wide
                    parts.append(even[begin : begin + inner, :])
    return jnp.concatenate(parts, axis=0)


def high_column(n, acc, planes, groups, group, height, wide, weights):
    left = jnp.concatenate(
        [
            grouped_taps(planes, groups, range(*groups[group]), height, wide, t // 3, t % 3)
            for t in range(9)
        ],
        axis=1,
    )
    acc[n] = transposed_dot(left, weights[n * LANES : (n + 1) * LANES, :])


def high_sum(acc, start, size):
    rows = pl.ds(start, size)
    center = jnp.concatenate([acc[0, rows, :], acc[1, rows, 0:128]], axis=1)
    side = jnp.concatenate([acc[1, rows, 128:256], acc[2, rows, :]], axis=1)
    channels = center.shape[1]
    first = lax.broadcasted_iota(jnp.int32, (1, channels), 1) < channels // 2
    return center + jnp.where(first, pltpu.roll(side, 1, 0), pltpu.roll(side, size - 1, 0))


def pack_kernel(
    wide,
    tile,
    part,
    place,
    latent,
    arrived,
    one,
    two,
    time,
    three,
    four,
    mine,
    theirs,
    tiles,
    spread,
    low,
    high,
):
    section, col = place[0], place[1]
    width, channels = latent.shape[1:]
    half = three.shape[-1]
    empty = jnp.zeros((spread.shape[1] - width, channels), F32)

    def put(slot, values):
        spread[slot] = pltpu.roll(
            jnp.concatenate([values.astype(F32), empty], axis=0), HALO, 0
        )

    for i in range(2):
        put(2 * section + i, latent[i])
        put(2 * (1 - section) + i, arrived[i])
        put(4 + i, one[i])
        put(6 + i, two[i])
    for slot in range(8):
        for ref, which in ((mine, col), (theirs, 1 - col)):
            begin = pl.multiple_of(which * tile + section * part, 8)
            ref[slot] = spread[slot, pl.ds(begin, wide), :].astype(BF16)

    lines = [time[f, y].astype(F32) for f in range(2) for y in range(2)]
    for ref in (three, four):
        for f in range(2):
            for y in range(4):
                values = ref[f, y].astype(F32)
                low[...] = values[:, :128]
                high[:, 0 : half - 128] = values[:, 128:]
                count = values.shape[0] // 2
                even, odd = (
                    jnp.concatenate(
                        [lanes[pl.ds(o, count, stride=2), :] for lanes in (low, high)], axis=1
                    )
                    for o in range(2)
                )
                lines.append(merge(even, odd, half))
    for i, line in enumerate(lines):
        tiles[i] = line.astype(BF16)

    left = col == 0
    upper = lax.broadcasted_iota(jnp.int32, (8, 1), 0) < HALO
    blocks = []
    for i in range(0, len(lines), 2):
        one_line, two_line = lines[i], lines[i + 1]
        last = jnp.where(upper, pltpu.roll(one_line[-8:], HALO, 0), two_line[-8:])
        first = jnp.where(upper, one_line[:8], pltpu.roll(two_line[:8], HALO, 0))
        blocks.append(jnp.where(left, last, first))
    gap = jnp.zeros_like(blocks[0])
    count = wide // 8
    for i in range(theirs.shape[0] - 8):
        group = (blocks + [gap] * count)[i * count : (i + 1) * count]
        theirs[8 + i] = jnp.concatenate(group, axis=0).astype(BF16)


def pack(place, latent, arrived, one, two, time, three, four, wide, tile, part):
    width, channels = latent.shape[1:]
    vmem = pl.BlockSpec(memory_space=pltpu.VMEM)
    lines = 20
    extra = -(-lines * HALO // wide)
    return pl.pallas_call(
        functools.partial(pack_kernel, wide, tile, part),
        out_shape=[
            jax.ShapeDtypeStruct((8, wide, channels), BF16),
            jax.ShapeDtypeStruct((8 + extra, wide, channels), BF16),
            jax.ShapeDtypeStruct((lines, tile, channels), BF16),
        ],
        in_specs=[pl.BlockSpec(memory_space=pltpu.SMEM)] + [vmem] * 7,
        out_specs=[vmem] * 3,
        scratch_shapes=[
            pltpu.VMEM((8, width + 16, channels), F32),
            pltpu.VMEM((three.shape[2], 128), F32),
            pltpu.VMEM((three.shape[2], 128), F32),
        ],
        compiler_params=pltpu.CompilerParams(vmem_limit_bytes=60 * 1024 * 1024),
        name="pack",
    )(place, latent, arrived, one, two, time, three, four)


def stack_kernel(
    wide, place, mine, theirs, tiles, later, own, near, far, windows, tile_near, tile_far
):
    del later
    section, col = place[0], place[1]
    count = mine.shape[0] - 2
    own[0], own[1] = mine[...], theirs[0 : count + 2]
    parity = lax.rem(place[3], 2)
    for ref, y in ((near, 1 - parity), (far, parity)):
        ref[0:count], ref[count : 2 * count] = mine[0:count], theirs[0:count]
        here = lax.rem(y + col, 2) == 0
        ref[2 * count :] = jnp.where(here, mine[count:], theirs[count : count + 2])

    part = wide - 2 * HALO
    upper = lax.broadcasted_iota(jnp.int32, (8, 1), 0) < HALO
    groups = wide // 8
    for i in range(tiles.shape[0]):
        line = tiles[i].astype(F32)
        block = i // 2
        begin = block % groups * 8
        edge = theirs[count + 2 + block // groups].astype(F32)[begin : begin + 8]
        turned = pltpu.roll(edge, HALO, 0)
        before, after = (edge, turned) if i % 2 == 0 else (turned, edge)
        first = pltpu.roll(line, HALO, 0)[:wide]
        head = jnp.where(upper, jnp.where(col == 1, before, 0.0), first[:8])
        first = jnp.concatenate([head, first[8:]], axis=0)
        last = pltpu.roll(line, line.shape[0] - (part - HALO), 0)[:wide]
        tail = jnp.where(upper, last[-8:], jnp.where(col == 0, after, 0.0))
        last = jnp.concatenate([last[:-8], tail], axis=0)
        line = jnp.where(section == 0, first, last).astype(BF16)
        windows[i] = line
    is_even = parity == 0
    for base, start, count, depth in ((0, 0, 2, 2), (4, 4, 4, 2), (12, 8, 4, 1)):
        for f in range(2):
            for j in range(depth):
                slot = start + depth * f + j
                high = windows[base + count * f + j]
                low = windows[base + count * f + count - depth + j]
                tile_near[slot] = jnp.where(is_even, low, high)
                tile_far[slot] = jnp.where(is_even, high, low)


def stack(place, mine, theirs, tiles, later):
    units, wide, channels = mine.shape
    vmem = pl.BlockSpec(memory_space=pltpu.VMEM)
    lines = 2 * units - 2
    shapes = [(2, units), (lines,), (lines,), (tiles.shape[0],), (10,), (10,)]
    return pl.pallas_call(
        functools.partial(stack_kernel, wide),
        out_shape=[jax.ShapeDtypeStruct(shape + (wide, channels), BF16) for shape in shapes],
        in_specs=[pl.BlockSpec(memory_space=pltpu.SMEM)]
        + [vmem] * 3
        + [pl.BlockSpec(memory_space=pl.ANY)],
        out_specs=[vmem] * 6,
        compiler_params=pltpu.CompilerParams(vmem_limit_bytes=8 * 1024 * 1024),
        name="stack",
    )(place, mine, theirs, tiles, later)


def align_kernel(weight, out):
    half = weight.shape[0]
    chunk = 16
    tail = half - 128
    low = lax.broadcasted_iota(jnp.int32, (1, 128), 1) < tail

    def move(k, carry):
        here = aligned(k, chunk)
        none = jnp.zeros((chunk, 128), F32)
        for t in range(9):
            base = 3 * t * half
            first = base // 128 * 128
            last = min(first + 640, weight.shape[1])
            values = weight[pl.ds(here, chunk), first:last].astype(F32)
            if last < first + 640:
                values = jnp.concatenate(
                    [values[:, :512], jnp.concatenate([values[:, 512:], none[:, tail:]], axis=1)],
                    axis=1,
                )
            turned = pltpu.roll(values, 640 - tail, 1)
            tiles = [values[:, 128 * i : 128 * (i + 1)] for i in range(5)]
            moved = [turned[:, 128 * i : 128 * (i + 1)] for i in range(5)]
            if base == first:
                blocks = (
                    moved[1:4],
                    tiles[0:3],
                    [none, jnp.where(low, 0.0, moved[4]), moved[0]],
                    [tiles[3], jnp.where(low, tiles[4], 0.0), none],
                )
            else:
                blocks = (
                    tiles[2:5],
                    moved[0:3],
                    [none, jnp.where(low, 0.0, tiles[0]), tiles[1]],
                    [moved[3], jnp.where(low, moved[4], 0.0), none],
                )
            for n, block in enumerate(blocks):
                into = pl.ds(here + n * half, chunk)
                out[into, 2 * half * t : 2 * half * (t + 1)] = jnp.concatenate(
                    block, axis=1
                ).astype(BF16)
        return carry

    lax.fori_loop(0, half // chunk, move, 0)


def align_weights(weight):
    half = weight.shape[1]
    vmem = pl.BlockSpec(memory_space=pltpu.VMEM)
    return pl.pallas_call(
        align_kernel,
        out_shape=jax.ShapeDtypeStruct((4 * half, 18 * half), BF16),
        in_specs=[vmem],
        out_specs=vmem,
        compiler_params=pltpu.CompilerParams(vmem_limit_bytes=8 * 1024 * 1024),
        name="align_weights",
    )(weight.T)


def combine_kernel(weight, out):
    half = weight.shape[0]
    channels = weight.shape[1] // 9
    chunk = 16

    def combine(k, carry):
        rows = pl.ds(aligned(k, chunk), chunk)
        taken = [
            [
                weight[rows, (3 * dy + dx) * channels : (3 * dy + dx + 1) * channels].astype(F32)
                for dx in range(3)
            ]
            for dy in range(3)
        ]
        for slot, dys in enumerate(((0,), (1, 2), (0, 1), (2,))):
            line = [sum(taken[dy][dx] for dy in dys) for dx in range(3)]
            lanes = slice(slot % 2 * channels, (slot % 2 + 1) * channels)
            for n, block in enumerate((line[1] + line[2], line[0] + line[1], line[0], line[2])):
                into = pl.ds(aligned(k, chunk) + n * half, chunk)
                out[slot // 2, into, lanes] = block.astype(BF16)
        return carry

    lax.fori_loop(0, half // chunk, combine, 0)


def combine_weights(weight):
    channels = 2 * weight.shape[1]
    vmem = pl.BlockSpec(memory_space=pltpu.VMEM)
    return pl.pallas_call(
        combine_kernel,
        out_shape=jax.ShapeDtypeStruct((2, 2 * channels, 2 * channels), BF16),
        in_specs=[vmem],
        out_specs=vmem,
        compiler_params=pltpu.CompilerParams(vmem_limit_bytes=8 * 1024 * 1024),
        name="combine_weights",
    )(weight.T)


def first_kernel(
    wide,
    sizes,
    place,
    near,
    own,
    far,
    gains,
    w1,
    w2,
    later_one,
    later_two,
    out_ref,
    acc,
    acc_two,
    x1e,
    x1o,
    x2e,
    x2o,
):
    channels = own.shape[-1]
    frames = own.shape[1] - 4
    height, width = sizes
    col, row = place[1], place[3]
    units = frames + 2
    del later_one, later_two

    slots = [lax.rem(y + col, 2) for y in range(2)]

    is_even = lax.rem(row, 2) == 0

    def own_rows(index):
        return [own[slot, index].astype(F32) for slot in slots]

    def above(line):
        return jnp.where(is_even, far[line].astype(F32), near[line].astype(F32))

    def below(line):
        return jnp.where(is_even, near[line].astype(F32), far[line].astype(F32))

    def rows_of(index):
        first = [above(slot * units + index) for slot in slots]
        last = [below(slot * units + index) for slot in slots]
        return jnp.concatenate(first + own_rows(index) + last, axis=0)

    for f in range(2):
        store(x1e, x1o, f, rows_of(frames + f), 6, wide)
        first, last = above(2 * units + f), below(2 * units + f)
        values = jnp.concatenate([first] + own_rows(units + f) + [last], axis=0)
        store(x2e, x2o, f, values, 4, wide)

    for f in range(frames):
        store(x1e, x1o, f + 2, activate(rows_of(f), gains[0:1, :], 1.0), 6, wide)
    low_product(acc, x1e, x1o, frames, 6, wide, w1)

    mask = line_mask(place, wide, 2 * row - 1, 4, height, width)
    for f in range(frames):
        size = 4 * wide
        values = activate(low_sum(acc, f * size, size), gains[1:2, :], mask)
        store(x2e, x2o, f + 2, values, 4, wide)
    low_product(acc_two, x2e, x2o, frames, 4, wide, w2)
    for f in range(frames):
        size = 2 * wide
        values = low_sum(acc_two, f * size, size) + jnp.concatenate(own_rows(f), axis=0)
        out_ref[f] = values.astype(BF16)


def planes(slots, height, wide, channels):
    return [
        pltpu.VMEM((slots * height * wide, channels), BF16),
        pltpu.VMEM((slots * (height - 2) * wide, channels), BF16),
    ]


def first_block(place, pieces, gains, weight_one, weight_two, later, sizes):
    _, units, wide, channels = pieces[1].shape
    frames = units - 4
    slots = -(-3 * channels // LANES)
    vmem = pl.BlockSpec(memory_space=pltpu.VMEM)
    anywhere = pl.BlockSpec(memory_space=pl.ANY)
    return pl.pallas_call(
        functools.partial(first_kernel, wide, sizes),
        out_shape=jax.ShapeDtypeStruct((frames, 2 * wide, channels), BF16),
        in_specs=[pl.BlockSpec(memory_space=pltpu.SMEM)]
        + [vmem] * 6
        + [anywhere] * 2,
        out_specs=vmem,
        scratch_shapes=[
            pltpu.VMEM((slots, frames * 4 * wide, LANES), F32),
            pltpu.VMEM((slots, frames * 2 * wide, LANES), F32),
            *planes(frames + 2, 6, wide, channels),
            *planes(frames + 2, 4, wide, channels),
        ],
        compiler_params=pltpu.CompilerParams(vmem_limit_bytes=12 * 1024 * 1024),
        cost_estimate=pl.CostEstimate(
            flops=2 * 27 * channels * channels * frames * 6 * wide,
            bytes_accessed=0,
            transcendentals=0,
        ),
        name="first_block",
    )(place, *pieces, gains, weight_one, weight_two, *later)


def second_kernel(
    wide,
    sizes,
    place,
    near,
    blocked,
    far,
    tile_near,
    windows,
    tile_far,
    gains,
    wt,
    wu,
    w3,
    w4,
    out_ref,
    acc,
    mixed,
    de,
    do,
    lifted_ref,
    *buffers,
):
    ups, threes, fours = buffers[0:3], buffers[3:6], buffers[6:9]
    planes_three = [buffers[9 + 2 * g : 11 + 2 * g] for g in range(3)]
    planes_four = [buffers[15 + 2 * g : 17 + 2 * g] for g in range(3)]
    channels = blocked.shape[-1]
    half = channels // 2
    size = 6 * wide
    frames = blocked.shape[0]
    count = 2 * frames
    groups = split_frames(count)
    height, width = sizes
    row = place[3]

    is_even = lax.rem(row, 2) == 0

    def chosen(when, one, other, index):
        return jnp.where(when, one[index].astype(F32), other[index].astype(F32))

    def cached(start, base, lines, depth, f):
        slots = [start + depth * f + i for i in range(depth)]
        parts = [chosen(is_even, tile_far, tile_near, slot) for slot in slots]
        parts += [windows[base + lines * f + i].astype(F32) for i in range(lines)]
        parts += [chosen(is_even, tile_near, tile_far, slot) for slot in slots]
        return jnp.concatenate(parts, axis=0)

    for f in range(2):
        mixed[f * size : (f + 1) * size, :] = cached(0, 0, 2, 2, f).astype(BF16)
    for f in range(frames):
        first, last = chosen(is_even, far, near, f), chosen(is_even, near, far, f)
        for i, values in enumerate((first.astype(BF16), blocked[f], last.astype(BF16))):
            begin = (f + 2) * size + i * 2 * wide
            mixed[begin : begin + 2 * wide, :] = values


    def mix(n, carry):
        lanes = pl.ds(pl.multiple_of(n * LANES, LANES), LANES)
        left = jnp.concatenate(
            [mixed[pl.ds(t * size, frames * size), :] for t in range(3)], axis=1
        )
        acc[n, 0 : frames * size, :] = jnp.dot(left, wt[:, lanes], preferred_element_type=F32)
        return carry

    lax.fori_loop(0, 2 * channels // LANES, mix, 0)
    mask_low = line_mask(place, wide, 2 * row - 2, 6, height, width)

    def double(t, carry):
        rows = pl.ds(aligned(t, size), size)
        first = jnp.concatenate([acc[0, rows, :], acc[1, rows, 0:128]], axis=1)
        second = jnp.concatenate([acc[1, rows, 128:256], acc[2, rows, :]], axis=1)
        store(de, do, 2 * t, first * mask_low, 6, wide)
        store(de, do, 2 * t + 1, second * mask_low, 6, wide)
        return carry

    lax.fori_loop(0, frames, double, 0)


    for f in range(2):
        store(*planes_three[0], f, cached(4, 4, 4, 2, f), 8, wide)
        store(*planes_four[0], f, cached(8, 12, 4, 1, f), 6, wide)
    gain3, gain4 = gains[2:3, :], gains[3:4, :]
    mask_three = line_mask(place, wide, 4 * row - 2, 8, 2 * height, width)
    mask_four = mask_three[wide : 7 * wide]
    part = 4 * wide

    def enlarge(group, n):
        first, last = groups[group]
        lanes = slice(n * LANES, (n + 1) * LANES)
        rows = (last - first) * part
        for py in range(2):
            left = jnp.concatenate(
                [
                    taps(de, do, first, last - first, 6, wide, 0, py),
                    taps(de, do, first, last - first, 6, wide, 0, py + 1),
                ],
                axis=1,
            )
            ups[group][n, py * rows : (py + 1) * rows, :] = transposed_dot(left, wu[py, lanes, :])

    def norm_three(group, f):
        first, last = groups[group]
        values = [
            high_sum(ups[group], aligned(f + py * (last - first), part), part)
            .astype(BF16)
            .astype(F32)
            for py in range(2)
        ]
        lifted = jnp.concatenate(
            [values[h % 2][(h // 2) * wide : (h // 2 + 1) * wide] for h in range(8)], axis=0
        )
        lifted_ref[pl.ds(aligned(f + first, part), part), :] = lifted[2 * wide : 6 * wide]
        slot = f + (2 if group == 0 else 0)
        store(*planes_three[group], slot, activate_pairs(lifted, gain3, mask_three), 8, wide)

    def norm_four(group, f):
        values = high_sum(threes[group], aligned(f, size), size)
        slot = f + (2 if group == 0 else 0)
        store(*planes_four[group], slot, activate_pairs(values, gain4, mask_four), 6, wide)

    def finish(group, f):
        first = groups[group][0]
        rows = pl.ds(aligned(f + first, part), part)
        values = high_sum(fours[group], aligned(f, part), part) + lifted_ref[rows, :]
        values = pltpu.roll(values, part - HALO, 0)
        for y in range(4):
            inner = wide - 2 * HALO
            out_ref[f + first, y] = values[y * wide : y * wide + inner].astype(BF16)

    def third(group, n):
        high_column(n, threes[group], planes_three, groups, group, 8, wide, w3)

    def fourth(group, n):
        high_column(n, fours[group], planes_four, groups, group, 6, wide, w4)

    for product, vector in (
        ((enlarge, 0), None),
        ((enlarge, 1), (norm_three, 0)),
        ((enlarge, 2), (norm_three, 1)),
        ((third, 0), (norm_three, 2)),
        ((third, 1), (norm_four, 0)),
        ((third, 2), (norm_four, 1)),
        ((fourth, 0), (norm_four, 2)),
        ((fourth, 1), (finish, 0)),
        ((fourth, 2), (finish, 1)),
        (None, (finish, 2)),
    ):
        for n in range(max(2 * channels // LANES, *(last - first for first, last in groups))):
            if product is not None and n < 2 * channels // LANES:
                product[0](product[1], n)
            if vector is not None and n < groups[vector[1]][1] - groups[vector[1]][0]:
                vector[0](vector[1], n)


def second_block(place, pieces, tiles, gains, weights, sizes, wide):
    frames, _, channels = pieces[0].shape
    count = 2 * frames
    groups = split_frames(count)
    sizes_of = [last - first for first, last in groups]
    slots = [last - first for first, last in (group_slots(g, groups) for g in range(3))]
    vmem = pl.BlockSpec(memory_space=pltpu.VMEM)
    return pl.pallas_call(
        functools.partial(second_kernel, wide, sizes),
        out_shape=jax.ShapeDtypeStruct((count, 4, wide - 2 * HALO, channels), BF16),
        in_specs=[pl.BlockSpec(memory_space=pltpu.SMEM)]
        + [vmem] * 11,
        out_specs=vmem,
        scratch_shapes=[
            pltpu.VMEM((3, frames * 6 * wide, LANES), F32),
            pltpu.VMEM(((frames + 2) * 6 * wide, channels), BF16),
            *planes(count, 6, wide, channels),
            pltpu.VMEM((count * 4 * wide, channels), F32),
            *(pltpu.VMEM((3, n * 8 * wide, LANES), F32) for n in sizes_of),
            *(pltpu.VMEM((3, n * 6 * wide, LANES), F32) for n in sizes_of),
            *(pltpu.VMEM((3, n * 4 * wide, LANES), F32) for n in sizes_of),
            *(ref for n in slots for ref in planes(n, 8, wide, channels)),
            *(ref for n in slots for ref in planes(n, 6, wide, channels)),
        ],
        compiler_params=pltpu.CompilerParams(vmem_limit_bytes=24 * 1024 * 1024),
        name="second_block",
    )(place, *pieces, *tiles, gains, *weights)


def body(
    latent,
    cache_one,
    cache_two,
    cache_time,
    cache_three,
    cache_four,
    gain_one,
    gain_two,
    gain_three,
    gain_four,
    weight_one,
    weight_two,
    weight_time,
    weight_upsample,
    weight_three,
    weight_four,
):
    section, row, col = (lax.axis_index(name) for name in ("section", "rows", "cols"))
    sections, row_count, col_count = (lax.axis_size(name) for name in ("section", "rows", "cols"))
    width, channels = latent.shape[2:]
    tile = width // col_count
    part = tile // sections
    wide = part + 2 * HALO
    half = weight_three.shape[1]
    sizes = (2 * row_count, width)
    place = jnp.stack([section, col, col * tile + section * part - HALO, row]).astype(jnp.int32)

    gains = jnp.stack([gain_one, gain_two, jnp.tile(gain_three, 2), jnp.tile(gain_four, 2)])

    latent = latent.reshape(latent.shape[0], width, channels)
    arrived = swapped(latent, "section")
    mine, theirs, tiles = pack(
        place,
        latent,
        arrived,
        cache_one[:, 0],
        cache_two[:, 0],
        cache_time,
        cache_three,
        cache_four,
        wide,
        tile,
        part,
    )
    weight_three, mine = lax.optimization_barrier((weight_three, mine))
    weight_three = align_weights(weight_three)
    own, near, far, windows, tile_near, tile_far = stack(
        place, mine, swapped(theirs, "cols"), tiles, weight_three
    )
    far = paired(far, "rows", 1)
    near = paired(near, "rows", 0)
    tile_far = paired(tile_far, "rows", 1)
    tile_near = paired(tile_near, "rows", 0)
    weight_upsample, weight_four, own = lax.optimization_barrier(
        (weight_upsample, weight_four, own)
    )
    weight_upsample = combine_weights(weight_upsample)
    weight_four = align_weights(weight_four)
    blocked = first_block(
        place,
        [near, own, far],
        gains,
        weight_one,
        weight_two,
        (weight_upsample, weight_four),
        sizes,
    )
    far = paired(blocked, "rows", 1)
    near = paired(blocked, "rows", 0)
    blocks = [near, blocked, far]
    tiles = [tile_near, windows, tile_far]
    frames = second_block(
        place,
        blocks,
        tiles,
        gains,
        (weight_time, weight_upsample, weight_three, weight_four),
        sizes,
        wide,
    )
    count = frames.shape[0] // sections
    given = lax.dynamic_slice_in_dim(frames, (1 - section) * count, count, 0)
    kept = lax.dynamic_slice_in_dim(frames, section * count, count, 0)
    arrived = swapped(given, "section")
    low = section == 0
    joined = jnp.concatenate(
        [jnp.where(low, kept, arrived), jnp.where(low, arrived, kept)], axis=2
    )
    return joined.reshape(count, 4, 2 * tile, half)


def solution(mesh):
    placed = (
        P("section", ("rows", "cols"), None, None),
        P(None, ("rows", "cols"), None, None),
        P(None, ("rows", "cols"), None, None),
        P(None, "rows", "cols", None),
        P(None, "rows", "cols", None),
        P(None, "rows", "cols", None),
    ) + (P(),) * 10
    return jax.shard_map(
        body,
        mesh=mesh,
        in_specs=placed,
        out_specs=P("section", "rows", "cols", None),
        check_vma=False,
    )
```

```python
import functools

import jax
import jax.numpy as jnp
from jax import lax
from jax.experimental import pallas as pl
from jax.experimental.pallas import tpu as pltpu
from jax.sharding import PartitionSpec as P

EPSILON = 1e-06
HALO = 4
LANES = 256
BF16 = jnp.bfloat16
F32 = jnp.float32


def swapped(value, axis):
    return lax.ppermute(value, axis, [(0, 1), (1, 0)])


def paired(value, axis, first):
    pairs = [(i, i + 1) for i in range(first, lax.axis_size(axis) - 1, 2)]
    return lax.ppermute(value, axis, pairs + [(high, low) for low, high in pairs])


def silu(scaled):
    half = scaled * 0.5
    return half * (1.0 + jnp.tanh(half))


def activate(values, gain, mask):
    mean = jnp.mean(values * values, axis=-1, keepdims=True)
    return silu(values * (lax.rsqrt(mean + EPSILON) * mask) * gain)


def activate_pairs(values, gain, mask):
    channels = values.shape[-1] // 2
    squares = values * values
    first = lax.broadcasted_iota(jnp.int32, (1, 2 * channels), 1) < channels
    total = jnp.sum(squares, axis=-1, keepdims=True)
    low = jnp.sum(jnp.where(first, squares, 0.0), axis=-1, keepdims=True)
    scale_low = lax.rsqrt(low / channels + EPSILON) * mask
    scale_high = lax.rsqrt((total - low) / channels + EPSILON) * mask
    return silu(values * jnp.where(first, scale_low, scale_high) * gain)


def merge(even, odd, channels):
    turned = pltpu.roll(odd, channels - 128, 1)
    first = lax.broadcasted_iota(jnp.int32, (1, 128), 1) < channels - 128
    middle = jnp.where(first, even[:, 128:], turned[:, :128])
    return jnp.concatenate([even[:, :128], middle, turned[:, 128:]], axis=1)


def aligned(index, size):
    return index * size if isinstance(index, int) else pl.multiple_of(index * size, 16)


def line_mask(place, wide, first, count, limit, width):
    columns = place[2] + lax.broadcasted_iota(jnp.int32, (wide, 1), 0)
    inside = jnp.where((columns >= 0) & (columns < width), 1.0, 0.0)
    lines = []
    for i in range(count):
        line = first + i
        lines.append(inside * jnp.where((line >= 0) & (line < limit), 1.0, 0.0))
    return jnp.concatenate(lines, axis=0)


def store(even, odd, slot, values, height, wide):
    even[pl.ds(slot * (height * wide), height * wide), :] = values.astype(BF16)
    odd[pl.ds(slot * ((height - 2) * wide), (height - 2) * wide), :] = values[
        wide : (height - 1) * wide
    ].astype(BF16)


def taps(even, odd, begin, count, height, wide, dt, dy, lanes=slice(None)):
    inner = (height - 2) * wide
    if dy == 1:
        parts = [odd[pl.ds((begin + f + dt) * inner, inner), lanes] for f in range(count)]
    else:
        parts = [
            even[pl.ds((begin + f + dt) * height * wide + dy * wide, inner), lanes]
            for f in range(count)
        ]
    return jnp.concatenate(parts, axis=0)


def low_product(acc, even, odd, count, height, wide, weights, copies):
    rows = count * (height - 2) * wide
    channels = weights.shape[1]
    lanes = 3 * channels
    waited = 0
    for n in range(-(-lanes // LANES)):
        begin, end = n * LANES, min((n + 1) * LANES, lanes)
        while waited * channels < end:
            copies[waited].wait()
            waited += 1
        left = jnp.concatenate(
            [taps(even, odd, 0, count, height, wide, t // 3, t % 3) for t in range(9)], axis=1
        )
        right = weights[:, :, begin:end].reshape(9 * channels, end - begin)
        acc[n, 0:rows, 0 : end - begin] = jnp.dot(left, right, preferred_element_type=F32)


def low_sum(acc, start, size):
    rows = pl.ds(start, size)
    before = jnp.concatenate([acc[0, rows, :], acc[1, rows, 0:128]], axis=1)
    center = jnp.concatenate([acc[1, rows, 128:256], acc[2, rows, :]], axis=1)
    after = jnp.concatenate([acc[3, rows, :], acc[4, rows, 0:128]], axis=1)
    return center + pltpu.roll(before, 1, 0) + pltpu.roll(after, size - 1, 0)


def transposed_dot(left, right):
    return lax.dot_general(left, right, (((1,), (1,)), ((), ())), preferred_element_type=F32)


def split_frames(count):
    first = count // 4
    second = first + (count - first) // 2
    return (0, first), (first, second), (second, count)


def group_slots(group, groups):
    first, last = groups[group]
    return (0 if group == 0 else first + 2), last + 2


def grouped_taps(planes, groups, frames, height, wide, dt, dy):
    inner = (height - 2) * wide
    parts = []
    for f in frames:
        for group, (even, odd) in enumerate(planes):
            first, last = group_slots(group, groups)
            if first <= f + dt < last:
                slot = f + dt - first
                if dy == 1:
                    parts.append(odd[slot * inner : (slot + 1) * inner, :])
                else:
                    begin = slot * height * wide + dy * wide
                    parts.append(even[begin : begin + inner, :])
    return jnp.concatenate(parts, axis=0)


def high_column(n, acc, planes, groups, group, height, wide, weights):
    left = jnp.concatenate(
        [
            grouped_taps(planes, groups, range(*groups[group]), height, wide, t // 3, t % 3)
            for t in range(9)
        ],
        axis=1,
    )
    acc[n] = transposed_dot(left, weights[n * LANES : (n + 1) * LANES, :])


def high_sum(acc, start, size):
    rows = pl.ds(start, size)
    center = jnp.concatenate([acc[0, rows, :], acc[1, rows, 0:128]], axis=1)
    side = jnp.concatenate([acc[1, rows, 128:256], acc[2, rows, :]], axis=1)
    channels = center.shape[1]
    first = lax.broadcasted_iota(jnp.int32, (1, channels), 1) < channels // 2
    return center + jnp.where(first, pltpu.roll(side, 1, 0), pltpu.roll(side, size - 1, 0))


def pack_kernel(
    wide,
    tile,
    part,
    place,
    latent,
    arrived,
    one,
    two,
    time,
    three,
    four,
    mine,
    theirs,
    tiles,
    spread,
    low,
    high,
):
    section, col = place[0], place[1]
    width, channels = latent.shape[1:]
    half = three.shape[-1]
    empty = jnp.zeros((spread.shape[1] - width, channels), F32)

    def put(slot, values):
        spread[slot] = pltpu.roll(
            jnp.concatenate([values.astype(F32), empty], axis=0), HALO, 0
        )

    for i in range(2):
        put(2 * section + i, latent[i])
        put(2 * (1 - section) + i, arrived[i])
        put(4 + i, one[i])
        put(6 + i, two[i])
    for slot in range(8):
        for ref, which in ((mine, col), (theirs, 1 - col)):
            begin = pl.multiple_of(which * tile + section * part, 8)
            ref[slot] = spread[slot, pl.ds(begin, wide), :].astype(BF16)

    lines = [time[f, y].astype(F32) for f in range(2) for y in range(2)]
    for ref in (three, four):
        for f in range(2):
            for y in range(4):
                values = ref[f, y].astype(F32)
                low[...] = values[:, :128]
                high[:, 0 : half - 128] = values[:, 128:]
                count = values.shape[0] // 2
                even, odd = (
                    jnp.concatenate(
                        [lanes[pl.ds(o, count, stride=2), :] for lanes in (low, high)], axis=1
                    )
                    for o in range(2)
                )
                lines.append(merge(even, odd, half))
    for i, line in enumerate(lines):
        tiles[i] = line.astype(BF16)

    left = col == 0
    upper = lax.broadcasted_iota(jnp.int32, (8, 1), 0) < HALO
    blocks = []
    for i in range(0, len(lines), 2):
        one_line, two_line = lines[i], lines[i + 1]
        last = jnp.where(upper, pltpu.roll(one_line[-8:], HALO, 0), two_line[-8:])
        first = jnp.where(upper, one_line[:8], pltpu.roll(two_line[:8], HALO, 0))
        blocks.append(jnp.where(left, last, first))
    gap = jnp.zeros_like(blocks[0])
    count = wide // 8
    for i in range(theirs.shape[0] - 8):
        group = (blocks + [gap] * count)[i * count : (i + 1) * count]
        theirs[8 + i] = jnp.concatenate(group, axis=0).astype(BF16)


def pack(place, latent, arrived, one, two, time, three, four, wide, tile, part):
    width, channels = latent.shape[1:]
    vmem = pl.BlockSpec(memory_space=pltpu.VMEM)
    lines = 20
    extra = -(-lines * HALO // wide)
    return pl.pallas_call(
        functools.partial(pack_kernel, wide, tile, part),
        out_shape=[
            jax.ShapeDtypeStruct((8, wide, channels), BF16),
            jax.ShapeDtypeStruct((8 + extra, wide, channels), BF16),
            jax.ShapeDtypeStruct((lines, tile, channels), BF16),
        ],
        in_specs=[pl.BlockSpec(memory_space=pltpu.SMEM)] + [vmem] * 7,
        out_specs=[vmem] * 3,
        scratch_shapes=[
            pltpu.VMEM((8, width + 16, channels), F32),
            pltpu.VMEM((three.shape[2], 128), F32),
            pltpu.VMEM((three.shape[2], 128), F32),
        ],
        compiler_params=pltpu.CompilerParams(vmem_limit_bytes=60 * 1024 * 1024),
        name="pack",
    )(place, latent, arrived, one, two, time, three, four)


def stack_kernel(
    wide, place, mine, theirs, tiles, later, own, near, far, windows, tile_near, tile_far
):
    del later
    section, col = place[0], place[1]
    count = mine.shape[0] - 2
    own[0], own[1] = mine[...], theirs[0 : count + 2]
    parity = lax.rem(place[3], 2)
    for ref, y in ((near, 1 - parity), (far, parity)):
        ref[0:count], ref[count : 2 * count] = mine[0:count], theirs[0:count]
        here = lax.rem(y + col, 2) == 0
        ref[2 * count :] = jnp.where(here, mine[count:], theirs[count : count + 2])

    part = wide - 2 * HALO
    upper = lax.broadcasted_iota(jnp.int32, (8, 1), 0) < HALO
    groups = wide // 8
    for i in range(tiles.shape[0]):
        line = tiles[i].astype(F32)
        block = i // 2
        begin = block % groups * 8
        edge = theirs[count + 2 + block // groups].astype(F32)[begin : begin + 8]
        turned = pltpu.roll(edge, HALO, 0)
        before, after = (edge, turned) if i % 2 == 0 else (turned, edge)
        first = pltpu.roll(line, HALO, 0)[:wide]
        head = jnp.where(upper, jnp.where(col == 1, before, 0.0), first[:8])
        first = jnp.concatenate([head, first[8:]], axis=0)
        last = pltpu.roll(line, line.shape[0] - (part - HALO), 0)[:wide]
        tail = jnp.where(upper, last[-8:], jnp.where(col == 0, after, 0.0))
        last = jnp.concatenate([last[:-8], tail], axis=0)
        line = jnp.where(section == 0, first, last).astype(BF16)
        windows[i] = line
    is_even = parity == 0
    for base, start, count, depth in ((0, 0, 2, 2), (4, 4, 4, 2), (12, 8, 4, 1)):
        for f in range(2):
            for j in range(depth):
                slot = start + depth * f + j
                high = windows[base + count * f + j]
                low = windows[base + count * f + count - depth + j]
                tile_near[slot] = jnp.where(is_even, low, high)
                tile_far[slot] = jnp.where(is_even, high, low)


def stack(place, mine, theirs, tiles, later):
    units, wide, channels = mine.shape
    vmem = pl.BlockSpec(memory_space=pltpu.VMEM)
    lines = 2 * units - 2
    shapes = [(2, units), (lines,), (lines,), (tiles.shape[0],), (10,), (10,)]
    return pl.pallas_call(
        functools.partial(stack_kernel, wide),
        out_shape=[jax.ShapeDtypeStruct(shape + (wide, channels), BF16) for shape in shapes],
        in_specs=[pl.BlockSpec(memory_space=pltpu.SMEM)]
        + [vmem] * 3
        + [pl.BlockSpec(memory_space=pl.ANY)],
        out_specs=[vmem] * 6,
        compiler_params=pltpu.CompilerParams(vmem_limit_bytes=8 * 1024 * 1024),
        name="stack",
    )(place, mine, theirs, tiles, later)


def align_kernel(weight, out):
    half = weight.shape[0]
    chunk = 16
    tail = half - 128
    low = lax.broadcasted_iota(jnp.int32, (1, 128), 1) < tail

    def move(k, carry):
        here = aligned(k, chunk)
        none = jnp.zeros((chunk, 128), F32)
        for t in range(9):
            base = 3 * t * half
            first = base // 128 * 128
            last = min(first + 640, weight.shape[1])
            values = weight[pl.ds(here, chunk), first:last].astype(F32)
            if last < first + 640:
                values = jnp.concatenate(
                    [values[:, :512], jnp.concatenate([values[:, 512:], none[:, tail:]], axis=1)],
                    axis=1,
                )
            turned = pltpu.roll(values, 640 - tail, 1)
            tiles = [values[:, 128 * i : 128 * (i + 1)] for i in range(5)]
            moved = [turned[:, 128 * i : 128 * (i + 1)] for i in range(5)]
            if base == first:
                blocks = (
                    moved[1:4],
                    tiles[0:3],
                    [none, jnp.where(low, 0.0, moved[4]), moved[0]],
                    [tiles[3], jnp.where(low, tiles[4], 0.0), none],
                )
            else:
                blocks = (
                    tiles[2:5],
                    moved[0:3],
                    [none, jnp.where(low, 0.0, tiles[0]), tiles[1]],
                    [moved[3], jnp.where(low, moved[4], 0.0), none],
                )
            for n, block in enumerate(blocks):
                into = pl.ds(here + n * half, chunk)
                out[into, 2 * half * t : 2 * half * (t + 1)] = jnp.concatenate(
                    block, axis=1
                ).astype(BF16)
        return carry

    lax.fori_loop(0, half // chunk, move, 0)


def align_weights(weight):
    half = weight.shape[1]
    vmem = pl.BlockSpec(memory_space=pltpu.VMEM)
    return pl.pallas_call(
        align_kernel,
        out_shape=jax.ShapeDtypeStruct((4 * half, 18 * half), BF16),
        in_specs=[vmem],
        out_specs=vmem,
        compiler_params=pltpu.CompilerParams(vmem_limit_bytes=8 * 1024 * 1024),
        name="align_weights",
    )(weight.T)


def combine_kernel(weight, out):
    half = weight.shape[0]
    channels = weight.shape[1] // 9
    chunk = 16

    def combine(k, carry):
        rows = pl.ds(aligned(k, chunk), chunk)
        taken = [
            [
                weight[rows, (3 * dy + dx) * channels : (3 * dy + dx + 1) * channels].astype(F32)
                for dx in range(3)
            ]
            for dy in range(3)
        ]
        for slot, dys in enumerate(((0,), (1, 2), (0, 1), (2,))):
            line = [sum(taken[dy][dx] for dy in dys) for dx in range(3)]
            lanes = slice(slot % 2 * channels, (slot % 2 + 1) * channels)
            for n, block in enumerate((line[1] + line[2], line[0] + line[1], line[0], line[2])):
                into = pl.ds(aligned(k, chunk) + n * half, chunk)
                out[slot // 2, into, lanes] = block.astype(BF16)
        return carry

    lax.fori_loop(0, half // chunk, combine, 0)


def combine_weights(weight):
    channels = 2 * weight.shape[1]
    vmem = pl.BlockSpec(memory_space=pltpu.VMEM)
    return pl.pallas_call(
        combine_kernel,
        out_shape=jax.ShapeDtypeStruct((2, 2 * channels, 2 * channels), BF16),
        in_specs=[vmem],
        out_specs=vmem,
        compiler_params=pltpu.CompilerParams(vmem_limit_bytes=8 * 1024 * 1024),
        name="combine_weights",
    )(weight.T)


def weight_copies(source, target, sems, base):
    channels = source.shape[-1]
    return [
        pltpu.make_async_copy(
            source.at[:, dx], target.at[:, :, pl.ds(dx * channels, channels)], sems.at[base + dx]
        )
        for dx in range(3)
    ]


def first_kernel(
    wide,
    sizes,
    place,
    near,
    own,
    far,
    gains,
    weight_one,
    weight_two,
    later_one,
    later_two,
    out_ref,
    w1,
    w2,
    acc,
    acc_two,
    x1e,
    x1o,
    x2e,
    x2o,
    sems,
):
    channels = own.shape[-1]
    frames = own.shape[1] - 4
    height, width = sizes
    col, row = place[1], place[3]
    units = frames + 2
    del later_one, later_two

    copies_one = weight_copies(weight_one, w1, sems, 0)
    copies_two = weight_copies(weight_two, w2, sems, 3)
    copies_one[0].start()

    slots = [lax.rem(y + col, 2) for y in range(2)]

    is_even = lax.rem(row, 2) == 0

    def own_rows(index):
        return [own[slot, index].astype(F32) for slot in slots]

    def above(line):
        return jnp.where(is_even, far[line].astype(F32), near[line].astype(F32))

    def below(line):
        return jnp.where(is_even, near[line].astype(F32), far[line].astype(F32))

    def rows_of(index):
        first = [above(slot * units + index) for slot in slots]
        last = [below(slot * units + index) for slot in slots]
        return jnp.concatenate(first + own_rows(index) + last, axis=0)

    for f in range(2):
        store(x1e, x1o, f, rows_of(frames + f), 6, wide)
        first, last = above(2 * units + f), below(2 * units + f)
        values = jnp.concatenate([first] + own_rows(units + f) + [last], axis=0)
        store(x2e, x2o, f, values, 4, wide)

    copies_one[1].start()
    for f in range(frames):
        store(x1e, x1o, f + 2, activate(rows_of(f), gains[0:1, :], 1.0), 6, wide)
    for copy in [copies_one[2]] + copies_two:
        copy.start()
    low_product(acc, x1e, x1o, frames, 6, wide, w1, copies_one)

    mask = line_mask(place, wide, 2 * row - 1, 4, height, width)
    for f in range(frames):
        size = 4 * wide
        values = activate(low_sum(acc, f * size, size), gains[1:2, :], mask)
        store(x2e, x2o, f + 2, values, 4, wide)
    low_product(acc_two, x2e, x2o, frames, 4, wide, w2, copies_two)
    for f in range(frames):
        size = 2 * wide
        values = low_sum(acc_two, f * size, size) + jnp.concatenate(own_rows(f), axis=0)
        out_ref[f] = values.astype(BF16)


def planes(slots, height, wide, channels):
    return [
        pltpu.VMEM((slots * height * wide, channels), BF16),
        pltpu.VMEM((slots * (height - 2) * wide, channels), BF16),
    ]


def first_block(place, pieces, gains, weight_one, weight_two, later, sizes):
    _, units, wide, channels = pieces[1].shape
    frames = units - 4
    slots = -(-3 * channels // LANES)
    vmem = pl.BlockSpec(memory_space=pltpu.VMEM)
    anywhere = pl.BlockSpec(memory_space=pl.ANY)
    return pl.pallas_call(
        functools.partial(first_kernel, wide, sizes),
        out_shape=jax.ShapeDtypeStruct((frames, 2 * wide, channels), BF16),
        in_specs=[pl.BlockSpec(memory_space=pltpu.SMEM)]
        + [vmem] * 4
        + [pl.BlockSpec(memory_space=pltpu.HBM)] * 2
        + [anywhere] * 2,
        out_specs=vmem,
        scratch_shapes=[
            pltpu.VMEM((9, channels, slots * LANES), BF16),
            pltpu.VMEM((9, channels, slots * LANES), BF16),
            pltpu.VMEM((slots, frames * 4 * wide, LANES), F32),
            pltpu.VMEM((slots, frames * 2 * wide, LANES), F32),
            *planes(frames + 2, 6, wide, channels),
            *planes(frames + 2, 4, wide, channels),
            pltpu.SemaphoreType.DMA((6,)),
        ],
        compiler_params=pltpu.CompilerParams(vmem_limit_bytes=50 * 1024 * 1024),
        cost_estimate=pl.CostEstimate(
            flops=2 * 27 * channels * channels * frames * 6 * wide,
            bytes_accessed=2 * 54 * channels * channels,
            transcendentals=0,
        ),
        name="first_block",
    )(place, *pieces, gains, weight_one, weight_two, *later)


def second_kernel(
    wide,
    sizes,
    place,
    near,
    blocked,
    far,
    tile_near,
    windows,
    tile_far,
    gains,
    wt,
    wu,
    weight_three,
    weight_four,
    out_ref,
    w3,
    w4,
    sems,
    acc,
    mixed,
    de,
    do,
    lifted_ref,
    *buffers,
):
    ups, threes, fours = buffers[0:3], buffers[3:6], buffers[6:9]
    planes_three = [buffers[9 + 2 * g : 11 + 2 * g] for g in range(3)]
    planes_four = [buffers[15 + 2 * g : 17 + 2 * g] for g in range(3)]
    copies = [
        pltpu.make_async_copy(source, target, sems.at[i])
        for i, (source, target) in enumerate(((weight_three, w3), (weight_four, w4)))
    ]
    for copy in copies:
        copy.start()
    channels = blocked.shape[-1]
    half = channels // 2
    size = 6 * wide
    frames = blocked.shape[0]
    count = 2 * frames
    groups = split_frames(count)
    height, width = sizes
    row = place[3]

    is_even = lax.rem(row, 2) == 0

    def chosen(when, one, other, index):
        return jnp.where(when, one[index].astype(F32), other[index].astype(F32))

    def cached(start, base, lines, depth, f):
        slots = [start + depth * f + i for i in range(depth)]
        parts = [chosen(is_even, tile_far, tile_near, slot) for slot in slots]
        parts += [windows[base + lines * f + i].astype(F32) for i in range(lines)]
        parts += [chosen(is_even, tile_near, tile_far, slot) for slot in slots]
        return jnp.concatenate(parts, axis=0)

    for f in range(2):
        mixed[f * size : (f + 1) * size, :] = cached(0, 0, 2, 2, f).astype(BF16)
    for f in range(frames):
        first, last = chosen(is_even, far, near, f), chosen(is_even, near, far, f)
        for i, values in enumerate((first.astype(BF16), blocked[f], last.astype(BF16))):
            begin = (f + 2) * size + i * 2 * wide
            mixed[begin : begin + 2 * wide, :] = values


    def mix(n, carry):
        lanes = pl.ds(pl.multiple_of(n * LANES, LANES), LANES)
        left = jnp.concatenate(
            [mixed[pl.ds(t * size, frames * size), :] for t in range(3)], axis=1
        )
        acc[n, 0 : frames * size, :] = jnp.dot(left, wt[:, lanes], preferred_element_type=F32)
        return carry

    lax.fori_loop(0, 2 * channels // LANES, mix, 0)
    mask_low = line_mask(place, wide, 2 * row - 2, 6, height, width)

    def double(t, carry):
        rows = pl.ds(aligned(t, size), size)
        first = jnp.concatenate([acc[0, rows, :], acc[1, rows, 0:128]], axis=1)
        second = jnp.concatenate([acc[1, rows, 128:256], acc[2, rows, :]], axis=1)
        store(de, do, 2 * t, first * mask_low, 6, wide)
        store(de, do, 2 * t + 1, second * mask_low, 6, wide)
        return carry

    lax.fori_loop(0, frames, double, 0)


    for f in range(2):
        store(*planes_three[0], f, cached(4, 4, 4, 2, f), 8, wide)
        store(*planes_four[0], f, cached(8, 12, 4, 1, f), 6, wide)
    gain3, gain4 = gains[2:3, :], gains[3:4, :]
    mask_three = line_mask(place, wide, 4 * row - 2, 8, 2 * height, width)
    mask_four = mask_three[wide : 7 * wide]
    part = 4 * wide

    def enlarge(group, n):
        first, last = groups[group]
        lanes = slice(n * LANES, (n + 1) * LANES)
        rows = (last - first) * part
        for py in range(2):
            left = jnp.concatenate(
                [
                    taps(de, do, first, last - first, 6, wide, 0, py),
                    taps(de, do, first, last - first, 6, wide, 0, py + 1),
                ],
                axis=1,
            )
            ups[group][n, py * rows : (py + 1) * rows, :] = transposed_dot(left, wu[py, lanes, :])

    def norm_three(group, f):
        first, last = groups[group]
        values = [
            high_sum(ups[group], aligned(f + py * (last - first), part), part)
            .astype(BF16)
            .astype(F32)
            for py in range(2)
        ]
        lifted = jnp.concatenate(
            [values[h % 2][(h // 2) * wide : (h // 2 + 1) * wide] for h in range(8)], axis=0
        )
        lifted_ref[pl.ds(aligned(f + first, part), part), :] = lifted[2 * wide : 6 * wide]
        slot = f + (2 if group == 0 else 0)
        store(*planes_three[group], slot, activate_pairs(lifted, gain3, mask_three), 8, wide)

    def norm_four(group, f):
        values = high_sum(threes[group], aligned(f, size), size)
        slot = f + (2 if group == 0 else 0)
        store(*planes_four[group], slot, activate_pairs(values, gain4, mask_four), 6, wide)

    def finish(group, f):
        first = groups[group][0]
        rows = pl.ds(aligned(f + first, part), part)
        values = high_sum(fours[group], aligned(f, part), part) + lifted_ref[rows, :]
        values = pltpu.roll(values, part - HALO, 0)
        for y in range(4):
            inner = wide - 2 * HALO
            out_ref[f + first, y] = values[y * wide : y * wide + inner].astype(BF16)

    def third(group, n):
        high_column(n, threes[group], planes_three, groups, group, 8, wide, w3)

    def fourth(group, n):
        high_column(n, fours[group], planes_four, groups, group, 6, wide, w4)

    for product, vector in (
        ((enlarge, 0), None),
        ((enlarge, 1), (norm_three, 0)),
        ((enlarge, 2), (norm_three, 1)),
        ((third, 0), (norm_three, 2)),
        ((third, 1), (norm_four, 0)),
        ((third, 2), (norm_four, 1)),
        ((fourth, 0), (norm_four, 2)),
        ((fourth, 1), (finish, 0)),
        ((fourth, 2), (finish, 1)),
        (None, (finish, 2)),
    ):
        if product in ((third, 0), (fourth, 0)):
            copies[0 if product[0] is third else 1].wait()
        for n in range(max(2 * channels // LANES, *(last - first for first, last in groups))):
            if product is not None and n < 2 * channels // LANES:
                product[0](product[1], n)
            if vector is not None and n < groups[vector[1]][1] - groups[vector[1]][0]:
                vector[0](vector[1], n)


def second_block(place, pieces, tiles, gains, weights, sizes, wide):
    frames, _, channels = pieces[0].shape
    count = 2 * frames
    groups = split_frames(count)
    sizes_of = [last - first for first, last in groups]
    slots = [last - first for first, last in (group_slots(g, groups) for g in range(3))]
    vmem = pl.BlockSpec(memory_space=pltpu.VMEM)
    return pl.pallas_call(
        functools.partial(second_kernel, wide, sizes),
        out_shape=jax.ShapeDtypeStruct((count, 4, wide - 2 * HALO, channels), BF16),
        in_specs=[pl.BlockSpec(memory_space=pltpu.SMEM)]
        + [vmem] * 9
        + [pl.BlockSpec(memory_space=pl.ANY)] * 2,
        out_specs=vmem,
        scratch_shapes=[
            pltpu.VMEM(weights[2].shape, BF16),
            pltpu.VMEM(weights[3].shape, BF16),
            pltpu.SemaphoreType.DMA((2,)),
            pltpu.VMEM((3, frames * 6 * wide, LANES), F32),
            pltpu.VMEM(((frames + 2) * 6 * wide, channels), BF16),
            *planes(count, 6, wide, channels),
            pltpu.VMEM((count * 4 * wide, channels), F32),
            *(pltpu.VMEM((3, n * 8 * wide, LANES), F32) for n in sizes_of),
            *(pltpu.VMEM((3, n * 6 * wide, LANES), F32) for n in sizes_of),
            *(pltpu.VMEM((3, n * 4 * wide, LANES), F32) for n in sizes_of),
            *(ref for n in slots for ref in planes(n, 8, wide, channels)),
            *(ref for n in slots for ref in planes(n, 6, wide, channels)),
        ],
        compiler_params=pltpu.CompilerParams(vmem_limit_bytes=50 * 1024 * 1024),
        name="second_block",
    )(place, *pieces, *tiles, gains, *weights)


def body(
    latent,
    cache_one,
    cache_two,
    cache_time,
    cache_three,
    cache_four,
    gain_one,
    gain_two,
    gain_three,
    gain_four,
    weight_one,
    weight_two,
    weight_time,
    weight_upsample,
    weight_three,
    weight_four,
):
    section, row, col = (lax.axis_index(name) for name in ("section", "rows", "cols"))
    sections, row_count, col_count = (lax.axis_size(name) for name in ("section", "rows", "cols"))
    width, channels = latent.shape[2:]
    tile = width // col_count
    part = tile // sections
    wide = part + 2 * HALO
    half = weight_three.shape[1]
    sizes = (2 * row_count, width)
    place = jnp.stack([section, col, col * tile + section * part - HALO, row]).astype(jnp.int32)

    gains = jnp.stack([gain_one, gain_two, jnp.tile(gain_three, 2), jnp.tile(gain_four, 2)])

    latent = latent.reshape(latent.shape[0], width, channels)
    arrived = swapped(latent, "section")
    mine, theirs, tiles = pack(
        place,
        latent,
        arrived,
        cache_one[:, 0],
        cache_two[:, 0],
        cache_time,
        cache_three,
        cache_four,
        wide,
        tile,
        part,
    )
    weight_three, mine = lax.optimization_barrier((weight_three, mine))
    weight_three = align_weights(weight_three)
    own, near, far, windows, tile_near, tile_far = stack(
        place, mine, swapped(theirs, "cols"), tiles, weight_three
    )
    far = paired(far, "rows", 1)
    near = paired(near, "rows", 0)
    tile_far = paired(tile_far, "rows", 1)
    tile_near = paired(tile_near, "rows", 0)
    weight_upsample, weight_four, own = lax.optimization_barrier(
        (weight_upsample, weight_four, own)
    )
    weight_upsample = combine_weights(weight_upsample)
    weight_four = align_weights(weight_four)
    blocked = first_block(
        place,
        [near, own, far],
        gains,
        weight_one.reshape(9, 3, channels, channels),
        weight_two.reshape(9, 3, channels, channels),
        (weight_upsample, weight_four),
        sizes,
    )
    far = paired(blocked, "rows", 1)
    near = paired(blocked, "rows", 0)
    blocks = [near, blocked, far]
    tiles = [tile_near, windows, tile_far]
    frames = second_block(
        place,
        blocks,
        tiles,
        gains,
        (weight_time, weight_upsample, weight_three, weight_four),
        sizes,
        wide,
    )
    count = frames.shape[0] // sections
    given = lax.dynamic_slice_in_dim(frames, (1 - section) * count, count, 0)
    kept = lax.dynamic_slice_in_dim(frames, section * count, count, 0)
    arrived = swapped(given, "section")
    low = section == 0
    joined = jnp.concatenate(
        [jnp.where(low, kept, arrived), jnp.where(low, arrived, kept)], axis=2
    )
    return joined.reshape(count, 4, 2 * tile, half)


def solution(mesh):
    placed = (
        P("section", ("rows", "cols"), None, None),
        P(None, ("rows", "cols"), None, None),
        P(None, ("rows", "cols"), None, None),
        P(None, "rows", "cols", None),
        P(None, "rows", "cols", None),
        P(None, "rows", "cols", None),
    ) + (P(),) * 10
    return jax.shard_map(
        body,
        mesh=mesh,
        in_specs=placed,
        out_specs=P("section", "rows", "cols", None),
        check_vma=False,
    )
```

```python
import functools

import jax
import jax.numpy as jnp
from jax import lax
from jax.experimental import pallas as pl
from jax.experimental.pallas import tpu as pltpu
from jax.sharding import PartitionSpec as P

EPSILON = 1e-06
HALO = 4
LANES = 256
BF16 = jnp.bfloat16
F32 = jnp.float32


def swapped(value, axis):
    return lax.ppermute(value, axis, [(0, 1), (1, 0)])


def paired(value, axis, first):
    pairs = [(i, i + 1) for i in range(first, lax.axis_size(axis) - 1, 2)]
    return lax.ppermute(value, axis, pairs + [(high, low) for low, high in pairs])


def silu(scaled):
    half = scaled * 0.5
    return half * (1.0 + jnp.tanh(half))


def activate(values, gain, mask):
    mean = jnp.mean(values * values, axis=-1, keepdims=True)
    return silu(values * (lax.rsqrt(mean + EPSILON) * mask) * gain)


def activate_pairs(values, gain, mask):
    channels = values.shape[-1] // 2
    squares = values * values
    first = lax.broadcasted_iota(jnp.int32, (1, 2 * channels), 1) < channels
    total = jnp.sum(squares, axis=-1, keepdims=True)
    low = jnp.sum(jnp.where(first, squares, 0.0), axis=-1, keepdims=True)
    scale_low = lax.rsqrt(low / channels + EPSILON) * mask
    scale_high = lax.rsqrt((total - low) / channels + EPSILON) * mask
    return silu(values * jnp.where(first, scale_low, scale_high) * gain)


def merge(even, odd, channels):
    turned = pltpu.roll(odd, channels - 128, 1)
    first = lax.broadcasted_iota(jnp.int32, (1, 128), 1) < channels - 128
    middle = jnp.where(first, even[:, 128:], turned[:, :128])
    return jnp.concatenate([even[:, :128], middle, turned[:, 128:]], axis=1)


def aligned(index, size):
    return index * size if isinstance(index, int) else pl.multiple_of(index * size, 16)


def line_mask(place, wide, first, count, limit, width):
    columns = place[2] + lax.broadcasted_iota(jnp.int32, (wide, 1), 0)
    inside = jnp.where((columns >= 0) & (columns < width), 1.0, 0.0)
    lines = []
    for i in range(count):
        line = first + i
        lines.append(inside * jnp.where((line >= 0) & (line < limit), 1.0, 0.0))
    return jnp.concatenate(lines, axis=0)


def store(even, odd, slot, values, height, wide):
    even[pl.ds(slot * (height * wide), height * wide), :] = values.astype(BF16)
    odd[pl.ds(slot * ((height - 2) * wide), (height - 2) * wide), :] = values[
        wide : (height - 1) * wide
    ].astype(BF16)


def taps(even, odd, begin, count, height, wide, dt, dy, lanes=slice(None)):
    inner = (height - 2) * wide
    if dy == 1:
        parts = [odd[pl.ds((begin + f + dt) * inner, inner), lanes] for f in range(count)]
    else:
        parts = [
            even[pl.ds((begin + f + dt) * height * wide + dy * wide, inner), lanes]
            for f in range(count)
        ]
    return jnp.concatenate(parts, axis=0)


def low_product(acc, even, odd, count, height, wide, weights, copies, following):
    rows = count * (height - 2) * wide
    channels = weights.shape[1]
    lanes = 3 * channels
    waited = 0
    for n in range(-(-lanes // LANES)):
        begin, end = n * LANES, min((n + 1) * LANES, lanes)
        while waited * channels < end:
            copies[waited].wait()
            if waited < len(following):
                following[waited].start()
            waited += 1
        left = jnp.concatenate(
            [taps(even, odd, 0, count, height, wide, t // 3, t % 3) for t in range(9)], axis=1
        )
        right = weights[:, :, begin:end].reshape(9 * channels, end - begin)
        acc[n, 0:rows, 0 : end - begin] = jnp.dot(left, right, preferred_element_type=F32)


def low_sum(acc, start, size):
    rows = pl.ds(start, size)
    before = jnp.concatenate([acc[0, rows, :], acc[1, rows, 0:128]], axis=1)
    center = jnp.concatenate([acc[1, rows, 128:256], acc[2, rows, :]], axis=1)
    after = jnp.concatenate([acc[3, rows, :], acc[4, rows, 0:128]], axis=1)
    return center + pltpu.roll(before, 1, 0) + pltpu.roll(after, size - 1, 0)


def transposed_dot(left, right):
    return lax.dot_general(left, right, (((1,), (1,)), ((), ())), preferred_element_type=F32)


def split_frames(count):
    first = count // 4
    second = first + (count - first) // 2
    return (0, first), (first, second), (second, count)


def group_slots(group, groups):
    first, last = groups[group]
    return (0 if group == 0 else first + 2), last + 2


def grouped_taps(planes, groups, frames, height, wide, dt, dy):
    inner = (height - 2) * wide
    parts = []
    for f in frames:
        for group, (even, odd) in enumerate(planes):
            first, last = group_slots(group, groups)
            if first <= f + dt < last:
                slot = f + dt - first
                if dy == 1:
                    parts.append(odd[slot * inner : (slot + 1) * inner, :])
                else:
                    begin = slot * height * wide + dy * wide
                    parts.append(even[begin : begin + inner, :])
    return jnp.concatenate(parts, axis=0)


def high_column(n, acc, planes, groups, group, height, wide, weights):
    left = jnp.concatenate(
        [
            grouped_taps(planes, groups, range(*groups[group]), height, wide, t // 3, t % 3)
            for t in range(9)
        ],
        axis=1,
    )
    acc[n] = transposed_dot(left, weights[n * LANES : (n + 1) * LANES, :])


def high_sum(acc, start, size):
    rows = pl.ds(start, size)
    center = jnp.concatenate([acc[0, rows, :], acc[1, rows, 0:128]], axis=1)
    side = jnp.concatenate([acc[1, rows, 128:256], acc[2, rows, :]], axis=1)
    channels = center.shape[1]
    first = lax.broadcasted_iota(jnp.int32, (1, channels), 1) < channels // 2
    return center + jnp.where(first, pltpu.roll(side, 1, 0), pltpu.roll(side, size - 1, 0))


def pack_kernel(
    wide,
    tile,
    part,
    place,
    latent,
    arrived,
    one,
    two,
    time,
    three,
    four,
    mine,
    theirs,
    tiles,
    spread,
    low,
    high,
):
    section, col = place[0], place[1]
    width, channels = latent.shape[1:]
    half = three.shape[-1]
    empty = jnp.zeros((spread.shape[1] - width, channels), F32)

    def put(slot, values):
        spread[slot] = pltpu.roll(
            jnp.concatenate([values.astype(F32), empty], axis=0), HALO, 0
        )

    for i in range(2):
        put(2 * section + i, latent[i])
        put(2 * (1 - section) + i, arrived[i])
        put(4 + i, one[i])
        put(6 + i, two[i])
    for slot in range(8):
        for ref, which in ((mine, col), (theirs, 1 - col)):
            begin = pl.multiple_of(which * tile + section * part, 8)
            ref[slot] = spread[slot, pl.ds(begin, wide), :].astype(BF16)

    lines = [time[f, y].astype(F32) for f in range(2) for y in range(2)]
    for ref in (three, four):
        for f in range(2):
            for y in range(4):
                values = ref[f, y].astype(F32)
                low[...] = values[:, :128]
                high[:, 0 : half - 128] = values[:, 128:]
                count = values.shape[0] // 2
                even, odd = (
                    jnp.concatenate(
                        [lanes[pl.ds(o, count, stride=2), :] for lanes in (low, high)], axis=1
                    )
                    for o in range(2)
                )
                lines.append(merge(even, odd, half))
    for i, line in enumerate(lines):
        tiles[i] = line.astype(BF16)

    left = col == 0
    upper = lax.broadcasted_iota(jnp.int32, (8, 1), 0) < HALO
    blocks = []
    for i in range(0, len(lines), 2):
        one_line, two_line = lines[i], lines[i + 1]
        last = jnp.where(upper, pltpu.roll(one_line[-8:], HALO, 0), two_line[-8:])
        first = jnp.where(upper, one_line[:8], pltpu.roll(two_line[:8], HALO, 0))
        blocks.append(jnp.where(left, last, first))
    gap = jnp.zeros_like(blocks[0])
    count = wide // 8
    for i in range(theirs.shape[0] - 8):
        group = (blocks + [gap] * count)[i * count : (i + 1) * count]
        theirs[8 + i] = jnp.concatenate(group, axis=0).astype(BF16)


def pack(place, latent, arrived, one, two, time, three, four, wide, tile, part):
    width, channels = latent.shape[1:]
    vmem = pl.BlockSpec(memory_space=pltpu.VMEM)
    lines = 20
    extra = -(-lines * HALO // wide)
    return pl.pallas_call(
        functools.partial(pack_kernel, wide, tile, part),
        out_shape=[
            jax.ShapeDtypeStruct((8, wide, channels), BF16),
            jax.ShapeDtypeStruct((8 + extra, wide, channels), BF16),
            jax.ShapeDtypeStruct((lines, tile, channels), BF16),
        ],
        in_specs=[pl.BlockSpec(memory_space=pltpu.SMEM)] + [vmem] * 7,
        out_specs=[vmem] * 3,
        scratch_shapes=[
            pltpu.VMEM((8, width + 16, channels), F32),
            pltpu.VMEM((three.shape[2], 128), F32),
            pltpu.VMEM((three.shape[2], 128), F32),
        ],
        compiler_params=pltpu.CompilerParams(vmem_limit_bytes=60 * 1024 * 1024),
        name="pack",
    )(place, latent, arrived, one, two, time, three, four)


def stack_kernel(
    wide, place, mine, theirs, tiles, later, own, near, far, windows, tile_near, tile_far
):
    del later
    section, col = place[0], place[1]
    count = mine.shape[0] - 2
    own[0], own[1] = mine[...], theirs[0 : count + 2]
    parity = lax.rem(place[3], 2)
    for ref, y in ((near, 1 - parity), (far, parity)):
        ref[0:count], ref[count : 2 * count] = mine[0:count], theirs[0:count]
        here = lax.rem(y + col, 2) == 0
        ref[2 * count :] = jnp.where(here, mine[count:], theirs[count : count + 2])

    part = wide - 2 * HALO
    upper = lax.broadcasted_iota(jnp.int32, (8, 1), 0) < HALO
    groups = wide // 8
    for i in range(tiles.shape[0]):
        line = tiles[i].astype(F32)
        block = i // 2
        begin = block % groups * 8
        edge = theirs[count + 2 + block // groups].astype(F32)[begin : begin + 8]
        turned = pltpu.roll(edge, HALO, 0)
        before, after = (edge, turned) if i % 2 == 0 else (turned, edge)
        first = pltpu.roll(line, HALO, 0)[:wide]
        head = jnp.where(upper, jnp.where(col == 1, before, 0.0), first[:8])
        first = jnp.concatenate([head, first[8:]], axis=0)
        last = pltpu.roll(line, line.shape[0] - (part - HALO), 0)[:wide]
        tail = jnp.where(upper, last[-8:], jnp.where(col == 0, after, 0.0))
        last = jnp.concatenate([last[:-8], tail], axis=0)
        line = jnp.where(section == 0, first, last).astype(BF16)
        windows[i] = line
    is_even = parity == 0
    for base, start, count, depth in ((0, 0, 2, 2), (4, 4, 4, 2), (12, 8, 4, 1)):
        for f in range(2):
            for j in range(depth):
                slot = start + depth * f + j
                high = windows[base + count * f + j]
                low = windows[base + count * f + count - depth + j]
                tile_near[slot] = jnp.where(is_even, low, high)
                tile_far[slot] = jnp.where(is_even, high, low)


def stack(place, mine, theirs, tiles, later):
    units, wide, channels = mine.shape
    vmem = pl.BlockSpec(memory_space=pltpu.VMEM)
    lines = 2 * units - 2
    shapes = [(2, units), (lines,), (lines,), (tiles.shape[0],), (10,), (10,)]
    return pl.pallas_call(
        functools.partial(stack_kernel, wide),
        out_shape=[jax.ShapeDtypeStruct(shape + (wide, channels), BF16) for shape in shapes],
        in_specs=[pl.BlockSpec(memory_space=pltpu.SMEM)]
        + [vmem] * 3
        + [pl.BlockSpec(memory_space=pl.ANY)],
        out_specs=[vmem] * 6,
        compiler_params=pltpu.CompilerParams(vmem_limit_bytes=8 * 1024 * 1024),
        name="stack",
    )(place, mine, theirs, tiles, later)


def align_kernel(weight, out):
    half = weight.shape[0]
    chunk = 16
    tail = half - 128
    low = lax.broadcasted_iota(jnp.int32, (1, 128), 1) < tail

    def move(k, carry):
        here = aligned(k, chunk)
        none = jnp.zeros((chunk, 128), F32)
        for t in range(9):
            base = 3 * t * half
            first = base // 128 * 128
            last = min(first + 640, weight.shape[1])
            values = weight[pl.ds(here, chunk), first:last].astype(F32)
            if last < first + 640:
                values = jnp.concatenate(
                    [values[:, :512], jnp.concatenate([values[:, 512:], none[:, tail:]], axis=1)],
                    axis=1,
                )
            turned = pltpu.roll(values, 640 - tail, 1)
            tiles = [values[:, 128 * i : 128 * (i + 1)] for i in range(5)]
            moved = [turned[:, 128 * i : 128 * (i + 1)] for i in range(5)]
            if base == first:
                blocks = (
                    moved[1:4],
                    tiles[0:3],
                    [none, jnp.where(low, 0.0, moved[4]), moved[0]],
                    [tiles[3], jnp.where(low, tiles[4], 0.0), none],
                )
            else:
                blocks = (
                    tiles[2:5],
                    moved[0:3],
                    [none, jnp.where(low, 0.0, tiles[0]), tiles[1]],
                    [moved[3], jnp.where(low, moved[4], 0.0), none],
                )
            for n, block in enumerate(blocks):
                into = pl.ds(here + n * half, chunk)
                out[into, 2 * half * t : 2 * half * (t + 1)] = jnp.concatenate(
                    block, axis=1
                ).astype(BF16)
        return carry

    lax.fori_loop(0, half // chunk, move, 0)


def align_weights(weight):
    half = weight.shape[1]
    vmem = pl.BlockSpec(memory_space=pltpu.VMEM)
    return pl.pallas_call(
        align_kernel,
        out_shape=jax.ShapeDtypeStruct((4 * half, 18 * half), BF16),
        in_specs=[vmem],
        out_specs=vmem,
        compiler_params=pltpu.CompilerParams(vmem_limit_bytes=8 * 1024 * 1024),
        name="align_weights",
    )(weight.T)


def combine_kernel(weight, out):
    half = weight.shape[0]
    channels = weight.shape[1] // 9
    chunk = 16

    def combine(k, carry):
        rows = pl.ds(aligned(k, chunk), chunk)
        taken = [
            [
                weight[rows, (3 * dy + dx) * channels : (3 * dy + dx + 1) * channels].astype(F32)
                for dx in range(3)
            ]
            for dy in range(3)
        ]
        for slot, dys in enumerate(((0,), (1, 2), (0, 1), (2,))):
            line = [sum(taken[dy][dx] for dy in dys) for dx in range(3)]
            lanes = slice(slot % 2 * channels, (slot % 2 + 1) * channels)
            for n, block in enumerate((line[1] + line[2], line[0] + line[1], line[0], line[2])):
                into = pl.ds(aligned(k, chunk) + n * half, chunk)
                out[slot // 2, into, lanes] = block.astype(BF16)
        return carry

    lax.fori_loop(0, half // chunk, combine, 0)


def combine_weights(weight):
    channels = 2 * weight.shape[1]
    vmem = pl.BlockSpec(memory_space=pltpu.VMEM)
    return pl.pallas_call(
        combine_kernel,
        out_shape=jax.ShapeDtypeStruct((2, 2 * channels, 2 * channels), BF16),
        in_specs=[vmem],
        out_specs=vmem,
        compiler_params=pltpu.CompilerParams(vmem_limit_bytes=8 * 1024 * 1024),
        name="combine_weights",
    )(weight.T)


def weight_copies(source, target, sems, base):
    channels = source.shape[-1]
    return [
        pltpu.make_async_copy(
            source.at[:, dx], target.at[:, :, pl.ds(dx * channels, channels)], sems.at[base + dx]
        )
        for dx in range(3)
    ]


def first_kernel(
    wide,
    sizes,
    place,
    near,
    own,
    far,
    gains,
    weight_one,
    weight_two,
    later_one,
    later_two,
    out_ref,
    w1,
    w2,
    acc,
    acc_two,
    x1e,
    x1o,
    x2e,
    x2o,
    sems,
):
    channels = own.shape[-1]
    frames = own.shape[1] - 4
    height, width = sizes
    col, row = place[1], place[3]
    units = frames + 2
    del later_one, later_two

    copies_one = weight_copies(weight_one, w1, sems, 0)
    copies_two = weight_copies(weight_two, w2, sems, 3)
    copies_one[0].start()

    slots = [lax.rem(y + col, 2) for y in range(2)]

    is_even = lax.rem(row, 2) == 0

    def own_rows(index):
        return [own[slot, index].astype(F32) for slot in slots]

    def above(line):
        return jnp.where(is_even, far[line].astype(F32), near[line].astype(F32))

    def below(line):
        return jnp.where(is_even, near[line].astype(F32), far[line].astype(F32))

    def rows_of(index):
        first = [above(slot * units + index) for slot in slots]
        last = [below(slot * units + index) for slot in slots]
        return jnp.concatenate(first + own_rows(index) + last, axis=0)

    for f in range(2):
        store(x1e, x1o, f, rows_of(frames + f), 6, wide)
        first, last = above(2 * units + f), below(2 * units + f)
        values = jnp.concatenate([first] + own_rows(units + f) + [last], axis=0)
        store(x2e, x2o, f, values, 4, wide)

    copies_one[1].start()
    for f in range(frames):
        store(x1e, x1o, f + 2, activate(rows_of(f), gains[0:1, :], 1.0), 6, wide)
    low_product(
        acc, x1e, x1o, frames, 6, wide, w1, copies_one, [copies_one[2]] + copies_two[:2]
    )
    copies_two[2].start()

    mask = line_mask(place, wide, 2 * row - 1, 4, height, width)
    for f in range(frames):
        size = 4 * wide
        values = activate(low_sum(acc, f * size, size), gains[1:2, :], mask)
        store(x2e, x2o, f + 2, values, 4, wide)
    low_product(acc_two, x2e, x2o, frames, 4, wide, w2, copies_two, [])
    for f in range(frames):
        size = 2 * wide
        values = low_sum(acc_two, f * size, size) + jnp.concatenate(own_rows(f), axis=0)
        out_ref[f] = values.astype(BF16)


def planes(slots, height, wide, channels):
    return [
        pltpu.VMEM((slots * height * wide, channels), BF16),
        pltpu.VMEM((slots * (height - 2) * wide, channels), BF16),
    ]


def first_block(place, pieces, gains, weight_one, weight_two, later, sizes):
    _, units, wide, channels = pieces[1].shape
    frames = units - 4
    slots = -(-3 * channels // LANES)
    vmem = pl.BlockSpec(memory_space=pltpu.VMEM)
    anywhere = pl.BlockSpec(memory_space=pl.ANY)
    return pl.pallas_call(
        functools.partial(first_kernel, wide, sizes),
        out_shape=jax.ShapeDtypeStruct((frames, 2 * wide, channels), BF16),
        in_specs=[pl.BlockSpec(memory_space=pltpu.SMEM)]
        + [vmem] * 4
        + [pl.BlockSpec(memory_space=pltpu.HBM)] * 2
        + [anywhere] * 2,
        out_specs=vmem,
        scratch_shapes=[
            pltpu.VMEM((9, channels, slots * LANES), BF16),
            pltpu.VMEM((9, channels, slots * LANES), BF16),
            pltpu.VMEM((slots, frames * 4 * wide, LANES), F32),
            pltpu.VMEM((slots, frames * 2 * wide, LANES), F32),
            *planes(frames + 2, 6, wide, channels),
            *planes(frames + 2, 4, wide, channels),
            pltpu.SemaphoreType.DMA((6,)),
        ],
        compiler_params=pltpu.CompilerParams(vmem_limit_bytes=50 * 1024 * 1024),
        cost_estimate=pl.CostEstimate(
            flops=2 * 27 * channels * channels * frames * 6 * wide,
            bytes_accessed=2 * 54 * channels * channels,
            transcendentals=0,
        ),
        name="first_block",
    )(place, *pieces, gains, weight_one, weight_two, *later)


def second_kernel(
    wide,
    sizes,
    place,
    near,
    blocked,
    far,
    tile_near,
    windows,
    tile_far,
    gains,
    wt,
    wu,
    weight_three,
    weight_four,
    out_ref,
    w3,
    w4,
    sems,
    acc,
    mixed,
    de,
    do,
    lifted_ref,
    *buffers,
):
    ups, threes, fours = buffers[0:3], buffers[3:6], buffers[6:9]
    planes_three = [buffers[9 + 2 * g : 11 + 2 * g] for g in range(3)]
    planes_four = [buffers[15 + 2 * g : 17 + 2 * g] for g in range(3)]
    copies = [
        pltpu.make_async_copy(source, target, sems.at[i])
        for i, (source, target) in enumerate(((weight_three, w3), (weight_four, w4)))
    ]
    copies[0].start()
    channels = blocked.shape[-1]
    half = channels // 2
    size = 6 * wide
    frames = blocked.shape[0]
    count = 2 * frames
    groups = split_frames(count)
    height, width = sizes
    row = place[3]

    is_even = lax.rem(row, 2) == 0

    def chosen(when, one, other, index):
        return jnp.where(when, one[index].astype(F32), other[index].astype(F32))

    def cached(start, base, lines, depth, f):
        slots = [start + depth * f + i for i in range(depth)]
        parts = [chosen(is_even, tile_far, tile_near, slot) for slot in slots]
        parts += [windows[base + lines * f + i].astype(F32) for i in range(lines)]
        parts += [chosen(is_even, tile_near, tile_far, slot) for slot in slots]
        return jnp.concatenate(parts, axis=0)

    for f in range(2):
        mixed[f * size : (f + 1) * size, :] = cached(0, 0, 2, 2, f).astype(BF16)
    for f in range(frames):
        first, last = chosen(is_even, far, near, f), chosen(is_even, near, far, f)
        for i, values in enumerate((first.astype(BF16), blocked[f], last.astype(BF16))):
            begin = (f + 2) * size + i * 2 * wide
            mixed[begin : begin + 2 * wide, :] = values


    def mix(n, carry):
        lanes = pl.ds(pl.multiple_of(n * LANES, LANES), LANES)
        left = jnp.concatenate(
            [mixed[pl.ds(t * size, frames * size), :] for t in range(3)], axis=1
        )
        acc[n, 0 : frames * size, :] = jnp.dot(left, wt[:, lanes], preferred_element_type=F32)
        return carry

    lax.fori_loop(0, 2 * channels // LANES, mix, 0)
    mask_low = line_mask(place, wide, 2 * row - 2, 6, height, width)

    def double(t, carry):
        rows = pl.ds(aligned(t, size), size)
        first = jnp.concatenate([acc[0, rows, :], acc[1, rows, 0:128]], axis=1)
        second = jnp.concatenate([acc[1, rows, 128:256], acc[2, rows, :]], axis=1)
        store(de, do, 2 * t, first * mask_low, 6, wide)
        store(de, do, 2 * t + 1, second * mask_low, 6, wide)
        return carry

    lax.fori_loop(0, frames, double, 0)


    for f in range(2):
        store(*planes_three[0], f, cached(4, 4, 4, 2, f), 8, wide)
        store(*planes_four[0], f, cached(8, 12, 4, 1, f), 6, wide)
    gain3, gain4 = gains[2:3, :], gains[3:4, :]
    mask_three = line_mask(place, wide, 4 * row - 2, 8, 2 * height, width)
    mask_four = mask_three[wide : 7 * wide]
    part = 4 * wide

    def enlarge(group, n):
        first, last = groups[group]
        lanes = slice(n * LANES, (n + 1) * LANES)
        rows = (last - first) * part
        for py in range(2):
            left = jnp.concatenate(
                [
                    taps(de, do, first, last - first, 6, wide, 0, py),
                    taps(de, do, first, last - first, 6, wide, 0, py + 1),
                ],
                axis=1,
            )
            ups[group][n, py * rows : (py + 1) * rows, :] = transposed_dot(left, wu[py, lanes, :])

    def norm_three(group, f):
        first, last = groups[group]
        values = [
            high_sum(ups[group], aligned(f + py * (last - first), part), part)
            .astype(BF16)
            .astype(F32)
            for py in range(2)
        ]
        lifted = jnp.concatenate(
            [values[h % 2][(h // 2) * wide : (h // 2 + 1) * wide] for h in range(8)], axis=0
        )
        lifted_ref[pl.ds(aligned(f + first, part), part), :] = lifted[2 * wide : 6 * wide]
        slot = f + (2 if group == 0 else 0)
        store(*planes_three[group], slot, activate_pairs(lifted, gain3, mask_three), 8, wide)

    def norm_four(group, f):
        values = high_sum(threes[group], aligned(f, size), size)
        slot = f + (2 if group == 0 else 0)
        store(*planes_four[group], slot, activate_pairs(values, gain4, mask_four), 6, wide)

    def finish(group, f):
        first = groups[group][0]
        rows = pl.ds(aligned(f + first, part), part)
        values = high_sum(fours[group], aligned(f, part), part) + lifted_ref[rows, :]
        values = pltpu.roll(values, part - HALO, 0)
        for y in range(4):
            inner = wide - 2 * HALO
            out_ref[f + first, y] = values[y * wide : y * wide + inner].astype(BF16)

    def third(group, n):
        high_column(n, threes[group], planes_three, groups, group, 8, wide, w3)

    def fourth(group, n):
        high_column(n, fours[group], planes_four, groups, group, 6, wide, w4)

    for product, vector in (
        ((enlarge, 0), None),
        ((enlarge, 1), (norm_three, 0)),
        ((enlarge, 2), (norm_three, 1)),
        ((third, 0), (norm_three, 2)),
        ((third, 1), (norm_four, 0)),
        ((third, 2), (norm_four, 1)),
        ((fourth, 0), (norm_four, 2)),
        ((fourth, 1), (finish, 0)),
        ((fourth, 2), (finish, 1)),
        (None, (finish, 2)),
    ):
        if product == (third, 0):
            copies[0].wait()
            copies[1].start()
        if product == (fourth, 0):
            copies[1].wait()
        for n in range(max(2 * channels // LANES, *(last - first for first, last in groups))):
            if product is not None and n < 2 * channels // LANES:
                product[0](product[1], n)
            if vector is not None and n < groups[vector[1]][1] - groups[vector[1]][0]:
                vector[0](vector[1], n)


def second_block(place, pieces, tiles, gains, weights, sizes, wide):
    frames, _, channels = pieces[0].shape
    count = 2 * frames
    groups = split_frames(count)
    sizes_of = [last - first for first, last in groups]
    slots = [last - first for first, last in (group_slots(g, groups) for g in range(3))]
    vmem = pl.BlockSpec(memory_space=pltpu.VMEM)
    return pl.pallas_call(
        functools.partial(second_kernel, wide, sizes),
        out_shape=jax.ShapeDtypeStruct((count, 4, wide - 2 * HALO, channels), BF16),
        in_specs=[pl.BlockSpec(memory_space=pltpu.SMEM)]
        + [vmem] * 9
        + [pl.BlockSpec(memory_space=pl.ANY)] * 2,
        out_specs=vmem,
        scratch_shapes=[
            pltpu.VMEM(weights[2].shape, BF16),
            pltpu.VMEM(weights[3].shape, BF16),
            pltpu.SemaphoreType.DMA((2,)),
            pltpu.VMEM((3, frames * 6 * wide, LANES), F32),
            pltpu.VMEM(((frames + 2) * 6 * wide, channels), BF16),
            *planes(count, 6, wide, channels),
            pltpu.VMEM((count * 4 * wide, channels), F32),
            *(pltpu.VMEM((3, n * 8 * wide, LANES), F32) for n in sizes_of),
            *(pltpu.VMEM((3, n * 6 * wide, LANES), F32) for n in sizes_of),
            *(pltpu.VMEM((3, n * 4 * wide, LANES), F32) for n in sizes_of),
            *(ref for n in slots for ref in planes(n, 8, wide, channels)),
            *(ref for n in slots for ref in planes(n, 6, wide, channels)),
        ],
        compiler_params=pltpu.CompilerParams(vmem_limit_bytes=50 * 1024 * 1024),
        name="second_block",
    )(place, *pieces, *tiles, gains, *weights)


def body(
    latent,
    cache_one,
    cache_two,
    cache_time,
    cache_three,
    cache_four,
    gain_one,
    gain_two,
    gain_three,
    gain_four,
    weight_one,
    weight_two,
    weight_time,
    weight_upsample,
    weight_three,
    weight_four,
):
    section, row, col = (lax.axis_index(name) for name in ("section", "rows", "cols"))
    sections, row_count, col_count = (lax.axis_size(name) for name in ("section", "rows", "cols"))
    width, channels = latent.shape[2:]
    tile = width // col_count
    part = tile // sections
    wide = part + 2 * HALO
    half = weight_three.shape[1]
    sizes = (2 * row_count, width)
    place = jnp.stack([section, col, col * tile + section * part - HALO, row]).astype(jnp.int32)

    gains = jnp.stack([gain_one, gain_two, jnp.tile(gain_three, 2), jnp.tile(gain_four, 2)])

    latent = latent.reshape(latent.shape[0], width, channels)
    arrived = swapped(latent, "section")
    mine, theirs, tiles = pack(
        place,
        latent,
        arrived,
        cache_one[:, 0],
        cache_two[:, 0],
        cache_time,
        cache_three,
        cache_four,
        wide,
        tile,
        part,
    )
    weight_three, mine = lax.optimization_barrier((weight_three, mine))
    weight_three = align_weights(weight_three)
    own, near, far, windows, tile_near, tile_far = stack(
        place, mine, swapped(theirs, "cols"), tiles, weight_three
    )
    far = paired(far, "rows", 1)
    near = paired(near, "rows", 0)
    tile_far = paired(tile_far, "rows", 1)
    tile_near = paired(tile_near, "rows", 0)
    weight_upsample, weight_four, own = lax.optimization_barrier(
        (weight_upsample, weight_four, own)
    )
    weight_upsample = combine_weights(weight_upsample)
    weight_four = align_weights(weight_four)
    blocked = first_block(
        place,
        [near, own, far],
        gains,
        weight_one.reshape(9, 3, channels, channels),
        weight_two.reshape(9, 3, channels, channels),
        (weight_upsample, weight_four),
        sizes,
    )
    far = paired(blocked, "rows", 1)
    near = paired(blocked, "rows", 0)
    blocks = [near, blocked, far]
    tiles = [tile_near, windows, tile_far]
    frames = second_block(
        place,
        blocks,
        tiles,
        gains,
        (weight_time, weight_upsample, weight_three, weight_four),
        sizes,
        wide,
    )
    count = frames.shape[0] // sections
    given = lax.dynamic_slice_in_dim(frames, (1 - section) * count, count, 0)
    kept = lax.dynamic_slice_in_dim(frames, section * count, count, 0)
    arrived = swapped(given, "section")
    low = section == 0
    joined = jnp.concatenate(
        [jnp.where(low, kept, arrived), jnp.where(low, arrived, kept)], axis=2
    )
    return joined.reshape(count, 4, 2 * tile, half)


def solution(mesh):
    placed = (
        P("section", ("rows", "cols"), None, None),
        P(None, ("rows", "cols"), None, None),
        P(None, ("rows", "cols"), None, None),
        P(None, "rows", "cols", None),
        P(None, "rows", "cols", None),
        P(None, "rows", "cols", None),
    ) + (P(),) * 10
    return jax.shard_map(
        body,
        mesh=mesh,
        in_specs=placed,
        out_specs=P("section", "rows", "cols", None),
        check_vma=False,
    )
```

```python
import functools

import jax
import jax.numpy as jnp
from jax import lax
from jax.experimental import pallas as pl
from jax.experimental.pallas import tpu as pltpu
from jax.sharding import PartitionSpec as P

EPSILON = 1e-06
HALO = 4
LANES = 256
BF16 = jnp.bfloat16
F32 = jnp.float32


def swapped(value, axis):
    return lax.ppermute(value, axis, [(0, 1), (1, 0)])


def paired(value, axis, first):
    pairs = [(i, i + 1) for i in range(first, lax.axis_size(axis) - 1, 2)]
    return lax.ppermute(value, axis, pairs + [(high, low) for low, high in pairs])


def silu(scaled):
    half = scaled * 0.5
    return half * (1.0 + jnp.tanh(half))


def activate(values, gain, mask):
    mean = jnp.mean(values * values, axis=-1, keepdims=True)
    return silu(values * (lax.rsqrt(mean + EPSILON) * mask) * gain)


def activate_pairs(values, gain, mask):
    channels = values.shape[-1] // 2
    squares = values * values
    first = lax.broadcasted_iota(jnp.int32, (1, 2 * channels), 1) < channels
    total = jnp.sum(squares, axis=-1, keepdims=True)
    low = jnp.sum(jnp.where(first, squares, 0.0), axis=-1, keepdims=True)
    scale_low = lax.rsqrt(low / channels + EPSILON) * mask
    scale_high = lax.rsqrt((total - low) / channels + EPSILON) * mask
    return silu(values * jnp.where(first, scale_low, scale_high) * gain)


def merge(even, odd, channels):
    turned = pltpu.roll(odd, channels - 128, 1)
    first = lax.broadcasted_iota(jnp.int32, (1, 128), 1) < channels - 128
    middle = jnp.where(first, even[:, 128:], turned[:, :128])
    return jnp.concatenate([even[:, :128], middle, turned[:, 128:]], axis=1)


def aligned(index, size):
    return index * size if isinstance(index, int) else pl.multiple_of(index * size, 16)


def line_mask(place, wide, first, count, limit, width):
    columns = place[2] + lax.broadcasted_iota(jnp.int32, (wide, 1), 0)
    inside = jnp.where((columns >= 0) & (columns < width), 1.0, 0.0)
    lines = []
    for i in range(count):
        line = first + i
        lines.append(inside * jnp.where((line >= 0) & (line < limit), 1.0, 0.0))
    return jnp.concatenate(lines, axis=0)


def store(even, odd, slot, values, height, wide):
    even[pl.ds(slot * (height * wide), height * wide), :] = values.astype(BF16)
    odd[pl.ds(slot * ((height - 2) * wide), (height - 2) * wide), :] = values[
        wide : (height - 1) * wide
    ].astype(BF16)


def taps(even, odd, begin, count, height, wide, dt, dy, lanes=slice(None)):
    inner = (height - 2) * wide
    if dy == 1:
        parts = [odd[pl.ds((begin + f + dt) * inner, inner), lanes] for f in range(count)]
    else:
        parts = [
            even[pl.ds((begin + f + dt) * height * wide + dy * wide, inner), lanes]
            for f in range(count)
        ]
    return jnp.concatenate(parts, axis=0)


def low_product(acc, even, odd, count, height, wide, weights, copies, following):
    rows = count * (height - 2) * wide
    channels = weights.shape[1]
    lanes = 3 * channels
    waited = 0
    for n in range(-(-lanes // LANES)):
        begin, end = n * LANES, min((n + 1) * LANES, lanes)
        while waited * channels < end:
            copies[waited].wait()
            if waited < len(following):
                following[waited].start()
            waited += 1
        left = jnp.concatenate(
            [taps(even, odd, 0, count, height, wide, t // 3, t % 3) for t in range(9)], axis=1
        )
        right = weights[:, :, begin:end].reshape(9 * channels, end - begin)
        acc[n, 0:rows, 0 : end - begin] = jnp.dot(left, right, preferred_element_type=F32)


def low_sum(acc, start, size):
    rows = pl.ds(start, size)
    before = jnp.concatenate([acc[0, rows, :], acc[1, rows, 0:128]], axis=1)
    center = jnp.concatenate([acc[1, rows, 128:256], acc[2, rows, :]], axis=1)
    after = jnp.concatenate([acc[3, rows, :], acc[4, rows, 0:128]], axis=1)
    return center + pltpu.roll(before, 1, 0) + pltpu.roll(after, size - 1, 0)


def transposed_dot(left, right):
    return lax.dot_general(left, right, (((1,), (1,)), ((), ())), preferred_element_type=F32)


def split_frames(count):
    first = count // 4
    second = first + (count - first) // 2
    return (0, first), (first, second), (second, count)


def group_slots(group, groups):
    first, last = groups[group]
    return (0 if group == 0 else first + 2), last + 2


def grouped_taps(planes, groups, frames, height, wide, dt, dy):
    inner = (height - 2) * wide
    parts = []
    for f in frames:
        for group, (even, odd) in enumerate(planes):
            first, last = group_slots(group, groups)
            if first <= f + dt < last:
                slot = f + dt - first
                if dy == 1:
                    parts.append(odd[slot * inner : (slot + 1) * inner, :])
                else:
                    begin = slot * height * wide + dy * wide
                    parts.append(even[begin : begin + inner, :])
    return jnp.concatenate(parts, axis=0)


def high_column(n, acc, planes, groups, group, height, wide, weights):
    left = jnp.concatenate(
        [
            grouped_taps(planes, groups, range(*groups[group]), height, wide, t // 3, t % 3)
            for t in range(9)
        ],
        axis=1,
    )
    acc[n] = transposed_dot(left, weights[n * LANES : (n + 1) * LANES, :])


def high_sum(acc, start, size):
    rows = pl.ds(start, size)
    center = jnp.concatenate([acc[0, rows, :], acc[1, rows, 0:128]], axis=1)
    side = jnp.concatenate([acc[1, rows, 128:256], acc[2, rows, :]], axis=1)
    channels = center.shape[1]
    first = lax.broadcasted_iota(jnp.int32, (1, channels), 1) < channels // 2
    return center + jnp.where(first, pltpu.roll(side, 1, 0), pltpu.roll(side, size - 1, 0))


def pack_kernel(
    wide,
    tile,
    part,
    place,
    latent,
    arrived_ref,
    one,
    two,
    time,
    three,
    four,
    mine,
    theirs,
    tiles,
    spread,
    low,
    high,
    arrived,
    sem,
):
    copy = pltpu.make_async_copy(arrived_ref, arrived, sem)
    copy.start()
    section, col = place[0], place[1]
    width, channels = latent.shape[1:]
    half = three.shape[-1]
    empty = jnp.zeros((spread.shape[1] - width, channels), F32)

    def put(slot, values):
        spread[slot] = pltpu.roll(
            jnp.concatenate([values.astype(F32), empty], axis=0), HALO, 0
        )

    lines = [time[f, y].astype(F32) for f in range(2) for y in range(2)]
    for ref in (three, four):
        for f in range(2):
            for y in range(4):
                values = ref[f, y].astype(F32)
                low[...] = values[:, :128]
                high[:, 0 : half - 128] = values[:, 128:]
                count = values.shape[0] // 2
                even, odd = (
                    jnp.concatenate(
                        [lanes[pl.ds(o, count, stride=2), :] for lanes in (low, high)], axis=1
                    )
                    for o in range(2)
                )
                lines.append(merge(even, odd, half))
    for i, line in enumerate(lines):
        tiles[i] = line.astype(BF16)

    left = col == 0
    upper = lax.broadcasted_iota(jnp.int32, (8, 1), 0) < HALO
    blocks = []
    for i in range(0, len(lines), 2):
        one_line, two_line = lines[i], lines[i + 1]
        last = jnp.where(upper, pltpu.roll(one_line[-8:], HALO, 0), two_line[-8:])
        first = jnp.where(upper, one_line[:8], pltpu.roll(two_line[:8], HALO, 0))
        blocks.append(jnp.where(left, last, first))
    gap = jnp.zeros_like(blocks[0])
    count = wide // 8
    for i in range(theirs.shape[0] - 8):
        group = (blocks + [gap] * count)[i * count : (i + 1) * count]
        theirs[8 + i] = jnp.concatenate(group, axis=0).astype(BF16)

    copy.wait()
    for i in range(2):
        put(2 * section + i, latent[i])
        put(2 * (1 - section) + i, arrived[i])
        put(4 + i, one[i])
        put(6 + i, two[i])
    for slot in range(8):
        for ref, which in ((mine, col), (theirs, 1 - col)):
            begin = pl.multiple_of(which * tile + section * part, 8)
            ref[slot] = spread[slot, pl.ds(begin, wide), :].astype(BF16)


def pack(place, latent, arrived, one, two, time, three, four, wide, tile, part):
    width, channels = latent.shape[1:]
    vmem = pl.BlockSpec(memory_space=pltpu.VMEM)
    lines = 20
    extra = -(-lines * HALO // wide)
    return pl.pallas_call(
        functools.partial(pack_kernel, wide, tile, part),
        out_shape=[
            jax.ShapeDtypeStruct((8, wide, channels), BF16),
            jax.ShapeDtypeStruct((8 + extra, wide, channels), BF16),
            jax.ShapeDtypeStruct((lines, tile, channels), BF16),
        ],
        in_specs=[
            pl.BlockSpec(memory_space=pltpu.SMEM),
            vmem,
            pl.BlockSpec(memory_space=pl.ANY),
        ]
        + [vmem] * 5,
        out_specs=[vmem] * 3,
        scratch_shapes=[
            pltpu.VMEM((8, width + 16, channels), F32),
            pltpu.VMEM((three.shape[2], 128), F32),
            pltpu.VMEM((three.shape[2], 128), F32),
            pltpu.VMEM(arrived.shape, BF16),
            pltpu.SemaphoreType.DMA,
        ],
        compiler_params=pltpu.CompilerParams(vmem_limit_bytes=60 * 1024 * 1024),
        name="pack",
    )(place, latent, arrived, one, two, time, three, four)


def stack_kernel(
    wide, place, mine, theirs, tiles, later, own, near, far, windows, tile_near, tile_far
):
    del later
    section, col = place[0], place[1]
    count = mine.shape[0] - 2
    own[0], own[1] = mine[...], theirs[0 : count + 2]
    parity = lax.rem(place[3], 2)
    for ref, y in ((near, 1 - parity), (far, parity)):
        ref[0:count], ref[count : 2 * count] = mine[0:count], theirs[0:count]
        here = lax.rem(y + col, 2) == 0
        ref[2 * count :] = jnp.where(here, mine[count:], theirs[count : count + 2])

    part = wide - 2 * HALO
    upper = lax.broadcasted_iota(jnp.int32, (8, 1), 0) < HALO
    groups = wide // 8
    for i in range(tiles.shape[0]):
        line = tiles[i].astype(F32)
        block = i // 2
        begin = block % groups * 8
        edge = theirs[count + 2 + block // groups].astype(F32)[begin : begin + 8]
        turned = pltpu.roll(edge, HALO, 0)
        before, after = (edge, turned) if i % 2 == 0 else (turned, edge)
        first = pltpu.roll(line, HALO, 0)[:wide]
        head = jnp.where(upper, jnp.where(col == 1, before, 0.0), first[:8])
        first = jnp.concatenate([head, first[8:]], axis=0)
        last = pltpu.roll(line, line.shape[0] - (part - HALO), 0)[:wide]
        tail = jnp.where(upper, last[-8:], jnp.where(col == 0, after, 0.0))
        last = jnp.concatenate([last[:-8], tail], axis=0)
        line = jnp.where(section == 0, first, last).astype(BF16)
        windows[i] = line
    is_even = parity == 0
    for base, start, count, depth in ((0, 0, 2, 2), (4, 4, 4, 2), (12, 8, 4, 1)):
        for f in range(2):
            for j in range(depth):
                slot = start + depth * f + j
                high = windows[base + count * f + j]
                low = windows[base + count * f + count - depth + j]
                tile_near[slot] = jnp.where(is_even, low, high)
                tile_far[slot] = jnp.where(is_even, high, low)


def stack(place, mine, theirs, tiles, later):
    units, wide, channels = mine.shape
    vmem = pl.BlockSpec(memory_space=pltpu.VMEM)
    lines = 2 * units - 2
    shapes = [(2, units), (lines,), (lines,), (tiles.shape[0],), (10,), (10,)]
    return pl.pallas_call(
        functools.partial(stack_kernel, wide),
        out_shape=[jax.ShapeDtypeStruct(shape + (wide, channels), BF16) for shape in shapes],
        in_specs=[pl.BlockSpec(memory_space=pltpu.SMEM)]
        + [vmem] * 3
        + [pl.BlockSpec(memory_space=pl.ANY)],
        out_specs=[vmem] * 6,
        compiler_params=pltpu.CompilerParams(vmem_limit_bytes=8 * 1024 * 1024),
        name="stack",
    )(place, mine, theirs, tiles, later)


def align_kernel(weight, out):
    half = weight.shape[0]
    chunk = 16
    tail = half - 128
    low = lax.broadcasted_iota(jnp.int32, (1, 128), 1) < tail

    def move(k, carry):
        here = aligned(k, chunk)
        none = jnp.zeros((chunk, 128), F32)
        for t in range(9):
            base = 3 * t * half
            first = base // 128 * 128
            last = min(first + 640, weight.shape[1])
            values = weight[pl.ds(here, chunk), first:last].astype(F32)
            if last < first + 640:
                values = jnp.concatenate(
                    [values[:, :512], jnp.concatenate([values[:, 512:], none[:, tail:]], axis=1)],
                    axis=1,
                )
            turned = pltpu.roll(values, 640 - tail, 1)
            tiles = [values[:, 128 * i : 128 * (i + 1)] for i in range(5)]
            moved = [turned[:, 128 * i : 128 * (i + 1)] for i in range(5)]
            if base == first:
                blocks = (
                    moved[1:4],
                    tiles[0:3],
                    [none, jnp.where(low, 0.0, moved[4]), moved[0]],
                    [tiles[3], jnp.where(low, tiles[4], 0.0), none],
                )
            else:
                blocks = (
                    tiles[2:5],
                    moved[0:3],
                    [none, jnp.where(low, 0.0, tiles[0]), tiles[1]],
                    [moved[3], jnp.where(low, moved[4], 0.0), none],
                )
            for n, block in enumerate(blocks):
                into = pl.ds(here + n * half, chunk)
                out[into, 2 * half * t : 2 * half * (t + 1)] = jnp.concatenate(
                    block, axis=1
                ).astype(BF16)
        return carry

    lax.fori_loop(0, half // chunk, move, 0)


def align_weights(weight):
    half = weight.shape[1]
    vmem = pl.BlockSpec(memory_space=pltpu.VMEM)
    return pl.pallas_call(
        align_kernel,
        out_shape=jax.ShapeDtypeStruct((4 * half, 18 * half), BF16),
        in_specs=[vmem],
        out_specs=vmem,
        compiler_params=pltpu.CompilerParams(vmem_limit_bytes=8 * 1024 * 1024),
        name="align_weights",
    )(weight.T)


def combine_kernel(weight, out):
    half = weight.shape[0]
    channels = weight.shape[1] // 9
    chunk = 16

    def combine(k, carry):
        rows = pl.ds(aligned(k, chunk), chunk)
        taken = [
            [
                weight[rows, (3 * dy + dx) * channels : (3 * dy + dx + 1) * channels].astype(F32)
                for dx in range(3)
            ]
            for dy in range(3)
        ]
        for slot, dys in enumerate(((0,), (1, 2), (0, 1), (2,))):
            line = [sum(taken[dy][dx] for dy in dys) for dx in range(3)]
            lanes = slice(slot % 2 * channels, (slot % 2 + 1) * channels)
            for n, block in enumerate((line[1] + line[2], line[0] + line[1], line[0], line[2])):
                into = pl.ds(aligned(k, chunk) + n * half, chunk)
                out[slot // 2, into, lanes] = block.astype(BF16)
        return carry

    lax.fori_loop(0, half // chunk, combine, 0)


def combine_weights(weight):
    channels = 2 * weight.shape[1]
    vmem = pl.BlockSpec(memory_space=pltpu.VMEM)
    return pl.pallas_call(
        combine_kernel,
        out_shape=jax.ShapeDtypeStruct((2, 2 * channels, 2 * channels), BF16),
        in_specs=[vmem],
        out_specs=vmem,
        compiler_params=pltpu.CompilerParams(vmem_limit_bytes=8 * 1024 * 1024),
        name="combine_weights",
    )(weight.T)


def weight_copies(source, target, sems, base):
    channels = source.shape[-1]
    return [
        pltpu.make_async_copy(
            source.at[:, dx], target.at[:, :, pl.ds(dx * channels, channels)], sems.at[base + dx]
        )
        for dx in range(3)
    ]


def first_kernel(
    wide,
    sizes,
    place,
    near,
    own,
    far,
    gains,
    weight_one,
    weight_two,
    later,
    out_ref,
    w1,
    w2,
    acc,
    acc_two,
    x1e,
    x1o,
    x2e,
    x2o,
    sems,
):
    channels = own.shape[-1]
    frames = own.shape[1] - 4
    height, width = sizes
    col, row = place[1], place[3]
    units = frames + 2
    del later

    copies_one = weight_copies(weight_one, w1, sems, 0)
    copies_two = weight_copies(weight_two, w2, sems, 3)
    copies_one[0].start()

    slots = [lax.rem(y + col, 2) for y in range(2)]

    is_even = lax.rem(row, 2) == 0

    def own_rows(index):
        return [own[slot, index].astype(F32) for slot in slots]

    def above(line):
        return jnp.where(is_even, far[line].astype(F32), near[line].astype(F32))

    def below(line):
        return jnp.where(is_even, near[line].astype(F32), far[line].astype(F32))

    def rows_of(index):
        first = [above(slot * units + index) for slot in slots]
        last = [below(slot * units + index) for slot in slots]
        return jnp.concatenate(first + own_rows(index) + last, axis=0)

    for f in range(2):
        store(x1e, x1o, f, rows_of(frames + f), 6, wide)
        first, last = above(2 * units + f), below(2 * units + f)
        values = jnp.concatenate([first] + own_rows(units + f) + [last], axis=0)
        store(x2e, x2o, f, values, 4, wide)

    copies_one[1].start()
    for f in range(frames):
        store(x1e, x1o, f + 2, activate(rows_of(f), gains[0:1, :], 1.0), 6, wide)
    low_product(
        acc, x1e, x1o, frames, 6, wide, w1, copies_one, [copies_one[2]] + copies_two[:2]
    )
    copies_two[2].start()

    mask = line_mask(place, wide, 2 * row - 1, 4, height, width)
    for f in range(frames):
        size = 4 * wide
        values = activate(low_sum(acc, f * size, size), gains[1:2, :], mask)
        store(x2e, x2o, f + 2, values, 4, wide)
    low_product(acc_two, x2e, x2o, frames, 4, wide, w2, copies_two, [])
    for f in range(frames):
        size = 2 * wide
        values = low_sum(acc_two, f * size, size) + jnp.concatenate(own_rows(f), axis=0)
        out_ref[f] = values.astype(BF16)


def planes(slots, height, wide, channels):
    return [
        pltpu.VMEM((slots * height * wide, channels), BF16),
        pltpu.VMEM((slots * (height - 2) * wide, channels), BF16),
    ]


def first_block(place, pieces, gains, weight_one, weight_two, later, sizes):
    _, units, wide, channels = pieces[1].shape
    frames = units - 4
    slots = -(-3 * channels // LANES)
    vmem = pl.BlockSpec(memory_space=pltpu.VMEM)
    anywhere = pl.BlockSpec(memory_space=pl.ANY)
    return pl.pallas_call(
        functools.partial(first_kernel, wide, sizes),
        out_shape=jax.ShapeDtypeStruct((frames, 2 * wide, channels), BF16),
        in_specs=[pl.BlockSpec(memory_space=pltpu.SMEM)]
        + [vmem] * 4
        + [pl.BlockSpec(memory_space=pltpu.HBM)] * 2
        + [anywhere],
        out_specs=vmem,
        scratch_shapes=[
            pltpu.VMEM((9, channels, slots * LANES), BF16),
            pltpu.VMEM((9, channels, slots * LANES), BF16),
            pltpu.VMEM((slots, frames * 4 * wide, LANES), F32),
            pltpu.VMEM((slots, frames * 2 * wide, LANES), F32),
            *planes(frames + 2, 6, wide, channels),
            *planes(frames + 2, 4, wide, channels),
            pltpu.SemaphoreType.DMA((6,)),
        ],
        compiler_params=pltpu.CompilerParams(vmem_limit_bytes=50 * 1024 * 1024),
        cost_estimate=pl.CostEstimate(
            flops=2 * 27 * channels * channels * frames * 6 * wide,
            bytes_accessed=2 * 54 * channels * channels,
            transcendentals=0,
        ),
        name="first_block",
    )(place, *pieces, gains, weight_one, weight_two, later)


def second_kernel(
    wide,
    sizes,
    place,
    near_ref,
    blocked,
    far_ref,
    tile_near,
    windows,
    tile_far,
    gains,
    wt,
    wu,
    w3,
    w4,
    out_ref,
    near,
    far,
    sems,
    acc,
    mixed,
    de,
    do,
    lifted_ref,
    *buffers,
):
    ups, threes, fours = buffers[0:3], buffers[3:6], buffers[6:9]
    planes_three = [buffers[9 + 2 * g : 11 + 2 * g] for g in range(3)]
    planes_four = [buffers[15 + 2 * g : 17 + 2 * g] for g in range(3)]
    copies = [
        pltpu.make_async_copy(source, target, sems.at[i])
        for i, (source, target) in enumerate(((near_ref, near), (far_ref, far)))
    ]
    for copy in copies:
        copy.start()
    channels = blocked.shape[-1]
    half = channels // 2
    size = 6 * wide
    frames = blocked.shape[0]
    count = 2 * frames
    groups = split_frames(count)
    height, width = sizes
    row = place[3]

    is_even = lax.rem(row, 2) == 0

    def chosen(when, one, other, index):
        return jnp.where(when, one[index].astype(F32), other[index].astype(F32))

    def cached(start, base, lines, depth, f):
        slots = [start + depth * f + i for i in range(depth)]
        parts = [chosen(is_even, tile_far, tile_near, slot) for slot in slots]
        parts += [windows[base + lines * f + i].astype(F32) for i in range(lines)]
        parts += [chosen(is_even, tile_near, tile_far, slot) for slot in slots]
        return jnp.concatenate(parts, axis=0)

    for f in range(2):
        store(*planes_three[0], f, cached(4, 4, 4, 2, f), 8, wide)
        store(*planes_four[0], f, cached(8, 12, 4, 1, f), 6, wide)
    for copy in copies:
        copy.wait()

    for f in range(2):
        mixed[f * size : (f + 1) * size, :] = cached(0, 0, 2, 2, f).astype(BF16)
    for f in range(frames):
        first, last = chosen(is_even, far, near, f), chosen(is_even, near, far, f)
        for i, values in enumerate((first.astype(BF16), blocked[f], last.astype(BF16))):
            begin = (f + 2) * size + i * 2 * wide
            mixed[begin : begin + 2 * wide, :] = values


    def mix(n, carry):
        lanes = pl.ds(pl.multiple_of(n * LANES, LANES), LANES)
        left = jnp.concatenate(
            [mixed[pl.ds(t * size, frames * size), :] for t in range(3)], axis=1
        )
        acc[n, 0 : frames * size, :] = jnp.dot(left, wt[:, lanes], preferred_element_type=F32)
        return carry

    lax.fori_loop(0, 2 * channels // LANES, mix, 0)
    mask_low = line_mask(place, wide, 2 * row - 2, 6, height, width)

    def double(t, carry):
        rows = pl.ds(aligned(t, size), size)
        first = jnp.concatenate([acc[0, rows, :], acc[1, rows, 0:128]], axis=1)
        second = jnp.concatenate([acc[1, rows, 128:256], acc[2, rows, :]], axis=1)
        store(de, do, 2 * t, first * mask_low, 6, wide)
        store(de, do, 2 * t + 1, second * mask_low, 6, wide)
        return carry

    lax.fori_loop(0, frames, double, 0)


    gain3, gain4 = gains[2:3, :], gains[3:4, :]
    mask_three = line_mask(place, wide, 4 * row - 2, 8, 2 * height, width)
    mask_four = mask_three[wide : 7 * wide]
    part = 4 * wide

    def enlarge(group, n):
        first, last = groups[group]
        lanes = slice(n * LANES, (n + 1) * LANES)
        rows = (last - first) * part
        for py in range(2):
            left = jnp.concatenate(
                [
                    taps(de, do, first, last - first, 6, wide, 0, py),
                    taps(de, do, first, last - first, 6, wide, 0, py + 1),
                ],
                axis=1,
            )
            ups[group][n, py * rows : (py + 1) * rows, :] = transposed_dot(left, wu[py, lanes, :])

    def norm_three(group, f):
        first, last = groups[group]
        values = [
            high_sum(ups[group], aligned(f + py * (last - first), part), part)
            .astype(BF16)
            .astype(F32)
            for py in range(2)
        ]
        lifted = jnp.concatenate(
            [values[h % 2][(h // 2) * wide : (h // 2 + 1) * wide] for h in range(8)], axis=0
        )
        lifted_ref[pl.ds(aligned(f + first, part), part), :] = lifted[2 * wide : 6 * wide]
        slot = f + (2 if group == 0 else 0)
        store(*planes_three[group], slot, activate_pairs(lifted, gain3, mask_three), 8, wide)

    def norm_four(group, f):
        values = high_sum(threes[group], aligned(f, size), size)
        slot = f + (2 if group == 0 else 0)
        store(*planes_four[group], slot, activate_pairs(values, gain4, mask_four), 6, wide)

    def finish(group, f):
        first = groups[group][0]
        rows = pl.ds(aligned(f + first, part), part)
        values = high_sum(fours[group], aligned(f, part), part) + lifted_ref[rows, :]
        values = pltpu.roll(values, part - HALO, 0)
        for y in range(4):
            inner = wide - 2 * HALO
            out_ref[f + first, y] = values[y * wide : y * wide + inner].astype(BF16)

    def third(group, n):
        high_column(n, threes[group], planes_three, groups, group, 8, wide, w3)

    def fourth(group, n):
        high_column(n, fours[group], planes_four, groups, group, 6, wide, w4)

    for product, vector in (
        ((enlarge, 0), None),
        ((enlarge, 1), (norm_three, 0)),
        ((enlarge, 2), (norm_three, 1)),
        ((third, 0), (norm_three, 2)),
        ((third, 1), (norm_four, 0)),
        ((third, 2), (norm_four, 1)),
        ((fourth, 0), (norm_four, 2)),
        ((fourth, 1), (finish, 0)),
        ((fourth, 2), (finish, 1)),
        (None, (finish, 2)),
    ):
        for n in range(max(2 * channels // LANES, *(last - first for first, last in groups))):
            if product is not None and n < 2 * channels // LANES:
                product[0](product[1], n)
            if vector is not None and n < groups[vector[1]][1] - groups[vector[1]][0]:
                vector[0](vector[1], n)


def second_block(place, pieces, tiles, gains, weights, sizes, wide):
    frames, _, channels = pieces[0].shape
    count = 2 * frames
    groups = split_frames(count)
    sizes_of = [last - first for first, last in groups]
    slots = [last - first for first, last in (group_slots(g, groups) for g in range(3))]
    vmem = pl.BlockSpec(memory_space=pltpu.VMEM)
    anywhere = pl.BlockSpec(memory_space=pl.ANY)
    return pl.pallas_call(
        functools.partial(second_kernel, wide, sizes),
        out_shape=jax.ShapeDtypeStruct((count, 4, wide - 2 * HALO, channels), BF16),
        in_specs=[pl.BlockSpec(memory_space=pltpu.SMEM), anywhere, vmem, anywhere] + [vmem] * 8,
        out_specs=vmem,
        scratch_shapes=[
            pltpu.VMEM(pieces[0].shape, BF16),
            pltpu.VMEM(pieces[2].shape, BF16),
            pltpu.SemaphoreType.DMA((2,)),
            pltpu.VMEM((3, frames * 6 * wide, LANES), F32),
            pltpu.VMEM(((frames + 2) * 6 * wide, channels), BF16),
            *planes(count, 6, wide, channels),
            pltpu.VMEM((count * 4 * wide, channels), F32),
            *(pltpu.VMEM((3, n * 8 * wide, LANES), F32) for n in sizes_of),
            *(pltpu.VMEM((3, n * 6 * wide, LANES), F32) for n in sizes_of),
            *(pltpu.VMEM((3, n * 4 * wide, LANES), F32) for n in sizes_of),
            *(ref for n in slots for ref in planes(n, 8, wide, channels)),
            *(ref for n in slots for ref in planes(n, 6, wide, channels)),
        ],
        compiler_params=pltpu.CompilerParams(vmem_limit_bytes=34 * 1024 * 1024),
        name="second_block",
    )(place, *pieces, *tiles, gains, *weights)


def body(
    latent,
    cache_one,
    cache_two,
    cache_time,
    cache_three,
    cache_four,
    gain_one,
    gain_two,
    gain_three,
    gain_four,
    weight_one,
    weight_two,
    weight_time,
    weight_upsample,
    weight_three,
    weight_four,
):
    section, row, col = (lax.axis_index(name) for name in ("section", "rows", "cols"))
    sections, row_count, col_count = (lax.axis_size(name) for name in ("section", "rows", "cols"))
    width, channels = latent.shape[2:]
    tile = width // col_count
    part = tile // sections
    wide = part + 2 * HALO
    half = weight_three.shape[1]
    sizes = (2 * row_count, width)
    place = jnp.stack([section, col, col * tile + section * part - HALO, row]).astype(jnp.int32)

    gains = jnp.stack([gain_one, gain_two, jnp.tile(gain_three, 2), jnp.tile(gain_four, 2)])

    latent = latent.reshape(latent.shape[0], width, channels)
    arrived = swapped(latent, "section")
    mine, theirs, tiles = pack(
        place,
        latent,
        arrived,
        cache_one[:, 0],
        cache_two[:, 0],
        cache_time,
        cache_three,
        cache_four,
        wide,
        tile,
        part,
    )
    weight_three, mine = lax.optimization_barrier((weight_three, mine))
    weight_three = align_weights(weight_three)
    own, near, far, windows, tile_near, tile_far = stack(
        place, mine, swapped(theirs, "cols"), tiles, weight_three
    )
    far = paired(far, "rows", 1)
    near = paired(near, "rows", 0)
    tile_far = paired(tile_far, "rows", 1)
    tile_near = paired(tile_near, "rows", 0)
    weight_upsample, own = lax.optimization_barrier((weight_upsample, own))
    weight_upsample = combine_weights(weight_upsample)
    blocked = first_block(
        place,
        [near, own, far],
        gains,
        weight_one.reshape(9, 3, channels, channels),
        weight_two.reshape(9, 3, channels, channels),
        weight_upsample,
        sizes,
    )
    far = paired(blocked, "rows", 1)
    near = paired(blocked, "rows", 0)
    blocks = [near, blocked, far]
    weight_four, _ = lax.optimization_barrier((weight_four, blocked))
    weight_four = align_weights(weight_four)
    tiles = [tile_near, windows, tile_far]
    frames = second_block(
        place,
        blocks,
        tiles,
        gains,
        (weight_time, weight_upsample, weight_three, weight_four),
        sizes,
        wide,
    )
    count = frames.shape[0] // sections
    given = lax.dynamic_slice_in_dim(frames, (1 - section) * count, count, 0)
    kept = lax.dynamic_slice_in_dim(frames, section * count, count, 0)
    arrived = swapped(given, "section")
    low = section == 0
    joined = jnp.concatenate(
        [jnp.where(low, kept, arrived), jnp.where(low, arrived, kept)], axis=2
    )
    return joined.reshape(count, 4, 2 * tile, half)


def solution(mesh):
    placed = (
        P("section", ("rows", "cols"), None, None),
        P(None, ("rows", "cols"), None, None),
        P(None, ("rows", "cols"), None, None),
        P(None, "rows", "cols", None),
        P(None, "rows", "cols", None),
        P(None, "rows", "cols", None),
    ) + (P(),) * 10
    return jax.shard_map(
        body,
        mesh=mesh,
        in_specs=placed,
        out_specs=P("section", "rows", "cols", None),
        check_vma=False,
    )
```

```python
import functools

import jax
import jax.numpy as jnp
from jax import lax
from jax.experimental import pallas as pl
from jax.experimental.pallas import tpu as pltpu
from jax.sharding import PartitionSpec as P

EPSILON = 1e-06
HALO = 4
LANES = 256
BF16 = jnp.bfloat16
F32 = jnp.float32


def swapped(value, axis):
    return lax.ppermute(value, axis, [(0, 1), (1, 0)])


def paired(value, axis, first):
    pairs = [(i, i + 1) for i in range(first, lax.axis_size(axis) - 1, 2)]
    return lax.ppermute(value, axis, pairs + [(high, low) for low, high in pairs])


def silu(scaled):
    half = scaled * 0.5
    return half * (1.0 + jnp.tanh(half))


def activate(values, gain, mask):
    mean = jnp.mean(values * values, axis=-1, keepdims=True)
    return silu(values * (lax.rsqrt(mean + EPSILON) * mask) * gain)


def activate_pairs(values, gain, mask):
    channels = values.shape[-1] // 2
    squares = values * values
    first = lax.broadcasted_iota(jnp.int32, (1, 2 * channels), 1) < channels
    total = jnp.sum(squares, axis=-1, keepdims=True)
    low = jnp.sum(jnp.where(first, squares, 0.0), axis=-1, keepdims=True)
    scale_low = lax.rsqrt(low / channels + EPSILON) * mask
    scale_high = lax.rsqrt((total - low) / channels + EPSILON) * mask
    return silu(values * jnp.where(first, scale_low, scale_high) * gain)


def merge(even, odd, channels):
    turned = pltpu.roll(odd, channels - 128, 1)
    first = lax.broadcasted_iota(jnp.int32, (1, 128), 1) < channels - 128
    middle = jnp.where(first, even[:, 128:], turned[:, :128])
    return jnp.concatenate([even[:, :128], middle, turned[:, 128:]], axis=1)


def aligned(index, size):
    return index * size if isinstance(index, int) else pl.multiple_of(index * size, 16)


def line_mask(place, wide, first, count, limit, width):
    columns = place[2] + lax.broadcasted_iota(jnp.int32, (wide, 1), 0)
    inside = jnp.where((columns >= 0) & (columns < width), 1.0, 0.0)
    lines = []
    for i in range(count):
        line = first + i
        lines.append(inside * jnp.where((line >= 0) & (line < limit), 1.0, 0.0))
    return jnp.concatenate(lines, axis=0)


def store(even, odd, slot, values, height, wide):
    even[pl.ds(slot * (height * wide), height * wide), :] = values.astype(BF16)
    odd[pl.ds(slot * ((height - 2) * wide), (height - 2) * wide), :] = values[
        wide : (height - 1) * wide
    ].astype(BF16)


def taps(even, odd, begin, count, height, wide, dt, dy, lanes=slice(None)):
    inner = (height - 2) * wide
    if dy == 1:
        parts = [odd[pl.ds((begin + f + dt) * inner, inner), lanes] for f in range(count)]
    else:
        parts = [
            even[pl.ds((begin + f + dt) * height * wide + dy * wide, inner), lanes]
            for f in range(count)
        ]
    return jnp.concatenate(parts, axis=0)


def low_product(acc, even, odd, count, height, wide, weights, copies, following):
    rows = count * (height - 2) * wide
    channels = weights.shape[1]
    lanes = 3 * channels
    waited = 0
    for n in range(-(-lanes // LANES)):
        begin, end = n * LANES, min((n + 1) * LANES, lanes)
        while waited * channels < end:
            copies[waited].wait()
            if waited < len(following):
                following[waited].start()
            waited += 1
        left = jnp.concatenate(
            [taps(even, odd, 0, count, height, wide, t // 3, t % 3) for t in range(9)], axis=1
        )
        right = weights[:, :, begin:end].reshape(9 * channels, end - begin)
        acc[n, 0:rows, 0 : end - begin] = jnp.dot(left, right, preferred_element_type=F32)


def low_sum(acc, start, size):
    rows = pl.ds(start, size)
    before = jnp.concatenate([acc[0, rows, :], acc[1, rows, 0:128]], axis=1)
    center = jnp.concatenate([acc[1, rows, 128:256], acc[2, rows, :]], axis=1)
    after = jnp.concatenate([acc[3, rows, :], acc[4, rows, 0:128]], axis=1)
    return center + pltpu.roll(before, 1, 0) + pltpu.roll(after, size - 1, 0)


def transposed_dot(left, right):
    return lax.dot_general(left, right, (((1,), (1,)), ((), ())), preferred_element_type=F32)


def split_frames(count):
    first = count // 4
    second = first + (count - first) // 2
    return (0, first), (first, second), (second, count)


def group_slots(group, groups):
    first, last = groups[group]
    return (0 if group == 0 else first + 2), last + 2


def grouped_taps(planes, groups, frames, height, wide, dt, dy):
    inner = (height - 2) * wide
    parts = []
    for f in frames:
        for group, (even, odd) in enumerate(planes):
            first, last = group_slots(group, groups)
            if first <= f + dt < last:
                slot = f + dt - first
                if dy == 1:
                    parts.append(odd[slot * inner : (slot + 1) * inner, :])
                else:
                    begin = slot * height * wide + dy * wide
                    parts.append(even[begin : begin + inner, :])
    return jnp.concatenate(parts, axis=0)


def high_column(n, acc, planes, groups, group, height, wide, weights):
    left = jnp.concatenate(
        [
            grouped_taps(planes, groups, range(*groups[group]), height, wide, t // 3, t % 3)
            for t in range(9)
        ],
        axis=1,
    )
    acc[n] = transposed_dot(left, weights[n * LANES : (n + 1) * LANES, :])


def high_sum(acc, start, size):
    rows = pl.ds(start, size)
    center = jnp.concatenate([acc[0, rows, :], acc[1, rows, 0:128]], axis=1)
    side = jnp.concatenate([acc[1, rows, 128:256], acc[2, rows, :]], axis=1)
    channels = center.shape[1]
    first = lax.broadcasted_iota(jnp.int32, (1, channels), 1) < channels // 2
    return center + jnp.where(first, pltpu.roll(side, 1, 0), pltpu.roll(side, size - 1, 0))


def pack_kernel(
    wide,
    tile,
    part,
    place,
    latent,
    arrived,
    one,
    two,
    time,
    three,
    four,
    mine,
    theirs,
    tiles,
    spread,
    low,
    high,
):
    section, col = place[0], place[1]
    width, channels = latent.shape[1:]
    half = three.shape[-1]
    empty = jnp.zeros((spread.shape[1] - width, channels), F32)

    def put(slot, values):
        spread[slot] = pltpu.roll(
            jnp.concatenate([values.astype(F32), empty], axis=0), HALO, 0
        )

    for i in range(2):
        put(2 * section + i, latent[i])
        put(2 * (1 - section) + i, arrived[i])
        put(4 + i, one[i])
        put(6 + i, two[i])
    for slot in range(8):
        for ref, which in ((mine, col), (theirs, 1 - col)):
            begin = pl.multiple_of(which * tile + section * part, 8)
            ref[slot] = spread[slot, pl.ds(begin, wide), :].astype(BF16)

    lines = [time[f, y].astype(F32) for f in range(2) for y in range(2)]
    for ref in (three, four):
        for f in range(2):
            for y in range(4):
                values = ref[f, y].astype(F32)
                low[...] = values[:, :128]
                high[:, 0 : half - 128] = values[:, 128:]
                count = values.shape[0] // 2
                even, odd = (
                    jnp.concatenate(
                        [lanes[pl.ds(o, count, stride=2), :] for lanes in (low, high)], axis=1
                    )
                    for o in range(2)
                )
                lines.append(merge(even, odd, half))
    for i, line in enumerate(lines):
        tiles[i] = line.astype(BF16)

    left = col == 0
    upper = lax.broadcasted_iota(jnp.int32, (8, 1), 0) < HALO
    blocks = []
    for i in range(0, len(lines), 2):
        one_line, two_line = lines[i], lines[i + 1]
        last = jnp.where(upper, pltpu.roll(one_line[-8:], HALO, 0), two_line[-8:])
        first = jnp.where(upper, one_line[:8], pltpu.roll(two_line[:8], HALO, 0))
        blocks.append(jnp.where(left, last, first))
    gap = jnp.zeros_like(blocks[0])
    count = wide // 8
    for i in range(theirs.shape[0] - 8):
        group = (blocks + [gap] * count)[i * count : (i + 1) * count]
        theirs[8 + i] = jnp.concatenate(group, axis=0).astype(BF16)


def pack(place, latent, arrived, one, two, time, three, four, wide, tile, part):
    width, channels = latent.shape[1:]
    vmem = pl.BlockSpec(memory_space=pltpu.VMEM)
    lines = 20
    extra = -(-lines * HALO // wide)
    return pl.pallas_call(
        functools.partial(pack_kernel, wide, tile, part),
        out_shape=[
            jax.ShapeDtypeStruct((8, wide, channels), BF16),
            jax.ShapeDtypeStruct((8 + extra, wide, channels), BF16),
            jax.ShapeDtypeStruct((lines, tile, channels), BF16),
        ],
        in_specs=[pl.BlockSpec(memory_space=pltpu.SMEM)] + [vmem] * 7,
        out_specs=[vmem] * 3,
        scratch_shapes=[
            pltpu.VMEM((8, width + 16, channels), F32),
            pltpu.VMEM((three.shape[2], 128), F32),
            pltpu.VMEM((three.shape[2], 128), F32),
        ],
        compiler_params=pltpu.CompilerParams(vmem_limit_bytes=60 * 1024 * 1024),
        name="pack",
    )(place, latent, arrived, one, two, time, three, four)


def stack_kernel(
    wide, place, mine, theirs, tiles, later, own, near, far, windows, tile_near, tile_far
):
    del later
    section, col = place[0], place[1]
    count = mine.shape[0] - 2
    own[0], own[1] = mine[...], theirs[0 : count + 2]
    parity = lax.rem(place[3], 2)
    for ref, y in ((near, 1 - parity), (far, parity)):
        ref[0:count], ref[count : 2 * count] = mine[0:count], theirs[0:count]
        here = lax.rem(y + col, 2) == 0
        ref[2 * count :] = jnp.where(here, mine[count:], theirs[count : count + 2])

    part = wide - 2 * HALO
    upper = lax.broadcasted_iota(jnp.int32, (8, 1), 0) < HALO
    groups = wide // 8
    for i in range(tiles.shape[0]):
        line = tiles[i].astype(F32)
        block = i // 2
        begin = block % groups * 8
        edge = theirs[count + 2 + block // groups].astype(F32)[begin : begin + 8]
        turned = pltpu.roll(edge, HALO, 0)
        before, after = (edge, turned) if i % 2 == 0 else (turned, edge)
        first = pltpu.roll(line, HALO, 0)[:wide]
        head = jnp.where(upper, jnp.where(col == 1, before, 0.0), first[:8])
        first = jnp.concatenate([head, first[8:]], axis=0)
        last = pltpu.roll(line, line.shape[0] - (part - HALO), 0)[:wide]
        tail = jnp.where(upper, last[-8:], jnp.where(col == 0, after, 0.0))
        last = jnp.concatenate([last[:-8], tail], axis=0)
        line = jnp.where(section == 0, first, last).astype(BF16)
        windows[i] = line
    is_even = parity == 0
    for base, start, count, depth in ((0, 0, 2, 2), (4, 4, 4, 2), (12, 8, 4, 1)):
        for f in range(2):
            for j in range(depth):
                slot = start + depth * f + j
                high = windows[base + count * f + j]
                low = windows[base + count * f + count - depth + j]
                tile_near[slot] = jnp.where(is_even, low, high)
                tile_far[slot] = jnp.where(is_even, high, low)


def stack(place, mine, theirs, tiles, later):
    units, wide, channels = mine.shape
    vmem = pl.BlockSpec(memory_space=pltpu.VMEM)
    lines = 2 * units - 2
    shapes = [(2, units), (lines,), (lines,), (tiles.shape[0],), (10,), (10,)]
    return pl.pallas_call(
        functools.partial(stack_kernel, wide),
        out_shape=[jax.ShapeDtypeStruct(shape + (wide, channels), BF16) for shape in shapes],
        in_specs=[pl.BlockSpec(memory_space=pltpu.SMEM)]
        + [vmem] * 3
        + [pl.BlockSpec(memory_space=pl.ANY)],
        out_specs=[vmem] * 6,
        compiler_params=pltpu.CompilerParams(vmem_limit_bytes=8 * 1024 * 1024),
        name="stack",
    )(place, mine, theirs, tiles, later)


def align_kernel(weight, out):
    half = weight.shape[0]
    chunk = 16
    tail = half - 128
    low = lax.broadcasted_iota(jnp.int32, (1, 128), 1) < tail

    def move(k, carry):
        here = aligned(k, chunk)
        none = jnp.zeros((chunk, 128), F32)
        for t in range(9):
            base = 3 * t * half
            first = base // 128 * 128
            last = min(first + 640, weight.shape[1])
            values = weight[pl.ds(here, chunk), first:last].astype(F32)
            if last < first + 640:
                values = jnp.concatenate(
                    [values[:, :512], jnp.concatenate([values[:, 512:], none[:, tail:]], axis=1)],
                    axis=1,
                )
            turned = pltpu.roll(values, 640 - tail, 1)
            tiles = [values[:, 128 * i : 128 * (i + 1)] for i in range(5)]
            moved = [turned[:, 128 * i : 128 * (i + 1)] for i in range(5)]
            if base == first:
                blocks = (
                    moved[1:4],
                    tiles[0:3],
                    [none, jnp.where(low, 0.0, moved[4]), moved[0]],
                    [tiles[3], jnp.where(low, tiles[4], 0.0), none],
                )
            else:
                blocks = (
                    tiles[2:5],
                    moved[0:3],
                    [none, jnp.where(low, 0.0, tiles[0]), tiles[1]],
                    [moved[3], jnp.where(low, moved[4], 0.0), none],
                )
            for n, block in enumerate(blocks):
                into = pl.ds(here + n * half, chunk)
                out[into, 2 * half * t : 2 * half * (t + 1)] = jnp.concatenate(
                    block, axis=1
                ).astype(BF16)
        return carry

    lax.fori_loop(0, half // chunk, move, 0)


def align_weights(weight):
    half = weight.shape[1]
    vmem = pl.BlockSpec(memory_space=pltpu.VMEM)
    return pl.pallas_call(
        align_kernel,
        out_shape=jax.ShapeDtypeStruct((4 * half, 18 * half), BF16),
        in_specs=[vmem],
        out_specs=vmem,
        compiler_params=pltpu.CompilerParams(vmem_limit_bytes=8 * 1024 * 1024),
        name="align_weights",
    )(weight.T)


def combine_kernel(weight, later, out):
    del later
    half = weight.shape[0]
    channels = weight.shape[1] // 9
    chunk = 16

    def combine(k, carry):
        rows = pl.ds(aligned(k, chunk), chunk)
        taken = [
            [
                weight[rows, (3 * dy + dx) * channels : (3 * dy + dx + 1) * channels].astype(F32)
                for dx in range(3)
            ]
            for dy in range(3)
        ]
        for slot, dys in enumerate(((0,), (1, 2), (0, 1), (2,))):
            line = [sum(taken[dy][dx] for dy in dys) for dx in range(3)]
            lanes = slice(slot % 2 * channels, (slot % 2 + 1) * channels)
            for n, block in enumerate((line[1] + line[2], line[0] + line[1], line[0], line[2])):
                into = pl.ds(aligned(k, chunk) + n * half, chunk)
                out[slot // 2, into, lanes] = block.astype(BF16)
        return carry

    lax.fori_loop(0, half // chunk, combine, 0)


def combine_weights(weight, later):
    channels = 2 * weight.shape[1]
    vmem = pl.BlockSpec(memory_space=pltpu.VMEM)
    return pl.pallas_call(
        combine_kernel,
        out_shape=jax.ShapeDtypeStruct((2, 2 * channels, 2 * channels), BF16),
        in_specs=[vmem, pl.BlockSpec(memory_space=pl.ANY)],
        out_specs=vmem,
        compiler_params=pltpu.CompilerParams(vmem_limit_bytes=8 * 1024 * 1024),
        name="combine_weights",
    )(weight.T, later)


def weight_copies(source, target, sems, base):
    channels = source.shape[-1]
    return [
        pltpu.make_async_copy(
            source.at[:, dx], target.at[:, :, pl.ds(dx * channels, channels)], sems.at[base + dx]
        )
        for dx in range(3)
    ]


def first_kernel(
    wide,
    sizes,
    place,
    near,
    own,
    far,
    gains,
    weight_one,
    weight_two,
    later,
    out_ref,
    w1,
    w2,
    acc,
    acc_two,
    x1e,
    x1o,
    x2e,
    x2o,
    sems,
):
    channels = own.shape[-1]
    frames = own.shape[1] - 4
    height, width = sizes
    col, row = place[1], place[3]
    units = frames + 2
    del later

    copies_one = weight_copies(weight_one, w1, sems, 0)
    copies_two = weight_copies(weight_two, w2, sems, 3)
    copies_one[0].start()

    slots = [lax.rem(y + col, 2) for y in range(2)]

    is_even = lax.rem(row, 2) == 0

    def own_rows(index):
        return [own[slot, index].astype(F32) for slot in slots]

    def above(line):
        return jnp.where(is_even, far[line].astype(F32), near[line].astype(F32))

    def below(line):
        return jnp.where(is_even, near[line].astype(F32), far[line].astype(F32))

    def rows_of(index):
        first = [above(slot * units + index) for slot in slots]
        last = [below(slot * units + index) for slot in slots]
        return jnp.concatenate(first + own_rows(index) + last, axis=0)

    for f in range(2):
        store(x1e, x1o, f, rows_of(frames + f), 6, wide)
        first, last = above(2 * units + f), below(2 * units + f)
        values = jnp.concatenate([first] + own_rows(units + f) + [last], axis=0)
        store(x2e, x2o, f, values, 4, wide)

    copies_one[1].start()
    for f in range(frames):
        store(x1e, x1o, f + 2, activate(rows_of(f), gains[0:1, :], 1.0), 6, wide)
    low_product(
        acc, x1e, x1o, frames, 6, wide, w1, copies_one, [copies_one[2]] + copies_two[:2]
    )
    copies_two[2].start()

    mask = line_mask(place, wide, 2 * row - 1, 4, height, width)
    for f in range(frames):
        size = 4 * wide
        values = activate(low_sum(acc, f * size, size), gains[1:2, :], mask)
        store(x2e, x2o, f + 2, values, 4, wide)
    low_product(acc_two, x2e, x2o, frames, 4, wide, w2, copies_two, [])
    for f in range(frames):
        size = 2 * wide
        values = low_sum(acc_two, f * size, size) + jnp.concatenate(own_rows(f), axis=0)
        out_ref[f] = values.astype(BF16)


def planes(slots, height, wide, channels):
    return [
        pltpu.VMEM((slots * height * wide, channels), BF16),
        pltpu.VMEM((slots * (height - 2) * wide, channels), BF16),
    ]


def first_block(place, pieces, gains, weight_one, weight_two, later, sizes):
    _, units, wide, channels = pieces[1].shape
    frames = units - 4
    slots = -(-3 * channels // LANES)
    vmem = pl.BlockSpec(memory_space=pltpu.VMEM)
    anywhere = pl.BlockSpec(memory_space=pl.ANY)
    return pl.pallas_call(
        functools.partial(first_kernel, wide, sizes),
        out_shape=jax.ShapeDtypeStruct((frames, 2 * wide, channels), BF16),
        in_specs=[pl.BlockSpec(memory_space=pltpu.SMEM)]
        + [vmem] * 4
        + [pl.BlockSpec(memory_space=pltpu.HBM)] * 2
        + [anywhere],
        out_specs=vmem,
        scratch_shapes=[
            pltpu.VMEM((9, channels, slots * LANES), BF16),
            pltpu.VMEM((9, channels, slots * LANES), BF16),
            pltpu.VMEM((slots, frames * 4 * wide, LANES), F32),
            pltpu.VMEM((slots, frames * 2 * wide, LANES), F32),
            *planes(frames + 2, 6, wide, channels),
            *planes(frames + 2, 4, wide, channels),
            pltpu.SemaphoreType.DMA((6,)),
        ],
        compiler_params=pltpu.CompilerParams(vmem_limit_bytes=50 * 1024 * 1024),
        cost_estimate=pl.CostEstimate(
            flops=2 * 27 * channels * channels * frames * 6 * wide,
            bytes_accessed=2 * 54 * channels * channels,
            transcendentals=0,
        ),
        name="first_block",
    )(place, *pieces, gains, weight_one, weight_two, later)


def second_kernel(
    wide,
    sizes,
    place,
    near,
    blocked,
    far,
    tile_near,
    windows,
    tile_far,
    gains,
    wt,
    wu,
    weight_three,
    weight_four,
    out_ref,
    w3,
    w4,
    sems,
    acc,
    mixed,
    de,
    do,
    lifted_ref,
    *buffers,
):
    ups, threes, fours = buffers[0:3], buffers[3:6], buffers[6:9]
    planes_three = [buffers[9 + 2 * g : 11 + 2 * g] for g in range(3)]
    planes_four = [buffers[15 + 2 * g : 17 + 2 * g] for g in range(3)]
    copies = [
        pltpu.make_async_copy(source, target, sems.at[i])
        for i, (source, target) in enumerate(((weight_three, w3), (weight_four, w4)))
    ]
    copies[0].start()
    channels = blocked.shape[-1]
    half = channels // 2
    size = 6 * wide
    frames = blocked.shape[0]
    count = 2 * frames
    groups = split_frames(count)
    height, width = sizes
    row = place[3]

    is_even = lax.rem(row, 2) == 0

    def chosen(when, one, other, index):
        return jnp.where(when, one[index].astype(F32), other[index].astype(F32))

    def cached(start, base, lines, depth, f):
        slots = [start + depth * f + i for i in range(depth)]
        parts = [chosen(is_even, tile_far, tile_near, slot) for slot in slots]
        parts += [windows[base + lines * f + i].astype(F32) for i in range(lines)]
        parts += [chosen(is_even, tile_near, tile_far, slot) for slot in slots]
        return jnp.concatenate(parts, axis=0)

    for f in range(2):
        mixed[f * size : (f + 1) * size, :] = cached(0, 0, 2, 2, f).astype(BF16)
    for f in range(frames):
        first, last = chosen(is_even, far, near, f), chosen(is_even, near, far, f)
        for i, values in enumerate((first.astype(BF16), blocked[f], last.astype(BF16))):
            begin = (f + 2) * size + i * 2 * wide
            mixed[begin : begin + 2 * wide, :] = values


    def mix(n, carry):
        lanes = pl.ds(pl.multiple_of(n * LANES, LANES), LANES)
        left = jnp.concatenate(
            [mixed[pl.ds(t * size, frames * size), :] for t in range(3)], axis=1
        )
        acc[n, 0 : frames * size, :] = jnp.dot(left, wt[:, lanes], preferred_element_type=F32)
        return carry

    lax.fori_loop(0, 2 * channels // LANES, mix, 0)
    mask_low = line_mask(place, wide, 2 * row - 2, 6, height, width)

    def double(t, carry):
        rows = pl.ds(aligned(t, size), size)
        first = jnp.concatenate([acc[0, rows, :], acc[1, rows, 0:128]], axis=1)
        second = jnp.concatenate([acc[1, rows, 128:256], acc[2, rows, :]], axis=1)
        store(de, do, 2 * t, first * mask_low, 6, wide)
        store(de, do, 2 * t + 1, second * mask_low, 6, wide)
        return carry

    lax.fori_loop(0, frames, double, 0)
    copies[0].wait()
    copies[1].start()


    for f in range(2):
        store(*planes_three[0], f, cached(4, 4, 4, 2, f), 8, wide)
        store(*planes_four[0], f, cached(8, 12, 4, 1, f), 6, wide)
    gain3, gain4 = gains[2:3, :], gains[3:4, :]
    mask_three = line_mask(place, wide, 4 * row - 2, 8, 2 * height, width)
    mask_four = mask_three[wide : 7 * wide]
    part = 4 * wide

    def enlarge(group, n):
        first, last = groups[group]
        lanes = slice(n * LANES, (n + 1) * LANES)
        rows = (last - first) * part
        for py in range(2):
            left = jnp.concatenate(
                [
                    taps(de, do, first, last - first, 6, wide, 0, py),
                    taps(de, do, first, last - first, 6, wide, 0, py + 1),
                ],
                axis=1,
            )
            ups[group][n, py * rows : (py + 1) * rows, :] = transposed_dot(left, wu[py, lanes, :])

    def norm_three(group, f):
        first, last = groups[group]
        values = [
            high_sum(ups[group], aligned(f + py * (last - first), part), part)
            .astype(BF16)
            .astype(F32)
            for py in range(2)
        ]
        lifted = jnp.concatenate(
            [values[h % 2][(h // 2) * wide : (h // 2 + 1) * wide] for h in range(8)], axis=0
        )
        lifted_ref[pl.ds(aligned(f + first, part), part), :] = lifted[2 * wide : 6 * wide]
        slot = f + (2 if group == 0 else 0)
        store(*planes_three[group], slot, activate_pairs(lifted, gain3, mask_three), 8, wide)

    def norm_four(group, f):
        values = high_sum(threes[group], aligned(f, size), size)
        slot = f + (2 if group == 0 else 0)
        store(*planes_four[group], slot, activate_pairs(values, gain4, mask_four), 6, wide)

    def finish(group, f):
        first = groups[group][0]
        rows = pl.ds(aligned(f + first, part), part)
        values = high_sum(fours[group], aligned(f, part), part) + lifted_ref[rows, :]
        values = pltpu.roll(values, part - HALO, 0)
        for y in range(4):
            inner = wide - 2 * HALO
            out_ref[f + first, y] = values[y * wide : y * wide + inner].astype(BF16)

    def third(group, n):
        high_column(n, threes[group], planes_three, groups, group, 8, wide, w3)

    def fourth(group, n):
        high_column(n, fours[group], planes_four, groups, group, 6, wide, w4)

    for product, vector in (
        ((enlarge, 0), None),
        ((enlarge, 1), (norm_three, 0)),
        ((enlarge, 2), (norm_three, 1)),
        ((third, 0), (norm_three, 2)),
        ((third, 1), (norm_four, 0)),
        ((third, 2), (norm_four, 1)),
        ((fourth, 0), (norm_four, 2)),
        ((fourth, 1), (finish, 0)),
        ((fourth, 2), (finish, 1)),
        (None, (finish, 2)),
    ):
        if product == (fourth, 0):
            copies[1].wait()
        for n in range(max(2 * channels // LANES, *(last - first for first, last in groups))):
            if product is not None and n < 2 * channels // LANES:
                product[0](product[1], n)
            if vector is not None and n < groups[vector[1]][1] - groups[vector[1]][0]:
                vector[0](vector[1], n)


def second_block(place, pieces, tiles, gains, weights, sizes, wide):
    frames, _, channels = pieces[0].shape
    count = 2 * frames
    groups = split_frames(count)
    sizes_of = [last - first for first, last in groups]
    slots = [last - first for first, last in (group_slots(g, groups) for g in range(3))]
    vmem = pl.BlockSpec(memory_space=pltpu.VMEM)
    return pl.pallas_call(
        functools.partial(second_kernel, wide, sizes),
        out_shape=jax.ShapeDtypeStruct((count, 4, wide - 2 * HALO, channels), BF16),
        in_specs=[pl.BlockSpec(memory_space=pltpu.SMEM)]
        + [vmem] * 9
        + [pl.BlockSpec(memory_space=pl.ANY)] * 2,
        out_specs=vmem,
        scratch_shapes=[
            pltpu.VMEM(weights[2].shape, BF16),
            pltpu.VMEM(weights[3].shape, BF16),
            pltpu.SemaphoreType.DMA((2,)),
            pltpu.VMEM((3, frames * 6 * wide, LANES), F32),
            pltpu.VMEM(((frames + 2) * 6 * wide, channels), BF16),
            *planes(count, 6, wide, channels),
            pltpu.VMEM((count * 4 * wide, channels), F32),
            *(pltpu.VMEM((3, n * 8 * wide, LANES), F32) for n in sizes_of),
            *(pltpu.VMEM((3, n * 6 * wide, LANES), F32) for n in sizes_of),
            *(pltpu.VMEM((3, n * 4 * wide, LANES), F32) for n in sizes_of),
            *(ref for n in slots for ref in planes(n, 8, wide, channels)),
            *(ref for n in slots for ref in planes(n, 6, wide, channels)),
        ],
        compiler_params=pltpu.CompilerParams(vmem_limit_bytes=50 * 1024 * 1024),
        name="second_block",
    )(place, *pieces, *tiles, gains, *weights)


def body(
    latent,
    cache_one,
    cache_two,
    cache_time,
    cache_three,
    cache_four,
    gain_one,
    gain_two,
    gain_three,
    gain_four,
    weight_one,
    weight_two,
    weight_time,
    weight_upsample,
    weight_three,
    weight_four,
):
    section, row, col = (lax.axis_index(name) for name in ("section", "rows", "cols"))
    sections, row_count, col_count = (lax.axis_size(name) for name in ("section", "rows", "cols"))
    width, channels = latent.shape[2:]
    tile = width // col_count
    part = tile // sections
    wide = part + 2 * HALO
    half = weight_three.shape[1]
    sizes = (2 * row_count, width)
    place = jnp.stack([section, col, col * tile + section * part - HALO, row]).astype(jnp.int32)

    gains = jnp.stack([gain_one, gain_two, jnp.tile(gain_three, 2), jnp.tile(gain_four, 2)])

    latent = latent.reshape(latent.shape[0], width, channels)
    arrived = swapped(latent, "section")
    mine, theirs, tiles = pack(
        place,
        latent,
        arrived,
        cache_one[:, 0],
        cache_two[:, 0],
        cache_time,
        cache_three,
        cache_four,
        wide,
        tile,
        part,
    )
    weight_three, mine = lax.optimization_barrier((weight_three, mine))
    weight_three = align_weights(weight_three)
    own, near, far, windows, tile_near, tile_far = stack(
        place, mine, swapped(theirs, "cols"), tiles, weight_three
    )
    far = paired(far, "rows", 1)
    near = paired(near, "rows", 0)
    tile_far = paired(tile_far, "rows", 1)
    tile_near = paired(tile_near, "rows", 0)
    weight_upsample, weight_four, own = lax.optimization_barrier(
        (weight_upsample, weight_four, own)
    )
    weight_four = align_weights(weight_four)
    weight_upsample = combine_weights(weight_upsample, weight_four)
    blocked = first_block(
        place,
        [near, own, far],
        gains,
        weight_one.reshape(9, 3, channels, channels),
        weight_two.reshape(9, 3, channels, channels),
        weight_upsample,
        sizes,
    )
    far = paired(blocked, "rows", 1)
    near = paired(blocked, "rows", 0)
    blocks = [near, blocked, far]
    tiles = [tile_near, windows, tile_far]
    frames = second_block(
        place,
        blocks,
        tiles,
        gains,
        (weight_time, weight_upsample, weight_three, weight_four),
        sizes,
        wide,
    )
    count = frames.shape[0] // sections
    given = lax.dynamic_slice_in_dim(frames, (1 - section) * count, count, 0)
    kept = lax.dynamic_slice_in_dim(frames, section * count, count, 0)
    arrived = swapped(given, "section")
    low = section == 0
    joined = jnp.concatenate(
        [jnp.where(low, kept, arrived), jnp.where(low, arrived, kept)], axis=2
    )
    return joined.reshape(count, 4, 2 * tile, half)


def solution(mesh):
    placed = (
        P("section", ("rows", "cols"), None, None),
        P(None, ("rows", "cols"), None, None),
        P(None, ("rows", "cols"), None, None),
        P(None, "rows", "cols", None),
        P(None, "rows", "cols", None),
        P(None, "rows", "cols", None),
    ) + (P(),) * 10
    return jax.shard_map(
        body,
        mesh=mesh,
        in_specs=placed,
        out_specs=P("section", "rows", "cols", None),
        check_vma=False,
    )
```

```python
import functools

import jax
import jax.numpy as jnp
from jax import lax
from jax.experimental import pallas as pl
from jax.experimental.pallas import tpu as pltpu
from jax.sharding import PartitionSpec as P

EPSILON = 1e-06
HALO = 4
LANES = 256
BF16 = jnp.bfloat16
F32 = jnp.float32


def swapped(value, axis):
    return lax.ppermute(value, axis, [(0, 1), (1, 0)])


def paired(value, axis, first):
    pairs = [(i, i + 1) for i in range(first, lax.axis_size(axis) - 1, 2)]
    return lax.ppermute(value, axis, pairs + [(high, low) for low, high in pairs])


def silu(scaled):
    half = scaled * 0.5
    return half * (1.0 + jnp.tanh(half))


def activate(values, gain, mask):
    mean = jnp.mean(values * values, axis=-1, keepdims=True)
    return silu(values * (lax.rsqrt(mean + EPSILON) * mask) * gain)


def activate_pairs(values, gain, mask):
    channels = values.shape[-1] // 2
    squares = values * values
    first = lax.broadcasted_iota(jnp.int32, (1, 2 * channels), 1) < channels
    total = jnp.sum(squares, axis=-1, keepdims=True)
    low = jnp.sum(jnp.where(first, squares, 0.0), axis=-1, keepdims=True)
    scale_low = lax.rsqrt(low / channels + EPSILON) * mask
    scale_high = lax.rsqrt((total - low) / channels + EPSILON) * mask
    return silu(values * jnp.where(first, scale_low, scale_high) * gain)


def merge(even, odd, channels):
    turned = pltpu.roll(odd, channels - 128, 1)
    first = lax.broadcasted_iota(jnp.int32, (1, 128), 1) < channels - 128
    middle = jnp.where(first, even[:, 128:], turned[:, :128])
    return jnp.concatenate([even[:, :128], middle, turned[:, 128:]], axis=1)


def aligned(index, size):
    return index * size if isinstance(index, int) else pl.multiple_of(index * size, 16)


def line_mask(place, wide, first, count, limit, width):
    columns = place[2] + lax.broadcasted_iota(jnp.int32, (wide, 1), 0)
    inside = jnp.where((columns >= 0) & (columns < width), 1.0, 0.0)
    lines = []
    for i in range(count):
        line = first + i
        lines.append(inside * jnp.where((line >= 0) & (line < limit), 1.0, 0.0))
    return jnp.concatenate(lines, axis=0)


def store(even, odd, slot, values, height, wide):
    even[pl.ds(slot * (height * wide), height * wide), :] = values.astype(BF16)
    odd[pl.ds(slot * ((height - 2) * wide), (height - 2) * wide), :] = values[
        wide : (height - 1) * wide
    ].astype(BF16)


def taps(even, odd, begin, count, height, wide, dt, dy, lanes=slice(None)):
    inner = (height - 2) * wide
    if dy == 1:
        parts = [odd[pl.ds((begin + f + dt) * inner, inner), lanes] for f in range(count)]
    else:
        parts = [
            even[pl.ds((begin + f + dt) * height * wide + dy * wide, inner), lanes]
            for f in range(count)
        ]
    return jnp.concatenate(parts, axis=0)


def low_product(acc, even, odd, count, height, wide, weights, copies):
    rows = count * (height - 2) * wide
    channels = weights.shape[1]
    needed = [dx * channels // LANES for dx in range(3)]

    def column(n, carry):
        for copy, when in zip(copies, needed):
            pl.when(n == when)(copy.wait)
        lanes = pl.ds(pl.multiple_of(n * LANES, LANES), LANES)
        left = jnp.concatenate(
            [taps(even, odd, 0, count, height, wide, t // 3, t % 3) for t in range(9)], axis=1
        )
        right = weights[:, :, lanes].reshape(9 * channels, LANES)
        acc[n, 0:rows, :] = jnp.dot(left, right, preferred_element_type=F32)
        return carry

    lax.fori_loop(0, weights.shape[-1] // LANES, column, 0)


def low_sum(acc, start, size):
    rows = pl.ds(start, size)
    before = jnp.concatenate([acc[0, rows, :], acc[1, rows, 0:128]], axis=1)
    center = jnp.concatenate([acc[1, rows, 128:256], acc[2, rows, :]], axis=1)
    after = jnp.concatenate([acc[3, rows, :], acc[4, rows, 0:128]], axis=1)
    return center + pltpu.roll(before, 1, 0) + pltpu.roll(after, size - 1, 0)


def transposed_dot(left, right):
    return lax.dot_general(left, right, (((1,), (1,)), ((), ())), preferred_element_type=F32)


def split_frames(count):
    first = count // 4
    second = first + (count - first) // 2
    return (0, first), (first, second), (second, count)


def group_slots(group, groups):
    first, last = groups[group]
    return (0 if group == 0 else first + 2), last + 2


def grouped_taps(planes, groups, frames, height, wide, dt, dy):
    inner = (height - 2) * wide
    parts = []
    for f in frames:
        for group, (even, odd) in enumerate(planes):
            first, last = group_slots(group, groups)
            if first <= f + dt < last:
                slot = f + dt - first
                if dy == 1:
                    parts.append(odd[slot * inner : (slot + 1) * inner, :])
                else:
                    begin = slot * height * wide + dy * wide
                    parts.append(even[begin : begin + inner, :])
    return jnp.concatenate(parts, axis=0)


def high_column(n, acc, planes, groups, group, height, wide, weights):
    left = jnp.concatenate(
        [
            grouped_taps(planes, groups, range(*groups[group]), height, wide, t // 3, t % 3)
            for t in range(9)
        ],
        axis=1,
    )
    acc[n] = transposed_dot(left, weights[n * LANES : (n + 1) * LANES, :])


def high_sum(acc, start, size):
    rows = pl.ds(start, size)
    center = jnp.concatenate([acc[0, rows, :], acc[1, rows, 0:128]], axis=1)
    side = jnp.concatenate([acc[1, rows, 128:256], acc[2, rows, :]], axis=1)
    channels = center.shape[1]
    first = lax.broadcasted_iota(jnp.int32, (1, channels), 1) < channels // 2
    return center + jnp.where(first, pltpu.roll(side, 1, 0), pltpu.roll(side, size - 1, 0))


def pack_kernel(
    wide,
    tile,
    part,
    place,
    latent,
    arrived,
    one,
    two,
    time,
    three,
    four,
    mine,
    theirs,
    tiles,
    spread,
    low,
    high,
):
    section, col = place[0], place[1]
    width, channels = latent.shape[1:]
    half = three.shape[-1]
    empty = jnp.zeros((spread.shape[1] - width, channels), F32)

    def put(slot, values):
        spread[slot] = pltpu.roll(
            jnp.concatenate([values.astype(F32), empty], axis=0), HALO, 0
        )

    for i in range(2):
        put(2 * section + i, latent[i])
        put(2 * (1 - section) + i, arrived[i])
        put(4 + i, one[i])
        put(6 + i, two[i])
    for slot in range(8):
        for ref, which in ((mine, col), (theirs, 1 - col)):
            begin = pl.multiple_of(which * tile + section * part, 8)
            ref[slot] = spread[slot, pl.ds(begin, wide), :].astype(BF16)

    lines = [time[f, y].astype(F32) for f in range(2) for y in range(2)]
    for ref in (three, four):
        for f in range(2):
            for y in range(4):
                values = ref[f, y].astype(F32)
                low[...] = values[:, :128]
                high[:, 0 : half - 128] = values[:, 128:]
                count = values.shape[0] // 2
                even, odd = (
                    jnp.concatenate(
                        [lanes[pl.ds(o, count, stride=2), :] for lanes in (low, high)], axis=1
                    )
                    for o in range(2)
                )
                lines.append(merge(even, odd, half))
    for i, line in enumerate(lines):
        tiles[i] = line.astype(BF16)

    left = col == 0
    upper = lax.broadcasted_iota(jnp.int32, (8, 1), 0) < HALO
    blocks = []
    for i in range(0, len(lines), 2):
        one_line, two_line = lines[i], lines[i + 1]
        last = jnp.where(upper, pltpu.roll(one_line[-8:], HALO, 0), two_line[-8:])
        first = jnp.where(upper, one_line[:8], pltpu.roll(two_line[:8], HALO, 0))
        blocks.append(jnp.where(left, last, first))
    gap = jnp.zeros_like(blocks[0])
    count = wide // 8
    for i in range(theirs.shape[0] - 8):
        group = (blocks + [gap] * count)[i * count : (i + 1) * count]
        theirs[8 + i] = jnp.concatenate(group, axis=0).astype(BF16)


def pack(place, latent, arrived, one, two, time, three, four, wide, tile, part):
    width, channels = latent.shape[1:]
    vmem = pl.BlockSpec(memory_space=pltpu.VMEM)
    lines = 20
    extra = -(-lines * HALO // wide)
    return pl.pallas_call(
        functools.partial(pack_kernel, wide, tile, part),
        out_shape=[
            jax.ShapeDtypeStruct((8, wide, channels), BF16),
            jax.ShapeDtypeStruct((8 + extra, wide, channels), BF16),
            jax.ShapeDtypeStruct((lines, tile, channels), BF16),
        ],
        in_specs=[pl.BlockSpec(memory_space=pltpu.SMEM)] + [vmem] * 7,
        out_specs=[vmem] * 3,
        scratch_shapes=[
            pltpu.VMEM((8, width + 16, channels), F32),
            pltpu.VMEM((three.shape[2], 128), F32),
            pltpu.VMEM((three.shape[2], 128), F32),
        ],
        compiler_params=pltpu.CompilerParams(vmem_limit_bytes=60 * 1024 * 1024),
        name="pack",
    )(place, latent, arrived, one, two, time, three, four)


def stack_kernel(
    wide, place, mine, theirs, tiles, own, near, far, windows, tile_near, tile_far
):
    section, col = place[0], place[1]
    count = mine.shape[0] - 2
    own[0], own[1] = mine[...], theirs[0 : count + 2]
    parity = lax.rem(place[3], 2)
    for ref, y in ((near, 1 - parity), (far, parity)):
        ref[0:count], ref[count : 2 * count] = mine[0:count], theirs[0:count]
        here = lax.rem(y + col, 2) == 0
        ref[2 * count :] = jnp.where(here, mine[count:], theirs[count : count + 2])

    part = wide - 2 * HALO
    upper = lax.broadcasted_iota(jnp.int32, (8, 1), 0) < HALO
    groups = wide // 8
    for i in range(tiles.shape[0]):
        line = tiles[i].astype(F32)
        block = i // 2
        begin = block % groups * 8
        edge = theirs[count + 2 + block // groups].astype(F32)[begin : begin + 8]
        turned = pltpu.roll(edge, HALO, 0)
        before, after = (edge, turned) if i % 2 == 0 else (turned, edge)
        first = pltpu.roll(line, HALO, 0)[:wide]
        head = jnp.where(upper, jnp.where(col == 1, before, 0.0), first[:8])
        first = jnp.concatenate([head, first[8:]], axis=0)
        last = pltpu.roll(line, line.shape[0] - (part - HALO), 0)[:wide]
        tail = jnp.where(upper, last[-8:], jnp.where(col == 0, after, 0.0))
        last = jnp.concatenate([last[:-8], tail], axis=0)
        line = jnp.where(section == 0, first, last).astype(BF16)
        windows[i] = line
    is_even = parity == 0
    for base, start, count, depth in ((0, 0, 2, 2), (4, 4, 4, 2), (12, 8, 4, 1)):
        for f in range(2):
            for j in range(depth):
                slot = start + depth * f + j
                high = windows[base + count * f + j]
                low = windows[base + count * f + count - depth + j]
                tile_near[slot] = jnp.where(is_even, low, high)
                tile_far[slot] = jnp.where(is_even, high, low)


def stack(place, mine, theirs, tiles):
    units, wide, channels = mine.shape
    vmem = pl.BlockSpec(memory_space=pltpu.VMEM)
    lines = 2 * units - 2
    shapes = [(2, units), (lines,), (lines,), (tiles.shape[0],), (10,), (10,)]
    return pl.pallas_call(
        functools.partial(stack_kernel, wide),
        out_shape=[jax.ShapeDtypeStruct(shape + (wide, channels), BF16) for shape in shapes],
        in_specs=[pl.BlockSpec(memory_space=pltpu.SMEM)]
        + [vmem] * 3,
        out_specs=[vmem] * 6,
        compiler_params=pltpu.CompilerParams(vmem_limit_bytes=8 * 1024 * 1024),
        name="stack",
    )(place, mine, theirs, tiles)


def align_kernel(weight, out):
    half = weight.shape[0]
    chunk = 16
    tail = half - 128
    low = lax.broadcasted_iota(jnp.int32, (1, 128), 1) < tail

    def move(k, carry):
        here = aligned(k, chunk)
        none = jnp.zeros((chunk, 128), F32)
        for t in range(9):
            base = 3 * t * half
            first = base // 128 * 128
            last = min(first + 640, weight.shape[1])
            values = weight[pl.ds(here, chunk), first:last].astype(F32)
            if last < first + 640:
                values = jnp.concatenate(
                    [values[:, :512], jnp.concatenate([values[:, 512:], none[:, tail:]], axis=1)],
                    axis=1,
                )
            turned = pltpu.roll(values, 640 - tail, 1)
            tiles = [values[:, 128 * i : 128 * (i + 1)] for i in range(5)]
            moved = [turned[:, 128 * i : 128 * (i + 1)] for i in range(5)]
            if base == first:
                blocks = (
                    moved[1:4],
                    tiles[0:3],
                    [none, jnp.where(low, 0.0, moved[4]), moved[0]],
                    [tiles[3], jnp.where(low, tiles[4], 0.0), none],
                )
            else:
                blocks = (
                    tiles[2:5],
                    moved[0:3],
                    [none, jnp.where(low, 0.0, tiles[0]), tiles[1]],
                    [moved[3], jnp.where(low, moved[4], 0.0), none],
                )
            for n, block in enumerate(blocks):
                into = pl.ds(here + n * half, chunk)
                out[into, 2 * half * t : 2 * half * (t + 1)] = jnp.concatenate(
                    block, axis=1
                ).astype(BF16)
        return carry

    lax.fori_loop(0, half // chunk, move, 0)


def align_weights(weight):
    half = weight.shape[1]
    vmem = pl.BlockSpec(memory_space=pltpu.VMEM)
    return pl.pallas_call(
        align_kernel,
        out_shape=jax.ShapeDtypeStruct((4 * half, 18 * half), BF16),
        in_specs=[vmem],
        out_specs=vmem,
        compiler_params=pltpu.CompilerParams(vmem_limit_bytes=8 * 1024 * 1024),
        name="align_weights",
    )(weight.T)


def combine_kernel(weight, out):
    half = weight.shape[0]
    channels = weight.shape[1] // 9
    chunk = 16

    def combine(k, carry):
        rows = pl.ds(aligned(k, chunk), chunk)
        taken = [
            [
                weight[rows, (3 * dy + dx) * channels : (3 * dy + dx + 1) * channels].astype(F32)
                for dx in range(3)
            ]
            for dy in range(3)
        ]
        for slot, dys in enumerate(((0,), (1, 2), (0, 1), (2,))):
            line = [sum(taken[dy][dx] for dy in dys) for dx in range(3)]
            lanes = slice(slot % 2 * channels, (slot % 2 + 1) * channels)
            for n, block in enumerate((line[1] + line[2], line[0] + line[1], line[0], line[2])):
                into = pl.ds(aligned(k, chunk) + n * half, chunk)
                out[slot // 2, into, lanes] = block.astype(BF16)
        return carry

    lax.fori_loop(0, half // chunk, combine, 0)


def combine_weights(weight):
    channels = 2 * weight.shape[1]
    vmem = pl.BlockSpec(memory_space=pltpu.VMEM)
    return pl.pallas_call(
        combine_kernel,
        out_shape=jax.ShapeDtypeStruct((2, 2 * channels, 2 * channels), BF16),
        in_specs=[vmem],
        out_specs=vmem,
        compiler_params=pltpu.CompilerParams(vmem_limit_bytes=8 * 1024 * 1024),
        name="combine_weights",
    )(weight.T)


def weight_copies(source, target, sems, base):
    channels = source.shape[-1]
    return [
        pltpu.make_async_copy(
            source.at[:, dx], target.at[:, :, pl.ds(dx * channels, channels)], sems.at[base + dx]
        )
        for dx in range(3)
    ]


def first_kernel(
    wide,
    sizes,
    place,
    near,
    own,
    far,
    gains,
    weight_one,
    weight_two,
    later,
    out_ref,
    w1,
    w2,
    acc,
    x1e,
    x1o,
    x2e,
    x2o,
    sems,
):
    channels = own.shape[-1]
    frames = own.shape[1] - 4
    height, width = sizes
    col, row = place[1], place[3]
    units = frames + 2
    del later

    copies_one = weight_copies(weight_one, w1, sems, 0)
    copies_two = weight_copies(weight_two, w2, sems, 3)
    copies_one[0].start()
    copies_one[1].start()

    slots = [lax.rem(y + col, 2) for y in range(2)]

    is_even = lax.rem(row, 2) == 0

    def own_rows(index):
        return [own[slot, index].astype(F32) for slot in slots]

    def above(line):
        return jnp.where(is_even, far[line].astype(F32), near[line].astype(F32))

    def below(line):
        return jnp.where(is_even, near[line].astype(F32), far[line].astype(F32))

    def rows_of(index):
        first = [above(slot * units + index) for slot in slots]
        last = [below(slot * units + index) for slot in slots]
        return jnp.concatenate(first + own_rows(index) + last, axis=0)

    for f in range(2):
        store(x1e, x1o, f, rows_of(frames + f), 6, wide)
        first, last = above(2 * units + f), below(2 * units + f)
        values = jnp.concatenate([first] + own_rows(units + f) + [last], axis=0)
        store(x2e, x2o, f, values, 4, wide)

    def norm_one(f, carry):
        values = activate(rows_of(f), gains[0:1, :], 1.0)
        store(x1e, x1o, f + 2, values, 6, wide)
        return carry

    lax.fori_loop(0, frames, norm_one, 0)
    for copy in [copies_one[2]] + copies_two:
        copy.start()
    low_product(acc, x1e, x1o, frames, 6, wide, w1, copies_one)

    mask = line_mask(place, wide, 2 * row - 1, 4, height, width)

    def norm_two(f, carry):
        size = 4 * wide
        values = activate(low_sum(acc, aligned(f, size), size), gains[1:2, :], mask)
        store(x2e, x2o, f + 2, values, 4, wide)
        return carry

    lax.fori_loop(0, frames, norm_two, 0)
    low_product(acc, x2e, x2o, frames, 4, wide, w2, copies_two)

    def residual(f, carry):
        size = 2 * wide
        values = low_sum(acc, aligned(f, size), size) + jnp.concatenate(own_rows(f), axis=0)
        out_ref[f] = values.astype(BF16)
        return carry

    lax.fori_loop(0, frames, residual, 0)


def planes(slots, height, wide, channels):
    return [
        pltpu.VMEM((slots * height * wide, channels), BF16),
        pltpu.VMEM((slots * (height - 2) * wide, channels), BF16),
    ]


def first_block(place, pieces, gains, weight_one, weight_two, later, sizes):
    _, units, wide, channels = pieces[1].shape
    frames = units - 4
    slots = -(-3 * channels // LANES)
    vmem = pl.BlockSpec(memory_space=pltpu.VMEM)
    anywhere = pl.BlockSpec(memory_space=pl.ANY)
    return pl.pallas_call(
        functools.partial(first_kernel, wide, sizes),
        out_shape=jax.ShapeDtypeStruct((frames, 2 * wide, channels), BF16),
        in_specs=[pl.BlockSpec(memory_space=pltpu.SMEM)]
        + [vmem] * 4
        + [pl.BlockSpec(memory_space=pltpu.HBM)] * 2
        + [anywhere],
        out_specs=vmem,
        scratch_shapes=[
            pltpu.VMEM((9, channels, slots * LANES), BF16),
            pltpu.VMEM((9, channels, slots * LANES), BF16),
            pltpu.VMEM((slots, frames * 4 * wide, LANES), F32),
            *planes(frames + 2, 6, wide, channels),
            *planes(frames + 2, 4, wide, channels),
            pltpu.SemaphoreType.DMA((6,)),
        ],
        compiler_params=pltpu.CompilerParams(vmem_limit_bytes=50 * 1024 * 1024),
        cost_estimate=pl.CostEstimate(
            flops=2 * 27 * channels * channels * frames * 6 * wide,
            bytes_accessed=2 * 54 * channels * channels,
            transcendentals=0,
        ),
        name="first_block",
    )(place, *pieces, gains, weight_one, weight_two, later)


def second_kernel(
    wide,
    sizes,
    place,
    near,
    blocked,
    far,
    tile_near,
    windows,
    tile_far,
    gains,
    wt,
    wu,
    w3,
    w4,
    out_ref,
    acc,
    mixed,
    de,
    do,
    lifted_ref,
    *buffers,
):
    ups, threes, fours = buffers[0:3], buffers[3:6], buffers[6:9]
    planes_three = [buffers[9 + 2 * g : 11 + 2 * g] for g in range(3)]
    planes_four = [buffers[15 + 2 * g : 17 + 2 * g] for g in range(3)]
    channels = blocked.shape[-1]
    half = channels // 2
    size = 6 * wide
    frames = blocked.shape[0]
    count = 2 * frames
    groups = split_frames(count)
    height, width = sizes
    row = place[3]

    is_even = lax.rem(row, 2) == 0

    def chosen(when, one, other, index):
        return jnp.where(when, one[index].astype(F32), other[index].astype(F32))

    def cached(start, base, lines, depth, f):
        slots = [start + depth * f + i for i in range(depth)]
        parts = [chosen(is_even, tile_far, tile_near, slot) for slot in slots]
        parts += [windows[base + lines * f + i].astype(F32) for i in range(lines)]
        parts += [chosen(is_even, tile_near, tile_far, slot) for slot in slots]
        return jnp.concatenate(parts, axis=0)

    for f in range(2):
        mixed[f * size : (f + 1) * size, :] = cached(0, 0, 2, 2, f).astype(BF16)
    for f in range(frames):
        first, last = chosen(is_even, far, near, f), chosen(is_even, near, far, f)
        for i, values in enumerate((first.astype(BF16), blocked[f], last.astype(BF16))):
            begin = (f + 2) * size + i * 2 * wide
            mixed[begin : begin + 2 * wide, :] = values


    def mix(n, carry):
        lanes = pl.ds(pl.multiple_of(n * LANES, LANES), LANES)
        left = jnp.concatenate(
            [mixed[pl.ds(t * size, frames * size), :] for t in range(3)], axis=1
        )
        acc[n, 0 : frames * size, :] = jnp.dot(left, wt[:, lanes], preferred_element_type=F32)
        return carry

    lax.fori_loop(0, 2 * channels // LANES, mix, 0)
    mask_low = line_mask(place, wide, 2 * row - 2, 6, height, width)

    def double(t, carry):
        rows = pl.ds(aligned(t, size), size)
        first = jnp.concatenate([acc[0, rows, :], acc[1, rows, 0:128]], axis=1)
        second = jnp.concatenate([acc[1, rows, 128:256], acc[2, rows, :]], axis=1)
        store(de, do, 2 * t, first * mask_low, 6, wide)
        store(de, do, 2 * t + 1, second * mask_low, 6, wide)
        return carry

    lax.fori_loop(0, frames, double, 0)


    for f in range(2):
        store(*planes_three[0], f, cached(4, 4, 4, 2, f), 8, wide)
        store(*planes_four[0], f, cached(8, 12, 4, 1, f), 6, wide)
    gain3, gain4 = gains[2:3, :], gains[3:4, :]
    mask_three = line_mask(place, wide, 4 * row - 2, 8, 2 * height, width)
    mask_four = mask_three[wide : 7 * wide]
    part = 4 * wide

    def enlarge(group, n):
        first, last = groups[group]
        lanes = slice(n * LANES, (n + 1) * LANES)
        rows = (last - first) * part
        for py in range(2):
            left = jnp.concatenate(
                [
                    taps(de, do, first, last - first, 6, wide, 0, py),
                    taps(de, do, first, last - first, 6, wide, 0, py + 1),
                ],
                axis=1,
            )
            ups[group][n, py * rows : (py + 1) * rows, :] = transposed_dot(left, wu[py, lanes, :])

    def norm_three(group, f):
        first, last = groups[group]
        values = [
            high_sum(ups[group], aligned(f + py * (last - first), part), part)
            .astype(BF16)
            .astype(F32)
            for py in range(2)
        ]
        lifted = jnp.concatenate(
            [values[h % 2][(h // 2) * wide : (h // 2 + 1) * wide] for h in range(8)], axis=0
        )
        lifted_ref[pl.ds(aligned(f + first, part), part), :] = lifted[2 * wide : 6 * wide]
        slot = f + (2 if group == 0 else 0)
        store(*planes_three[group], slot, activate_pairs(lifted, gain3, mask_three), 8, wide)

    def norm_four(group, f):
        values = high_sum(threes[group], aligned(f, size), size)
        slot = f + (2 if group == 0 else 0)
        store(*planes_four[group], slot, activate_pairs(values, gain4, mask_four), 6, wide)

    def finish(group, f):
        first = groups[group][0]
        rows = pl.ds(aligned(f + first, part), part)
        values = high_sum(fours[group], aligned(f, part), part) + lifted_ref[rows, :]
        values = pltpu.roll(values, part - HALO, 0)
        for y in range(4):
            inner = wide - 2 * HALO
            out_ref[f + first, y] = values[y * wide : y * wide + inner].astype(BF16)

    def third(group, n):
        high_column(n, threes[group], planes_three, groups, group, 8, wide, w3)

    def fourth(group, n):
        high_column(n, fours[group], planes_four, groups, group, 6, wide, w4)

    for product, vector in (
        ((enlarge, 0), None),
        ((enlarge, 1), (norm_three, 0)),
        ((enlarge, 2), (norm_three, 1)),
        ((third, 0), (norm_three, 2)),
        ((third, 1), (norm_four, 0)),
        ((third, 2), (norm_four, 1)),
        ((fourth, 0), (norm_four, 2)),
        ((fourth, 1), (finish, 0)),
        ((fourth, 2), (finish, 1)),
        (None, (finish, 2)),
    ):
        for n in range(max(2 * channels // LANES, *(last - first for first, last in groups))):
            if product is not None and n < 2 * channels // LANES:
                product[0](product[1], n)
            if vector is not None and n < groups[vector[1]][1] - groups[vector[1]][0]:
                vector[0](vector[1], n)


def second_block(place, pieces, tiles, gains, weights, sizes, wide):
    frames, _, channels = pieces[0].shape
    count = 2 * frames
    groups = split_frames(count)
    sizes_of = [last - first for first, last in groups]
    slots = [last - first for first, last in (group_slots(g, groups) for g in range(3))]
    vmem = pl.BlockSpec(memory_space=pltpu.VMEM)
    return pl.pallas_call(
        functools.partial(second_kernel, wide, sizes),
        out_shape=jax.ShapeDtypeStruct((count, 4, wide - 2 * HALO, channels), BF16),
        in_specs=[pl.BlockSpec(memory_space=pltpu.SMEM)]
        + [vmem] * 11,
        out_specs=vmem,
        scratch_shapes=[
            pltpu.VMEM((3, frames * 6 * wide, LANES), F32),
            pltpu.VMEM(((frames + 2) * 6 * wide, channels), BF16),
            *planes(count, 6, wide, channels),
            pltpu.VMEM((count * 4 * wide, channels), F32),
            *(pltpu.VMEM((3, n * 8 * wide, LANES), F32) for n in sizes_of),
            *(pltpu.VMEM((3, n * 6 * wide, LANES), F32) for n in sizes_of),
            *(pltpu.VMEM((3, n * 4 * wide, LANES), F32) for n in sizes_of),
            *(ref for n in slots for ref in planes(n, 8, wide, channels)),
            *(ref for n in slots for ref in planes(n, 6, wide, channels)),
        ],
        compiler_params=pltpu.CompilerParams(vmem_limit_bytes=34 * 1024 * 1024),
        name="second_block",
    )(place, *pieces, *tiles, gains, *weights)


def body(
    latent,
    cache_one,
    cache_two,
    cache_time,
    cache_three,
    cache_four,
    gain_one,
    gain_two,
    gain_three,
    gain_four,
    weight_one,
    weight_two,
    weight_time,
    weight_upsample,
    weight_three,
    weight_four,
):
    section, row, col = (lax.axis_index(name) for name in ("section", "rows", "cols"))
    sections, row_count, col_count = (lax.axis_size(name) for name in ("section", "rows", "cols"))
    width, channels = latent.shape[2:]
    tile = width // col_count
    part = tile // sections
    wide = part + 2 * HALO
    half = weight_three.shape[1]
    sizes = (2 * row_count, width)
    place = jnp.stack([section, col, col * tile + section * part - HALO, row]).astype(jnp.int32)

    gains = jnp.stack([gain_one, gain_two, jnp.tile(gain_three, 2), jnp.tile(gain_four, 2)])

    latent = latent.reshape(latent.shape[0], width, channels)
    arrived = swapped(latent, "section")
    mine, theirs, tiles = pack(
        place,
        latent,
        arrived,
        cache_one[:, 0],
        cache_two[:, 0],
        cache_time,
        cache_three,
        cache_four,
        wide,
        tile,
        part,
    )
    own, near, far, windows, tile_near, tile_far = stack(
        place, mine, swapped(theirs, "cols"), tiles
    )
    pieces = [paired(near, "rows", 0), own, paired(far, "rows", 1)]
    weight_upsample, weight_three, own = lax.optimization_barrier(
        (weight_upsample, weight_three, own)
    )
    weight_upsample = combine_weights(weight_upsample)
    weight_three = align_weights(weight_three)
    tile_near, tile_far, weight_upsample, weight_three = lax.optimization_barrier(
        (tile_near, tile_far, weight_upsample, weight_three)
    )
    tiles = [paired(tile_near, "rows", 0), windows, paired(tile_far, "rows", 1)]
    blocked = first_block(
        place,
        pieces,
        gains,
        weight_one.reshape(9, 3, channels, channels),
        weight_two.reshape(9, 3, channels, channels),
        weight_upsample,
        sizes,
    )
    blocks = [paired(blocked, "rows", 0), blocked, paired(blocked, "rows", 1)]
    weight_four, _ = lax.optimization_barrier((weight_four, blocked))
    weight_four = align_weights(weight_four)
    frames = second_block(
        place,
        blocks,
        tiles,
        gains,
        (weight_time, weight_upsample, weight_three, weight_four),
        sizes,
        wide,
    )
    count = frames.shape[0] // sections
    given = lax.dynamic_slice_in_dim(frames, (1 - section) * count, count, 0)
    kept = lax.dynamic_slice_in_dim(frames, section * count, count, 0)
    arrived = swapped(given, "section")
    low = section == 0
    joined = jnp.concatenate(
        [jnp.where(low, kept, arrived), jnp.where(low, arrived, kept)], axis=2
    )
    return joined.reshape(count, 4, 2 * tile, half)


def solution(mesh):
    placed = (
        P("section", ("rows", "cols"), None, None),
        P(None, ("rows", "cols"), None, None),
        P(None, ("rows", "cols"), None, None),
        P(None, "rows", "cols", None),
        P(None, "rows", "cols", None),
        P(None, "rows", "cols", None),
    ) + (P(),) * 10
    return jax.shard_map(
        body,
        mesh=mesh,
        in_specs=placed,
        out_specs=P("section", "rows", "cols", None),
        check_vma=False,
    )
```
